32 devices in a mesh: ctx: 8 (over y, x, core), fsdp: 4 (over z).
Axes of the slice: x: 2, y: 2, z: 4, core: 2. Of those that a mesh axis runs over, the one named last changes fastest.
Arguments:
- hidden_in: bfloat16 [4, 2048, 1536], P('fsdp', 'ctx'), may hold values from -6 to 6
- positions: int32 [4, 2048], P('fsdp', 'ctx'), may hold values from 0 to 6142, as said below
- attn_gain: bfloat16 [1536], P('fsdp'), may hold values from 0.5 to 1.5
- w_query: bfloat16 [1536, 1536], P('fsdp'), may hold values from -0.15625 to 0.15625
- key_projection: bfloat16 [1536, 768], P('fsdp'), may hold values from -0.15625 to 0.15625
- value_projection: bfloat16 [1536, 768], P('fsdp'), may hold values from -0.15625 to 0.15625
- w_out: bfloat16 [1536, 1536], P('fsdp'), may hold values from -1.75 to 1.75
- mlp_gain: bfloat16 [1536], P('fsdp'), may hold values from 0.5 to 1.5
- w_gate: bfloat16 [1536, 4096], P('fsdp'), may hold values from -0.15625 to 0.15625
- w_up: bfloat16 [1536, 4096], P('fsdp'), may hold values from -0.15625 to 0.15625
- w_down: bfloat16 [4096, 1536], P('fsdp'), may hold values from -0.09375 to 0.09375
- out_grad: bfloat16 [4, 2048, 1536], P('fsdp', 'ctx'), may hold values from -6 to 6
Outputs:
- layer_out: bfloat16 [4, 2048, 1536], P('fsdp', 'ctx')
- input_grad: bfloat16 [4, 2048, 1536], P('fsdp', 'ctx')
- attn_gain_grad: float32 [1536], P('fsdp')
- w_query_grad: float32 [1536, 1536], P('fsdp')
- w_key_grad: float32 [1536, 768], P('fsdp')
- w_value_grad: float32 [1536, 768], P('fsdp')
- w_out_grad: float32 [1536, 1536], P('fsdp')
- mlp_gain_grad: float32 [1536], P('fsdp')
- w_gate_grad: float32 [1536, 4096], P('fsdp')
- w_up_grad: float32 [1536, 4096], P('fsdp')
- w_down_grad: float32 [4096, 1536], P('fsdp')
The draws below stay inside these ranges and needn't reach their ends.
Inputs may be any that keep to these rules, and one draw needn't show every extreme that they name: For each sequence the positions are s, s + 1, ..., s + 2047, each once, with a start s of 0 to 4095; one sequence starts at 0 and another at 4095; every device along ctx holds two blocks of 128 consecutive positions whose block numbers counted from s add up to 15, in either order.
All inputs are finite; a program needn't handle non-finite values.
Results may differ from the reference program's by a relative error of at most 0.023.
Values may be sent and summed in bfloat16 or wider, within the bound.
A program may use at most 448 MiB of HBM per device.

```python
import jax
import jax.numpy as jnp
from jax import lax

MODEL_WIDTH = 1536
QUERY_HEADS = 16
KEY_VALUE_HEADS = 8
HEAD_SIZE = 96
FF = 4096
BLK = 128
SEQ_LEN = 2048
SEQS = 4


def draw_positions(key, part):
    key = jax.random.fold_in(key, 11)
    order_key, flip_key, start_key, pick_key = jax.random.split(key, 4)
    blocks = SEQ_LEN // BLK
    pairs = blocks // 2
    pair_of_rank = jax.vmap(lambda item: jax.random.permutation(item, pairs))(jax.random.split(order_key, SEQS))
    flips = jax.random.randint(flip_key, (SEQS, pairs), 0, 2)
    mirror = blocks - 1 - pair_of_rank
    first = jnp.where(flips == 1, mirror, pair_of_rank)
    second = jnp.where(flips == 1, pair_of_rank, mirror)
    dealt = jnp.stack([first, second], -1).reshape(SEQS, blocks)
    picked = jax.random.permutation(pick_key, SEQS)
    drawn = jax.random.randint(start_key, (SEQS,), 0, 4096)
    starts = jnp.where(picked == 0, 0, jnp.where(picked == 1, 4095, drawn)).astype(jnp.int32)[:, None, None]
    offsets = jnp.arange(BLK, dtype=jnp.int32)[None, None, :]
    return (starts + dealt[:, :, None] * BLK + offsets).reshape(SEQS, SEQ_LEN).astype(jnp.int32)


def block_levels(stream_key, extent, shards, least, top_value):
    def one(axis_at, shards_of):
        heights = jax.random.uniform(jax.random.fold_in(jax.random.fold_in(stream_key, 6), axis_at), (shards_of,), jnp.float32, least / len(shards), top_value / len(shards))
        return jnp.repeat(jnp.exp(heights), extent[axis_at] // shards_of).reshape((-1,) + (1,) * (len(extent) - axis_at - 1))

    factor_of = one(*shards[0])
    for cut in shards[1:]:
        factor_of = factor_of * one(*cut)
    return factor_of


def centred(own_key, extent, spread, bound, cuts=(), kind=jnp.bfloat16):
    values = jax.random.normal(own_key, extent, jnp.float32) * spread
    if len(cuts) > 0:
        values = block_levels(own_key, extent, cuts, -0.22, 0.18) * values
    return jnp.clip(values, min=-bound, max=bound).astype(kind)


def setup_inputs(seed: int = 0) -> dict:
    key_of = jax.random.split(jax.random.key(seed), 13)
    hidden_in = centred(key_of[0], (SEQS, SEQ_LEN, MODEL_WIDTH), 1.0, 6.0, ((0, 4), (1, 8)))
    positions = draw_positions(jax.random.fold_in(key_of[12], 71), 0)
    attn_gain = jnp.clip(1.0 + 0.1 * jax.random.normal(key_of[2], (MODEL_WIDTH,), jnp.float32), 0.5, 1.5).astype(jnp.bfloat16)
    w_query = centred(key_of[3], (MODEL_WIDTH, QUERY_HEADS * HEAD_SIZE), MODEL_WIDTH ** -0.5, 0.15625, ((0, 4),))
    key_projection = centred(key_of[4], (MODEL_WIDTH, KEY_VALUE_HEADS * HEAD_SIZE), MODEL_WIDTH ** -0.5, 0.15625, ((0, 4),))
    value_projection = centred(key_of[5], (MODEL_WIDTH, KEY_VALUE_HEADS * HEAD_SIZE), MODEL_WIDTH ** -0.5, 0.15625, ((0, 4),))
    w_out = centred(key_of[6], (QUERY_HEADS * HEAD_SIZE, MODEL_WIDTH), (max(1, QUERY_HEADS * HEAD_SIZE * 16 // SEQ_LEN)) ** -0.5, 1.75, ((0, 4),))
    mlp_gain = jnp.clip(1.0 + 0.1 * jax.random.normal(key_of[7], (MODEL_WIDTH,), jnp.float32), 0.5, 1.5).astype(jnp.bfloat16)
    w_gate = centred(key_of[8], (MODEL_WIDTH, FF), MODEL_WIDTH ** -0.5, 0.15625, ((0, 4),))
    w_up = centred(key_of[9], (MODEL_WIDTH, FF), MODEL_WIDTH ** -0.5, 0.15625, ((0, 4),))
    w_down = centred(key_of[10], (FF, MODEL_WIDTH), FF ** -0.5, 0.09375, ((0, 4),))
    out_grad = centred(key_of[11], (SEQS, SEQ_LEN, MODEL_WIDTH), 1.0, 6.0, ((0, 4), (1, 8)))
    return {"hidden_in": hidden_in, "positions": positions, "attn_gain": attn_gain, "w_query": w_query, "key_projection": key_projection, "value_projection": value_projection, "w_out": w_out, "mlp_gain": mlp_gain, "w_gate": w_gate, "w_up": w_up, "w_down": w_down, "out_grad": out_grad}


EPS = 1e-05
THETA = 100000.0
HIGH = lax.Precision.HIGHEST

@jax.custom_vjp
def reduced_precision(v):
    return lax.optimization_barrier(v.astype(jnp.bfloat16)).astype(jnp.float32)

@jax.custom_vjp
def reduced_precision_backward(v):
    return v

def low_keep(v):
    return (reduced_precision(v), None)

def low_pass(kept, grad):
    return (grad,)

def back_keep(v):
    return (v, None)

def back_low(kept, grad):
    return (reduced_precision(grad),)
reduced_precision.defvjp(low_keep, low_pass)
reduced_precision_backward.defvjp(back_keep, back_low)

def matrix_product(left, right):
    return jnp.dot(left, right, precision=HIGH, preferred_element_type=jnp.float32)

def rotary_embed(value_rows, token_position):
    half = value_rows.shape[-1] // 2
    freq = THETA ** (-(jnp.arange(half, dtype=jnp.float32) * 2.0 / value_rows.shape[-1]))
    angle = token_position.astype(jnp.float32)[:, None] * freq[None, :]
    cosine_table = jnp.cos(angle)[:, None, :]
    sine_table = jnp.sin(angle)[:, None, :]
    first = value_rows[..., :half]
    second = value_rows[..., half:]
    return jnp.concatenate([first * cosine_table - second * sine_table, second * cosine_table + first * sine_table], -1)

def rms_norm(value_rows, gain):
    return value_rows * lax.rsqrt(lax.optimization_barrier(jnp.mean(value_rows * value_rows, -1, keepdims=True)) + EPS) * gain

def one_sequence(params, hidden, token_position):
    gain_one, query_w, key_matrix, value_matrix, out_w, gain_two, gate_w, up_w, down_w = params
    local_length = hidden.shape[0]
    query_groups = QUERY_HEADS // KEY_VALUE_HEADS
    first_normed = reduced_precision(rms_norm(hidden, gain_one))
    query_rows = reduced_precision(rotary_embed(reduced_precision_backward(matrix_product(first_normed, query_w)).reshape(local_length, QUERY_HEADS, HEAD_SIZE), token_position))
    query_rows = query_rows.reshape(local_length, KEY_VALUE_HEADS, query_groups, HEAD_SIZE)
    key_rows = reduced_precision(rotary_embed(reduced_precision_backward(matrix_product(first_normed, key_matrix)).reshape(local_length, KEY_VALUE_HEADS, HEAD_SIZE), token_position))
    value_rows = reduced_precision(reduced_precision_backward(matrix_product(first_normed, value_matrix))).reshape(local_length, KEY_VALUE_HEADS, HEAD_SIZE)
    rows_per_block = min(512, local_length)

    def attend_blocks(inputs):
        query_block, query_pos = inputs
        scores = jnp.einsum('tkgd,nkd->kgtn', query_block, key_rows, precision=HIGH) * HEAD_SIZE ** (-0.5)
        scores = reduced_precision_backward(scores)
        visible = query_pos[None, None, :, None] >= token_position[None, None, None, :]
        scores = jnp.where(visible, scores, -jnp.inf)
        top = lax.optimization_barrier(jnp.max(scores, -1, keepdims=True))
        weights = jnp.exp(scores - top)
        probs = reduced_precision(weights / lax.optimization_barrier(jnp.sum(weights, -1, keepdims=True)))
        return jnp.einsum('kgtn,nkd->tkgd', probs, value_rows, precision=HIGH)
    attended_output = lax.map(jax.checkpoint(attend_blocks), (query_rows.reshape(local_length // rows_per_block, rows_per_block, KEY_VALUE_HEADS, query_groups, HEAD_SIZE), token_position.reshape(local_length // rows_per_block, rows_per_block)))
    attended_output = reduced_precision(reduced_precision_backward(attended_output.reshape(local_length, QUERY_HEADS * HEAD_SIZE)))
    mixed = hidden + reduced_precision_backward(matrix_product(attended_output, out_w))
    normed_two = reduced_precision(rms_norm(mixed, gain_two))
    gate = reduced_precision_backward(matrix_product(normed_two, gate_w))
    up = reduced_precision_backward(matrix_product(normed_two, up_w))
    active = reduced_precision(jax.nn.silu(gate) * up)
    return mixed + reduced_precision_backward(matrix_product(active, down_w))

def reference(hidden_in, positions, attn_gain, w_query, key_projection, value_projection, w_out, mlp_gain, w_gate, w_up, w_down, out_grad):
    params = (attn_gain.astype(jnp.float32), w_query.astype(jnp.float32), key_projection.astype(jnp.float32), value_projection.astype(jnp.float32), w_out.astype(jnp.float32), mlp_gain.astype(jnp.float32), w_gate.astype(jnp.float32), w_up.astype(jnp.float32), w_down.astype(jnp.float32))
    inputs = hidden_in.astype(jnp.float32)

    def forward(weights, hidden_all):
        return lax.map(lambda item: one_sequence(weights, item[0], item[1]), (hidden_all, positions))
    result, pull = jax.vjp(forward, params, inputs)
    weight_grads, input_grads = pull(out_grad.astype(jnp.float32))
    return (result.astype(jnp.bfloat16), input_grads.astype(jnp.bfloat16), weight_grads[0], weight_grads[1], weight_grads[2], weight_grads[3], weight_grads[4], weight_grads[5], weight_grads[6], weight_grads[7], weight_grads[8])
```

```python
import functools
import math

import jax
import jax.numpy as jnp
from jax import lax
from jax.experimental import pallas as pl
from jax.experimental.pallas import tpu as pltpu
from jax.sharding import PartitionSpec as P

QUERY_HEADS = 16
KEY_VALUE_HEADS = 8
HEAD_SIZE = 96


EPS = 1e-05
THETA = 100000.0


def tables(token_position):
    half = HEAD_SIZE // 2
    freq = THETA ** (-(jnp.arange(half, dtype=jnp.float32) * 2.0 / HEAD_SIZE))
    angle = token_position.astype(jnp.float32)[:, None] * freq[None, :]
    return (jnp.cos(angle)[:, None, :], jnp.sin(angle)[:, None, :])


def rotary_embed(value_rows, cosine_table, sine_table):
    half = value_rows.shape[-1] // 2
    first = value_rows[..., :half]
    second = value_rows[..., half:]
    return jnp.concatenate(
        [first * cosine_table - second * sine_table, second * cosine_table + first * sine_table], -1
    )


def rotary_embed_backward(grads, cosine_table, sine_table):
    half = grads.shape[-1] // 2
    first = grads[..., :half]
    second = grads[..., half:]
    return jnp.concatenate(
        [first * cosine_table + second * sine_table, second * cosine_table - first * sine_table], -1
    )


def norm_forward(hidden, gain):
    return (
        hidden
        * lax.rsqrt(jnp.mean(hidden * hidden, -1, keepdims=True) + EPS)
        * gain.astype(jnp.float32)
    )


def norm_back(hidden, gain, grad):
    factor = lax.rsqrt(jnp.mean(hidden * hidden, -1, keepdims=True) + EPS)
    scaled = grad * gain.astype(jnp.float32)
    hidden_grad = factor * scaled - hidden * factor * factor * factor * jnp.mean(
        scaled * hidden, -1, keepdims=True
    )
    gain_grad = jnp.sum(grad * hidden * factor, 0)
    return (hidden_grad, gain_grad)


def dot_first(left, right):
    return lax.dot_general(
        left, right, (((0,), (0,)), ((), ())), preferred_element_type=jnp.float32
    )


def dot_last(left, right):
    return lax.dot_general(
        left, right, (((1,), (1,)), ((), ())), preferred_element_type=jnp.float32
    )


def over_blocks(step_fn, carry, arrays):
    block_count = arrays[0].shape[0]
    size = math.gcd(block_count, 512)
    parts = block_count // size
    shaped = tuple((item.reshape((parts, size) + item.shape[1:]) for item in arrays))

    def advance(state, inputs):
        index, pieces = inputs
        return (step_fn(state, pieces, index * size), None)

    final, unused = lax.scan(advance, carry, (jnp.arange(parts, dtype=jnp.int32), shaped))
    return final


def per_device(
    hidden_in,
    positions,
    attn_gain,
    w_query,
    key_projection,
    value_projection,
    w_out,
    mlp_gain,
    w_gate,
    w_up,
    w_down,
    out_grad,
):
    hidden = hidden_in[0].astype(jnp.float32)
    local_rows = hidden.shape[0]
    query_pos = positions[0]
    query_groups = QUERY_HEADS // KEY_VALUE_HEADS
    scale = HEAD_SIZE ** (-0.5)
    cosine_table, sine_table = tables(query_pos)
    attn_set = (
        lax.all_gather(attn_gain, "fsdp", axis=0, tiled=True),
        lax.all_gather(w_query, "fsdp", axis=0, tiled=True),
        lax.all_gather(key_projection, "fsdp", axis=0, tiled=True),
        lax.all_gather(value_projection, "fsdp", axis=0, tiled=True),
        lax.all_gather(w_out, "fsdp", axis=0, tiled=True),
    )
    gain_one, query_w, key_matrix, value_matrix, out_w = attn_set
    first_normed = norm_forward(hidden, gain_one).astype(jnp.bfloat16)
    query_raw = jnp.dot(first_normed, query_w, preferred_element_type=jnp.float32)
    unrotated_key = jnp.dot(first_normed, key_matrix, preferred_element_type=jnp.float32)
    value_raw = jnp.dot(first_normed, value_matrix, preferred_element_type=jnp.float32)
    query_rows = (
        rotary_embed(
            query_raw.reshape(local_rows, QUERY_HEADS, HEAD_SIZE), cosine_table, sine_table
        )
        .astype(jnp.bfloat16)
        .reshape(local_rows, KEY_VALUE_HEADS, query_groups, HEAD_SIZE)
    )
    keys_flat = (
        rotary_embed(
            unrotated_key.reshape(local_rows, KEY_VALUE_HEADS, HEAD_SIZE), cosine_table, sine_table
        )
        .astype(jnp.bfloat16)
        .reshape(local_rows, KEY_VALUE_HEADS * HEAD_SIZE)
    )
    values_flat = value_raw.astype(jnp.bfloat16)
    key_pos_all = lax.all_gather(query_pos, "ctx", axis=0, tiled=True)
    sequence_length = key_pos_all.shape[0]

    def masked_scores(partial_keys, first):
        block_count = partial_keys.shape[0]
        key_pos = lax.dynamic_slice_in_dim(key_pos_all, first, block_count)
        scores = (
            jnp.einsum(
                "tkgd,nkd->kgtn",
                query_rows,
                partial_keys.reshape(block_count, KEY_VALUE_HEADS, HEAD_SIZE),
                preferred_element_type=jnp.float32,
            )
            * scale
        )
        visible = key_pos[None, None, None, :] <= query_pos[None, None, :, None]
        return jnp.where(visible, scores, -jnp.inf)

    def forward_part(carry, part, first):
        top, denom, accum = carry
        partial_keys, partial_values = part
        block_count = partial_keys.shape[0]
        scores = masked_scores(partial_keys, first)
        new_top = jnp.maximum(top, jnp.max(scores, -1))
        weights = jnp.exp(scores - new_top[..., None])
        factor = jnp.exp(top - new_top)
        denom = denom * factor + jnp.sum(weights, -1)
        accum = accum * factor[..., None] + jnp.einsum(
            "kgtn,nkd->kgtd",
            weights.astype(jnp.bfloat16),
            partial_values.reshape(block_count, KEY_VALUE_HEADS, HEAD_SIZE),
            preferred_element_type=jnp.float32,
        )
        return (new_top, denom, accum)

    start_state = (
        jnp.full((KEY_VALUE_HEADS, query_groups, local_rows), -1e30, jnp.float32),
        jnp.zeros((KEY_VALUE_HEADS, query_groups, local_rows), jnp.float32),
        jnp.zeros((KEY_VALUE_HEADS, query_groups, local_rows, HEAD_SIZE), jnp.float32),
    )
    top, denom, accum = over_blocks(
        forward_part,
        start_state,
        (
            lax.all_gather(keys_flat, "ctx", axis=0, tiled=True),
            lax.all_gather(values_flat, "ctx", axis=0, tiled=True),
        ),
    )
    attended_output = accum / denom[..., None]
    log_total = top + jnp.log(denom)
    attended_low = (
        attended_output.transpose(2, 0, 1, 3)
        .reshape(local_rows, QUERY_HEADS * HEAD_SIZE)
        .astype(jnp.bfloat16)
    )
    mixed = hidden + jnp.dot(attended_low, out_w, preferred_element_type=jnp.float32)
    mlp_set = (
        lax.all_gather(mlp_gain, "fsdp", axis=0, tiled=True),
        lax.all_gather(w_gate, "fsdp", axis=0, tiled=True),
        lax.all_gather(w_up, "fsdp", axis=0, tiled=True),
        lax.all_gather(w_down, "fsdp", axis=0, tiled=True),
    )
    gain_two, gate_w, up_w, down_w = mlp_set
    normed_two = norm_forward(mixed, gain_two).astype(jnp.bfloat16)
    gate = jnp.dot(normed_two, gate_w, preferred_element_type=jnp.float32)
    up = jnp.dot(normed_two, up_w, preferred_element_type=jnp.float32)
    sigma = jax.nn.sigmoid(gate)
    active = (gate * sigma * up).astype(jnp.bfloat16)
    result = mixed + jnp.dot(active, down_w, preferred_element_type=jnp.float32)
    layer_out = result.astype(jnp.bfloat16)[None]
    grad_low = out_grad[0]
    grad_out = grad_low.astype(jnp.float32)
    gain_back, gate_back, up_back, down_back = (
        lax.all_gather(mlp_gain, "fsdp", axis=0, tiled=True),
        lax.all_gather(w_gate, "fsdp", axis=0, tiled=True),
        lax.all_gather(w_up, "fsdp", axis=0, tiled=True),
        lax.all_gather(w_down, "fsdp", axis=0, tiled=True),
    )
    down_grad = dot_first(active, grad_low)
    active_grad = dot_last(grad_low, down_back)
    gate_grad = (active_grad * up * sigma * (1.0 + gate * (1.0 - sigma))).astype(jnp.bfloat16)
    up_grad = (active_grad * gate * sigma).astype(jnp.bfloat16)
    gate_wgrad = dot_first(normed_two, gate_grad)
    up_wgrad = dot_first(normed_two, up_grad)
    normed_two_grad = dot_last(gate_grad, gate_back) + dot_last(up_grad, up_back)
    mixed_part, gain_two_grad = norm_back(mixed, gain_back, normed_two_grad)
    mixed_grad = grad_out + mixed_part
    mlp_shards = (
        lax.psum_scatter(
            gain_two_grad.astype(jnp.bfloat16), "fsdp", scatter_dimension=0, tiled=True
        ).astype(jnp.float32),
        lax.psum_scatter(
            gate_wgrad.astype(jnp.bfloat16), "fsdp", scatter_dimension=0, tiled=True
        ).astype(jnp.float32),
        lax.psum_scatter(
            up_wgrad.astype(jnp.bfloat16), "fsdp", scatter_dimension=0, tiled=True
        ).astype(jnp.float32),
        lax.psum_scatter(
            down_grad.astype(jnp.bfloat16), "fsdp", scatter_dimension=0, tiled=True
        ).astype(jnp.float32),
    )
    gain_first, query_back, key_back, value_back, out_back = (
        lax.all_gather(attn_gain, "fsdp", axis=0, tiled=True),
        lax.all_gather(w_query, "fsdp", axis=0, tiled=True),
        lax.all_gather(key_projection, "fsdp", axis=0, tiled=True),
        lax.all_gather(value_projection, "fsdp", axis=0, tiled=True),
        lax.all_gather(w_out, "fsdp", axis=0, tiled=True),
    )
    branch_grad = mixed_grad.astype(jnp.bfloat16)
    out_wgrad = dot_first(attended_low, branch_grad)
    attended_grad = (
        dot_last(branch_grad, out_back)
        .astype(jnp.bfloat16)
        .reshape(local_rows, KEY_VALUE_HEADS, query_groups, HEAD_SIZE)
        .transpose(1, 2, 0, 3)
    )
    delta = jnp.sum(attended_grad.astype(jnp.float32) * attended_output, -1)

    def backward_part(carry, part, first):
        query_acc, key_value_acc = carry
        partial_keys, partial_values = part
        block_count = partial_keys.shape[0]
        probs = jnp.exp(masked_scores(partial_keys, first) - log_total[..., None])
        gradient_of_value = jnp.einsum(
            "kgtn,kgtd->nkd",
            probs.astype(jnp.bfloat16),
            attended_grad,
            preferred_element_type=jnp.float32,
        )
        prob_grad = jnp.einsum(
            "kgtd,nkd->kgtn",
            attended_grad,
            partial_values.reshape(block_count, KEY_VALUE_HEADS, HEAD_SIZE),
            preferred_element_type=jnp.float32,
        )
        score_grad = (probs * (prob_grad - delta[..., None])).astype(jnp.bfloat16)
        query_acc = (
            query_acc
            + jnp.einsum(
                "kgtn,nkd->kgtd",
                score_grad,
                partial_keys.reshape(block_count, KEY_VALUE_HEADS, HEAD_SIZE),
                preferred_element_type=jnp.float32,
            )
            * scale
        )
        gradient_of_key = (
            jnp.einsum("kgtn,tkgd->nkd", score_grad, query_rows, preferred_element_type=jnp.float32)
            * scale
        )
        joined = jnp.concatenate(
            [
                gradient_of_key.reshape(block_count, KEY_VALUE_HEADS * HEAD_SIZE),
                gradient_of_value.reshape(block_count, KEY_VALUE_HEADS * HEAD_SIZE),
            ],
            1,
        )
        key_value_acc = lax.dynamic_update_slice_in_dim(key_value_acc, joined, first, 0)
        return (query_acc, key_value_acc)

    back_state = (
        jnp.zeros((KEY_VALUE_HEADS, query_groups, local_rows, HEAD_SIZE), jnp.float32),
        jnp.zeros((sequence_length, 2 * KEY_VALUE_HEADS * HEAD_SIZE), jnp.float32),
    )
    query_acc, key_value_acc = over_blocks(
        backward_part,
        back_state,
        (
            lax.all_gather(keys_flat, "ctx", axis=0, tiled=True),
            lax.all_gather(values_flat, "ctx", axis=0, tiled=True),
        ),
    )
    local_key_value = lax.psum_scatter(
        key_value_acc.astype(jnp.bfloat16), "ctx", scatter_dimension=0, tiled=True
    ).astype(jnp.float32)
    query_raw_grad = (
        rotary_embed_backward(
            query_acc.transpose(2, 0, 1, 3).reshape(local_rows, QUERY_HEADS, HEAD_SIZE),
            cosine_table,
            sine_table,
        )
        .reshape(local_rows, QUERY_HEADS * HEAD_SIZE)
        .astype(jnp.bfloat16)
    )
    key_raw_grad = (
        rotary_embed_backward(
            local_key_value[:, : KEY_VALUE_HEADS * HEAD_SIZE].reshape(
                local_rows, KEY_VALUE_HEADS, HEAD_SIZE
            ),
            cosine_table,
            sine_table,
        )
        .reshape(local_rows, KEY_VALUE_HEADS * HEAD_SIZE)
        .astype(jnp.bfloat16)
    )
    unrotated_value_gradient = local_key_value[:, KEY_VALUE_HEADS * HEAD_SIZE :].astype(
        jnp.bfloat16
    )
    query_wgrad = dot_first(first_normed, query_raw_grad)
    key_wgrad = dot_first(first_normed, key_raw_grad)
    value_wgrad = dot_first(first_normed, unrotated_value_gradient)
    normed_one_grad = (
        dot_last(query_raw_grad, query_back)
        + dot_last(key_raw_grad, key_back)
        + dot_last(unrotated_value_gradient, value_back)
    )
    input_part, gain_one_grad = norm_back(hidden, gain_first, normed_one_grad)
    input_grad = (mixed_grad + input_part).astype(jnp.bfloat16)[None]
    attn_shards = (
        lax.psum_scatter(
            gain_one_grad.astype(jnp.bfloat16), "fsdp", scatter_dimension=0, tiled=True
        ).astype(jnp.float32),
        lax.psum_scatter(
            query_wgrad.astype(jnp.bfloat16), "fsdp", scatter_dimension=0, tiled=True
        ).astype(jnp.float32),
        lax.psum_scatter(
            key_wgrad.astype(jnp.bfloat16), "fsdp", scatter_dimension=0, tiled=True
        ).astype(jnp.float32),
        lax.psum_scatter(
            value_wgrad.astype(jnp.bfloat16), "fsdp", scatter_dimension=0, tiled=True
        ).astype(jnp.float32),
        lax.psum_scatter(
            out_wgrad.astype(jnp.bfloat16), "fsdp", scatter_dimension=0, tiled=True
        ).astype(jnp.float32),
    )
    totals = (
        lax.psum(attn_shards[0].astype(jnp.bfloat16), "ctx").astype(jnp.float32),
        lax.psum(attn_shards[1].astype(jnp.bfloat16), "ctx").astype(jnp.float32),
        lax.psum(attn_shards[2].astype(jnp.bfloat16), "ctx").astype(jnp.float32),
        lax.psum(attn_shards[3].astype(jnp.bfloat16), "ctx").astype(jnp.float32),
        lax.psum(attn_shards[4].astype(jnp.bfloat16), "ctx").astype(jnp.float32),
        lax.psum(mlp_shards[0].astype(jnp.bfloat16), "ctx").astype(jnp.float32),
        lax.psum(mlp_shards[1].astype(jnp.bfloat16), "ctx").astype(jnp.float32),
        lax.psum(mlp_shards[2].astype(jnp.bfloat16), "ctx").astype(jnp.float32),
        lax.psum(mlp_shards[3].astype(jnp.bfloat16), "ctx").astype(jnp.float32),
    )
    return (
        layer_out,
        input_grad,
        totals[0],
        totals[1],
        totals[2],
        totals[3],
        totals[4],
        totals[5],
        totals[6],
        totals[7],
        totals[8],
    )


MESH = pl.DeviceIdType.MESH
ANY = pl.ANY
VMEM = pltpu.VMEM
DMA = pltpu.SemaphoreType.DMA
LANES = 128
BLOCK = 128
F32 = jnp.float32
BF16 = jnp.bfloat16
VMEM_BYTES = 60 * 2**20


def flip(c, k):
    out = c
    for b in (1, 2, 4):
        if k & b:
            out = out + b - 2 * b * ((c // b) % 2)
    return out


def remote(src, dst, send, recv, **to):
    return pltpu.make_async_remote_copy(
        src_ref=src, dst_ref=dst, send_sem=send, recv_sem=recv, device_id=to, device_id_type=MESH
    )


def greet(peers):
    barrier = pltpu.get_barrier_semaphore()
    for peer in peers:
        pl.semaphore_signal(barrier, inc=1, device_id=peer, device_id_type=MESH)
    pl.semaphore_wait(barrier, len(peers))


class Gather:
    def __init__(self, c, own, buf, send, recv):
        self.c, self.own, self.buf, self.send, self.recv = c, own, buf, send, recv
        self.half = buf.shape[1] // 2
        self.pending = []

    def rows(self, h):
        return pl.ds(h * self.half, self.half)

    def start(self, channel, who, to, h, own=False):
        source = flip(self.c, who)
        there = self.buf.at[source, self.rows(h)]
        d = remote(
            self.own.at[self.rows(h)] if own else there,
            there,
            self.send.at[channel, h],
            self.recv.at[channel, h],
            ctx=flip(self.c, to),
        )
        d.start()
        self.pending.append(d)

    def arrived(self, channel, who, frm, h):
        ref = self.buf.at[flip(self.c, who), self.rows(h)]
        remote(
            ref, ref, self.send.at[channel, h], self.recv.at[channel, h], ctx=flip(self.c, frm)
        ).wait_recv()

    def begin(self):
        self.start(1, 0, 2, 0, own=True)
        self.start(2, 0, 4, 1, own=True)
        self.start(1, 0, 2, 1, own=True)
        self.start(2, 0, 4, 0, own=True)
        self.start(0, 0, 1, 0, own=True)
        self.start(0, 0, 1, 1, own=True)

    def finish(self):
        self.arrived(1, 2, 2, 0)
        self.start(6, 2, 4, 0)
        self.start(3, 2, 1, 0)
        self.arrived(2, 4, 4, 1)
        self.start(7, 4, 2, 1)
        self.start(4, 4, 1, 1)
        self.arrived(1, 2, 2, 1)
        self.start(3, 2, 1, 1)
        self.arrived(2, 4, 4, 0)
        self.start(4, 4, 1, 0)
        self.arrived(6, 6, 4, 0)
        self.start(5, 6, 1, 0)
        self.arrived(7, 6, 2, 1)
        self.start(5, 6, 1, 1)
        for channel, who in ((0, 1), (3, 3), (4, 5), (5, 7)):
            for h in (0, 1):
                self.arrived(channel, who, 1, h)
        for d in self.pending:
            d.wait_send()


def params(cid):
    return pltpu.CompilerParams(
        collective_id=cid, has_side_effects=True, vmem_limit_bytes=VMEM_BYTES
    )


def plane_gather(x, cid):
    rows, width = x.shape

    def kernel(x_ref, o_ref, send, recv, local):
        c = lax.axis_index("ctx")
        greet([{"ctx": flip(c, k)} for k in (1, 2, 4)])
        here = pltpu.make_async_copy(x_ref, o_ref.at[c], local)
        here.start()
        g = Gather(c, x_ref, o_ref, send, recv)
        g.begin()
        g.finish()
        here.wait()

    return pl.pallas_call(
        kernel,
        out_shape=jax.ShapeDtypeStruct((8, rows, width), x.dtype),
        in_specs=[pl.BlockSpec(memory_space=ANY)],
        out_specs=pl.BlockSpec(memory_space=ANY),
        scratch_shapes=[DMA((8, 2)), DMA((8, 2)), DMA],
        compiler_params=params(cid),
        cost_estimate=pl.CostEstimate(flops=0, bytes_accessed=16 * rows * width * 20, transcendentals=0),
        name="plane_gather",
    )(x)


def plane_exchange(x, cid):
    def kernel(x_ref, o_ref, send, recv, local):
        c = lax.axis_index("ctx")
        greet([{"ctx": flip(c, k)} for k in range(1, 8)])
        here = pltpu.make_async_copy(x_ref.at[c], o_ref.at[c], local)
        here.start()
        sent = []
        for k in (6, 7, 2, 4, 3, 5, 1):
            d = remote(
                x_ref.at[flip(c, k)], o_ref.at[c], send.at[k], recv.at[k], ctx=flip(c, k)
            )
            d.start()
            sent.append(d)
        here.wait()
        for k in (6, 7, 2, 4, 3, 5, 1):
            ref = o_ref.at[flip(c, k)]
            remote(ref, ref, send.at[k], recv.at[k], ctx=flip(c, k)).wait_recv()
        for d in sent:
            d.wait_send()

    return pl.pallas_call(
        kernel,
        out_shape=jax.ShapeDtypeStruct(x.shape, x.dtype),
        in_specs=[pl.BlockSpec(memory_space=ANY)],
        out_specs=pl.BlockSpec(memory_space=ANY),
        scratch_shapes=[DMA((8,)), DMA((8,)), DMA],
        compiler_params=params(cid),
        name="plane_exchange",
    )(x)


def scatter_kernel(p_ref, o_ref, first, total, last, diagonal, s1, v1, s2, v2):
    c = lax.axis_index("ctx")
    greet([{"ctx": flip(c, k)} for k in (1, 2, 4)])
    rows = p_ref.shape[1]
    piece = rows // 2
    pending = []

    def go(d):
        d.start()
        pending.append(d)

    def sl(q):
        return pl.ds(q * piece, piece)

    for j, k in enumerate((6, 2, 4, 0)):
        for q in (0, 1):
            go(
                remote(
                    p_ref.at[flip(c, 1 ^ k), sl(q)],
                    first.at[j, sl(q)],
                    s1.at[j, q],
                    v1.at[j, q],
                    ctx=flip(c, 1),
                )
            )

    def paired(j, q):
        ref = first.at[j, sl(q)]
        remote(ref, ref, s1.at[j, q], v1.at[j, q], ctx=flip(c, 1)).wait_recv()

    def chip(j, k, q):
        return p_ref[flip(c, k), sl(q)].astype(F32) + first[j, sl(q)].astype(F32)

    def came(channel, ref, q, frm):
        remote(ref, ref, s2.at[channel, q], v2.at[channel, q], ctx=flip(c, frm)).wait_recv()

    for q, to in ((0, 2), (1, 4)):
        paired(0, q)
        total[0, sl(q)] = chip(0, 6, q).astype(BF16)
        go(
            remote(
                total.at[0, sl(q)], diagonal.at[sl(q)], s2.at[2, q], v2.at[2, q], ctx=flip(c, to)
            )
        )

    def final(j, k, q, merged):
        v = chip(j, k, q)
        if merged:
            v = v + diagonal[sl(q)].astype(F32)
        total[j, sl(q)] = v.astype(BF16)
        go(
            remote(
                total.at[j, sl(q)],
                last.at[j - 1, sl(q)],
                s2.at[j - 1, q],
                v2.at[j - 1, q],
                ctx=flip(c, k),
            )
        )

    paired(1, 0)
    final(1, 2, 0, False)
    paired(2, 1)
    final(2, 4, 1, False)
    paired(2, 0)
    came(2, diagonal.at[sl(0)], 0, 2)
    final(2, 4, 0, True)
    paired(1, 1)
    came(2, diagonal.at[sl(1)], 1, 4)
    final(1, 2, 1, True)
    for q in (0, 1):
        paired(3, q)
    for q in (0, 1):
        came(0, last.at[0, sl(q)], q, 2)
        came(1, last.at[1, sl(q)], q, 4)
        o_ref[sl(q)] = chip(3, 0, q) + (last[0, sl(q)].astype(F32) + last[1, sl(q)].astype(F32))
    for d in pending:
        d.wait_send()


def plane_scatter(p, cid):
    rows, width = p.shape[1:]
    return pl.pallas_call(
        scatter_kernel,
        out_shape=jax.ShapeDtypeStruct((rows, width), F32),
        in_specs=[pl.BlockSpec(memory_space=VMEM)],
        out_specs=pl.BlockSpec(memory_space=VMEM),
        scratch_shapes=[
            VMEM((4, rows, width), BF16),
            VMEM((3, rows, width), BF16),
            VMEM((2, rows, width), BF16),
            VMEM((rows, width), BF16),
            DMA((4, 2)),
            DMA((4, 2)),
            DMA((3, 2)),
            DMA((3, 2)),
        ],
        compiler_params=params(cid),
        name="plane_scatter",
    )(p)


def first_kernel(x_ref, gain_ref, info_ref, all_ref, gains_ref, infos_ref, normed, *sems):
    gsend, grecv, isend, irecv, send, recv, local = sems
    c = lax.axis_index("ctx")
    z = lax.axis_index("fsdp")
    depth = gains_ref.shape[0]
    others = [lax.rem(z + k, depth) for k in range(1, depth)]
    greet([{"ctx": flip(c, k)} for k in range(1, 8)] + [{"fsdp": o} for o in others])
    sent = []
    for k, o in enumerate(others):
        d = remote(gain_ref, gains_ref.at[z], gsend.at[k], grecv.at[k], fsdp=o)
        d.start()
        sent.append(d)
    for k in range(1, 8):
        d = remote(info_ref, infos_ref.at[c], isend.at[k], irecv.at[k], ctx=flip(c, k))
        d.start()
        sent.append(d)
    gains_ref[z] = gain_ref[...]
    infos_ref[c] = info_ref[...]
    x = x_ref[...].astype(F32)
    factor = lax.rsqrt(jnp.mean(x * x, -1, keepdims=True) + EPS)
    for k in range(depth - 1):
        ref = gains_ref.at[lax.rem(z + depth - 1 - k, depth)]
        remote(ref, ref, gsend.at[k], grecv.at[k], fsdp=others[k]).wait_recv()
    gain = jnp.concatenate([gains_ref[k, 0:1, :] for k in range(depth)], 1)
    normed[...] = (x * factor * gain).astype(BF16)
    here = pltpu.make_async_copy(normed, all_ref.at[c], local)
    here.start()
    g = Gather(c, normed, all_ref, send, recv)
    g.begin()
    g.finish()
    here.wait()
    for k in range(1, 8):
        ref = infos_ref.at[flip(c, k)]
        remote(ref, ref, isend.at[k], irecv.at[k], ctx=flip(c, k)).wait_recv()
    for d in sent:
        d.wait_send()


def first_gather(x, gains, info, depth, cid):
    rows, width = x.shape
    vm = pl.BlockSpec(memory_space=VMEM)
    return pl.pallas_call(
        first_kernel,
        out_shape=(
            jax.ShapeDtypeStruct((8, rows, width), BF16),
            jax.ShapeDtypeStruct((depth,) + gains.shape, F32),
            jax.ShapeDtypeStruct((8,) + info.shape, jnp.int32),
        ),
        in_specs=[vm, vm, vm],
        out_specs=(pl.BlockSpec(memory_space=ANY), vm, vm),
        scratch_shapes=[
            VMEM((rows, width), BF16),
            DMA((depth,)),
            DMA((depth,)),
            DMA((8,)),
            DMA((8,)),
            DMA((8, 2)),
            DMA((8, 2)),
            DMA,
        ],
        compiler_params=params(cid),
        name="first_gather",
    )(x, gains, info)


def angles(base_cos, base_sin, step_cos, step_sin):
    return (
        base_cos * step_cos - base_sin * step_sin,
        base_sin * step_cos + base_cos * step_sin,
    )


def turn(u, cosine, sine, sign):
    lane = lax.broadcasted_iota(jnp.int32, u.shape, 1)
    signed = jnp.where(lane < LANES // 2, -sign, sign) * sine
    return u * cosine + pltpu.roll(u, LANES // 2, 1) * signed


def qkv_kernel(x_ref, w_ref, bc_ref, bs_ref, sc_ref, ss_ref, q_ref, k_ref, v_ref):
    i = pl.program_id(0)
    raw = jnp.dot(x_ref[...], w_ref[...], preferred_element_type=F32)
    blocks = x_ref.shape[0] // BLOCK
    for b in range(blocks):
        row = pl.ds(i * blocks + b, 1)
        cosine, sine = angles(bc_ref[row, :], bs_ref[row, :], sc_ref[...], ss_ref[...])
        rows = slice(b * BLOCK, (b + 1) * BLOCK)
        for h in (0, 1):
            cols = slice(h * LANES, (h + 1) * LANES)
            q_ref[rows, cols] = turn(raw[rows, cols], cosine, sine, 1.0).astype(BF16)
        k_ref[rows, :] = turn(raw[rows, 2 * LANES : 3 * LANES], cosine, sine, 1.0).astype(BF16)
        v_ref[rows, :] = raw[rows, 3 * LANES :].astype(BF16)


def project(x, w, tables_in):
    tokens, width = x.shape
    step = 512
    whole = lambda a: pl.BlockSpec(a.shape, lambda i: (0, 0))
    return pl.pallas_call(
        qkv_kernel,
        grid=(tokens // step,),
        out_shape=(
            jax.ShapeDtypeStruct((tokens, 2 * LANES), BF16),
            jax.ShapeDtypeStruct((tokens, LANES), BF16),
            jax.ShapeDtypeStruct((tokens, LANES), BF16),
        ),
        in_specs=[pl.BlockSpec((step, width), lambda i: (i, 0)), whole(w)] + [whole(t) for t in tables_in],
        out_specs=(
            pl.BlockSpec((step, 2 * LANES), lambda i: (i, 0)),
            pl.BlockSpec((step, LANES), lambda i: (i, 0)),
            pl.BlockSpec((step, LANES), lambda i: (i, 0)),
        ),
        compiler_params=pltpu.CompilerParams(vmem_limit_bytes=VMEM_BYTES),
        name="project",
    )(x, w, *tables_in)


CHUNK = 512


def both_heads(ref, start):
    rows = pl.ds(pl.multiple_of(start, BLOCK), BLOCK)
    return jnp.concatenate([ref[rows, :LANES], ref[rows, LANES:]], 0)


def order_rows(order_ref, tokens, pairs):
    for j in range(tokens // BLOCK):
        rows = pl.ds(pl.multiple_of(order_ref[j] * BLOCK, BLOCK), BLOCK)
        for source, target in pairs:
            target[j * BLOCK : (j + 1) * BLOCK, :] = source[rows, :]


def contract(a, b, dims):
    return lax.dot_general(a, b, ((dims[0], dims[1]), ((), ())), preferred_element_type=F32)


def attend_kernel(order_ref, q_ref, k_ref, v_ref, o_ref, low_ref, lse_ref, keys, values):
    j = pl.program_id(0)
    tokens = q_ref.shape[0]
    factor = HEAD_SIZE ** (-0.5) * math.log2(math.e)

    @pl.when(j == 0)
    def _():
        order_rows(order_ref, tokens, ((k_ref, keys), (v_ref, values)))

    start = order_ref[j] * BLOCK
    q = both_heads(q_ref, start)
    last = j // (CHUNK // BLOCK)

    def step(t, carry, masked):
        top, denom, acc = carry
        rows = pl.ds(pl.multiple_of(t * CHUNK, CHUNK), CHUNK)
        s = contract(keys[rows, :], q, ((1,), (1,)))
        if masked:
            key = t * CHUNK + lax.broadcasted_iota(jnp.int32, s.shape, 0)
            query = j * BLOCK + lax.broadcasted_iota(jnp.int32, s.shape, 1) % BLOCK
            s = jnp.where(key <= query, s, -jnp.inf)
        new_top = jnp.maximum(top, jnp.max(s, 0, keepdims=True))
        p = jnp.exp2((s - new_top) * factor)
        shrink = jnp.exp2((top - new_top) * factor)
        denom = denom * shrink + jnp.sum(p, 0, keepdims=True)
        acc = acc * shrink + contract(values[rows, :], p.astype(BF16), ((0,), (0,)))
        return new_top, denom, acc

    carry = (
        jnp.full((1, 2 * BLOCK), -1e30, F32),
        jnp.zeros((1, 2 * BLOCK), F32),
        jnp.zeros((LANES, 2 * BLOCK), F32),
    )
    carry = lax.fori_loop(0, last, lambda t, state: step(t, state, False), carry)
    top, denom, acc = step(last, carry, True)
    out = (acc / denom).T
    lse_ref[pl.ds(j, 1), :, :] = (top * factor + jnp.log2(denom)).reshape(1, 1, 2 * BLOCK)
    out = jnp.concatenate([out[:BLOCK], out[BLOCK:]], 1)
    rows = pl.ds(pl.multiple_of(start, BLOCK), BLOCK)
    o_ref[rows, :] = out
    low_ref[rows, :] = out.astype(BF16)


def attend(order, q, k, v):
    tokens = q.shape[0]
    blocks = tokens // BLOCK
    whole = lambda *shape: pl.BlockSpec(shape, lambda j, *_: (0,) * len(shape))
    return pl.pallas_call(
        attend_kernel,
        grid_spec=pltpu.PrefetchScalarGridSpec(
            num_scalar_prefetch=1,
            grid=(blocks,),
            in_specs=[whole(*q.shape), whole(*k.shape), whole(*v.shape)],
            out_specs=(whole(tokens, 2 * LANES), whole(tokens, 2 * LANES), whole(blocks, 1, 2 * BLOCK)),
            scratch_shapes=[VMEM(k.shape, BF16), VMEM(v.shape, BF16)],
        ),
        out_shape=(
            jax.ShapeDtypeStruct((tokens, 2 * LANES), F32),
            jax.ShapeDtypeStruct((tokens, 2 * LANES), BF16),
            jax.ShapeDtypeStruct((blocks, 1, 2 * BLOCK), F32),
        ),
        compiler_params=pltpu.CompilerParams(vmem_limit_bytes=VMEM_BYTES),
        name="attend",
    )(order, q, k, v)


def attend_back_kernel(
    order_ref, q_ref, k_ref, v_ref, o_ref, do_ref, lse_ref, bc_ref, bs_ref, sc_ref, ss_ref, d_ref, keys, values, dk, dv
):
    j = pl.program_id(0)
    tokens = q_ref.shape[0]
    scale = HEAD_SIZE ** (-0.5)
    factor = scale * math.log2(math.e)

    @pl.when(j == 0)
    def _():
        order_rows(order_ref, tokens, ((k_ref, keys), (v_ref, values)))
        dk[...] = jnp.zeros_like(dk)
        dv[...] = jnp.zeros_like(dv)

    block = order_ref[j]
    start = block * BLOCK
    q = both_heads(q_ref, start)
    do = both_heads(do_ref, start)
    delta = jnp.sum((both_heads(o_ref, start) * do.astype(F32)).T, 0, keepdims=True)
    lse = lse_ref[j]
    last = j // (CHUNK // BLOCK)

    def step(t, dq, masked):
        rows = pl.ds(pl.multiple_of(t * CHUNK, CHUNK), CHUNK)
        key_rows = keys[rows, :]
        s = contract(key_rows, q, ((1,), (1,)))
        if masked:
            key = t * CHUNK + lax.broadcasted_iota(jnp.int32, s.shape, 0)
            query = j * BLOCK + lax.broadcasted_iota(jnp.int32, s.shape, 1) % BLOCK
            s = jnp.where(key <= query, s, -jnp.inf)
        p = jnp.exp2(s * factor - lse)
        dp = contract(values[rows, :], do, ((1,), (1,)))
        ds = (p * (dp - delta)).astype(BF16)
        dv[rows, :] += jnp.dot(p.astype(BF16), do, preferred_element_type=F32)
        dk[rows, :] += jnp.dot(ds, q, preferred_element_type=F32)
        return dq + contract(key_rows, ds, ((0,), (0,)))

    dq = jnp.zeros((LANES, 2 * BLOCK), F32)
    dq = lax.fori_loop(0, last, lambda t, state: step(t, state, False), dq)
    dq = step(last, dq, True).T * scale

    def table(at):
        row = pl.ds(at, 1)
        return angles(bc_ref[row, :], bs_ref[row, :], sc_ref[...], ss_ref[...])

    cosine, sine = table(block)
    rows = pl.ds(pl.multiple_of(start, BLOCK), BLOCK)
    for h in (0, 1):
        part = dq[h * BLOCK : (h + 1) * BLOCK]
        d_ref[rows, h * LANES : (h + 1) * LANES] = turn(part, cosine, sine, -1.0).astype(BF16)

    @pl.when(j == tokens // BLOCK - 1)
    def _():
        def put(b, unused):
            at = order_ref[b]
            cosine, sine = table(at)
            source = pl.ds(pl.multiple_of(b * BLOCK, BLOCK), BLOCK)
            rows = pl.ds(pl.multiple_of(at * BLOCK, BLOCK), BLOCK)
            d_ref[rows, 2 * LANES : 3 * LANES] = turn(dk[source, :] * scale, cosine, sine, -1.0).astype(BF16)
            d_ref[rows, 3 * LANES :] = dv[source, :].astype(BF16)
            return unused

        lax.fori_loop(0, tokens // BLOCK, put, 0)


def attend_back(order, q, k, v, o, do, lse, tables_in):
    tokens = q.shape[0]
    blocks = tokens // BLOCK
    whole = lambda a: pl.BlockSpec(a.shape, lambda j, *_: (0,) * a.ndim)
    arrays = (q, k, v, o, do, lse) + tuple(tables_in)
    return pl.pallas_call(
        attend_back_kernel,
        grid_spec=pltpu.PrefetchScalarGridSpec(
            num_scalar_prefetch=1,
            grid=(blocks,),
            in_specs=[whole(a) for a in arrays],
            out_specs=pl.BlockSpec((tokens, 4 * LANES), lambda j, *_: (0, 0)),
            scratch_shapes=[VMEM(k.shape, BF16), VMEM(v.shape, BF16), VMEM(k.shape, F32), VMEM(v.shape, F32)],
        ),
        out_shape=jax.ShapeDtypeStruct((tokens, 4 * LANES), BF16),
        compiler_params=pltpu.CompilerParams(vmem_limit_bytes=VMEM_BYTES),
        name="attend_back",
    )(order, *arrays)


def in_plane(
    depth,
    hidden_in,
    positions,
    attn_gain,
    w_query,
    key_projection,
    value_projection,
    w_out,
    mlp_gain,
    w_gate,
    w_up,
    w_down,
    out_grad,
):
    c = lax.axis_index("ctx")
    plane = 8
    rows, width = hidden_in.shape[1:]
    tokens = plane * rows
    shard = width // depth
    half = HEAD_SIZE // 2
    columns = w_gate.shape[1]
    mine = columns // plane
    strip = mine // depth
    deep = w_down.shape[0]

    def share(a, axis):
        return lax.dynamic_index_in_dim(a, c, axis, keepdims=False)

    def halves(a, heads):
        a = share(a.reshape(shard, plane, heads, 2, half), 1)
        a = jnp.pad(a, ((0, 0), (0, 0), (0, 0), (0, LANES // 2 - half)))
        return a.reshape(shard, heads * LANES)

    value_part = jnp.pad(share(value_projection.reshape(shard, plane, HEAD_SIZE), 1), ((0, 0), (0, LANES - HEAD_SIZE)))
    qkv_part = jnp.concatenate([halves(w_query, 2), halves(key_projection, 1), value_part], 1)

    def cut(a):
        return share(a.reshape(shard, depth, plane, strip), 2).reshape(shard, mine)

    out_part = share(w_out.reshape(plane, shard // plane, width), 0)
    down_part = share(w_down.reshape(plane, deep // plane, width), 0)

    def over_depth(a):
        return lax.all_gather(a, "fsdp", axis=0, tiled=True)

    qkv_w = over_depth(qkv_part)
    out_slices = over_depth(out_part)
    gate_w = over_depth(cut(w_gate))
    up_w = over_depth(cut(w_up))
    down_w = over_depth(down_part)

    position = positions[0]
    lane = lax.broadcasted_iota(jnp.int32, (8, LANES), 1)
    info = jnp.where(lane < LANES // 2, position[0], position[BLOCK])
    gains = jnp.concatenate(
        [
            jnp.broadcast_to(attn_gain.astype(F32)[None], (4, shard)),
            jnp.broadcast_to(mlp_gain.astype(F32)[None], (4, shard)),
        ],
        0,
    )
    hidden_low = hidden_in[0]
    normed_all, gains_all, infos = first_gather(hidden_low, gains, info, depth, 0)
    gain_one = gains_all[:, 0].reshape(width)
    gain_two = gains_all[:, 4].reshape(width)
    starts = infos[:, 0].reshape(plane, 2, LANES // 2)[:, :, 0].reshape(2 * plane)
    ranks = (starts - jnp.min(starts)) // BLOCK
    blocks = 2 * plane
    order = jnp.sum(
        jnp.where(ranks[None, :] == jnp.arange(blocks)[:, None], jnp.arange(blocks)[None, :], 0), 1
    ).astype(jnp.int32)

    freq = THETA ** (-(jnp.arange(half, dtype=F32) * 2.0 / HEAD_SIZE))
    pad = jnp.zeros((LANES // 2 - half,), F32)
    freq = jnp.concatenate([freq, pad, freq, pad])
    base = starts.astype(F32)[:, None] * freq[None]
    inner = jnp.arange(BLOCK, dtype=F32)[:, None] * freq[None]
    tables_in = (jnp.cos(base), jnp.sin(base), jnp.cos(inner), jnp.sin(inner))

    normed_all = normed_all.reshape(tokens, width)
    q, k, v = project(normed_all, qkv_w, tables_in)
    attended, attended_low, lse = attend(order, q, k, v)

    out_all = plane_gather(out_slices.reshape(depth * (shard // plane), width), 1)
    out_w = (
        out_all.reshape(plane, depth, shard // plane, width).transpose(1, 0, 2, 3).reshape(width, width)
    )
    mixed_heads = plane_exchange(attended_low.reshape(plane, rows, 2 * LANES), 2)
    attended_tok = (
        mixed_heads.reshape(plane, rows, 2, LANES)[..., :HEAD_SIZE].transpose(1, 0, 2, 3).reshape(rows, width)
    )
    hidden = hidden_low.astype(F32)
    mixed = hidden + jnp.dot(attended_tok, out_w, preferred_element_type=F32)
    normed_two = norm_forward(mixed, gain_two).astype(BF16)
    two_all = plane_gather(normed_two, 3).reshape(tokens, width)
    grad_low = out_grad[0]
    grad_all = plane_gather(grad_low, 4).reshape(tokens, width)

    gate = jnp.dot(two_all, gate_w, preferred_element_type=F32)
    up = jnp.dot(two_all, up_w, preferred_element_type=F32)
    sigma = jax.nn.sigmoid(gate)
    active = (gate * sigma * up).astype(BF16)
    down_sum = jnp.dot(active, down_w, preferred_element_type=F32).astype(BF16)
    result = mixed + plane_scatter(down_sum.reshape(plane, rows, width), 5)
    layer_out = result.astype(BF16)[None]

    down_grad = dot_first(active, grad_all)
    active_grad = dot_last(grad_all, down_w)
    gate_grad = (active_grad * up * sigma * (1.0 + gate * (1.0 - sigma))).astype(BF16)
    up_grad = (active_grad * gate * sigma).astype(BF16)
    gate_wgrad = dot_first(two_all, gate_grad)
    up_wgrad = dot_first(two_all, up_grad)
    two_grad_sum = (dot_last(gate_grad, gate_w) + dot_last(up_grad, up_w)).astype(BF16)
    two_grad = plane_scatter(two_grad_sum.reshape(plane, rows, width), 6)
    mixed_part, gain_two_grad = norm_back(mixed, gain_two, two_grad)
    mixed_grad = grad_low.astype(F32) + mixed_part
    branch_grad = mixed_grad.astype(BF16)

    def scatter_depth(a):
        return lax.psum_scatter(a.astype(BF16), "fsdp", scatter_dimension=0, tiled=True)

    gate_shard = scatter_depth(gate_wgrad)
    up_shard = scatter_depth(up_wgrad)
    down_shard = scatter_depth(down_grad)

    attended_grad = dot_last(branch_grad, out_w).astype(BF16)
    out_wgrad = dot_first(attended_tok, branch_grad).astype(BF16)
    spread = jnp.pad(
        attended_grad.reshape(rows, plane, 2, HEAD_SIZE), ((0, 0), (0, 0), (0, 0), (0, LANES - HEAD_SIZE))
    )
    spread = spread.transpose(1, 0, 2, 3).reshape(plane, rows, 2 * LANES)
    do = plane_exchange(spread, 7).reshape(tokens, 2 * LANES)
    qkv_grad = attend_back(order, q, k, v, attended, do, lse, tables_in)
    one_grad_sum = dot_last(qkv_grad, qkv_w).astype(BF16)
    qkv_wgrad = dot_first(normed_all, qkv_grad).astype(BF16)
    qkv_shard = scatter_depth(qkv_wgrad)
    one_grad = plane_scatter(one_grad_sum.reshape(plane, rows, width), 8)
    input_part, gain_one_grad = norm_back(hidden, gain_one, one_grad)
    input_grad = (mixed_grad + input_part).astype(BF16)[None]

    out_rows = out_wgrad.reshape(depth, plane, shard // plane, width).transpose(1, 0, 2, 3)
    out_sum = plane_scatter(out_rows.reshape(plane, shard // plane * depth, width), 9)
    out_shard = scatter_depth(out_sum)

    joined = jnp.concatenate([gate_shard, up_shard, down_shard.reshape(-1, mine)], 0)
    joined = plane_gather(joined, 10).astype(F32)
    def columns_of(a):
        return a.reshape(plane, shard, depth, strip).transpose(1, 2, 0, 3).reshape(shard, columns)

    gate_total = columns_of(joined[:, :shard])
    up_total = columns_of(joined[:, shard : 2 * shard])
    down_total = joined[:, 2 * shard :].reshape(deep, width)

    tail = jnp.concatenate([qkv_shard, out_shard.reshape(-1, 4 * LANES)], 0)
    tail = plane_gather(tail, 11).astype(F32)
    out_total = tail[:, shard:].reshape(shard, width)
    heads = tail[:, :shard].reshape(plane, shard, 4, LANES)

    def unhalve(a, n):
        a = a.reshape(plane, shard, n, 2, LANES // 2)[..., :half]
        return a.transpose(1, 0, 2, 3, 4).reshape(shard, plane * n * HEAD_SIZE)

    query_total = unhalve(heads[:, :, :2], 2)
    key_total = unhalve(heads[:, :, 2:3], 1)
    value_total = heads[:, :, 3, :HEAD_SIZE].transpose(1, 0, 2).reshape(shard, plane * HEAD_SIZE)

    gain_sums = lax.psum(jnp.stack([gain_one_grad, gain_two_grad]), ("ctx", "fsdp"))
    gain_sums = lax.dynamic_slice_in_dim(gain_sums, lax.axis_index("fsdp") * shard, shard, 1)
    return (
        layer_out,
        input_grad,
        gain_sums[0],
        query_total,
        key_total,
        value_total,
        out_total,
        gain_sums[1],
        gate_total,
        up_total,
        down_total,
    )


def solution(mesh):
    placed = (
        P("fsdp", "ctx", None),
        P("fsdp", "ctx"),
        P("fsdp"),
        P("fsdp", None),
        P("fsdp", None),
        P("fsdp", None),
        P("fsdp", None),
        P("fsdp"),
        P("fsdp", None),
        P("fsdp", None),
        P("fsdp", None),
        P("fsdp", "ctx", None),
    )
    body = per_device
    if mesh.shape["ctx"] == KEY_VALUE_HEADS:
        body = functools.partial(in_plane, mesh.shape["fsdp"])
    return jax.shard_map(
        body,
        mesh=mesh,
        in_specs=placed,
        out_specs=(
            P("fsdp", "ctx", None),
            P("fsdp", "ctx", None),
            P("fsdp"),
            P("fsdp", None),
            P("fsdp", None),
            P("fsdp", None),
            P("fsdp", None),
            P("fsdp"),
            P("fsdp", None),
            P("fsdp", None),
            P("fsdp", None),
        ),
        check_vma=False,
    )
```

```python
import functools
import math

import jax
import jax.numpy as jnp
from jax import lax
from jax.experimental import pallas as pl
from jax.experimental.pallas import tpu as pltpu
from jax.sharding import PartitionSpec as P

QUERY_HEADS = 16
KEY_VALUE_HEADS = 8
HEAD_SIZE = 96


EPS = 1e-05
THETA = 100000.0


def tables(token_position):
    half = HEAD_SIZE // 2
    freq = THETA ** (-(jnp.arange(half, dtype=jnp.float32) * 2.0 / HEAD_SIZE))
    angle = token_position.astype(jnp.float32)[:, None] * freq[None, :]
    return (jnp.cos(angle)[:, None, :], jnp.sin(angle)[:, None, :])


def rotary_embed(value_rows, cosine_table, sine_table):
    half = value_rows.shape[-1] // 2
    first = value_rows[..., :half]
    second = value_rows[..., half:]
    return jnp.concatenate(
        [first * cosine_table - second * sine_table, second * cosine_table + first * sine_table], -1
    )


def rotary_embed_backward(grads, cosine_table, sine_table):
    half = grads.shape[-1] // 2
    first = grads[..., :half]
    second = grads[..., half:]
    return jnp.concatenate(
        [first * cosine_table + second * sine_table, second * cosine_table - first * sine_table], -1
    )


def norm_forward(hidden, gain):
    return (
        hidden
        * lax.rsqrt(jnp.mean(hidden * hidden, -1, keepdims=True) + EPS)
        * gain.astype(jnp.float32)
    )


def norm_back(hidden, gain, grad):
    factor = lax.rsqrt(jnp.mean(hidden * hidden, -1, keepdims=True) + EPS)
    scaled = grad * gain.astype(jnp.float32)
    hidden_grad = factor * scaled - hidden * factor * factor * factor * jnp.mean(
        scaled * hidden, -1, keepdims=True
    )
    gain_grad = jnp.sum(grad * hidden * factor, 0)
    return (hidden_grad, gain_grad)


def dot_first(left, right):
    return lax.dot_general(
        left, right, (((0,), (0,)), ((), ())), preferred_element_type=jnp.float32
    )


def dot_last(left, right):
    return lax.dot_general(
        left, right, (((1,), (1,)), ((), ())), preferred_element_type=jnp.float32
    )


def over_blocks(step_fn, carry, arrays):
    block_count = arrays[0].shape[0]
    size = math.gcd(block_count, 512)
    parts = block_count // size
    shaped = tuple((item.reshape((parts, size) + item.shape[1:]) for item in arrays))

    def advance(state, inputs):
        index, pieces = inputs
        return (step_fn(state, pieces, index * size), None)

    final, unused = lax.scan(advance, carry, (jnp.arange(parts, dtype=jnp.int32), shaped))
    return final


def per_device(
    hidden_in,
    positions,
    attn_gain,
    w_query,
    key_projection,
    value_projection,
    w_out,
    mlp_gain,
    w_gate,
    w_up,
    w_down,
    out_grad,
):
    hidden = hidden_in[0].astype(jnp.float32)
    local_rows = hidden.shape[0]
    query_pos = positions[0]
    query_groups = QUERY_HEADS // KEY_VALUE_HEADS
    scale = HEAD_SIZE ** (-0.5)
    cosine_table, sine_table = tables(query_pos)
    attn_set = (
        lax.all_gather(attn_gain, "fsdp", axis=0, tiled=True),
        lax.all_gather(w_query, "fsdp", axis=0, tiled=True),
        lax.all_gather(key_projection, "fsdp", axis=0, tiled=True),
        lax.all_gather(value_projection, "fsdp", axis=0, tiled=True),
        lax.all_gather(w_out, "fsdp", axis=0, tiled=True),
    )
    gain_one, query_w, key_matrix, value_matrix, out_w = attn_set
    first_normed = norm_forward(hidden, gain_one).astype(jnp.bfloat16)
    query_raw = jnp.dot(first_normed, query_w, preferred_element_type=jnp.float32)
    unrotated_key = jnp.dot(first_normed, key_matrix, preferred_element_type=jnp.float32)
    value_raw = jnp.dot(first_normed, value_matrix, preferred_element_type=jnp.float32)
    query_rows = (
        rotary_embed(
            query_raw.reshape(local_rows, QUERY_HEADS, HEAD_SIZE), cosine_table, sine_table
        )
        .astype(jnp.bfloat16)
        .reshape(local_rows, KEY_VALUE_HEADS, query_groups, HEAD_SIZE)
    )
    keys_flat = (
        rotary_embed(
            unrotated_key.reshape(local_rows, KEY_VALUE_HEADS, HEAD_SIZE), cosine_table, sine_table
        )
        .astype(jnp.bfloat16)
        .reshape(local_rows, KEY_VALUE_HEADS * HEAD_SIZE)
    )
    values_flat = value_raw.astype(jnp.bfloat16)
    key_pos_all = lax.all_gather(query_pos, "ctx", axis=0, tiled=True)
    sequence_length = key_pos_all.shape[0]

    def masked_scores(partial_keys, first):
        block_count = partial_keys.shape[0]
        key_pos = lax.dynamic_slice_in_dim(key_pos_all, first, block_count)
        scores = (
            jnp.einsum(
                "tkgd,nkd->kgtn",
                query_rows,
                partial_keys.reshape(block_count, KEY_VALUE_HEADS, HEAD_SIZE),
                preferred_element_type=jnp.float32,
            )
            * scale
        )
        visible = key_pos[None, None, None, :] <= query_pos[None, None, :, None]
        return jnp.where(visible, scores, -jnp.inf)

    def forward_part(carry, part, first):
        top, denom, accum = carry
        partial_keys, partial_values = part
        block_count = partial_keys.shape[0]
        scores = masked_scores(partial_keys, first)
        new_top = jnp.maximum(top, jnp.max(scores, -1))
        weights = jnp.exp(scores - new_top[..., None])
        factor = jnp.exp(top - new_top)
        denom = denom * factor + jnp.sum(weights, -1)
        accum = accum * factor[..., None] + jnp.einsum(
            "kgtn,nkd->kgtd",
            weights.astype(jnp.bfloat16),
            partial_values.reshape(block_count, KEY_VALUE_HEADS, HEAD_SIZE),
            preferred_element_type=jnp.float32,
        )
        return (new_top, denom, accum)

    start_state = (
        jnp.full((KEY_VALUE_HEADS, query_groups, local_rows), -1e30, jnp.float32),
        jnp.zeros((KEY_VALUE_HEADS, query_groups, local_rows), jnp.float32),
        jnp.zeros((KEY_VALUE_HEADS, query_groups, local_rows, HEAD_SIZE), jnp.float32),
    )
    top, denom, accum = over_blocks(
        forward_part,
        start_state,
        (
            lax.all_gather(keys_flat, "ctx", axis=0, tiled=True),
            lax.all_gather(values_flat, "ctx", axis=0, tiled=True),
        ),
    )
    attended_output = accum / denom[..., None]
    log_total = top + jnp.log(denom)
    attended_low = (
        attended_output.transpose(2, 0, 1, 3)
        .reshape(local_rows, QUERY_HEADS * HEAD_SIZE)
        .astype(jnp.bfloat16)
    )
    mixed = hidden + jnp.dot(attended_low, out_w, preferred_element_type=jnp.float32)
    mlp_set = (
        lax.all_gather(mlp_gain, "fsdp", axis=0, tiled=True),
        lax.all_gather(w_gate, "fsdp", axis=0, tiled=True),
        lax.all_gather(w_up, "fsdp", axis=0, tiled=True),
        lax.all_gather(w_down, "fsdp", axis=0, tiled=True),
    )
    gain_two, gate_w, up_w, down_w = mlp_set
    normed_two = norm_forward(mixed, gain_two).astype(jnp.bfloat16)
    gate = jnp.dot(normed_two, gate_w, preferred_element_type=jnp.float32)
    up = jnp.dot(normed_two, up_w, preferred_element_type=jnp.float32)
    sigma = jax.nn.sigmoid(gate)
    active = (gate * sigma * up).astype(jnp.bfloat16)
    result = mixed + jnp.dot(active, down_w, preferred_element_type=jnp.float32)
    layer_out = result.astype(jnp.bfloat16)[None]
    grad_low = out_grad[0]
    grad_out = grad_low.astype(jnp.float32)
    gain_back, gate_back, up_back, down_back = (
        lax.all_gather(mlp_gain, "fsdp", axis=0, tiled=True),
        lax.all_gather(w_gate, "fsdp", axis=0, tiled=True),
        lax.all_gather(w_up, "fsdp", axis=0, tiled=True),
        lax.all_gather(w_down, "fsdp", axis=0, tiled=True),
    )
    down_grad = dot_first(active, grad_low)
    active_grad = dot_last(grad_low, down_back)
    gate_grad = (active_grad * up * sigma * (1.0 + gate * (1.0 - sigma))).astype(jnp.bfloat16)
    up_grad = (active_grad * gate * sigma).astype(jnp.bfloat16)
    gate_wgrad = dot_first(normed_two, gate_grad)
    up_wgrad = dot_first(normed_two, up_grad)
    normed_two_grad = dot_last(gate_grad, gate_back) + dot_last(up_grad, up_back)
    mixed_part, gain_two_grad = norm_back(mixed, gain_back, normed_two_grad)
    mixed_grad = grad_out + mixed_part
    mlp_shards = (
        lax.psum_scatter(
            gain_two_grad.astype(jnp.bfloat16), "fsdp", scatter_dimension=0, tiled=True
        ).astype(jnp.float32),
        lax.psum_scatter(
            gate_wgrad.astype(jnp.bfloat16), "fsdp", scatter_dimension=0, tiled=True
        ).astype(jnp.float32),
        lax.psum_scatter(
            up_wgrad.astype(jnp.bfloat16), "fsdp", scatter_dimension=0, tiled=True
        ).astype(jnp.float32),
        lax.psum_scatter(
            down_grad.astype(jnp.bfloat16), "fsdp", scatter_dimension=0, tiled=True
        ).astype(jnp.float32),
    )
    gain_first, query_back, key_back, value_back, out_back = (
        lax.all_gather(attn_gain, "fsdp", axis=0, tiled=True),
        lax.all_gather(w_query, "fsdp", axis=0, tiled=True),
        lax.all_gather(key_projection, "fsdp", axis=0, tiled=True),
        lax.all_gather(value_projection, "fsdp", axis=0, tiled=True),
        lax.all_gather(w_out, "fsdp", axis=0, tiled=True),
    )
    branch_grad = mixed_grad.astype(jnp.bfloat16)
    out_wgrad = dot_first(attended_low, branch_grad)
    attended_grad = (
        dot_last(branch_grad, out_back)
        .astype(jnp.bfloat16)
        .reshape(local_rows, KEY_VALUE_HEADS, query_groups, HEAD_SIZE)
        .transpose(1, 2, 0, 3)
    )
    delta = jnp.sum(attended_grad.astype(jnp.float32) * attended_output, -1)

    def backward_part(carry, part, first):
        query_acc, key_value_acc = carry
        partial_keys, partial_values = part
        block_count = partial_keys.shape[0]
        probs = jnp.exp(masked_scores(partial_keys, first) - log_total[..., None])
        gradient_of_value = jnp.einsum(
            "kgtn,kgtd->nkd",
            probs.astype(jnp.bfloat16),
            attended_grad,
            preferred_element_type=jnp.float32,
        )
        prob_grad = jnp.einsum(
            "kgtd,nkd->kgtn",
            attended_grad,
            partial_values.reshape(block_count, KEY_VALUE_HEADS, HEAD_SIZE),
            preferred_element_type=jnp.float32,
        )
        score_grad = (probs * (prob_grad - delta[..., None])).astype(jnp.bfloat16)
        query_acc = (
            query_acc
            + jnp.einsum(
                "kgtn,nkd->kgtd",
                score_grad,
                partial_keys.reshape(block_count, KEY_VALUE_HEADS, HEAD_SIZE),
                preferred_element_type=jnp.float32,
            )
            * scale
        )
        gradient_of_key = (
            jnp.einsum("kgtn,tkgd->nkd", score_grad, query_rows, preferred_element_type=jnp.float32)
            * scale
        )
        joined = jnp.concatenate(
            [
                gradient_of_key.reshape(block_count, KEY_VALUE_HEADS * HEAD_SIZE),
                gradient_of_value.reshape(block_count, KEY_VALUE_HEADS * HEAD_SIZE),
            ],
            1,
        )
        key_value_acc = lax.dynamic_update_slice_in_dim(key_value_acc, joined, first, 0)
        return (query_acc, key_value_acc)

    back_state = (
        jnp.zeros((KEY_VALUE_HEADS, query_groups, local_rows, HEAD_SIZE), jnp.float32),
        jnp.zeros((sequence_length, 2 * KEY_VALUE_HEADS * HEAD_SIZE), jnp.float32),
    )
    query_acc, key_value_acc = over_blocks(
        backward_part,
        back_state,
        (
            lax.all_gather(keys_flat, "ctx", axis=0, tiled=True),
            lax.all_gather(values_flat, "ctx", axis=0, tiled=True),
        ),
    )
    local_key_value = lax.psum_scatter(
        key_value_acc.astype(jnp.bfloat16), "ctx", scatter_dimension=0, tiled=True
    ).astype(jnp.float32)
    query_raw_grad = (
        rotary_embed_backward(
            query_acc.transpose(2, 0, 1, 3).reshape(local_rows, QUERY_HEADS, HEAD_SIZE),
            cosine_table,
            sine_table,
        )
        .reshape(local_rows, QUERY_HEADS * HEAD_SIZE)
        .astype(jnp.bfloat16)
    )
    key_raw_grad = (
        rotary_embed_backward(
            local_key_value[:, : KEY_VALUE_HEADS * HEAD_SIZE].reshape(
                local_rows, KEY_VALUE_HEADS, HEAD_SIZE
            ),
            cosine_table,
            sine_table,
        )
        .reshape(local_rows, KEY_VALUE_HEADS * HEAD_SIZE)
        .astype(jnp.bfloat16)
    )
    unrotated_value_gradient = local_key_value[:, KEY_VALUE_HEADS * HEAD_SIZE :].astype(
        jnp.bfloat16
    )
    query_wgrad = dot_first(first_normed, query_raw_grad)
    key_wgrad = dot_first(first_normed, key_raw_grad)
    value_wgrad = dot_first(first_normed, unrotated_value_gradient)
    normed_one_grad = (
        dot_last(query_raw_grad, query_back)
        + dot_last(key_raw_grad, key_back)
        + dot_last(unrotated_value_gradient, value_back)
    )
    input_part, gain_one_grad = norm_back(hidden, gain_first, normed_one_grad)
    input_grad = (mixed_grad + input_part).astype(jnp.bfloat16)[None]
    attn_shards = (
        lax.psum_scatter(
            gain_one_grad.astype(jnp.bfloat16), "fsdp", scatter_dimension=0, tiled=True
        ).astype(jnp.float32),
        lax.psum_scatter(
            query_wgrad.astype(jnp.bfloat16), "fsdp", scatter_dimension=0, tiled=True
        ).astype(jnp.float32),
        lax.psum_scatter(
            key_wgrad.astype(jnp.bfloat16), "fsdp", scatter_dimension=0, tiled=True
        ).astype(jnp.float32),
        lax.psum_scatter(
            value_wgrad.astype(jnp.bfloat16), "fsdp", scatter_dimension=0, tiled=True
        ).astype(jnp.float32),
        lax.psum_scatter(
            out_wgrad.astype(jnp.bfloat16), "fsdp", scatter_dimension=0, tiled=True
        ).astype(jnp.float32),
    )
    totals = (
        lax.psum(attn_shards[0].astype(jnp.bfloat16), "ctx").astype(jnp.float32),
        lax.psum(attn_shards[1].astype(jnp.bfloat16), "ctx").astype(jnp.float32),
        lax.psum(attn_shards[2].astype(jnp.bfloat16), "ctx").astype(jnp.float32),
        lax.psum(attn_shards[3].astype(jnp.bfloat16), "ctx").astype(jnp.float32),
        lax.psum(attn_shards[4].astype(jnp.bfloat16), "ctx").astype(jnp.float32),
        lax.psum(mlp_shards[0].astype(jnp.bfloat16), "ctx").astype(jnp.float32),
        lax.psum(mlp_shards[1].astype(jnp.bfloat16), "ctx").astype(jnp.float32),
        lax.psum(mlp_shards[2].astype(jnp.bfloat16), "ctx").astype(jnp.float32),
        lax.psum(mlp_shards[3].astype(jnp.bfloat16), "ctx").astype(jnp.float32),
    )
    return (
        layer_out,
        input_grad,
        totals[0],
        totals[1],
        totals[2],
        totals[3],
        totals[4],
        totals[5],
        totals[6],
        totals[7],
        totals[8],
    )


MESH = pl.DeviceIdType.MESH
ANY = pl.ANY
VMEM = pltpu.VMEM
DMA = pltpu.SemaphoreType.DMA
LANES = 128
BLOCK = 128
F32 = jnp.float32
BF16 = jnp.bfloat16
VMEM_BYTES = 60 * 2**20


def flip(c, k):
    out = c
    for b in (1, 2, 4):
        if k & b:
            out = out + b - 2 * b * ((c // b) % 2)
    return out


def remote(src, dst, send, recv, **to):
    return pltpu.make_async_remote_copy(
        src_ref=src, dst_ref=dst, send_sem=send, recv_sem=recv, device_id=to, device_id_type=MESH
    )


def greet(peers):
    barrier = pltpu.get_barrier_semaphore()
    for peer in peers:
        pl.semaphore_signal(barrier, inc=1, device_id=peer, device_id_type=MESH)
    pl.semaphore_wait(barrier, len(peers))


class Gather:
    def __init__(self, c, own, buf, at, send, recv):
        self.c, self.own, self.buf, self.at, self.send, self.recv = c, own, buf, at, send, recv
        self.pending = []

    def start(self, channel, who, to, h, own=False):
        there = self.at(self.buf, flip(self.c, who), h)
        d = remote(
            self.own(h) if own else there,
            there,
            self.send.at[channel, h],
            self.recv.at[channel, h],
            ctx=flip(self.c, to),
        )
        d.start()
        self.pending.append(d)

    def arrived(self, channel, who, frm, h):
        ref = self.at(self.buf, flip(self.c, who), h)
        remote(
            ref, ref, self.send.at[channel, h], self.recv.at[channel, h], ctx=flip(self.c, frm)
        ).wait_recv()

    def begin(self):
        self.start(1, 0, 2, 0, own=True)
        self.start(2, 0, 4, 1, own=True)
        self.start(1, 0, 2, 1, own=True)
        self.start(2, 0, 4, 0, own=True)
        self.start(0, 0, 1, 0, own=True)
        self.start(0, 0, 1, 1, own=True)

    def near_half(self):
        self.arrived(1, 2, 2, 0)
        self.start(6, 2, 4, 0)
        self.start(3, 2, 1, 0)
        self.arrived(2, 4, 4, 1)
        self.start(7, 4, 2, 1)
        self.start(4, 4, 1, 1)

    def near_rest(self):
        self.arrived(1, 2, 2, 1)
        self.start(3, 2, 1, 1)
        self.arrived(2, 4, 4, 0)
        self.start(4, 4, 1, 0)

    def far(self):
        self.arrived(6, 6, 4, 0)
        self.start(5, 6, 1, 0)
        self.arrived(7, 6, 2, 1)
        self.start(5, 6, 1, 1)

    def paired(self, channel, who):
        for h in (0, 1):
            self.arrived(channel, who, 1, h)

    def finish(self):
        self.near_half()
        self.near_rest()
        self.far()
        for channel, who in ((0, 1), (3, 3), (4, 5), (5, 7)):
            self.paired(channel, who)

    def sent(self):
        for d in self.pending:
            d.wait_send()


def row_half(ref, d, h):
    half = ref.shape[1] // 2
    return ref.at[d, pl.ds(h * half, half)]


def column_half(ref, d, h):
    half = ref.shape[2] // 2
    return ref.at[d, :, pl.ds(h * half, half)]


def own_half(ref, axis=0):
    half = ref.shape[axis] // 2
    return lambda h: ref.at[(slice(None),) * axis + (pl.ds(h * half, half),)]


class Line:
    def __init__(self, z, depth, at, send, recv):
        self.z, self.depth, self.at, self.send, self.recv = z, depth, at, send, recv

    def copy(self, way, k, part, to):
        ref = self.at(part)
        return remote(ref, ref, self.send.at[way, k], self.recv.at[way, k], fsdp=to)

    def step(self, k):
        z, top = self.z, self.depth - 1

        @pl.when((z >= k) & (z < top))
        def _():
            self.copy(0, k, z - k, z + 1).start()

        @pl.when((z + k <= top) & (z > 0))
        def _():
            self.copy(1, k, z + k, z - 1).start()

    def landed(self, k):
        z, top = self.z, self.depth - 1

        @pl.when(z >= k + 1)
        def _():
            self.copy(0, k, z - 1 - k, z - 1).wait_recv()

        @pl.when(z + 1 + k <= top)
        def _():
            self.copy(1, k, z + 1 + k, z + 1).wait_recv()

    def sent(self):
        z, top = self.z, self.depth - 1
        for k in range(top):

            @pl.when((z >= k) & (z < top))
            def _():
                self.copy(0, k, z - k, z + 1).wait_send()

            @pl.when((z + k <= top) & (z > 0))
            def _():
                self.copy(1, k, z + k, z - 1).wait_send()


def params(cid):
    return pltpu.CompilerParams(
        collective_id=cid, has_side_effects=True, vmem_limit_bytes=VMEM_BYTES
    )


def plane_gather(arrays, cid):
    n = len(arrays)
    by_rows = [a.shape[0] % 32 == 0 for a in arrays]

    def kernel(*refs):
        ins, outs, (send, recv, local) = refs[:n], refs[n : 2 * n], refs[2 * n :]
        c = lax.axis_index("ctx")
        greet([{"ctx": flip(c, k)} for k in (1, 2, 4)])
        here = [pltpu.make_async_copy(ins[i], outs[i].at[c], local.at[i]) for i in range(n)]
        gathers = []
        for i in range(n):
            at, own = (row_half, own_half(ins[i])) if by_rows[i] else (column_half, own_half(ins[i], 1))
            gathers.append(Gather(c, own, outs[i], at, send.at[i], recv.at[i]))
        for g in gathers:
            g.begin()
        for h in here:
            h.start()
        for g in gathers:
            g.finish()
        for h in here:
            h.wait()
        for g in gathers:
            g.sent()

    return pl.pallas_call(
        kernel,
        out_shape=[jax.ShapeDtypeStruct((8,) + a.shape, a.dtype) for a in arrays],
        in_specs=[pl.BlockSpec(memory_space=ANY)] * n,
        out_specs=[pl.BlockSpec(memory_space=ANY)] * n,
        scratch_shapes=[DMA((n, 8, 2)), DMA((n, 8, 2)), DMA((n,))],
        compiler_params=params(cid),
        name="plane_gather",
    )(*arrays)


def plane_exchange(x, cid):
    def kernel(x_ref, o_ref, send, recv, local):
        c = lax.axis_index("ctx")
        greet([{"ctx": flip(c, k)} for k in range(1, 8)])
        here = pltpu.make_async_copy(x_ref.at[c], o_ref.at[c], local)
        here.start()
        sent = []
        for k in (6, 7, 2, 4, 3, 5, 1):
            d = remote(
                x_ref.at[flip(c, k)], o_ref.at[c], send.at[k], recv.at[k], ctx=flip(c, k)
            )
            d.start()
            sent.append(d)
        here.wait()
        for k in (6, 7, 2, 4, 3, 5, 1):
            ref = o_ref.at[flip(c, k)]
            remote(ref, ref, send.at[k], recv.at[k], ctx=flip(c, k)).wait_recv()
        for d in sent:
            d.wait_send()

    return pl.pallas_call(
        kernel,
        out_shape=jax.ShapeDtypeStruct(x.shape, x.dtype),
        in_specs=[pl.BlockSpec(memory_space=ANY)],
        out_specs=pl.BlockSpec(memory_space=ANY),
        scratch_shapes=[DMA((8,)), DMA((8,)), DMA],
        compiler_params=params(cid),
        name="plane_exchange",
    )(x)


def scatter_kernel(p_ref, o_ref, first, total, last, diagonal, s1, v1, s2, v2):
    c = lax.axis_index("ctx")
    greet([{"ctx": flip(c, k)} for k in (1, 2, 4)])
    rows = p_ref.shape[1]
    piece = rows // 2
    pending = []

    def go(d):
        d.start()
        pending.append(d)

    def sl(q):
        return pl.ds(q * piece, piece)

    for j, k in enumerate((6, 2, 4, 0)):
        for q in (0, 1):
            go(
                remote(
                    p_ref.at[flip(c, 1 ^ k), sl(q)],
                    first.at[j, sl(q)],
                    s1.at[j, q],
                    v1.at[j, q],
                    ctx=flip(c, 1),
                )
            )

    def paired(j, q):
        ref = first.at[j, sl(q)]
        remote(ref, ref, s1.at[j, q], v1.at[j, q], ctx=flip(c, 1)).wait_recv()

    def chip(j, k, q):
        return p_ref[flip(c, k), sl(q)].astype(F32) + first[j, sl(q)].astype(F32)

    def came(channel, ref, q, frm):
        remote(ref, ref, s2.at[channel, q], v2.at[channel, q], ctx=flip(c, frm)).wait_recv()

    for q, to in ((0, 2), (1, 4)):
        paired(0, q)
        total[0, sl(q)] = chip(0, 6, q).astype(BF16)
        go(
            remote(
                total.at[0, sl(q)], diagonal.at[sl(q)], s2.at[2, q], v2.at[2, q], ctx=flip(c, to)
            )
        )

    def final(j, k, q, merged):
        v = chip(j, k, q)
        if merged:
            v = v + diagonal[sl(q)].astype(F32)
        total[j, sl(q)] = v.astype(BF16)
        go(
            remote(
                total.at[j, sl(q)],
                last.at[j - 1, sl(q)],
                s2.at[j - 1, q],
                v2.at[j - 1, q],
                ctx=flip(c, k),
            )
        )

    paired(1, 0)
    final(1, 2, 0, False)
    paired(2, 1)
    final(2, 4, 1, False)
    paired(2, 0)
    came(2, diagonal.at[sl(0)], 0, 2)
    final(2, 4, 0, True)
    paired(1, 1)
    came(2, diagonal.at[sl(1)], 1, 4)
    final(1, 2, 1, True)
    for q in (0, 1):
        paired(3, q)
    for q in (0, 1):
        came(0, last.at[0, sl(q)], q, 2)
        came(1, last.at[1, sl(q)], q, 4)
        o_ref[sl(q)] = chip(3, 0, q) + (last[0, sl(q)].astype(F32) + last[1, sl(q)].astype(F32))
    for d in pending:
        d.wait_send()


def plane_scatter(p, cid):
    rows, width = p.shape[1:]
    return pl.pallas_call(
        scatter_kernel,
        out_shape=jax.ShapeDtypeStruct((rows, width), F32),
        in_specs=[pl.BlockSpec(memory_space=VMEM)],
        out_specs=pl.BlockSpec(memory_space=VMEM),
        scratch_shapes=[
            VMEM((4, rows, width), BF16),
            VMEM((3, rows, width), BF16),
            VMEM((2, rows, width), BF16),
            VMEM((rows, width), BF16),
            DMA((4, 2)),
            DMA((4, 2)),
            DMA((3, 2)),
            DMA((3, 2)),
        ],
        compiler_params=params(cid),
        name="plane_scatter",
    )(p)


def contract(a, b, dims):
    return lax.dot_general(a, b, ((dims[0], dims[1]), ((), ())), preferred_element_type=F32)


def lanes(start, size):
    return pl.ds(pl.multiple_of(start, LANES), size)


def turned(u, cosine, sine):
    half = HEAD_SIZE // 2
    a, b = u[:half], u[half:]
    return jnp.concatenate([a * cosine - b * sine, b * cosine + a * sine], 0)


def picked(weight, first, count):
    shape = (count, weight.shape[1])
    hit = lax.broadcasted_iota(jnp.int32, shape, 1) == first + lax.broadcasted_iota(jnp.int32, shape, 0)
    return contract(hit.astype(BF16), weight, ((1,), (1,))).astype(BF16)


def first_kernel(
    x_ref, gain_ref, info_ref, base_ref, step_ref, wq_ref, wk_ref, wv_ref, wo_ref, wg_ref, wu_ref, wd_ref,
    all_ref, qkv_ref, w_ref, table_ref, gains_ref, infos_ref, wo_all, gu_ref, down_ref,
    xs, bases, gsend, grecv, isend, irecv, bsend, brecv, send, recv, zsend, zrecv, osend, orecv, local, parts,
):
    c = lax.axis_index("ctx")
    z = lax.axis_index("fsdp")
    depth = gains_ref.shape[0]
    shard, width = wq_ref.shape
    rows = x_ref.shape[0]
    strip = gu_ref.shape[1] // 2 // depth
    others = [lax.rem(z + k, depth) for k in range(1, depth)]
    greet([{"ctx": flip(c, k)} for k in range(1, 8)] + [{"fsdp": o} for o in others])

    sent = []
    for k, o in enumerate(others):
        sent.append(remote(gain_ref, gains_ref.at[z], gsend.at[k], grecv.at[k], fsdp=o))
    for k in range(1, 8):
        sent.append(remote(info_ref, infos_ref.at[c], isend.at[k], irecv.at[k], ctx=flip(c, k)))
        sent.append(remote(base_ref, bases.at[c], bsend.at[k], brecv.at[k], ctx=flip(c, k)))
    for d in sent:
        d.start()
    out_rows = shard // 8
    mine = pltpu.make_async_copy(wo_ref.at[pl.ds(c * out_rows, out_rows)], wo_all.at[z], parts.at[0])
    mine.start()
    gains_ref[z] = gain_ref[...]
    infos_ref[c] = info_ref[...]
    bases[c] = base_ref[...]

    own = lanes(z * shard, shard)
    count = 2 * HEAD_SIZE
    w_ref[:count, own] = picked(wq_ref[...], c * count, count)
    w_ref[count : count + HEAD_SIZE, own] = picked(wk_ref[...], c * HEAD_SIZE, HEAD_SIZE)
    w_ref[count + HEAD_SIZE :, own] = picked(wv_ref[...], c * HEAD_SIZE, HEAD_SIZE)
    line = Line(z, depth, lambda d: w_ref.at[:, lanes(d * shard, shard)], zsend, zrecv)
    line.step(0)

    x = x_ref[...].astype(F32)
    factor = lax.rsqrt(jnp.mean(x * x, -1, keepdims=True) + EPS)
    for k in range(depth - 1):
        ref = gains_ref.at[lax.rem(z + depth - 1 - k, depth)]
        remote(ref, ref, gsend.at[k], grecv.at[k], fsdp=others[k]).wait_recv()
    gain = jnp.concatenate([gains_ref[k, 0:1, :] for k in range(depth)], 1)
    xs[c] = (x * factor * gain).astype(BF16)
    g = Gather(c, own_half(xs.at[c]), xs, row_half, send, recv)
    g.begin()
    mine.wait()
    out_line = Line(z, depth, lambda d: wo_all.at[d], osend, orecv)
    out_line.step(0)

    copies = [pltpu.make_async_copy(wd_ref.at[pl.ds(c * down_ref.shape[0], down_ref.shape[0])], down_ref, parts.at[1])]
    for i, weight in enumerate((wg_ref, wu_ref)):
        for s in range(depth):
            copies.append(
                pltpu.make_async_copy(
                    weight.at[:, lanes((s * 8 + c) * strip, strip)],
                    gu_ref.at[:, pl.ds((i * depth + s) * strip, strip)],
                    parts.at[2 + i * depth + s],
                )
            )
    for d in copies:
        d.start()

    def keep(k):
        d = pltpu.make_async_copy(xs.at[flip(c, k)], all_ref.at[flip(c, k)], local.at[k])
        d.start()
        copies.append(d)

    keep(0)

    def rotary(k):
        d = flip(c, k)
        if k:
            for ref, s, r in ((bases, bsend, brecv), (infos_ref, isend, irecv)):
                remote(ref.at[d], ref.at[d], s.at[k], r.at[k], ctx=d).wait_recv()
        half = HEAD_SIZE // 2
        step_cos, step_sin = step_ref[:half], step_ref[half:]
        for b in (0, 1):
            start = b * (LANES // 2)
            base_cos = bases[d, :, start : start + 1]
            base_sin = bases[d, :, start + LANES // 4 : start + LANES // 4 + 1]
            at = lanes(d * rows + b * BLOCK, BLOCK)
            table_ref[:half, at] = base_cos * step_cos - base_sin * step_sin
            table_ref[half:, at] = base_sin * step_cos + base_cos * step_sin

    for k in range(8):
        rotary(k)

    def project(k):
        d = flip(c, k)
        at = lanes(d * rows, rows)
        half = HEAD_SIZE // 2
        cosine, sine = table_ref[:half, at], table_ref[half:, at]
        raw = contract(w_ref[...], xs[d], ((1,), (1,)))
        for h in range(3):
            head = slice(h * HEAD_SIZE, (h + 1) * HEAD_SIZE)
            qkv_ref[head, at] = turned(raw[head], cosine, sine).astype(BF16)
        qkv_ref[3 * HEAD_SIZE :, at] = raw[3 * HEAD_SIZE :].astype(BF16)

    line.landed(0)
    line.step(1)
    g.near_half()
    out_line.landed(0)
    out_line.step(1)
    line.landed(1)
    line.step(2)
    g.near_rest()
    keep(2)
    keep(4)
    out_line.landed(1)
    out_line.step(2)
    line.landed(2)
    project(0)
    g.far()
    project(2)
    project(4)
    for channel, k in ((0, 1), (3, 3), (4, 5)):
        g.paired(channel, k)
        keep(k)
        project(k)
    keep(6)
    project(6)
    g.paired(5, 7)
    keep(7)
    project(7)
    out_line.landed(2)
    for d in copies:
        d.wait()
    for d in sent:
        d.wait_send()
    line.sent()
    out_line.sent()
    g.sent()


def first_part(x, gains, info, base, step, weights, depth, cid):
    rows, width = x.shape
    shard = gains.shape[1]
    columns = weights[4].shape[1]
    down_rows = weights[6].shape[0] // 8
    vm = pl.BlockSpec(memory_space=VMEM)
    hbm = pl.BlockSpec(memory_space=ANY)
    shape = jax.ShapeDtypeStruct
    return pl.pallas_call(
        first_kernel,
        out_shape=(
            shape((8, rows, width), BF16),
            shape((4 * HEAD_SIZE, 8 * rows), BF16),
            shape((4 * HEAD_SIZE, width), BF16),
            shape((HEAD_SIZE, 8 * rows), F32),
            shape((depth,) + gains.shape, F32),
            shape((8,) + info.shape, jnp.int32),
            shape((depth, shard // 8, width), BF16),
            shape((shard, 2 * columns // 8), BF16),
            shape((down_rows, width), BF16),
        ),
        in_specs=[vm] * 8 + [hbm] * 4,
        out_specs=(hbm, vm, vm, vm, vm, vm, hbm, hbm, hbm),
        scratch_shapes=[
            VMEM((8, rows, width), BF16),
            VMEM((8,) + base.shape, F32),
            DMA((depth,)),
            DMA((depth,)),
            DMA((8,)),
            DMA((8,)),
            DMA((8,)),
            DMA((8,)),
            DMA((8, 2)),
            DMA((8, 2)),
            DMA((2, depth)),
            DMA((2, depth)),
            DMA((2, depth)),
            DMA((2, depth)),
            DMA((8,)),
            DMA((2 + 2 * depth,)),
        ],
        compiler_params=params(cid),
        name="first_part",
    )(x, gains, info, base, step, *weights)


CHUNK = 512


def whole_block(a):
    return pl.BlockSpec(a.shape, lambda j, *_: (0,) * len(a.shape))


def two_heads(ref, at):
    return jnp.concatenate([ref[:HEAD_SIZE, at], ref[HEAD_SIZE : 2 * HEAD_SIZE, at]], 1)


def causal(s, t, j):
    key = t * CHUNK + lax.broadcasted_iota(jnp.int32, s.shape, 0)
    query = j * BLOCK + lax.broadcasted_iota(jnp.int32, s.shape, 1) % BLOCK
    return jnp.where(key <= query, s, -jnp.inf)


def attend_kernel(order_ref, qkv_ref, o_ref, low_ref, lse_ref, keys, values):
    j = pl.program_id(0)
    tokens = qkv_ref.shape[1]
    factor = HEAD_SIZE ** (-0.5) * math.log2(math.e)

    @pl.when(j == 0)
    def _():
        for b in range(tokens // BLOCK):
            at = lanes(order_ref[b] * BLOCK, BLOCK)
            there = slice(b * BLOCK, (b + 1) * BLOCK)
            keys[there, :] = qkv_ref[2 * HEAD_SIZE : 3 * HEAD_SIZE, at].T
            values[:, there] = qkv_ref[3 * HEAD_SIZE :, at]

    block = order_ref[j]
    at = lanes(block * BLOCK, BLOCK)
    q = two_heads(qkv_ref, at)
    last = j // (CHUNK // BLOCK)

    def step(t, carry, masked):
        top, denom, acc = carry
        s = jnp.dot(keys[pl.ds(pl.multiple_of(t * CHUNK, CHUNK), CHUNK), :], q, preferred_element_type=F32)
        if masked:
            s = causal(s, t, j)
        new_top = jnp.maximum(top, jnp.max(s, 0, keepdims=True))
        p = jnp.exp2((s - new_top) * factor)
        shrink = jnp.exp2((top - new_top) * factor)
        denom = denom * shrink + jnp.sum(p, 0, keepdims=True)
        acc = acc * shrink + jnp.dot(values[:, lanes(t * CHUNK, CHUNK)], p.astype(BF16), preferred_element_type=F32)
        return new_top, denom, acc

    carry = (
        jnp.full((1, 2 * BLOCK), -1e30, F32),
        jnp.zeros((1, 2 * BLOCK), F32),
        jnp.zeros((HEAD_SIZE, 2 * BLOCK), F32),
    )
    carry = lax.fori_loop(0, last, lambda t, state: step(t, state, False), carry)
    top, denom, acc = step(last, carry, True)
    out = acc / denom
    lse_ref[pl.ds(j, 1), :, :] = (top * factor + jnp.log2(denom)).reshape(1, 1, 2 * BLOCK)
    device = block // 2
    within = lanes((block - 2 * device) * BLOCK, BLOCK)
    for h in (0, 1):
        head = slice(h * HEAD_SIZE, (h + 1) * HEAD_SIZE)
        part = out[:, h * BLOCK : (h + 1) * BLOCK]
        o_ref[head, at] = part
        low_ref[device, head, within] = part.astype(BF16)


def attend(order, qkv):
    tokens = qkv.shape[1]
    blocks = tokens // BLOCK
    outs = (
        jax.ShapeDtypeStruct((2 * HEAD_SIZE, tokens), F32),
        jax.ShapeDtypeStruct((8, 2 * HEAD_SIZE, tokens // 8), BF16),
        jax.ShapeDtypeStruct((blocks, 1, 2 * BLOCK), F32),
    )
    return pl.pallas_call(
        attend_kernel,
        grid_spec=pltpu.PrefetchScalarGridSpec(
            num_scalar_prefetch=1,
            grid=(blocks,),
            in_specs=[whole_block(qkv)],
            out_specs=[whole_block(a) for a in outs],
            scratch_shapes=[VMEM((tokens, HEAD_SIZE), BF16), VMEM((HEAD_SIZE, tokens), BF16)],
        ),
        out_shape=outs,
        compiler_params=pltpu.CompilerParams(vmem_limit_bytes=VMEM_BYTES),
        name="attend",
    )(order, qkv)


def attend_back_kernel(
    order_ref, qkv_ref, o_ref, do_ref, lse_ref, table_ref, d_ref, keys, keys_t, values, dk, dv
):
    j = pl.program_id(0)
    tokens = qkv_ref.shape[1]
    scale = HEAD_SIZE ** (-0.5)
    factor = scale * math.log2(math.e)
    half = HEAD_SIZE // 2

    @pl.when(j == 0)
    def _():
        for b in range(tokens // BLOCK):
            at = lanes(order_ref[b] * BLOCK, BLOCK)
            there = slice(b * BLOCK, (b + 1) * BLOCK)
            key = qkv_ref[2 * HEAD_SIZE : 3 * HEAD_SIZE, at]
            keys[there, :] = key.T
            keys_t[:, there] = key
            values[there, :] = qkv_ref[3 * HEAD_SIZE :, at].T
        dk[...] = jnp.zeros_like(dk)
        dv[...] = jnp.zeros_like(dv)

    block = order_ref[j]
    at = lanes(block * BLOCK, BLOCK)
    q = two_heads(qkv_ref, at)
    device = block // 2
    within = lanes((block - 2 * device) * BLOCK, BLOCK)
    do = jnp.concatenate([do_ref[device, :HEAD_SIZE, within], do_ref[device, HEAD_SIZE:, within]], 1)
    delta = jnp.sum(two_heads(o_ref, at) * do.astype(F32), 0, keepdims=True)
    lse = lse_ref[j]
    last = j // (CHUNK // BLOCK)

    def step(t, dq, masked):
        rows = pl.ds(pl.multiple_of(t * CHUNK, CHUNK), CHUNK)
        s = jnp.dot(keys[rows, :], q, preferred_element_type=F32)
        if masked:
            s = causal(s, t, j)
        p = jnp.exp2(s * factor - lse)
        dp = jnp.dot(values[rows, :], do, preferred_element_type=F32)
        ds = (p * (dp - delta)).astype(BF16)
        dv[rows, :] += contract(p.astype(BF16), do, ((1,), (1,)))
        dk[rows, :] += contract(ds, q, ((1,), (1,)))
        return dq + jnp.dot(keys_t[:, lanes(t * CHUNK, CHUNK)], ds, preferred_element_type=F32)

    dq = jnp.zeros((HEAD_SIZE, 2 * BLOCK), F32)
    dq = lax.fori_loop(0, last, lambda t, state: step(t, state, False), dq)
    dq = step(last, dq, True) * scale
    for h in (0, 1):
        head = slice(h * HEAD_SIZE, (h + 1) * HEAD_SIZE)
        d_ref[head, at] = turned(dq[:, h * BLOCK : (h + 1) * BLOCK], table_ref[:half, at], -table_ref[half:, at]).astype(BF16)

    @pl.when(j == tokens // BLOCK - 1)
    def _():
        for b in range(tokens // BLOCK):
            to = lanes(order_ref[b] * BLOCK, BLOCK)
            there = slice(b * BLOCK, (b + 1) * BLOCK)
            d_ref[2 * HEAD_SIZE : 3 * HEAD_SIZE, to] = turned(
                dk[there, :].T * scale, table_ref[:half, to], -table_ref[half:, to]
            ).astype(BF16)
            d_ref[3 * HEAD_SIZE :, to] = dv[there, :].T.astype(BF16)


def attend_back(order, *arrays):
    tokens = arrays[0].shape[1]
    out = jax.ShapeDtypeStruct((4 * HEAD_SIZE, tokens), BF16)
    tall = (tokens, HEAD_SIZE)
    return pl.pallas_call(
        attend_back_kernel,
        grid_spec=pltpu.PrefetchScalarGridSpec(
            num_scalar_prefetch=1,
            grid=(tokens // BLOCK,),
            in_specs=[whole_block(a) for a in arrays],
            out_specs=whole_block(out),
            scratch_shapes=[VMEM(tall, BF16), VMEM(tall[::-1], BF16), VMEM(tall, BF16), VMEM(tall, F32), VMEM(tall, F32)],
        ),
        out_shape=out,
        compiler_params=pltpu.CompilerParams(vmem_limit_bytes=VMEM_BYTES),
        name="attend_back",
    )(order, *arrays)


def last_kernel(a_ref, b_ref, gain_ref, a_all, b_all, sum_ref, by_z, part, by_c, send, recv, local, zs, zr, cs, cr):
    c = lax.axis_index("ctx")
    z = lax.axis_index("fsdp")
    depth, _, shard = by_z.shape
    others = [lax.rem(z + k, depth) for k in range(1, depth)]
    greet([{"ctx": flip(c, k)} for k in range(1, 8)] + [{"fsdp": o} for o in others])
    sent = []
    for k, o in enumerate(others):
        d = remote(gain_ref.at[:, lanes(o * shard, shard)], by_z.at[z], zs.at[k], zr.at[k], fsdp=o)
        d.start()
        sent.append(d)
    gathers = [
        Gather(c, own_half(a_ref), a_all, row_half, send.at[0], recv.at[0]),
        Gather(c, own_half(b_ref, 1), b_all, column_half, send.at[1], recv.at[1]),
    ]
    here = [
        pltpu.make_async_copy(a_ref, a_all.at[c], local.at[0]),
        pltpu.make_async_copy(b_ref, b_all.at[c], local.at[1]),
    ]
    for g in gathers:
        g.begin()
    for d in here:
        d.start()
    total = gain_ref[:, lanes(z * shard, shard)]
    for k in range(depth - 1):
        ref = by_z.at[lax.rem(z + depth - 1 - k, depth)]
        remote(ref, ref, zs.at[k], zr.at[k], fsdp=others[k]).wait_recv()
        total = total + by_z[lax.rem(z + depth - 1 - k, depth)]
    part[...] = total
    for k in range(1, 8):
        d = remote(part, by_c.at[c], cs.at[k], cr.at[k], ctx=flip(c, k))
        d.start()
        sent.append(d)
    by_c[c] = total
    for g in gathers:
        g.finish()
    for k in range(1, 8):
        ref = by_c.at[flip(c, k)]
        remote(ref, ref, cs.at[k], cr.at[k], ctx=flip(c, k)).wait_recv()
    total = by_c[0]
    for k in range(1, 8):
        total = total + by_c[k]
    sum_ref[...] = total
    for d in here:
        d.wait()
    for d in sent:
        d.wait_send()
    for g in gathers:
        g.sent()


def last_gather(a, b, gains, depth, cid):
    shard = gains.shape[1] // depth
    hbm = pl.BlockSpec(memory_space=ANY)
    vm = pl.BlockSpec(memory_space=VMEM)
    small = (8, shard)
    return pl.pallas_call(
        last_kernel,
        out_shape=(
            jax.ShapeDtypeStruct((8,) + a.shape, BF16),
            jax.ShapeDtypeStruct((8,) + b.shape, BF16),
            jax.ShapeDtypeStruct(small, F32),
        ),
        in_specs=[hbm, hbm, vm],
        out_specs=(hbm, hbm, vm),
        scratch_shapes=[
            VMEM((depth,) + small, F32),
            VMEM(small, F32),
            VMEM((8,) + small, F32),
            DMA((2, 8, 2)),
            DMA((2, 8, 2)),
            DMA((2,)),
            DMA((depth,)),
            DMA((depth,)),
            DMA((8,)),
            DMA((8,)),
        ],
        compiler_params=params(cid),
        name="last_gather",
    )(a, b, gains)


def widen_mlp(gate_up, down):
    _, shard, both = gate_up.shape
    mine = both // 2
    depth = mine // LANES
    step = shard // 8

    def kernel(a_ref, d_ref, gate_ref, up_ref, down_ref):
        for i, out in enumerate((gate_ref, up_ref)):
            for c in range(8):
                for s in range(depth):
                    out[:, (s * 8 + c) * LANES : (s * 8 + c + 1) * LANES] = a_ref[
                        c, :, i * mine + s * LANES : i * mine + (s + 1) * LANES
                    ].astype(F32)
        down_ref[...] = d_ref[0].astype(F32)

    _, rows, width = down.shape
    wide = jax.ShapeDtypeStruct((shard, 8 * mine), F32)
    wide_spec = pl.BlockSpec((step, 8 * mine), lambda i: (i, 0))
    return pl.pallas_call(
        kernel,
        grid=(8,),
        out_shape=(wide, wide, jax.ShapeDtypeStruct((8 * rows, width), F32)),
        in_specs=[pl.BlockSpec((8, step, both), lambda i: (0, i, 0)), pl.BlockSpec((1, rows, width), lambda i: (i, 0, 0))],
        out_specs=(wide_spec, wide_spec, pl.BlockSpec((rows, width), lambda i: (i, 0))),
        compiler_params=pltpu.CompilerParams(vmem_limit_bytes=VMEM_BYTES),
        name="widen_mlp",
    )(gate_up, down)


def widen_attention(qkv, out):
    shard = qkv.shape[2]
    width = out.shape[2]

    def kernel(a_ref, o_ref, q_out, k_out, v_out, out_out):
        per_q = 2 * HEAD_SIZE
        for c in range(0, 8, 2):
            both = jnp.concatenate([a_ref[c + i, :per_q, :] for i in (0, 1)], 0)
            q_out[:, c * per_q : (c + 2) * per_q] = both.astype(F32).T
        for target, first in ((k_out, per_q), (v_out, per_q + HEAD_SIZE)):
            for c in range(0, 8, 4):
                four = jnp.concatenate([a_ref[c + i, first : first + HEAD_SIZE, :] for i in range(4)], 0)
                target[:, c * HEAD_SIZE : (c + 4) * HEAD_SIZE] = four.astype(F32).T
        for c in range(8):
            rows = out.shape[1]
            out_out[c * rows : (c + 1) * rows, :] = o_ref[c].astype(F32)

    vm = pl.BlockSpec(memory_space=VMEM)
    shape = lambda n: jax.ShapeDtypeStruct((shard, n), F32)
    heads = 8 * HEAD_SIZE
    return pl.pallas_call(
        kernel,
        out_shape=(shape(2 * heads), shape(heads), shape(heads), shape(width)),
        in_specs=[vm, vm],
        out_specs=(vm, vm, vm, vm),
        compiler_params=pltpu.CompilerParams(vmem_limit_bytes=VMEM_BYTES),
        name="widen_attention",
    )(qkv, out)


def in_plane(
    depth,
    hidden_in,
    positions,
    attn_gain,
    w_query,
    key_projection,
    value_projection,
    w_out,
    mlp_gain,
    w_gate,
    w_up,
    w_down,
    out_grad,
):
    plane = 8
    rows, width = hidden_in.shape[1:]
    tokens = plane * rows
    shard = width // depth
    half = HEAD_SIZE // 2
    mine = w_gate.shape[1] // plane

    position = positions[0]
    lane = lax.broadcasted_iota(jnp.int32, (8, LANES), 1)
    info = jnp.where(lane < LANES // 2, position[0], position[BLOCK])
    gains = jnp.concatenate(
        [
            jnp.broadcast_to(attn_gain.astype(F32)[None], (4, shard)),
            jnp.broadcast_to(mlp_gain.astype(F32)[None], (4, shard)),
        ],
        0,
    )
    freq = THETA ** (-(jnp.arange(half, dtype=F32) * 2.0 / HEAD_SIZE))
    start = freq[:, None] * info[:1].astype(F32)
    quarter = lane[:1] // (LANES // 4)
    base = jnp.where(quarter % 2 == 0, jnp.cos(start), jnp.sin(start))
    inner = freq[:, None] * jnp.arange(BLOCK, dtype=F32)[None]
    step = jnp.concatenate([jnp.cos(inner), jnp.sin(inner)], 0)

    hidden_low = hidden_in[0]
    weights = (w_query, key_projection, value_projection, w_out, w_gate, w_up, w_down)
    normed_all, qkv, qkv_w, table, gains_all, infos, out_slices, gate_up_part, down_part = first_part(
        hidden_low, gains, info, base, step, weights, depth, 0
    )

    def over_depth(a):
        return lax.all_gather(a, "fsdp", axis=0, tiled=True)

    gate_up_w = over_depth(gate_up_part)
    down_w = over_depth(down_part)
    gain_one = gains_all[:, 0].reshape(width)
    gain_two = gains_all[:, 4].reshape(width)
    starts = infos[:, 0].reshape(plane, 2, LANES // 2)[:, :, 0].reshape(2 * plane)
    ranks = (starts - jnp.min(starts)) // BLOCK
    blocks = 2 * plane
    order = jnp.sum(
        jnp.where(ranks[None, :] == jnp.arange(blocks)[:, None], jnp.arange(blocks)[None, :], 0), 1
    ).astype(jnp.int32)

    normed_all = normed_all.reshape(tokens, width)
    attended, attended_low, lse = attend(order, qkv)
    (out_all,) = plane_gather([out_slices.reshape(depth * (shard // plane), width)], 1)
    out_w = out_all.reshape(plane, depth, shard // plane, width).transpose(1, 0, 2, 3).reshape(width, width)
    attended_t = plane_exchange(attended_low, 2).reshape(width, rows)
    hidden = hidden_low.astype(F32)
    mixed = hidden + dot_first(attended_t, out_w)
    normed_two = norm_forward(mixed, gain_two).astype(BF16)
    grad_low = out_grad[0]
    two_all, grad_all = plane_gather([normed_two, grad_low], 3)
    two_all = two_all.reshape(tokens, width)
    grad_all = grad_all.reshape(tokens, width)

    gate_up = jnp.dot(two_all, gate_up_w, preferred_element_type=F32)
    gate, up = gate_up[:, :mine], gate_up[:, mine:]
    sigma = jax.nn.sigmoid(gate)
    active = (gate * sigma * up).astype(BF16)
    down_sum = jnp.dot(active, down_w, preferred_element_type=F32).astype(BF16)
    result = mixed + plane_scatter(down_sum.reshape(plane, rows, width), 5)
    layer_out = result.astype(BF16)[None]

    active_grad = dot_last(grad_all, down_w)
    gate_grad = active_grad * up * sigma * (1.0 + gate * (1.0 - sigma))
    up_grad = active_grad * gate * sigma
    both_grad = jnp.concatenate([gate_grad, up_grad], 1).astype(BF16)
    two_grad_sum = dot_last(both_grad, gate_up_w).astype(BF16)

    def scatter_depth(a, axis=0):
        return lax.psum_scatter(a.astype(BF16), "fsdp", scatter_dimension=axis, tiled=True)

    gate_up_shard = scatter_depth(dot_first(two_all, both_grad))
    down_shard = scatter_depth(dot_first(active, grad_all))

    two_grad = plane_scatter(two_grad_sum.reshape(plane, rows, width), 6)
    mixed_part, gain_two_grad = norm_back(mixed, gain_two, two_grad)
    mixed_grad = grad_low.astype(F32) + mixed_part
    branch_grad = mixed_grad.astype(BF16)

    attended_grad = dot_last(out_w, branch_grad).astype(BF16)
    do = plane_exchange(attended_grad.reshape(plane, 2 * HEAD_SIZE, rows), 7)
    out_wgrad = jnp.dot(attended_t, branch_grad, preferred_element_type=F32).astype(BF16)
    out_rows = out_wgrad.reshape(depth, plane, shard // plane, width).transpose(1, 0, 2, 3)
    out_sum = plane_scatter(out_rows.reshape(plane, shard // plane * depth, width), 9)
    out_shard = scatter_depth(out_sum)

    qkv_grad = attend_back(order, qkv, attended, do, lse, table)
    one_grad_sum = dot_first(qkv_grad, qkv_w).astype(BF16)
    qkv_wgrad = jnp.dot(qkv_grad, normed_all, preferred_element_type=F32).astype(BF16)
    qkv_wgrad = qkv_wgrad.reshape(4 * HEAD_SIZE, depth, shard).transpose(1, 0, 2).reshape(-1, shard)
    qkv_shard = scatter_depth(qkv_wgrad)
    gate_up_all, down_all = plane_gather([gate_up_shard, down_shard], 10)
    gate_total, up_total, down_total = widen_mlp(gate_up_all, down_all)
    one_grad = plane_scatter(one_grad_sum.reshape(plane, rows, width), 8)
    input_part, gain_one_grad = norm_back(hidden, gain_one, one_grad)
    input_grad = (mixed_grad + input_part).astype(BF16)[None]

    gain_rows = jnp.concatenate(
        [jnp.broadcast_to(gain_one_grad[None], (4, width)), jnp.broadcast_to(gain_two_grad[None], (4, width))], 0
    )
    qkv_all, out_grads, gain_sums = last_gather(qkv_shard, out_shard, gain_rows, depth, 11)
    query_total, key_total, value_total, out_total = widen_attention(qkv_all, out_grads)
    return (
        layer_out,
        input_grad,
        gain_sums[0],
        query_total,
        key_total,
        value_total,
        out_total,
        gain_sums[4],
        gate_total,
        up_total,
        down_total,
    )


def solution(mesh):
    placed = (
        P("fsdp", "ctx", None),
        P("fsdp", "ctx"),
        P("fsdp"),
        P("fsdp", None),
        P("fsdp", None),
        P("fsdp", None),
        P("fsdp", None),
        P("fsdp"),
        P("fsdp", None),
        P("fsdp", None),
        P("fsdp", None),
        P("fsdp", "ctx", None),
    )
    body = per_device
    if mesh.shape["ctx"] == KEY_VALUE_HEADS:
        body = functools.partial(in_plane, mesh.shape["fsdp"])
    return jax.shard_map(
        body,
        mesh=mesh,
        in_specs=placed,
        out_specs=(
            P("fsdp", "ctx", None),
            P("fsdp", "ctx", None),
            P("fsdp"),
            P("fsdp", None),
            P("fsdp", None),
            P("fsdp", None),
            P("fsdp", None),
            P("fsdp"),
            P("fsdp", None),
            P("fsdp", None),
            P("fsdp", None),
        ),
        check_vma=False,
    )
```

```python
import functools
import math

import jax
import jax.numpy as jnp
from jax import lax
from jax.experimental import pallas as pl
from jax.experimental.pallas import tpu as pltpu
from jax.sharding import PartitionSpec as P

QUERY_HEADS = 16
KEY_VALUE_HEADS = 8
HEAD_SIZE = 96


EPS = 1e-05
THETA = 100000.0


def tables(token_position):
    half = HEAD_SIZE // 2
    freq = THETA ** (-(jnp.arange(half, dtype=jnp.float32) * 2.0 / HEAD_SIZE))
    angle = token_position.astype(jnp.float32)[:, None] * freq[None, :]
    return (jnp.cos(angle)[:, None, :], jnp.sin(angle)[:, None, :])


def rotary_embed(value_rows, cosine_table, sine_table):
    half = value_rows.shape[-1] // 2
    first = value_rows[..., :half]
    second = value_rows[..., half:]
    return jnp.concatenate(
        [first * cosine_table - second * sine_table, second * cosine_table + first * sine_table], -1
    )


def rotary_embed_backward(grads, cosine_table, sine_table):
    half = grads.shape[-1] // 2
    first = grads[..., :half]
    second = grads[..., half:]
    return jnp.concatenate(
        [first * cosine_table + second * sine_table, second * cosine_table - first * sine_table], -1
    )


def norm_forward(hidden, gain):
    return (
        hidden
        * lax.rsqrt(jnp.mean(hidden * hidden, -1, keepdims=True) + EPS)
        * gain.astype(jnp.float32)
    )


def norm_back(hidden, gain, grad):
    factor = lax.rsqrt(jnp.mean(hidden * hidden, -1, keepdims=True) + EPS)
    scaled = grad * gain.astype(jnp.float32)
    hidden_grad = factor * scaled - hidden * factor * factor * factor * jnp.mean(
        scaled * hidden, -1, keepdims=True
    )
    gain_grad = jnp.sum(grad * hidden * factor, 0)
    return (hidden_grad, gain_grad)


def dot_first(left, right):
    return lax.dot_general(
        left, right, (((0,), (0,)), ((), ())), preferred_element_type=jnp.float32
    )


def dot_last(left, right):
    return lax.dot_general(
        left, right, (((1,), (1,)), ((), ())), preferred_element_type=jnp.float32
    )


def over_blocks(step_fn, carry, arrays):
    block_count = arrays[0].shape[0]
    size = math.gcd(block_count, 512)
    parts = block_count // size
    shaped = tuple((item.reshape((parts, size) + item.shape[1:]) for item in arrays))

    def advance(state, inputs):
        index, pieces = inputs
        return (step_fn(state, pieces, index * size), None)

    final, unused = lax.scan(advance, carry, (jnp.arange(parts, dtype=jnp.int32), shaped))
    return final


def per_device(
    hidden_in,
    positions,
    attn_gain,
    w_query,
    key_projection,
    value_projection,
    w_out,
    mlp_gain,
    w_gate,
    w_up,
    w_down,
    out_grad,
):
    hidden = hidden_in[0].astype(jnp.float32)
    local_rows = hidden.shape[0]
    query_pos = positions[0]
    query_groups = QUERY_HEADS // KEY_VALUE_HEADS
    scale = HEAD_SIZE ** (-0.5)
    cosine_table, sine_table = tables(query_pos)
    attn_set = (
        lax.all_gather(attn_gain, "fsdp", axis=0, tiled=True),
        lax.all_gather(w_query, "fsdp", axis=0, tiled=True),
        lax.all_gather(key_projection, "fsdp", axis=0, tiled=True),
        lax.all_gather(value_projection, "fsdp", axis=0, tiled=True),
        lax.all_gather(w_out, "fsdp", axis=0, tiled=True),
    )
    gain_one, query_w, key_matrix, value_matrix, out_w = attn_set
    first_normed = norm_forward(hidden, gain_one).astype(jnp.bfloat16)
    query_raw = jnp.dot(first_normed, query_w, preferred_element_type=jnp.float32)
    unrotated_key = jnp.dot(first_normed, key_matrix, preferred_element_type=jnp.float32)
    value_raw = jnp.dot(first_normed, value_matrix, preferred_element_type=jnp.float32)
    query_rows = (
        rotary_embed(
            query_raw.reshape(local_rows, QUERY_HEADS, HEAD_SIZE), cosine_table, sine_table
        )
        .astype(jnp.bfloat16)
        .reshape(local_rows, KEY_VALUE_HEADS, query_groups, HEAD_SIZE)
    )
    keys_flat = (
        rotary_embed(
            unrotated_key.reshape(local_rows, KEY_VALUE_HEADS, HEAD_SIZE), cosine_table, sine_table
        )
        .astype(jnp.bfloat16)
        .reshape(local_rows, KEY_VALUE_HEADS * HEAD_SIZE)
    )
    values_flat = value_raw.astype(jnp.bfloat16)
    key_pos_all = lax.all_gather(query_pos, "ctx", axis=0, tiled=True)
    sequence_length = key_pos_all.shape[0]

    def masked_scores(partial_keys, first):
        block_count = partial_keys.shape[0]
        key_pos = lax.dynamic_slice_in_dim(key_pos_all, first, block_count)
        scores = (
            jnp.einsum(
                "tkgd,nkd->kgtn",
                query_rows,
                partial_keys.reshape(block_count, KEY_VALUE_HEADS, HEAD_SIZE),
                preferred_element_type=jnp.float32,
            )
            * scale
        )
        visible = key_pos[None, None, None, :] <= query_pos[None, None, :, None]
        return jnp.where(visible, scores, -jnp.inf)

    def forward_part(carry, part, first):
        top, denom, accum = carry
        partial_keys, partial_values = part
        block_count = partial_keys.shape[0]
        scores = masked_scores(partial_keys, first)
        new_top = jnp.maximum(top, jnp.max(scores, -1))
        weights = jnp.exp(scores - new_top[..., None])
        factor = jnp.exp(top - new_top)
        denom = denom * factor + jnp.sum(weights, -1)
        accum = accum * factor[..., None] + jnp.einsum(
            "kgtn,nkd->kgtd",
            weights.astype(jnp.bfloat16),
            partial_values.reshape(block_count, KEY_VALUE_HEADS, HEAD_SIZE),
            preferred_element_type=jnp.float32,
        )
        return (new_top, denom, accum)

    start_state = (
        jnp.full((KEY_VALUE_HEADS, query_groups, local_rows), -1e30, jnp.float32),
        jnp.zeros((KEY_VALUE_HEADS, query_groups, local_rows), jnp.float32),
        jnp.zeros((KEY_VALUE_HEADS, query_groups, local_rows, HEAD_SIZE), jnp.float32),
    )
    top, denom, accum = over_blocks(
        forward_part,
        start_state,
        (
            lax.all_gather(keys_flat, "ctx", axis=0, tiled=True),
            lax.all_gather(values_flat, "ctx", axis=0, tiled=True),
        ),
    )
    attended_output = accum / denom[..., None]
    log_total = top + jnp.log(denom)
    attended_low = (
        attended_output.transpose(2, 0, 1, 3)
        .reshape(local_rows, QUERY_HEADS * HEAD_SIZE)
        .astype(jnp.bfloat16)
    )
    mixed = hidden + jnp.dot(attended_low, out_w, preferred_element_type=jnp.float32)
    mlp_set = (
        lax.all_gather(mlp_gain, "fsdp", axis=0, tiled=True),
        lax.all_gather(w_gate, "fsdp", axis=0, tiled=True),
        lax.all_gather(w_up, "fsdp", axis=0, tiled=True),
        lax.all_gather(w_down, "fsdp", axis=0, tiled=True),
    )
    gain_two, gate_w, up_w, down_w = mlp_set
    normed_two = norm_forward(mixed, gain_two).astype(jnp.bfloat16)
    gate = jnp.dot(normed_two, gate_w, preferred_element_type=jnp.float32)
    up = jnp.dot(normed_two, up_w, preferred_element_type=jnp.float32)
    sigma = jax.nn.sigmoid(gate)
    active = (gate * sigma * up).astype(jnp.bfloat16)
    result = mixed + jnp.dot(active, down_w, preferred_element_type=jnp.float32)
    layer_out = result.astype(jnp.bfloat16)[None]
    grad_low = out_grad[0]
    grad_out = grad_low.astype(jnp.float32)
    gain_back, gate_back, up_back, down_back = (
        lax.all_gather(mlp_gain, "fsdp", axis=0, tiled=True),
        lax.all_gather(w_gate, "fsdp", axis=0, tiled=True),
        lax.all_gather(w_up, "fsdp", axis=0, tiled=True),
        lax.all_gather(w_down, "fsdp", axis=0, tiled=True),
    )
    down_grad = dot_first(active, grad_low)
    active_grad = dot_last(grad_low, down_back)
    gate_grad = (active_grad * up * sigma * (1.0 + gate * (1.0 - sigma))).astype(jnp.bfloat16)
    up_grad = (active_grad * gate * sigma).astype(jnp.bfloat16)
    gate_wgrad = dot_first(normed_two, gate_grad)
    up_wgrad = dot_first(normed_two, up_grad)
    normed_two_grad = dot_last(gate_grad, gate_back) + dot_last(up_grad, up_back)
    mixed_part, gain_two_grad = norm_back(mixed, gain_back, normed_two_grad)
    mixed_grad = grad_out + mixed_part
    mlp_shards = (
        lax.psum_scatter(
            gain_two_grad.astype(jnp.bfloat16), "fsdp", scatter_dimension=0, tiled=True
        ).astype(jnp.float32),
        lax.psum_scatter(
            gate_wgrad.astype(jnp.bfloat16), "fsdp", scatter_dimension=0, tiled=True
        ).astype(jnp.float32),
        lax.psum_scatter(
            up_wgrad.astype(jnp.bfloat16), "fsdp", scatter_dimension=0, tiled=True
        ).astype(jnp.float32),
        lax.psum_scatter(
            down_grad.astype(jnp.bfloat16), "fsdp", scatter_dimension=0, tiled=True
        ).astype(jnp.float32),
    )
    gain_first, query_back, key_back, value_back, out_back = (
        lax.all_gather(attn_gain, "fsdp", axis=0, tiled=True),
        lax.all_gather(w_query, "fsdp", axis=0, tiled=True),
        lax.all_gather(key_projection, "fsdp", axis=0, tiled=True),
        lax.all_gather(value_projection, "fsdp", axis=0, tiled=True),
        lax.all_gather(w_out, "fsdp", axis=0, tiled=True),
    )
    branch_grad = mixed_grad.astype(jnp.bfloat16)
    out_wgrad = dot_first(attended_low, branch_grad)
    attended_grad = (
        dot_last(branch_grad, out_back)
        .astype(jnp.bfloat16)
        .reshape(local_rows, KEY_VALUE_HEADS, query_groups, HEAD_SIZE)
        .transpose(1, 2, 0, 3)
    )
    delta = jnp.sum(attended_grad.astype(jnp.float32) * attended_output, -1)

    def backward_part(carry, part, first):
        query_acc, key_value_acc = carry
        partial_keys, partial_values = part
        block_count = partial_keys.shape[0]
        probs = jnp.exp(masked_scores(partial_keys, first) - log_total[..., None])
        gradient_of_value = jnp.einsum(
            "kgtn,kgtd->nkd",
            probs.astype(jnp.bfloat16),
            attended_grad,
            preferred_element_type=jnp.float32,
        )
        prob_grad = jnp.einsum(
            "kgtd,nkd->kgtn",
            attended_grad,
            partial_values.reshape(block_count, KEY_VALUE_HEADS, HEAD_SIZE),
            preferred_element_type=jnp.float32,
        )
        score_grad = (probs * (prob_grad - delta[..., None])).astype(jnp.bfloat16)
        query_acc = (
            query_acc
            + jnp.einsum(
                "kgtn,nkd->kgtd",
                score_grad,
                partial_keys.reshape(block_count, KEY_VALUE_HEADS, HEAD_SIZE),
                preferred_element_type=jnp.float32,
            )
            * scale
        )
        gradient_of_key = (
            jnp.einsum("kgtn,tkgd->nkd", score_grad, query_rows, preferred_element_type=jnp.float32)
            * scale
        )
        joined = jnp.concatenate(
            [
                gradient_of_key.reshape(block_count, KEY_VALUE_HEADS * HEAD_SIZE),
                gradient_of_value.reshape(block_count, KEY_VALUE_HEADS * HEAD_SIZE),
            ],
            1,
        )
        key_value_acc = lax.dynamic_update_slice_in_dim(key_value_acc, joined, first, 0)
        return (query_acc, key_value_acc)

    back_state = (
        jnp.zeros((KEY_VALUE_HEADS, query_groups, local_rows, HEAD_SIZE), jnp.float32),
        jnp.zeros((sequence_length, 2 * KEY_VALUE_HEADS * HEAD_SIZE), jnp.float32),
    )
    query_acc, key_value_acc = over_blocks(
        backward_part,
        back_state,
        (
            lax.all_gather(keys_flat, "ctx", axis=0, tiled=True),
            lax.all_gather(values_flat, "ctx", axis=0, tiled=True),
        ),
    )
    local_key_value = lax.psum_scatter(
        key_value_acc.astype(jnp.bfloat16), "ctx", scatter_dimension=0, tiled=True
    ).astype(jnp.float32)
    query_raw_grad = (
        rotary_embed_backward(
            query_acc.transpose(2, 0, 1, 3).reshape(local_rows, QUERY_HEADS, HEAD_SIZE),
            cosine_table,
            sine_table,
        )
        .reshape(local_rows, QUERY_HEADS * HEAD_SIZE)
        .astype(jnp.bfloat16)
    )
    key_raw_grad = (
        rotary_embed_backward(
            local_key_value[:, : KEY_VALUE_HEADS * HEAD_SIZE].reshape(
                local_rows, KEY_VALUE_HEADS, HEAD_SIZE
            ),
            cosine_table,
            sine_table,
        )
        .reshape(local_rows, KEY_VALUE_HEADS * HEAD_SIZE)
        .astype(jnp.bfloat16)
    )
    unrotated_value_gradient = local_key_value[:, KEY_VALUE_HEADS * HEAD_SIZE :].astype(
        jnp.bfloat16
    )
    query_wgrad = dot_first(first_normed, query_raw_grad)
    key_wgrad = dot_first(first_normed, key_raw_grad)
    value_wgrad = dot_first(first_normed, unrotated_value_gradient)
    normed_one_grad = (
        dot_last(query_raw_grad, query_back)
        + dot_last(key_raw_grad, key_back)
        + dot_last(unrotated_value_gradient, value_back)
    )
    input_part, gain_one_grad = norm_back(hidden, gain_first, normed_one_grad)
    input_grad = (mixed_grad + input_part).astype(jnp.bfloat16)[None]
    attn_shards = (
        lax.psum_scatter(
            gain_one_grad.astype(jnp.bfloat16), "fsdp", scatter_dimension=0, tiled=True
        ).astype(jnp.float32),
        lax.psum_scatter(
            query_wgrad.astype(jnp.bfloat16), "fsdp", scatter_dimension=0, tiled=True
        ).astype(jnp.float32),
        lax.psum_scatter(
            key_wgrad.astype(jnp.bfloat16), "fsdp", scatter_dimension=0, tiled=True
        ).astype(jnp.float32),
        lax.psum_scatter(
            value_wgrad.astype(jnp.bfloat16), "fsdp", scatter_dimension=0, tiled=True
        ).astype(jnp.float32),
        lax.psum_scatter(
            out_wgrad.astype(jnp.bfloat16), "fsdp", scatter_dimension=0, tiled=True
        ).astype(jnp.float32),
    )
    totals = (
        lax.psum(attn_shards[0].astype(jnp.bfloat16), "ctx").astype(jnp.float32),
        lax.psum(attn_shards[1].astype(jnp.bfloat16), "ctx").astype(jnp.float32),
        lax.psum(attn_shards[2].astype(jnp.bfloat16), "ctx").astype(jnp.float32),
        lax.psum(attn_shards[3].astype(jnp.bfloat16), "ctx").astype(jnp.float32),
        lax.psum(attn_shards[4].astype(jnp.bfloat16), "ctx").astype(jnp.float32),
        lax.psum(mlp_shards[0].astype(jnp.bfloat16), "ctx").astype(jnp.float32),
        lax.psum(mlp_shards[1].astype(jnp.bfloat16), "ctx").astype(jnp.float32),
        lax.psum(mlp_shards[2].astype(jnp.bfloat16), "ctx").astype(jnp.float32),
        lax.psum(mlp_shards[3].astype(jnp.bfloat16), "ctx").astype(jnp.float32),
    )
    return (
        layer_out,
        input_grad,
        totals[0],
        totals[1],
        totals[2],
        totals[3],
        totals[4],
        totals[5],
        totals[6],
        totals[7],
        totals[8],
    )


MESH = pl.DeviceIdType.MESH
ANY = pl.ANY
VMEM = pltpu.VMEM
DMA = pltpu.SemaphoreType.DMA
LANES = 128
BLOCK = 128
F32 = jnp.float32
BF16 = jnp.bfloat16
VMEM_BYTES = 60 * 2**20


def flip(c, k):
    out = c
    for b in (1, 2, 4):
        if k & b:
            out = out + b - 2 * b * ((c // b) % 2)
    return out


def remote(src, dst, send, recv, **to):
    return pltpu.make_async_remote_copy(
        src_ref=src, dst_ref=dst, send_sem=send, recv_sem=recv, device_id=to, device_id_type=MESH
    )


def greet(peers):
    barrier = pltpu.get_barrier_semaphore()
    for peer in peers:
        pl.semaphore_signal(barrier, inc=1, device_id=peer, device_id_type=MESH)
    pl.semaphore_wait(barrier, len(peers))


class Gather:
    def __init__(self, c, own, buf, at, send, recv):
        self.c, self.own, self.buf, self.at, self.send, self.recv = c, own, buf, at, send, recv
        self.pending = []

    def start(self, channel, who, to, h, own=False):
        there = self.at(self.buf, flip(self.c, who), h)
        d = remote(
            self.own(h) if own else there,
            there,
            self.send.at[channel, h],
            self.recv.at[channel, h],
            ctx=flip(self.c, to),
        )
        d.start()
        self.pending.append(d)

    def arrived(self, channel, who, frm, h):
        ref = self.at(self.buf, flip(self.c, who), h)
        remote(
            ref, ref, self.send.at[channel, h], self.recv.at[channel, h], ctx=flip(self.c, frm)
        ).wait_recv()

    def begin(self):
        self.start(1, 0, 2, 0, own=True)
        self.start(2, 0, 4, 1, own=True)
        self.start(1, 0, 2, 1, own=True)
        self.start(2, 0, 4, 0, own=True)
        self.start(0, 0, 1, 0, own=True)
        self.start(0, 0, 1, 1, own=True)

    def near_half(self):
        self.arrived(1, 2, 2, 0)
        self.start(6, 2, 4, 0)
        self.start(3, 2, 1, 0)
        self.arrived(2, 4, 4, 1)
        self.start(7, 4, 2, 1)
        self.start(4, 4, 1, 1)

    def near_rest(self):
        self.arrived(1, 2, 2, 1)
        self.start(3, 2, 1, 1)
        self.arrived(2, 4, 4, 0)
        self.start(4, 4, 1, 0)

    def far(self):
        self.arrived(6, 6, 4, 0)
        self.start(5, 6, 1, 0)
        self.arrived(7, 6, 2, 1)
        self.start(5, 6, 1, 1)

    def paired(self, channel, who):
        for h in (0, 1):
            self.arrived(channel, who, 1, h)

    def finish(self):
        self.near_half()
        self.near_rest()
        self.far()
        for channel, who in ((0, 1), (3, 3), (4, 5), (5, 7)):
            self.paired(channel, who)

    def sent(self):
        for d in self.pending:
            d.wait_send()


def row_half(ref, d, h):
    half = ref.shape[1] // 2
    return ref.at[d, pl.ds(h * half, half)]


def column_half(ref, d, h):
    half = ref.shape[2] // 2
    return ref.at[d, :, pl.ds(h * half, half)]


def own_half(ref, axis=0):
    half = ref.shape[axis] // 2
    return lambda h: ref.at[(slice(None),) * axis + (pl.ds(h * half, half),)]


class Line:
    def __init__(self, z, depth, at, send, recv):
        self.z, self.depth, self.at, self.send, self.recv = z, depth, at, send, recv

    def copy(self, way, k, part, to):
        ref = self.at(part)
        return remote(ref, ref, self.send.at[way, k], self.recv.at[way, k], fsdp=to)

    def step(self, k):
        z, top = self.z, self.depth - 1

        @pl.when((z >= k) & (z < top))
        def _():
            self.copy(0, k, z - k, z + 1).start()

        @pl.when((z + k <= top) & (z > 0))
        def _():
            self.copy(1, k, z + k, z - 1).start()

    def landed(self, k):
        z, top = self.z, self.depth - 1

        @pl.when(z >= k + 1)
        def _():
            self.copy(0, k, z - 1 - k, z - 1).wait_recv()

        @pl.when(z + 1 + k <= top)
        def _():
            self.copy(1, k, z + 1 + k, z + 1).wait_recv()

    def sent(self, steps):
        z, top = self.z, self.depth - 1
        for k in steps:

            @pl.when((z >= k) & (z < top))
            def _():
                self.copy(0, k, z - k, z + 1).wait_send()

            @pl.when((z + k <= top) & (z > 0))
            def _():
                self.copy(1, k, z + k, z - 1).wait_send()


def params(cid):
    return pltpu.CompilerParams(
        collective_id=cid, has_side_effects=True, vmem_limit_bytes=VMEM_BYTES
    )


def contract(a, b, dims):
    return lax.dot_general(a, b, ((dims[0], dims[1]), ((), ())), preferred_element_type=F32)


def lanes(start, size):
    return pl.ds(pl.multiple_of(start, LANES), size)


def turned(u, cosine, sine):
    half = HEAD_SIZE // 2
    a, b = u[:half], u[half:]
    return jnp.concatenate([a * cosine - b * sine, b * cosine + a * sine], 0)


def picked(weight, first, count):
    shape = (count, weight.shape[1])
    hit = lax.broadcasted_iota(jnp.int32, shape, 1) == first + lax.broadcasted_iota(jnp.int32, shape, 0)
    return contract(hit.astype(BF16), weight, ((1,), (1,))).astype(BF16)


def first_kernel(
    x_ref, gain_ref, info_ref, base_ref, step_ref, wq_ref, wk_ref, wv_ref, wo_ref, wg_ref, wu_ref, wd_ref, grad_ref,
    all_ref, qkv_ref, w_ref, table_ref, gains_ref, infos_ref, wo_all, gu_all, down_all, grad_all,
    xs, bases, gsend, grecv, isend, irecv, bsend, brecv, send, recv, zsend, zrecv, osend, orecv,
    usend, urecv, dsend, drecv, send2, recv2, local, parts,
):
    c = lax.axis_index("ctx")
    z = lax.axis_index("fsdp")
    depth = gains_ref.shape[0]
    shard, width = wq_ref.shape
    rows = x_ref.shape[0]
    strip = gu_all.shape[2] // 2 // depth
    down_rows = down_all.shape[1]
    others = [lax.rem(z + k, depth) for k in range(1, depth)]
    greet([{"ctx": flip(c, k)} for k in range(1, 8)] + [{"fsdp": o} for o in others])

    sent = []
    for k, o in enumerate(others):
        sent.append(remote(gain_ref, gains_ref.at[z], gsend.at[k], grecv.at[k], fsdp=o))
    for k in range(1, 8):
        sent.append(remote(info_ref, infos_ref.at[c], isend.at[k], irecv.at[k], ctx=flip(c, k)))
        sent.append(remote(base_ref, bases.at[c], bsend.at[k], brecv.at[k], ctx=flip(c, k)))
    for d in sent:
        d.start()
    out_rows = shard // 8
    mine = pltpu.make_async_copy(wo_ref.at[pl.ds(c * out_rows, out_rows)], wo_all.at[z], parts.at[0])
    mine.start()
    gains_ref[z] = gain_ref[...]
    infos_ref[c] = info_ref[...]
    bases[c] = base_ref[...]

    own = lanes(z * shard, shard)
    count = 2 * HEAD_SIZE
    w_ref[:count, own] = picked(wq_ref[...], c * count, count)
    w_ref[count : count + HEAD_SIZE, own] = picked(wk_ref[...], c * HEAD_SIZE, HEAD_SIZE)
    w_ref[count + HEAD_SIZE :, own] = picked(wv_ref[...], c * HEAD_SIZE, HEAD_SIZE)
    line = Line(z, depth, lambda d: w_ref.at[:, lanes(d * shard, shard)], zsend, zrecv)
    line.step(0)

    x = x_ref[...].astype(F32)
    factor = lax.rsqrt(jnp.mean(x * x, -1, keepdims=True) + EPS)
    for k in range(depth - 1):
        ref = gains_ref.at[lax.rem(z + depth - 1 - k, depth)]
        remote(ref, ref, gsend.at[k], grecv.at[k], fsdp=others[k]).wait_recv()
    gain = jnp.concatenate([gains_ref[k, 0:1, :] for k in range(depth)], 1)
    xs[c] = (x * factor * gain).astype(BF16)
    g = Gather(c, own_half(xs.at[c]), xs, row_half, send, recv)
    g.begin()
    mine.wait()
    out_line = Line(z, depth, lambda d: wo_all.at[d], osend, orecv)
    out_line.step(0)

    first = [pltpu.make_async_copy(wd_ref.at[pl.ds(c * down_rows, down_rows)], down_all.at[z], parts.at[1])]
    for i, weight in enumerate((wg_ref, wu_ref)):
        for s in range(depth):
            first.append(
                pltpu.make_async_copy(
                    weight.at[:, lanes((s * 8 + c) * strip, strip)],
                    gu_all.at[z, :, pl.ds((i * depth + s) * strip, strip)],
                    parts.at[2 + i * depth + s],
                )
            )
    for d in first:
        d.start()
    copies = [pltpu.make_async_copy(grad_ref, grad_all.at[c], parts.at[2 + 2 * depth])]
    copies[0].start()

    def keep(k):
        d = pltpu.make_async_copy(xs.at[flip(c, k)], all_ref.at[flip(c, k)], local.at[k])
        d.start()
        copies.append(d)

    keep(0)

    def rotary(k):
        d = flip(c, k)
        if k:
            for ref, s, r in ((bases, bsend, brecv), (infos_ref, isend, irecv)):
                remote(ref.at[d], ref.at[d], s.at[k], r.at[k], ctx=d).wait_recv()
        half = HEAD_SIZE // 2
        step_cos, step_sin = step_ref[:half], step_ref[half:]
        for b in (0, 1):
            start = b * (LANES // 2)
            base_cos = bases[d, :, start : start + 1]
            base_sin = bases[d, :, start + LANES // 4 : start + LANES // 4 + 1]
            table_ref[2 * d + b, :half] = base_cos * step_cos - base_sin * step_sin
            table_ref[2 * d + b, half:] = base_sin * step_cos + base_cos * step_sin

    for k in range(8):
        rotary(k)

    def project(k):
        d = flip(c, k)
        half = HEAD_SIZE // 2
        raw = contract(w_ref[...], xs[d], ((1,), (1,)))
        for b in (0, 1):
            cosine, sine = table_ref[2 * d + b, :half], table_ref[2 * d + b, half:]
            part = raw[:, b * BLOCK : (b + 1) * BLOCK]
            for h in range(3):
                head = slice(h * HEAD_SIZE, (h + 1) * HEAD_SIZE)
                qkv_ref[2 * d + b, head] = turned(part[head], cosine, sine).astype(BF16)
            qkv_ref[2 * d + b, 3 * HEAD_SIZE :] = part[3 * HEAD_SIZE :].astype(BF16)

    line.landed(0)
    line.step(1)
    g.near_half()
    out_line.landed(0)
    out_line.step(1)
    line.landed(1)
    line.step(2)
    g.near_rest()
    keep(2)
    keep(4)
    out_line.landed(1)
    out_line.step(2)
    line.landed(2)
    for d in first:
        d.wait()
    gu_line = Line(z, depth, lambda d: gu_all.at[d], usend, urecv)
    down_line = Line(z, depth, lambda d: down_all.at[d], dsend, drecv)
    gu_line.step(0)
    down_line.step(0)
    g2 = Gather(c, own_half(grad_ref), grad_all, row_half, send2, recv2)
    g2.begin()
    project(0)
    g.far()
    project(2)
    project(4)
    for channel, k in ((0, 1), (3, 3)):
        g.paired(channel, k)
        keep(k)
        project(k)
    g2.near_half()
    g.paired(4, 5)
    keep(5)
    project(5)
    keep(6)
    project(6)
    g.paired(5, 7)
    keep(7)
    project(7)
    g2.near_rest()
    out_line.landed(2)
    gu_line.landed(0)
    down_line.landed(0)
    g2.far()
    for channel, k in ((0, 1), (3, 3), (4, 5), (5, 7)):
        g2.paired(channel, k)
    for d in copies:
        d.wait()
    for d in sent:
        d.wait_send()
    line.sent((0, 1, 2))
    out_line.sent((0, 1, 2))
    gu_line.sent((0,))
    down_line.sent((0,))
    g.sent()
    g2.sent()


def first_part(x, gains, info, base, step, weights, grad, depth, cid):
    rows, width = x.shape
    shard = gains.shape[1]
    columns = weights[4].shape[1]
    down_rows = weights[6].shape[0] // 8
    vm = pl.BlockSpec(memory_space=VMEM)
    hbm = pl.BlockSpec(memory_space=ANY)
    shape = jax.ShapeDtypeStruct
    return pl.pallas_call(
        first_kernel,
        out_shape=(
            shape((8, rows, width), BF16),
            shape((8 * rows // BLOCK, 4 * HEAD_SIZE, BLOCK), BF16),
            shape((4 * HEAD_SIZE, width), BF16),
            shape((8 * rows // BLOCK, HEAD_SIZE, BLOCK), F32),
            shape((depth,) + gains.shape, F32),
            shape((8,) + info.shape, jnp.int32),
            shape((depth, shard // 8, width), BF16),
            shape((depth, shard, 2 * columns // 8), BF16),
            shape((depth, down_rows, width), BF16),
            shape((8, rows, width), BF16),
        ),
        in_specs=[vm] * 8 + [hbm] * 5,
        out_specs=(hbm, vm, vm, vm, vm, vm, hbm, hbm, hbm, hbm),
        scratch_shapes=[
            VMEM((8, rows, width), BF16),
            VMEM((8,) + base.shape, F32),
            DMA((depth,)),
            DMA((depth,)),
            DMA((8,)),
            DMA((8,)),
            DMA((8,)),
            DMA((8,)),
            DMA((8, 2)),
            DMA((8, 2)),
        ]
        + [DMA((2, depth))] * 8
        + [DMA((8, 2)), DMA((8, 2)), DMA((8,)), DMA((3 + 2 * depth,))],
        compiler_params=params(cid),
        name="first_part",
    )(x, gains, info, base, step, *weights, grad)


CHUNK = 512


def whole_block(a):
    return pl.BlockSpec(a.shape, lambda j, *_: (0,) * len(a.shape))


def two_heads(ref, block):
    return jnp.concatenate([ref[block, :HEAD_SIZE], ref[block, HEAD_SIZE : 2 * HEAD_SIZE]], 1)


def causal(s, t, j):
    key = t * CHUNK + lax.broadcasted_iota(jnp.int32, s.shape, 0)
    query = j * BLOCK + lax.broadcasted_iota(jnp.int32, s.shape, 1) % BLOCK
    return jnp.where(key <= query, s, -jnp.inf)


def attend_kernel(
    order_ref, qkv_ref, ow_ref, gu_in, down_in, o_ref, low_ref, lse_ref, ow_all, gu_all, down_all,
    keys, values, send, recv, local, usend, urecv, dsend, drecv,
):
    c = lax.axis_index("ctx")
    z = lax.axis_index("fsdp")
    depth = gu_all.shape[0]
    others = [lax.rem(z + k, depth) for k in range(1, depth)]
    greet([{"ctx": flip(c, k)} for k in (1, 2, 4)] + [{"fsdp": o} for o in others])
    few = depth // 2
    g = Gather(
        c,
        lambda h: ow_ref.at[pl.ds(h * few, few)],
        ow_all,
        lambda ref, d, h: ref.at[pl.ds(h * few, few), d],
        send,
        recv,
    )
    here = pltpu.make_async_copy(ow_ref, ow_all.at[:, c], local)
    here.start()
    g.begin()
    gu_line = Line(z, depth, lambda d: gu_all.at[d], usend, urecv)
    down_line = Line(z, depth, lambda d: down_all.at[d], dsend, drecv)
    gu_line.step(1)
    down_line.step(1)

    blocks = qkv_ref.shape[0]
    per = CHUNK // BLOCK
    factor = HEAD_SIZE ** (-0.5) * math.log2(math.e)
    for b in range(blocks):
        there = slice(b * BLOCK, (b + 1) * BLOCK)
        keys[there, :] = qkv_ref[order_ref[b], 2 * HEAD_SIZE : 3 * HEAD_SIZE].T
        values[:, there] = qkv_ref[order_ref[b], 3 * HEAD_SIZE :]

    def attend_block(j, last):
        q = two_heads(qkv_ref, order_ref[j])

        def step(t, carry, masked):
            top, denom, acc = carry
            s = jnp.dot(keys[pl.ds(t * CHUNK, CHUNK), :], q, preferred_element_type=F32)
            if masked:
                s = causal(s, t, j)
            new_top = jnp.maximum(top, jnp.max(s, 0, keepdims=True))
            p = jnp.exp2((s - new_top) * factor)
            shrink = jnp.exp2((top - new_top) * factor)
            denom = denom * shrink + jnp.sum(p, 0, keepdims=True)
            acc = acc * shrink + jnp.dot(
                values[:, pl.ds(t * CHUNK, CHUNK)], p.astype(BF16), preferred_element_type=F32
            )
            return new_top, denom, acc

        carry = (
            jnp.full((1, 2 * BLOCK), -1e30, F32),
            jnp.zeros((1, 2 * BLOCK), F32),
            jnp.zeros((HEAD_SIZE, 2 * BLOCK), F32),
        )
        for t in range(last):
            carry = step(t, carry, False)
        top, denom, acc = step(last, carry, True)
        out = acc / denom
        lse_ref[pl.ds(j, 1), :, :] = (top * factor + jnp.log2(denom)).reshape(1, 1, 2 * BLOCK)
        for h in (0, 1):
            head = slice(h * HEAD_SIZE, (h + 1) * HEAD_SIZE)
            part = out[:, h * BLOCK : (h + 1) * BLOCK]
            o_ref[j, head] = part
            low_ref[j, head] = part.astype(BF16)

    turns = blocks // per
    for turn in range(turns):

        @pl.loop(turn * per, (turn + 1) * per)
        def _(j):
            attend_block(j, turn)

        if turn == 1:
            g.near_half()
        if turn == 2:
            g.near_rest()
    g.far()
    for channel, k in ((0, 1), (3, 3), (4, 5), (5, 7)):
        g.paired(channel, k)
    here.wait()
    gu_line.landed(1)
    down_line.landed(1)
    g.sent()
    gu_line.sent((1,))
    down_line.sent((1,))


def attend(order, qkv, out_part, gate_up, down, cid):
    blocks = qkv.shape[0]
    tokens = blocks * BLOCK
    depth, some, width = out_part.shape
    outs = (
        jax.ShapeDtypeStruct((blocks, 2 * HEAD_SIZE, BLOCK), F32),
        jax.ShapeDtypeStruct((blocks, 2 * HEAD_SIZE, BLOCK), BF16),
        jax.ShapeDtypeStruct((blocks, 1, 2 * BLOCK), F32),
        jax.ShapeDtypeStruct((depth, 8, some, width), BF16),
        jax.ShapeDtypeStruct(gate_up.shape, BF16),
        jax.ShapeDtypeStruct(down.shape, BF16),
    )
    vm = pl.BlockSpec(memory_space=VMEM)
    hbm = pl.BlockSpec(memory_space=ANY)
    return pl.pallas_call(
        attend_kernel,
        out_shape=outs,
        in_specs=[pl.BlockSpec(memory_space=pltpu.SMEM), vm, hbm, hbm, hbm],
        out_specs=(vm, vm, vm, hbm, hbm, hbm),
        scratch_shapes=[VMEM((tokens, HEAD_SIZE), BF16), VMEM((HEAD_SIZE, tokens), BF16), DMA((8, 2)), DMA((8, 2)), DMA]
        + [DMA((2, depth))] * 4,
        input_output_aliases={3: 4, 4: 5},
        compiler_params=params(cid),
        name="attend",
    )(order, qkv, out_part, gate_up, down)


class Scatter:
    ORDER = (6, 2, 4, 0)

    def __init__(self, c, p, first, last, diagonal, s1, v1, s2, v2):
        self.c, self.p, self.first = c, p, first
        self.last, self.diagonal = last, diagonal
        self.s1, self.v1, self.s2, self.v2 = s1, v1, s2, v2
        self.half = p.shape[1] // 2
        self.pending = []

    @staticmethod
    def scratch(rows, width):
        return [
            VMEM((4, rows, width), BF16),
            VMEM((2, rows, width), BF16),
            VMEM((rows, width), BF16),
            DMA((4, 2)),
            DMA((4, 2)),
            DMA((3, 2)),
            DMA((3, 2)),
        ]

    def sl(self, q):
        return pl.ds(q * self.half, self.half)

    def go(self, d):
        d.start()
        self.pending.append(d)

    def give(self, k):
        j = self.ORDER.index(k)
        for q in (0, 1):
            source = self.p.at[flip(self.c, 1 ^ k), self.sl(q)]
            there = self.first.at[j, self.sl(q)]
            self.go(remote(source, there, self.s1.at[j, q], self.v1.at[j, q], ctx=flip(self.c, 1)))

    def paired(self, j, q):
        ref = self.first.at[j, self.sl(q)]
        remote(ref, ref, self.s1.at[j, q], self.v1.at[j, q], ctx=flip(self.c, 1)).wait_recv()

    def chip(self, j, q):
        k = self.ORDER[j]
        return self.p[flip(self.c, k), self.sl(q)].astype(F32) + self.first[j, self.sl(q)].astype(F32)

    def came(self, channel, ref, q, frm):
        remote(
            ref, ref, self.s2.at[channel, q], self.v2.at[channel, q], ctx=flip(self.c, frm)
        ).wait_recv()

    def far(self):
        for q, to in ((0, 2), (1, 4)):
            self.paired(0, q)
            self.first[0, self.sl(q)] = self.chip(0, q).astype(BF16)
            self.go(
                remote(
                    self.first.at[0, self.sl(q)],
                    self.diagonal.at[self.sl(q)],
                    self.s2.at[2, q],
                    self.v2.at[2, q],
                    ctx=flip(self.c, to),
                )
            )

    def onward(self, j, q, merged):
        v = self.chip(j, q)
        if merged:
            v = v + self.diagonal[self.sl(q)].astype(F32)
        self.first[j, self.sl(q)] = v.astype(BF16)
        self.go(
            remote(
                self.first.at[j, self.sl(q)],
                self.last.at[j - 1, self.sl(q)],
                self.s2.at[j - 1, q],
                self.v2.at[j - 1, q],
                ctx=flip(self.c, self.ORDER[j]),
            )
        )

    def direct(self):
        self.paired(1, 0)
        self.onward(1, 0, False)
        self.paired(2, 1)
        self.onward(2, 1, False)

    def merged(self):
        self.paired(2, 0)
        self.came(2, self.diagonal.at[self.sl(0)], 0, 2)
        self.onward(2, 0, True)
        self.paired(1, 1)
        self.came(2, self.diagonal.at[self.sl(1)], 1, 4)
        self.onward(1, 1, True)

    def result(self, q):
        self.paired(3, q)
        self.came(0, self.last.at[0, self.sl(q)], q, 2)
        self.came(1, self.last.at[1, self.sl(q)], q, 4)
        return self.chip(3, q) + (
            self.last[0, self.sl(q)].astype(F32) + self.last[1, self.sl(q)].astype(F32)
        )

    def sent(self):
        for d in self.pending:
            d.wait_send()


def exchange_start(c, source, target, send, recv):
    sent = []
    for k in (6, 7, 2, 4, 3, 5, 1):
        there = target.at[pl.ds(2 * c, 2)]
        d = remote(source.at[pl.ds(2 * flip(c, k), 2)], there, send.at[k], recv.at[k], ctx=flip(c, k))
        d.start()
        sent.append(d)
    return sent


def exchange_landed(c, target, send, recv):
    for k in (6, 7, 2, 4, 3, 5, 1):
        ref = target.at[pl.ds(2 * flip(c, k), 2)]
        remote(ref, ref, send.at[k], recv.at[k], ctx=flip(c, k)).wait_recv()


def both_blocks(ref, i):
    return jnp.concatenate([ref[2 * i], ref[2 * i + 1]], 1)


def middle_kernel(
    rank_ref, low_ref, x_ref, gains_ref, g_ref, ow_ref, gu_in, down_in,
    mixed_ref, mgrad_ref, gsum_ref, do_ref, owg_ref, gug_ref, dg_ref, p1_ref, gu_all, down_all,
    out_w, wgu, wd, grads, two, p2, act, dgu, stage, give, got,
    first, last, diagonal, s1, v1, s2, v2,
    esend, erecv, fsend, frecv, send, recv, usend, urecv, dsend, drecv, load, put, wput,
):
    c = lax.axis_index("ctx")
    z = lax.axis_index("fsdp")
    depth, shard, both = gu_all.shape
    mine = both // 2
    rows, width = x_ref.shape
    rows_of_out = out_w.shape[1]
    others = [lax.rem(z + k, depth) for k in range(1, depth)]
    greet([{"ctx": flip(c, k)} for k in range(1, 8)] + [{"fsdp": o} for o in others])
    gu_line = Line(z, depth, lambda d: gu_all.at[d], usend, urecv)
    down_line = Line(z, depth, lambda d: down_all.at[d], dsend, drecv)
    gu_line.step(2)
    down_line.step(2)
    loads = [pltpu.make_async_copy(ow_ref, out_w, load.at[0]), pltpu.make_async_copy(g_ref, grads, load.at[1])]
    for d in loads:
        d.start()

    for i in range(rank_ref.shape[0]):
        give[i] = low_ref[rank_ref[i]]
    sent = exchange_start(c, give, got, esend, erecv)
    got[pl.ds(2 * c, 2)] = give[pl.ds(2 * c, 2)]
    loads[0].wait()
    exchange_landed(c, got, esend, erecv)
    x = lax.fori_loop(
        0, 8, lambda i, total: total + contract(both_blocks(got, i), out_w[i], ((0,), (0,))), x_ref[...].astype(F32)
    )
    mixed_ref[...] = x
    gain = jnp.concatenate([gains_ref[k, 4:5, :] for k in range(depth)], 1)
    factor = lax.rsqrt(jnp.mean(x * x, -1, keepdims=True) + EPS)
    two[c] = (x * factor * gain).astype(BF16)
    g = Gather(c, own_half(two.at[c]), two, row_half, send, recv)
    g.begin()
    loads[1].wait()
    gu_line.landed(2)
    weights = [pltpu.make_async_copy(gu_all, wgu, load.at[2])]
    weights[0].start()
    down_line.landed(2)
    weights.append(pltpu.make_async_copy(down_all, wd, load.at[3]))
    weights[1].start()
    for d in weights:
        d.wait()

    def block(d, slot):
        up_w = wgu[...].reshape(width, both)
        down_w = wd[...].reshape(mine, width)
        gate_up = jnp.dot(two[d], up_w, preferred_element_type=F32)
        gate, up = gate_up[:, :mine], gate_up[:, mine:]
        sigma = jax.nn.sigmoid(gate)
        silu = gate * sigma
        active = (silu * up).astype(BF16)
        act[d] = active
        active_grad = contract(grads[d], down_w, ((1,), (1,)))
        gate_grad = active_grad * up * sigma * (1.0 + gate * (1.0 - sigma))
        up_grad = active_grad * silu
        grad = jnp.concatenate([gate_grad, up_grad], 1).astype(BF16)
        dgu[d] = grad
        p2[d] = contract(grad, up_w, ((1,), (1,))).astype(BF16)
        stage[slot] = jnp.dot(active, down_w, preferred_element_type=F32).astype(BF16)
        pltpu.make_async_copy(stage.at[slot], p1_ref.at[d], put.at[slot]).start()

    def drain(slot):
        pltpu.make_async_copy(stage.at[slot], p1_ref.at[c], put.at[slot]).wait()

    def pair(k, again):
        d = flip(c, k)
        other = flip(c, 1 ^ k)

        @pl.loop(0, 2)
        def _(i):
            if again:
                drain(i)
            block(other + i * (d - other), i)

    scatter = Scatter(c, p2, first, last, diagonal, s1, v1, s2, v2)
    g.paired(0, 1)
    pair(0, False)
    scatter.give(0)
    g.near_half()
    g.near_rest()
    g.paired(3, 3)
    pair(2, True)
    scatter.give(2)
    g.far()
    g.paired(5, 7)
    pair(6, True)
    scatter.give(6)
    g.paired(4, 5)
    scatter.far()
    pair(4, True)
    scatter.give(4)
    scatter.direct()

    puts = []

    def wide(f):
        part = lambda i, total: total + contract(
            two[pl.ds(2 * i, 2), :, f * shard : (f + 1) * shard].reshape(2 * rows, shard),
            dgu[pl.ds(2 * i, 2)].reshape(2 * rows, both),
            ((0,), (0,)),
        )
        wgu[f] = lax.fori_loop(0, 4, part, jnp.zeros((shard, both), F32)).astype(BF16)
        puts.append(pltpu.make_async_copy(wgu.at[f], gug_ref.at[f], wput.at[f]))
        puts[-1].start()

    wide(0)
    scatter.merged()
    for f in range(1, depth):
        wide(f)
    strip = mine // depth
    for f in range(0, depth, 2):
        part = lambda i, total: total + contract(
            act[pl.ds(2 * i, 2), :, f * strip : (f + 2) * strip].reshape(2 * rows, 2 * strip),
            grads[pl.ds(2 * i, 2)].reshape(2 * rows, width),
            ((0,), (0,)),
        )
        part = lax.fori_loop(0, 4, part, jnp.zeros((2 * strip, width), F32))
        wd[f : f + 2] = part.astype(BF16).reshape(2, strip, width)
    puts.append(pltpu.make_async_copy(wd, dg_ref, wput.at[depth]))
    puts[-1].start()

    two_grad = jnp.concatenate([scatter.result(0), scatter.result(1)], 0)
    x = mixed_ref[...]
    factor = lax.rsqrt(jnp.mean(x * x, -1, keepdims=True) + EPS)
    scaled = two_grad * gain
    mixed_grad = (
        grads[c].astype(F32)
        + factor * scaled
        - x * (factor * factor * factor) * jnp.mean(scaled * x, -1, keepdims=True)
    )
    gsum_ref[...] = jnp.broadcast_to(jnp.sum(two_grad * x * factor, 0, keepdims=True), gsum_ref.shape)
    mgrad_ref[...] = mixed_grad
    branch = mixed_grad.astype(BF16)
    for d in sent:
        d.wait_send()
    for i in range(8):
        part = contract(out_w[i], branch, ((1,), (1,))).astype(BF16)
        give[2 * i] = part[:, :BLOCK]
        give[2 * i + 1] = part[:, BLOCK:]
    sent = exchange_start(c, give, do_ref, fsend, frecv)
    do_ref[pl.ds(2 * c, 2)] = give[pl.ds(2 * c, 2)]
    for d in puts:
        d.wait()
    for i in (0, 1):
        drain(i)
    few = rows_of_out // depth
    for i in range(8):
        part = jnp.dot(both_blocks(got, i), branch, preferred_element_type=F32).astype(BF16)
        f = i * depth // 8
        for t in range(depth):
            out_w[i * depth % 8 + t, f * few : (f + 1) * few] = part[t * few : (t + 1) * few]
    out_put = pltpu.make_async_copy(out_w, owg_ref, load.at[0])
    out_put.start()
    exchange_landed(c, do_ref, fsend, frecv)
    out_put.wait()
    for d in sent:
        d.wait_send()
    scatter.sent()
    g.sent()
    gu_line.sent((2,))
    down_line.sent((2,))


def middle(rank, low, x, gains, grad_all, out_w, gate_up, down, cid):
    rows, width = x.shape
    depth, shard, both = gate_up.shape
    shape = jax.ShapeDtypeStruct
    vm = pl.BlockSpec(memory_space=VMEM)
    hbm = pl.BlockSpec(memory_space=ANY)
    heads = (8 * rows // BLOCK, 2 * HEAD_SIZE, BLOCK)
    block = (8, rows, width)
    return pl.pallas_call(
        middle_kernel,
        out_shape=(
            shape((rows, width), F32),
            shape((rows, width), F32),
            shape((8, width), F32),
            shape(heads, BF16),
            shape(out_w.shape, BF16),
            shape(gate_up.shape, BF16),
            shape(down.shape, BF16),
            shape(block, BF16),
            shape(gate_up.shape, BF16),
            shape(down.shape, BF16),
        ),
        in_specs=[pl.BlockSpec(memory_space=pltpu.SMEM), vm, vm, vm, hbm, hbm, hbm, hbm],
        out_specs=(vm, vm, vm, vm, hbm, hbm, hbm, hbm, hbm, hbm),
        scratch_shapes=[
            VMEM(out_w.shape, BF16),
            VMEM(gate_up.shape, BF16),
            VMEM(down.shape, BF16),
            VMEM(block, BF16),
            VMEM(block, BF16),
            VMEM(block, BF16),
            VMEM((8, rows, both // 2), BF16),
            VMEM((8, rows, both), BF16),
            VMEM((2, rows, width), BF16),
            VMEM(heads, BF16),
            VMEM(heads, BF16),
        ]
        + Scatter.scratch(rows, width)
        + [DMA((8,))] * 4
        + [DMA((8, 2))] * 2
        + [DMA((2, depth))] * 4
        + [DMA((4,)), DMA((2,)), DMA((depth + 1,))],
        input_output_aliases={6: 8, 7: 9},
        compiler_params=params(cid),
        name="middle",
    )(rank, low, x, gains, grad_all, out_w, gate_up, down)


class LineScatter:
    def __init__(self, z, own, left, right, total, send, recv):
        self.z, self.own, self.left, self.right, self.total = z, own, left, right, total
        self.send, self.recv = send, recv
        self.top = own.shape[0] - 1

    @staticmethod
    def scratch(shape):
        depth = shape[0]
        hops = (depth - 1,) + tuple(shape[1:])
        return [VMEM(hops, BF16), VMEM(hops, BF16), VMEM(shape[1:], F32), DMA((2, depth)), DMA((2, depth))]

    def copy(self, way, s, part, to):
        there = (self.left, self.right)[way].at[s]
        return remote(self.own.at[part], there, self.send.at[way, s], self.recv.at[way, s], fsdp=to)

    def landed(self, way, s):
        ref = (self.left, self.right)[way].at[s]
        remote(ref, ref, self.send.at[way, s], self.recv.at[way, s], fsdp=self.z - 1 + 2 * way).wait_recv()

    def step(self, s):
        z, top = self.z, self.top
        for way in (0, 1):
            place = z if way == 0 else top - z
            part = top - s + z if way == 0 else s - top + z

            @pl.when((place <= s) & (place < top))
            def _():
                if s:

                    @pl.when(place > 0)
                    def _():
                        self.landed(way, s - 1)
                        came = (self.left, self.right)[way][s - 1]
                        self.own[part] = (self.own[part].astype(F32) + came.astype(F32)).astype(BF16)

                self.copy(way, s, part, z + 1 - 2 * way).start()

    def result(self):
        self.total[...] = self.own[self.z].astype(F32)
        for way in (0, 1):
            place = self.z if way == 0 else self.top - self.z

            @pl.when(place > 0)
            def _():
                self.landed(way, self.top - 1)
                self.total[...] += (self.left, self.right)[way][self.top - 1].astype(F32)

        return self.total[...].astype(BF16)

    def sent(self):
        z, top = self.z, self.top
        for s in range(top):
            for way in (0, 1):
                place = z if way == 0 else top - z
                part = top - s + z if way == 0 else s - top + z

                @pl.when((place <= s) & (place < top))
                def _():
                    self.copy(way, s, part, z + 1 - 2 * way).wait_send()


def back_kernel(
    order_ref, rank_ref, qkv_ref, o_ref, do_ref, lse_ref, table_ref, w_ref, mixed_ref, all_ref, p1_ref, owg_ref, gug_ref,
    layer_ref, osum_ref, gsum_ref, p3_ref, qg_ref,
    keys, keys_t, values, dk, dv, dqn, dqkv, acc, xs, stage, p1, owg, gug, *rest,
):
    first, second, third, (load, xload, put) = rest[:7], rest[7:14], rest[14:19], rest[19:]
    c = lax.axis_index("ctx")
    z = lax.axis_index("fsdp")
    depth, shard = qg_ref.shape[0], qg_ref.shape[2]
    rows, width = layer_ref.shape
    others = [lax.rem(z + k, depth) for k in range(1, depth)]
    greet([{"ctx": flip(c, k)} for k in (1, 2, 4)] + [{"fsdp": o} for o in others])
    loads = [
        pltpu.make_async_copy(a, t, load.at[i])
        for i, (a, t) in enumerate(((gug_ref, gug), (p1_ref, p1), (owg_ref, owg)))
    ]
    for d in loads:
        d.start()
    line = LineScatter(z, gug, *third)
    layer = Scatter(c, p1, *first)
    out = Scatter(c, owg, *second)

    blocks = qkv_ref.shape[0]
    per = CHUNK // BLOCK
    scale = HEAD_SIZE ** (-0.5)
    factor = scale * math.log2(math.e)
    half = HEAD_SIZE // 2
    for b in range(blocks):
        there = slice(b * BLOCK, (b + 1) * BLOCK)
        key = qkv_ref[order_ref[b], 2 * HEAD_SIZE : 3 * HEAD_SIZE]
        keys[there, :] = key.T
        keys_t[:, there] = key
        values[there, :] = qkv_ref[order_ref[b], 3 * HEAD_SIZE :].T
    dk[...] = jnp.zeros_like(dk)
    dv[...] = jnp.zeros_like(dv)
    loads[0].wait()
    line.step(0)
    loads[1].wait()
    for k in Scatter.ORDER:
        layer.give(k)
    loads[2].wait()
    for k in Scatter.ORDER:
        out.give(k)

    def attend_block(j, last):
        block = order_ref[j]
        q = two_heads(qkv_ref, block)
        do = two_heads(do_ref, block)
        delta = jnp.sum(two_heads(o_ref, j) * do.astype(F32), 0, keepdims=True)
        lse = lse_ref[j]

        def step(t, dq, masked):
            there = pl.ds(t * CHUNK, CHUNK)
            s = jnp.dot(keys[there, :], q, preferred_element_type=F32)
            if masked:
                s = causal(s, t, j)
            p = jnp.exp2(s * factor - lse)
            dp = jnp.dot(values[there, :], do, preferred_element_type=F32)
            ds = (p * (dp - delta)).astype(BF16)
            wide = pl.ds(t * per, per)
            dv[wide] += contract(p.astype(BF16), do, ((1,), (1,))).reshape(per, BLOCK, HEAD_SIZE)
            dk[wide] += contract(ds, q, ((1,), (1,))).reshape(per, BLOCK, HEAD_SIZE)
            return dq + jnp.dot(keys_t[:, there], ds, preferred_element_type=F32)

        dq = jnp.zeros((HEAD_SIZE, 2 * BLOCK), F32)
        for t in range(last):
            dq = step(t, dq, False)
        dq = step(last, dq, True) * scale
        cosine, sine = table_ref[block, :half], table_ref[block, half:]
        for h in (0, 1):
            part = dq[:, h * BLOCK : (h + 1) * BLOCK]
            dqn[j, h * HEAD_SIZE : (h + 1) * HEAD_SIZE] = turned(part, cosine, -sine).astype(BF16)

    for turn in range(blocks // per):

        @pl.loop(turn * per, (turn + 1) * per)
        def _(j):
            attend_block(j, turn)

        if turn == 0:
            layer.far()
        if turn == 1:
            layer.direct()
        if turn == 2:
            layer.merged()
            line.step(1)
            out.far()
    for q in (0, 1):
        at = pl.ds(q * (rows // 2), rows // 2)
        layer_ref[at] = (mixed_ref[at] + layer.result(q)).astype(BF16)
    out.direct()

    for i in range(blocks):
        to = slice(i * BLOCK, (i + 1) * BLOCK)
        natural = rank_ref[i]
        dqkv[: 2 * HEAD_SIZE, to] = dqn[natural]
        dqkv[2 * HEAD_SIZE : 3 * HEAD_SIZE, to] = turned(
            dk[natural].T * scale, table_ref[i, :half], -table_ref[i, half:]
        ).astype(BF16)
        dqkv[3 * HEAD_SIZE :, to] = dv[natural].T.astype(BF16)

    def x_load(d, slot):
        return pltpu.make_async_copy(all_ref.at[d], xs.at[slot], xload.at[slot])

    def p_put(d, slot):
        return pltpu.make_async_copy(stage.at[slot], p3_ref.at[d], put.at[slot])

    x_load(0, 0).start()
    acc[...] = jnp.zeros_like(acc)
    for d in range(8):
        slot = d % 2
        if d + 1 < 8:
            x_load(d + 1, 1 - slot).start()
        if d > 1:
            p_put(d - 2, slot).wait()
        part = dqkv[:, d * rows : (d + 1) * rows]
        stage[slot] = contract(part, w_ref[...], ((0,), (0,))).astype(BF16)
        p_put(d, slot).start()
        x_load(d, slot).wait()
        acc[...] += jnp.dot(part, xs[slot], preferred_element_type=F32)
        if d == 1:
            out.merged()
        if d == 3:
            line.step(2)
    for f in range(depth):
        qg_ref[f] = acc[:, f * shard : (f + 1) * shard].astype(BF16)
    osum = jnp.concatenate([out.result(0), out.result(1)], 0)
    osum_ref[...] = osum.astype(BF16).reshape(osum_ref.shape)
    gsum_ref[...] = line.result()
    for d in (6, 7):
        p_put(d, d % 2).wait()
    layer.sent()
    out.sent()
    line.sent()


def back(order, rank, arrays, big, depth, cid):
    blocks = arrays[0].shape[0]
    tokens = blocks * BLOCK
    rows, width = arrays[-1].shape
    out_rows = big[2].shape[1]
    shard, both = big[3].shape[1:]
    shape = jax.ShapeDtypeStruct
    vm = pl.BlockSpec(memory_space=VMEM)
    hbm = pl.BlockSpec(memory_space=ANY)
    sm = pl.BlockSpec(memory_space=pltpu.SMEM)
    tall = (tokens, HEAD_SIZE)
    block = (8, rows, width)
    return pl.pallas_call(
        back_kernel,
        out_shape=(
            shape((rows, width), BF16),
            shape((depth, out_rows // depth, width), BF16),
            shape((shard, both), BF16),
            shape(block, BF16),
            shape((depth, 4 * HEAD_SIZE, shard), BF16),
        ),
        in_specs=[sm, sm] + [vm] * len(arrays) + [hbm] * len(big),
        out_specs=(vm, vm, vm, hbm, vm),
        scratch_shapes=[
            VMEM(tall, BF16),
            VMEM(tall[::-1], BF16),
            VMEM(tall, BF16),
            VMEM((blocks, BLOCK, HEAD_SIZE), F32),
            VMEM((blocks, BLOCK, HEAD_SIZE), F32),
            VMEM((blocks, 2 * HEAD_SIZE, BLOCK), BF16),
            VMEM((4 * HEAD_SIZE, tokens), BF16),
            VMEM((4 * HEAD_SIZE, width), F32),
            VMEM((2, rows, width), BF16),
            VMEM((2, rows, width), BF16),
            VMEM(block, BF16),
            VMEM((8, out_rows, width), BF16),
            VMEM(big[3].shape, BF16),
        ]
        + Scatter.scratch(rows, width)
        + Scatter.scratch(out_rows, width)
        + LineScatter.scratch(big[3].shape)
        + [DMA((3,)), DMA((2,)), DMA((2,))],
        compiler_params=params(cid),
        name="back",
    )(order, rank, *arrays, *big)


def last_kernel(
    x_ref, mgrad_ref, gains_ref, gain_two_ref, p3_ref, gu_ref, dg_ref, qg_ref, og_ref,
    input_ref, sum_ref, gu_all, down_all, q_all, o_all,
    p3, down, heads, outs, down_sum, q_sum, o_sum, gain_rows, by_z, part, by_c, *rest,
):
    scatter_refs, lines = rest[:7], (rest[7:12], rest[12:17], rest[17:22])
    send, recv, local, load, zs, zr, cs, cr = rest[22:]
    c = lax.axis_index("ctx")
    z = lax.axis_index("fsdp")
    depth, _, shard = by_z.shape
    rows, width = x_ref.shape
    others = [lax.rem(z + k, depth) for k in range(1, depth)]
    greet([{"ctx": flip(c, k)} for k in range(1, 8)] + [{"fsdp": o} for o in others])
    loads = [
        pltpu.make_async_copy(a, t, load.at[i])
        for i, (a, t) in enumerate(((dg_ref, down), (qg_ref, heads), (og_ref, outs), (p3_ref, p3)))
    ]
    for d in loads:
        d.start()
    here = [pltpu.make_async_copy(gu_ref, gu_all.at[c], local.at[0])]
    here[0].start()
    gate_up = Gather(c, own_half(gu_ref), gu_all, row_half, send.at[0], recv.at[0])
    down_line, q_line, o_line = (LineScatter(z, a, *refs) for a, refs in zip((down, heads, outs), lines))
    loads[0].wait()
    down_line.step(0)
    loads[1].wait()
    q_line.step(0)
    loads[2].wait()
    o_line.step(0)
    loads[3].wait()
    scatter = Scatter(c, p3, *scatter_refs)
    for k in Scatter.ORDER:
        scatter.give(k)
    scatter.far()
    gate_up.begin()
    scatter.direct()
    down_line.step(1)
    scatter.merged()
    q_line.step(1)
    o_line.step(1)

    gain = jnp.concatenate([gains_ref[k, 0:1, :] for k in range(depth)], 1)
    one_grad = jnp.concatenate([scatter.result(0), scatter.result(1)], 0)
    gate_up.near_half()
    x = x_ref[...].astype(F32)
    factor = lax.rsqrt(jnp.mean(x * x, -1, keepdims=True) + EPS)
    scaled = one_grad * gain
    back = factor * scaled - x * (factor * factor * factor) * jnp.mean(scaled * x, -1, keepdims=True)
    input_ref[...] = (mgrad_ref[...] + back).astype(BF16)
    gain_rows[:4] = jnp.broadcast_to(jnp.sum(one_grad * x * factor, 0, keepdims=True), (4, width))
    gain_rows[4:] = gain_two_ref[4:]
    sent = []
    for k, o in enumerate(others):
        d = remote(gain_rows.at[:, lanes(o * shard, shard)], by_z.at[z], zs.at[k], zr.at[k], fsdp=o)
        d.start()
        sent.append(d)
    gate_up.near_rest()
    down_line.step(2)
    q_line.step(2)
    o_line.step(2)
    gate_up.far()

    total = gain_rows[:, lanes(z * shard, shard)]
    for k in range(depth - 1):
        ref = by_z.at[lax.rem(z + depth - 1 - k, depth)]
        remote(ref, ref, zs.at[k], zr.at[k], fsdp=others[k]).wait_recv()
        total = total + by_z[lax.rem(z + depth - 1 - k, depth)]
    part[...] = total
    for k in range(1, 8):
        d = remote(part, by_c.at[c], cs.at[k], cr.at[k], ctx=flip(c, k))
        d.start()
        sent.append(d)
    by_c[c] = total

    gathers = [gate_up]
    tails = ((down_line, down_sum, down_all), (q_line, q_sum, q_all), (o_line, o_sum, o_all))
    for i, (line, mine, everyone) in enumerate(tails):
        mine[...] = line.result()
        here.append(pltpu.make_async_copy(mine, everyone.at[c], local.at[i + 1]))
        here[-1].start()
        at, own = (row_half, own_half(mine)) if mine.shape[0] % 32 == 0 else (column_half, own_half(mine, 1))
        gathers.append(Gather(c, own, everyone, at, send.at[i + 1], recv.at[i + 1]))
        gathers[-1].begin()
    for g in gathers[1:]:
        g.near_half()
    for g in gathers[1:]:
        g.near_rest()
    for g in gathers[1:]:
        g.far()
    for g in gathers:
        for channel, k in ((0, 1), (3, 3), (4, 5), (5, 7)):
            g.paired(channel, k)
    for k in range(1, 8):
        ref = by_c.at[flip(c, k)]
        remote(ref, ref, cs.at[k], cr.at[k], ctx=flip(c, k)).wait_recv()
    total = by_c[0]
    for k in range(1, 8):
        total = total + by_c[k]
    sum_ref[...] = total
    for d in here:
        d.wait()
    for d in sent:
        d.wait_send()
    scatter.sent()
    for line in (down_line, q_line, o_line):
        line.sent()
    for g in gathers:
        g.sent()


def last_part(x, mixed_grad, gains, gain_two, p3, gate_up, down, heads, outs, cid):
    rows, width = x.shape
    depth, _, shard = gains.shape
    shape = jax.ShapeDtypeStruct
    vm = pl.BlockSpec(memory_space=VMEM)
    hbm = pl.BlockSpec(memory_space=ANY)
    small = (8, shard)
    threes = (down, heads, outs)
    return pl.pallas_call(
        last_kernel,
        out_shape=[shape((rows, width), BF16), shape(small, F32), shape((8,) + gate_up.shape, BF16)]
        + [shape((8,) + a.shape[1:], BF16) for a in threes],
        in_specs=[vm] * 4 + [hbm] * 5,
        out_specs=[vm, vm] + [hbm] * 4,
        scratch_shapes=[VMEM(p3.shape, BF16)]
        + [VMEM(a.shape, BF16) for a in threes]
        + [VMEM(a.shape[1:], BF16) for a in threes]
        + [VMEM((8, width), F32), VMEM((depth,) + small, F32), VMEM(small, F32), VMEM((8,) + small, F32)]
        + Scatter.scratch(rows, width)
        + [r for a in threes for r in LineScatter.scratch(a.shape)]
        + [DMA((4, 8, 2)), DMA((4, 8, 2)), DMA((4,)), DMA((4,)), DMA((depth,)), DMA((depth,)), DMA((8,)), DMA((8,))],
        compiler_params=params(cid),
        name="last_part",
    )(x, mixed_grad, gains, gain_two, p3, gate_up, down, heads, outs)


def widen_mlp(gate_up, down):
    _, shard, both = gate_up.shape
    mine = both // 2
    depth = mine // LANES
    step = shard // 8

    def kernel(a_ref, d_ref, gate_ref, up_ref, down_ref):
        for i, out in enumerate((gate_ref, up_ref)):
            for c in range(8):
                for s in range(depth):
                    out[:, (s * 8 + c) * LANES : (s * 8 + c + 1) * LANES] = a_ref[
                        c, :, i * mine + s * LANES : i * mine + (s + 1) * LANES
                    ].astype(F32)
        down_ref[...] = d_ref[0].astype(F32)

    _, rows, width = down.shape
    wide = jax.ShapeDtypeStruct((shard, 8 * mine), F32)
    wide_spec = pl.BlockSpec((step, 8 * mine), lambda i: (i, 0))
    return pl.pallas_call(
        kernel,
        grid=(8,),
        out_shape=(wide, wide, jax.ShapeDtypeStruct((8 * rows, width), F32)),
        in_specs=[pl.BlockSpec((8, step, both), lambda i: (0, i, 0)), pl.BlockSpec((1, rows, width), lambda i: (i, 0, 0))],
        out_specs=(wide_spec, wide_spec, pl.BlockSpec((rows, width), lambda i: (i, 0))),
        compiler_params=pltpu.CompilerParams(vmem_limit_bytes=VMEM_BYTES),
        name="widen_mlp",
    )(gate_up, down)


def widen_attention(qkv, out):
    shard = qkv.shape[2]
    width = out.shape[2]

    def kernel(a_ref, o_ref, q_out, k_out, v_out, out_out):
        per_q = 2 * HEAD_SIZE
        for c in range(0, 8, 2):
            both = jnp.concatenate([a_ref[c + i, :per_q, :] for i in (0, 1)], 0)
            q_out[:, c * per_q : (c + 2) * per_q] = both.astype(F32).T
        for target, first in ((k_out, per_q), (v_out, per_q + HEAD_SIZE)):
            for c in range(0, 8, 4):
                four = jnp.concatenate([a_ref[c + i, first : first + HEAD_SIZE, :] for i in range(4)], 0)
                target[:, c * HEAD_SIZE : (c + 4) * HEAD_SIZE] = four.astype(F32).T
        for c in range(8):
            rows = out.shape[1]
            out_out[c * rows : (c + 1) * rows, :] = o_ref[c].astype(F32)

    vm = pl.BlockSpec(memory_space=VMEM)
    shape = lambda n: jax.ShapeDtypeStruct((shard, n), F32)
    heads = 8 * HEAD_SIZE
    return pl.pallas_call(
        kernel,
        out_shape=(shape(2 * heads), shape(heads), shape(heads), shape(width)),
        in_specs=[vm, vm],
        out_specs=(vm, vm, vm, vm),
        compiler_params=pltpu.CompilerParams(vmem_limit_bytes=VMEM_BYTES),
        name="widen_attention",
    )(qkv, out)


def in_plane(
    depth,
    hidden_in,
    positions,
    attn_gain,
    w_query,
    key_projection,
    value_projection,
    w_out,
    mlp_gain,
    w_gate,
    w_up,
    w_down,
    out_grad,
):
    plane = 8
    rows, width = hidden_in.shape[1:]
    shard = width // depth
    half = HEAD_SIZE // 2

    position = positions[0]
    lane = lax.broadcasted_iota(jnp.int32, (8, LANES), 1)
    info = jnp.where(lane < LANES // 2, position[0], position[BLOCK])
    gains = jnp.concatenate(
        [
            jnp.broadcast_to(attn_gain.astype(F32)[None], (4, shard)),
            jnp.broadcast_to(mlp_gain.astype(F32)[None], (4, shard)),
        ],
        0,
    )
    freq = THETA ** (-(jnp.arange(half, dtype=F32) * 2.0 / HEAD_SIZE))
    start = freq[:, None] * info[:1].astype(F32)
    quarter = lane[:1] // (LANES // 4)
    base = jnp.where(quarter % 2 == 0, jnp.cos(start), jnp.sin(start))
    inner = freq[:, None] * jnp.arange(BLOCK, dtype=F32)[None]
    step = jnp.concatenate([jnp.cos(inner), jnp.sin(inner)], 0)

    hidden_low = hidden_in[0]
    weights = (w_query, key_projection, value_projection, w_out, w_gate, w_up, w_down)
    grad_low = out_grad[0]
    (normed_all, qkv, qkv_w, table, gains_all, infos, out_part, gate_up_w, down_w, grad_all) = first_part(
        hidden_low, gains, info, base, step, weights, grad_low, depth, 0
    )
    starts = infos[:, 0].reshape(plane, 2, LANES // 2)[:, :, 0].reshape(2 * plane)
    rank = ((starts - jnp.min(starts)) // BLOCK).astype(jnp.int32)
    blocks = 2 * plane
    order = jnp.sum(
        jnp.where(rank[None, :] == jnp.arange(blocks)[:, None], jnp.arange(blocks)[None, :], 0), 1
    ).astype(jnp.int32)

    attended, attended_low, lse, out_w, gate_up_w, down_w = attend(order, qkv, out_part, gate_up_w, down_w, 1)
    mixed, mixed_grad, gain_two_grad, do, out_wgrad, gate_up_wgrad, down_wgrad, down_sum, _, _ = middle(
        rank, attended_low, hidden_low, gains_all, grad_all, out_w.reshape(plane, -1, width), gate_up_w, down_w, 2
    )
    arrays = (qkv, attended, do, lse, table, qkv_w, mixed)
    layer_out, out_sum, gate_up_sum, one_sum, qkv_wgrad = back(
        order, rank, arrays, (normed_all, down_sum, out_wgrad, gate_up_wgrad), depth, 3
    )
    input_grad, gain_sums, gate_up_all, down_all, qkv_all, out_grads = last_part(
        hidden_low, mixed_grad, gains_all, gain_two_grad, one_sum, gate_up_sum, down_wgrad, qkv_wgrad, out_sum, 4
    )
    gate_total, up_total, down_total = widen_mlp(gate_up_all, down_all)
    query_total, key_total, value_total, out_total = widen_attention(qkv_all, out_grads)
    return (
        layer_out[None],
        input_grad[None],
        gain_sums[0],
        query_total,
        key_total,
        value_total,
        out_total,
        gain_sums[4],
        gate_total,
        up_total,
        down_total,
    )


def solution(mesh):
    placed = (
        P("fsdp", "ctx", None),
        P("fsdp", "ctx"),
        P("fsdp"),
        P("fsdp", None),
        P("fsdp", None),
        P("fsdp", None),
        P("fsdp", None),
        P("fsdp"),
        P("fsdp", None),
        P("fsdp", None),
        P("fsdp", None),
        P("fsdp", "ctx", None),
    )
    body = per_device
    if mesh.shape["ctx"] == KEY_VALUE_HEADS:
        body = functools.partial(in_plane, mesh.shape["fsdp"])
    return jax.shard_map(
        body,
        mesh=mesh,
        in_specs=placed,
        out_specs=(
            P("fsdp", "ctx", None),
            P("fsdp", "ctx", None),
            P("fsdp"),
            P("fsdp", None),
            P("fsdp", None),
            P("fsdp", None),
            P("fsdp", None),
            P("fsdp"),
            P("fsdp", None),
            P("fsdp", None),
            P("fsdp", None),
        ),
        check_vma=False,
    )
```

```python
import functools
import math

import jax
import jax.numpy as jnp
from jax import lax
from jax.experimental import pallas as pl
from jax.experimental.pallas import tpu as pltpu
from jax.sharding import PartitionSpec as P

QUERY_HEADS = 16
KEY_VALUE_HEADS = 8
HEAD_SIZE = 96


EPS = 1e-05
THETA = 100000.0


def tables(token_position):
    half = HEAD_SIZE // 2
    freq = THETA ** (-(jnp.arange(half, dtype=jnp.float32) * 2.0 / HEAD_SIZE))
    angle = token_position.astype(jnp.float32)[:, None] * freq[None, :]
    return (jnp.cos(angle)[:, None, :], jnp.sin(angle)[:, None, :])


def rotary_embed(value_rows, cosine_table, sine_table):
    half = value_rows.shape[-1] // 2
    first = value_rows[..., :half]
    second = value_rows[..., half:]
    return jnp.concatenate(
        [first * cosine_table - second * sine_table, second * cosine_table + first * sine_table], -1
    )


def rotary_embed_backward(grads, cosine_table, sine_table):
    half = grads.shape[-1] // 2
    first = grads[..., :half]
    second = grads[..., half:]
    return jnp.concatenate(
        [first * cosine_table + second * sine_table, second * cosine_table - first * sine_table], -1
    )


def norm_forward(hidden, gain):
    return (
        hidden
        * lax.rsqrt(jnp.mean(hidden * hidden, -1, keepdims=True) + EPS)
        * gain.astype(jnp.float32)
    )


def norm_back(hidden, gain, grad):
    factor = lax.rsqrt(jnp.mean(hidden * hidden, -1, keepdims=True) + EPS)
    scaled = grad * gain.astype(jnp.float32)
    hidden_grad = factor * scaled - hidden * factor * factor * factor * jnp.mean(
        scaled * hidden, -1, keepdims=True
    )
    gain_grad = jnp.sum(grad * hidden * factor, 0)
    return (hidden_grad, gain_grad)


def dot_first(left, right):
    return lax.dot_general(
        left, right, (((0,), (0,)), ((), ())), preferred_element_type=jnp.float32
    )


def dot_last(left, right):
    return lax.dot_general(
        left, right, (((1,), (1,)), ((), ())), preferred_element_type=jnp.float32
    )


def over_blocks(step_fn, carry, arrays):
    block_count = arrays[0].shape[0]
    size = math.gcd(block_count, 512)
    parts = block_count // size
    shaped = tuple((item.reshape((parts, size) + item.shape[1:]) for item in arrays))

    def advance(state, inputs):
        index, pieces = inputs
        return (step_fn(state, pieces, index * size), None)

    final, unused = lax.scan(advance, carry, (jnp.arange(parts, dtype=jnp.int32), shaped))
    return final


def per_device(
    hidden_in,
    positions,
    attn_gain,
    w_query,
    key_projection,
    value_projection,
    w_out,
    mlp_gain,
    w_gate,
    w_up,
    w_down,
    out_grad,
):
    hidden = hidden_in[0].astype(jnp.float32)
    local_rows = hidden.shape[0]
    query_pos = positions[0]
    query_groups = QUERY_HEADS // KEY_VALUE_HEADS
    scale = HEAD_SIZE ** (-0.5)
    cosine_table, sine_table = tables(query_pos)
    attn_set = (
        lax.all_gather(attn_gain, "fsdp", axis=0, tiled=True),
        lax.all_gather(w_query, "fsdp", axis=0, tiled=True),
        lax.all_gather(key_projection, "fsdp", axis=0, tiled=True),
        lax.all_gather(value_projection, "fsdp", axis=0, tiled=True),
        lax.all_gather(w_out, "fsdp", axis=0, tiled=True),
    )
    gain_one, query_w, key_matrix, value_matrix, out_w = attn_set
    first_normed = norm_forward(hidden, gain_one).astype(jnp.bfloat16)
    query_raw = jnp.dot(first_normed, query_w, preferred_element_type=jnp.float32)
    unrotated_key = jnp.dot(first_normed, key_matrix, preferred_element_type=jnp.float32)
    value_raw = jnp.dot(first_normed, value_matrix, preferred_element_type=jnp.float32)
    query_rows = (
        rotary_embed(
            query_raw.reshape(local_rows, QUERY_HEADS, HEAD_SIZE), cosine_table, sine_table
        )
        .astype(jnp.bfloat16)
        .reshape(local_rows, KEY_VALUE_HEADS, query_groups, HEAD_SIZE)
    )
    keys_flat = (
        rotary_embed(
            unrotated_key.reshape(local_rows, KEY_VALUE_HEADS, HEAD_SIZE), cosine_table, sine_table
        )
        .astype(jnp.bfloat16)
        .reshape(local_rows, KEY_VALUE_HEADS * HEAD_SIZE)
    )
    values_flat = value_raw.astype(jnp.bfloat16)
    key_pos_all = lax.all_gather(query_pos, "ctx", axis=0, tiled=True)
    sequence_length = key_pos_all.shape[0]

    def masked_scores(partial_keys, first):
        block_count = partial_keys.shape[0]
        key_pos = lax.dynamic_slice_in_dim(key_pos_all, first, block_count)
        scores = (
            jnp.einsum(
                "tkgd,nkd->kgtn",
                query_rows,
                partial_keys.reshape(block_count, KEY_VALUE_HEADS, HEAD_SIZE),
                preferred_element_type=jnp.float32,
            )
            * scale
        )
        visible = key_pos[None, None, None, :] <= query_pos[None, None, :, None]
        return jnp.where(visible, scores, -jnp.inf)

    def forward_part(carry, part, first):
        top, denom, accum = carry
        partial_keys, partial_values = part
        block_count = partial_keys.shape[0]
        scores = masked_scores(partial_keys, first)
        new_top = jnp.maximum(top, jnp.max(scores, -1))
        weights = jnp.exp(scores - new_top[..., None])
        factor = jnp.exp(top - new_top)
        denom = denom * factor + jnp.sum(weights, -1)
        accum = accum * factor[..., None] + jnp.einsum(
            "kgtn,nkd->kgtd",
            weights.astype(jnp.bfloat16),
            partial_values.reshape(block_count, KEY_VALUE_HEADS, HEAD_SIZE),
            preferred_element_type=jnp.float32,
        )
        return (new_top, denom, accum)

    start_state = (
        jnp.full((KEY_VALUE_HEADS, query_groups, local_rows), -1e30, jnp.float32),
        jnp.zeros((KEY_VALUE_HEADS, query_groups, local_rows), jnp.float32),
        jnp.zeros((KEY_VALUE_HEADS, query_groups, local_rows, HEAD_SIZE), jnp.float32),
    )
    top, denom, accum = over_blocks(
        forward_part,
        start_state,
        (
            lax.all_gather(keys_flat, "ctx", axis=0, tiled=True),
            lax.all_gather(values_flat, "ctx", axis=0, tiled=True),
        ),
    )
    attended_output = accum / denom[..., None]
    log_total = top + jnp.log(denom)
    attended_low = (
        attended_output.transpose(2, 0, 1, 3)
        .reshape(local_rows, QUERY_HEADS * HEAD_SIZE)
        .astype(jnp.bfloat16)
    )
    mixed = hidden + jnp.dot(attended_low, out_w, preferred_element_type=jnp.float32)
    mlp_set = (
        lax.all_gather(mlp_gain, "fsdp", axis=0, tiled=True),
        lax.all_gather(w_gate, "fsdp", axis=0, tiled=True),
        lax.all_gather(w_up, "fsdp", axis=0, tiled=True),
        lax.all_gather(w_down, "fsdp", axis=0, tiled=True),
    )
    gain_two, gate_w, up_w, down_w = mlp_set
    normed_two = norm_forward(mixed, gain_two).astype(jnp.bfloat16)
    gate = jnp.dot(normed_two, gate_w, preferred_element_type=jnp.float32)
    up = jnp.dot(normed_two, up_w, preferred_element_type=jnp.float32)
    sigma = jax.nn.sigmoid(gate)
    active = (gate * sigma * up).astype(jnp.bfloat16)
    result = mixed + jnp.dot(active, down_w, preferred_element_type=jnp.float32)
    layer_out = result.astype(jnp.bfloat16)[None]
    grad_low = out_grad[0]
    grad_out = grad_low.astype(jnp.float32)
    gain_back, gate_back, up_back, down_back = (
        lax.all_gather(mlp_gain, "fsdp", axis=0, tiled=True),
        lax.all_gather(w_gate, "fsdp", axis=0, tiled=True),
        lax.all_gather(w_up, "fsdp", axis=0, tiled=True),
        lax.all_gather(w_down, "fsdp", axis=0, tiled=True),
    )
    down_grad = dot_first(active, grad_low)
    active_grad = dot_last(grad_low, down_back)
    gate_grad = (active_grad * up * sigma * (1.0 + gate * (1.0 - sigma))).astype(jnp.bfloat16)
    up_grad = (active_grad * gate * sigma).astype(jnp.bfloat16)
    gate_wgrad = dot_first(normed_two, gate_grad)
    up_wgrad = dot_first(normed_two, up_grad)
    normed_two_grad = dot_last(gate_grad, gate_back) + dot_last(up_grad, up_back)
    mixed_part, gain_two_grad = norm_back(mixed, gain_back, normed_two_grad)
    mixed_grad = grad_out + mixed_part
    mlp_shards = (
        lax.psum_scatter(
            gain_two_grad.astype(jnp.bfloat16), "fsdp", scatter_dimension=0, tiled=True
        ).astype(jnp.float32),
        lax.psum_scatter(
            gate_wgrad.astype(jnp.bfloat16), "fsdp", scatter_dimension=0, tiled=True
        ).astype(jnp.float32),
        lax.psum_scatter(
            up_wgrad.astype(jnp.bfloat16), "fsdp", scatter_dimension=0, tiled=True
        ).astype(jnp.float32),
        lax.psum_scatter(
            down_grad.astype(jnp.bfloat16), "fsdp", scatter_dimension=0, tiled=True
        ).astype(jnp.float32),
    )
    gain_first, query_back, key_back, value_back, out_back = (
        lax.all_gather(attn_gain, "fsdp", axis=0, tiled=True),
        lax.all_gather(w_query, "fsdp", axis=0, tiled=True),
        lax.all_gather(key_projection, "fsdp", axis=0, tiled=True),
        lax.all_gather(value_projection, "fsdp", axis=0, tiled=True),
        lax.all_gather(w_out, "fsdp", axis=0, tiled=True),
    )
    branch_grad = mixed_grad.astype(jnp.bfloat16)
    out_wgrad = dot_first(attended_low, branch_grad)
    attended_grad = (
        dot_last(branch_grad, out_back)
        .astype(jnp.bfloat16)
        .reshape(local_rows, KEY_VALUE_HEADS, query_groups, HEAD_SIZE)
        .transpose(1, 2, 0, 3)
    )
    delta = jnp.sum(attended_grad.astype(jnp.float32) * attended_output, -1)

    def backward_part(carry, part, first):
        query_acc, key_value_acc = carry
        partial_keys, partial_values = part
        block_count = partial_keys.shape[0]
        probs = jnp.exp(masked_scores(partial_keys, first) - log_total[..., None])
        gradient_of_value = jnp.einsum(
            "kgtn,kgtd->nkd",
            probs.astype(jnp.bfloat16),
            attended_grad,
            preferred_element_type=jnp.float32,
        )
        prob_grad = jnp.einsum(
            "kgtd,nkd->kgtn",
            attended_grad,
            partial_values.reshape(block_count, KEY_VALUE_HEADS, HEAD_SIZE),
            preferred_element_type=jnp.float32,
        )
        score_grad = (probs * (prob_grad - delta[..., None])).astype(jnp.bfloat16)
        query_acc = (
            query_acc
            + jnp.einsum(
                "kgtn,nkd->kgtd",
                score_grad,
                partial_keys.reshape(block_count, KEY_VALUE_HEADS, HEAD_SIZE),
                preferred_element_type=jnp.float32,
            )
            * scale
        )
        gradient_of_key = (
            jnp.einsum("kgtn,tkgd->nkd", score_grad, query_rows, preferred_element_type=jnp.float32)
            * scale
        )
        joined = jnp.concatenate(
            [
                gradient_of_key.reshape(block_count, KEY_VALUE_HEADS * HEAD_SIZE),
                gradient_of_value.reshape(block_count, KEY_VALUE_HEADS * HEAD_SIZE),
            ],
            1,
        )
        key_value_acc = lax.dynamic_update_slice_in_dim(key_value_acc, joined, first, 0)
        return (query_acc, key_value_acc)

    back_state = (
        jnp.zeros((KEY_VALUE_HEADS, query_groups, local_rows, HEAD_SIZE), jnp.float32),
        jnp.zeros((sequence_length, 2 * KEY_VALUE_HEADS * HEAD_SIZE), jnp.float32),
    )
    query_acc, key_value_acc = over_blocks(
        backward_part,
        back_state,
        (
            lax.all_gather(keys_flat, "ctx", axis=0, tiled=True),
            lax.all_gather(values_flat, "ctx", axis=0, tiled=True),
        ),
    )
    local_key_value = lax.psum_scatter(
        key_value_acc.astype(jnp.bfloat16), "ctx", scatter_dimension=0, tiled=True
    ).astype(jnp.float32)
    query_raw_grad = (
        rotary_embed_backward(
            query_acc.transpose(2, 0, 1, 3).reshape(local_rows, QUERY_HEADS, HEAD_SIZE),
            cosine_table,
            sine_table,
        )
        .reshape(local_rows, QUERY_HEADS * HEAD_SIZE)
        .astype(jnp.bfloat16)
    )
    key_raw_grad = (
        rotary_embed_backward(
            local_key_value[:, : KEY_VALUE_HEADS * HEAD_SIZE].reshape(
                local_rows, KEY_VALUE_HEADS, HEAD_SIZE
            ),
            cosine_table,
            sine_table,
        )
        .reshape(local_rows, KEY_VALUE_HEADS * HEAD_SIZE)
        .astype(jnp.bfloat16)
    )
    unrotated_value_gradient = local_key_value[:, KEY_VALUE_HEADS * HEAD_SIZE :].astype(
        jnp.bfloat16
    )
    query_wgrad = dot_first(first_normed, query_raw_grad)
    key_wgrad = dot_first(first_normed, key_raw_grad)
    value_wgrad = dot_first(first_normed, unrotated_value_gradient)
    normed_one_grad = (
        dot_last(query_raw_grad, query_back)
        + dot_last(key_raw_grad, key_back)
        + dot_last(unrotated_value_gradient, value_back)
    )
    input_part, gain_one_grad = norm_back(hidden, gain_first, normed_one_grad)
    input_grad = (mixed_grad + input_part).astype(jnp.bfloat16)[None]
    attn_shards = (
        lax.psum_scatter(
            gain_one_grad.astype(jnp.bfloat16), "fsdp", scatter_dimension=0, tiled=True
        ).astype(jnp.float32),
        lax.psum_scatter(
            query_wgrad.astype(jnp.bfloat16), "fsdp", scatter_dimension=0, tiled=True
        ).astype(jnp.float32),
        lax.psum_scatter(
            key_wgrad.astype(jnp.bfloat16), "fsdp", scatter_dimension=0, tiled=True
        ).astype(jnp.float32),
        lax.psum_scatter(
            value_wgrad.astype(jnp.bfloat16), "fsdp", scatter_dimension=0, tiled=True
        ).astype(jnp.float32),
        lax.psum_scatter(
            out_wgrad.astype(jnp.bfloat16), "fsdp", scatter_dimension=0, tiled=True
        ).astype(jnp.float32),
    )
    totals = (
        lax.psum(attn_shards[0].astype(jnp.bfloat16), "ctx").astype(jnp.float32),
        lax.psum(attn_shards[1].astype(jnp.bfloat16), "ctx").astype(jnp.float32),
        lax.psum(attn_shards[2].astype(jnp.bfloat16), "ctx").astype(jnp.float32),
        lax.psum(attn_shards[3].astype(jnp.bfloat16), "ctx").astype(jnp.float32),
        lax.psum(attn_shards[4].astype(jnp.bfloat16), "ctx").astype(jnp.float32),
        lax.psum(mlp_shards[0].astype(jnp.bfloat16), "ctx").astype(jnp.float32),
        lax.psum(mlp_shards[1].astype(jnp.bfloat16), "ctx").astype(jnp.float32),
        lax.psum(mlp_shards[2].astype(jnp.bfloat16), "ctx").astype(jnp.float32),
        lax.psum(mlp_shards[3].astype(jnp.bfloat16), "ctx").astype(jnp.float32),
    )
    return (
        layer_out,
        input_grad,
        totals[0],
        totals[1],
        totals[2],
        totals[3],
        totals[4],
        totals[5],
        totals[6],
        totals[7],
        totals[8],
    )


MESH = pl.DeviceIdType.MESH
ANY = pl.ANY
VMEM = pltpu.VMEM
DMA = pltpu.SemaphoreType.DMA
LANES = 128
BLOCK = 128
F32 = jnp.float32
BF16 = jnp.bfloat16
VMEM_BYTES = 60 * 2**20


def flip(c, k):
    out = c
    for b in (1, 2, 4):
        if k & b:
            out = out + b - 2 * b * ((c // b) % 2)
    return out


def remote(src, dst, send, recv, **to):
    return pltpu.make_async_remote_copy(
        src_ref=src, dst_ref=dst, send_sem=send, recv_sem=recv, device_id=to, device_id_type=MESH
    )


def greet(peers):
    barrier = pltpu.get_barrier_semaphore()
    for peer in peers:
        pl.semaphore_signal(barrier, inc=1, device_id=peer, device_id_type=MESH)
    pl.semaphore_wait(barrier, len(peers))


class Gather:
    def __init__(self, c, own, buf, at, send, recv):
        self.c, self.own, self.buf, self.at, self.send, self.recv = c, own, buf, at, send, recv
        self.pending = []

    def start(self, channel, who, to, h, own=False):
        there = self.at(self.buf, flip(self.c, who), h)
        d = remote(
            self.own(h) if own else there,
            there,
            self.send.at[channel, h],
            self.recv.at[channel, h],
            ctx=flip(self.c, to),
        )
        d.start()
        self.pending.append(d)

    def arrived(self, channel, who, frm, h):
        ref = self.at(self.buf, flip(self.c, who), h)
        remote(
            ref, ref, self.send.at[channel, h], self.recv.at[channel, h], ctx=flip(self.c, frm)
        ).wait_recv()

    def begin(self):
        self.start(1, 0, 2, 0, own=True)
        self.start(2, 0, 4, 1, own=True)
        self.start(1, 0, 2, 1, own=True)
        self.start(2, 0, 4, 0, own=True)
        self.start(0, 0, 1, 0, own=True)
        self.start(0, 0, 1, 1, own=True)

    def near_half(self):
        self.arrived(1, 2, 2, 0)
        self.start(6, 2, 4, 0)
        self.start(3, 2, 1, 0)
        self.arrived(2, 4, 4, 1)
        self.start(7, 4, 2, 1)
        self.start(4, 4, 1, 1)

    def near_rest(self):
        self.arrived(1, 2, 2, 1)
        self.start(3, 2, 1, 1)
        self.arrived(2, 4, 4, 0)
        self.start(4, 4, 1, 0)

    def far(self):
        self.arrived(6, 6, 4, 0)
        self.start(5, 6, 1, 0)
        self.arrived(7, 6, 2, 1)
        self.start(5, 6, 1, 1)

    def paired(self, channel, who):
        for h in (0, 1):
            self.arrived(channel, who, 1, h)

    def finish(self):
        self.near_half()
        self.near_rest()
        self.far()
        for channel, who in ((0, 1), (3, 3), (4, 5), (5, 7)):
            self.paired(channel, who)

    def sent(self):
        for d in self.pending:
            d.wait_send()


def row_half(ref, d, h):
    half = ref.shape[1] // 2
    return ref.at[d, pl.ds(h * half, half)]


def column_half(ref, d, h):
    half = ref.shape[2] // 2
    return ref.at[d, :, pl.ds(h * half, half)]


def own_half(ref, axis=0):
    half = ref.shape[axis] // 2
    return lambda h: ref.at[(slice(None),) * axis + (pl.ds(h * half, half),)]


class Line:
    def __init__(self, z, depth, at, send, recv, own=None):
        self.z, self.depth, self.at, self.send, self.recv, self.own = z, depth, at, send, recv, own

    def copy(self, way, k, part, to):
        ref = self.at(part)
        source = ref if k or self.own is None else self.own
        return remote(source, ref, self.send.at[way, k], self.recv.at[way, k], fsdp=to)

    def step(self, k):
        z, top = self.z, self.depth - 1

        @pl.when((z >= k) & (z < top))
        def _():
            self.copy(0, k, z - k, z + 1).start()

        @pl.when((z + k <= top) & (z > 0))
        def _():
            self.copy(1, k, z + k, z - 1).start()

    def landed(self, k):
        z, top = self.z, self.depth - 1

        @pl.when(z >= k + 1)
        def _():
            self.copy(0, k, z - 1 - k, z - 1).wait_recv()

        @pl.when(z + 1 + k <= top)
        def _():
            self.copy(1, k, z + 1 + k, z + 1).wait_recv()

    def sent(self, steps):
        z, top = self.z, self.depth - 1
        for k in steps:

            @pl.when((z >= k) & (z < top))
            def _():
                self.copy(0, k, z - k, z + 1).wait_send()

            @pl.when((z + k <= top) & (z > 0))
            def _():
                self.copy(1, k, z + k, z - 1).wait_send()


def params(cid):
    return pltpu.CompilerParams(
        collective_id=cid, has_side_effects=True, vmem_limit_bytes=VMEM_BYTES
    )


def contract(a, b, dims):
    return lax.dot_general(a, b, ((dims[0], dims[1]), ((), ())), preferred_element_type=F32)


def lanes(start, size):
    return pl.ds(pl.multiple_of(start, LANES), size)


def turned(u, cosine, sine):
    half = HEAD_SIZE // 2
    a, b = u[:half], u[half:]
    return jnp.concatenate([a * cosine - b * sine, b * cosine + a * sine], 0)


def picked(weight, first, count):
    shape = (count, weight.shape[1])
    hit = lax.broadcasted_iota(jnp.int32, shape, 1) == first + lax.broadcasted_iota(jnp.int32, shape, 0)
    return contract(hit.astype(BF16), weight, ((1,), (1,))).astype(BF16)


def first_kernel(
    x_ref, gain_ref, info_ref, base_ref, step_ref, wq_ref, wk_ref, wv_ref, wo_ref, wg_ref, wu_ref, wd_ref, grad_ref,
    all_ref, qkv_ref, w_ref, table_ref, gains_ref, infos_ref, wo_all, gu_all, down_all, grad_all,
    xs, gu_own, bases, gsend, grecv, isend, irecv, bsend, brecv, send, recv, zsend, zrecv, osend, orecv,
    usend, urecv, dsend, drecv, send2, recv2, local, parts,
):
    c = lax.axis_index("ctx")
    z = lax.axis_index("fsdp")
    depth = gains_ref.shape[0]
    shard, width = wq_ref.shape
    rows = x_ref.shape[0]
    strip = gu_all.shape[2] // 2 // depth
    down_rows = down_all.shape[1]
    others = [lax.rem(z + k, depth) for k in range(1, depth)]
    greet([{"ctx": flip(c, k)} for k in range(1, 8)] + [{"fsdp": o} for o in others])

    sent = []
    for k, o in enumerate(others):
        sent.append(remote(gain_ref, gains_ref.at[z], gsend.at[k], grecv.at[k], fsdp=o))
    for k in range(1, 8):
        sent.append(remote(info_ref, infos_ref.at[c], isend.at[k], irecv.at[k], ctx=flip(c, k)))
        sent.append(remote(base_ref, bases.at[c], bsend.at[k], brecv.at[k], ctx=flip(c, k)))
    for d in sent:
        d.start()
    out_rows = shard // 8
    out_own = wo_ref.at[pl.ds(c * out_rows, out_rows)]
    down_own = wd_ref.at[pl.ds(c * down_rows, down_rows)]
    strips = []
    for i, weight in enumerate((wg_ref, wu_ref)):
        for s in range(depth):
            strips.append(
                pltpu.make_async_copy(
                    weight.at[:, lanes((s * 8 + c) * strip, strip)],
                    gu_own.at[:, pl.ds((i * depth + s) * strip, strip)],
                    parts.at[4 + i * depth + s],
                )
            )
    for d in strips:
        d.start()
    copies = [
        pltpu.make_async_copy(out_own, wo_all.at[z], parts.at[0]),
        pltpu.make_async_copy(down_own, down_all.at[z], parts.at[1]),
        pltpu.make_async_copy(grad_ref, grad_all.at[c], parts.at[2]),
    ]
    gains_ref[z] = gain_ref[...]
    infos_ref[c] = info_ref[...]
    bases[c] = base_ref[...]

    own = lanes(z * shard, shard)
    count = 2 * HEAD_SIZE
    w_ref[:count, own] = picked(wq_ref[...], c * count, count)
    w_ref[count : count + HEAD_SIZE, own] = picked(wk_ref[...], c * HEAD_SIZE, HEAD_SIZE)
    w_ref[count + HEAD_SIZE :, own] = picked(wv_ref[...], c * HEAD_SIZE, HEAD_SIZE)
    line = Line(z, depth, lambda d: w_ref.at[:, lanes(d * shard, shard)], zsend, zrecv)
    line.step(0)

    x = x_ref[...].astype(F32)
    factor = lax.rsqrt(jnp.mean(x * x, -1, keepdims=True) + EPS)
    for k in range(depth - 1):
        ref = gains_ref.at[lax.rem(z + depth - 1 - k, depth)]
        remote(ref, ref, gsend.at[k], grecv.at[k], fsdp=others[k]).wait_recv()
    gain = jnp.concatenate([gains_ref[k, 0:1, :] for k in range(depth)], 1)
    xs[c] = (x * factor * gain).astype(BF16)
    g = Gather(c, own_half(xs.at[c]), xs, row_half, send, recv)
    g.begin()
    out_line = Line(z, depth, lambda d: wo_all.at[d], osend, orecv, out_own)
    out_line.step(0)
    for d in copies:
        d.start()

    def keep(k):
        d = pltpu.make_async_copy(xs.at[flip(c, k)], all_ref.at[flip(c, k)], local.at[k])
        d.start()
        copies.append(d)

    keep(0)

    def rotary(k):
        d = flip(c, k)
        if k:
            for ref, s, r in ((bases, bsend, brecv), (infos_ref, isend, irecv)):
                remote(ref.at[d], ref.at[d], s.at[k], r.at[k], ctx=d).wait_recv()
        half = HEAD_SIZE // 2
        step_cos, step_sin = step_ref[:half], step_ref[half:]
        for b in (0, 1):
            start = b * (LANES // 2)
            base_cos = bases[d, :, start : start + 1]
            base_sin = bases[d, :, start + LANES // 4 : start + LANES // 4 + 1]
            table_ref[2 * d + b, :half] = base_cos * step_cos - base_sin * step_sin
            table_ref[2 * d + b, half:] = base_sin * step_cos + base_cos * step_sin

    for k in range(8):
        rotary(k)

    def project(k):
        d = flip(c, k)
        half = HEAD_SIZE // 2
        raw = contract(w_ref[...], xs[d], ((1,), (1,)))
        for b in (0, 1):
            cosine, sine = table_ref[2 * d + b, :half], table_ref[2 * d + b, half:]
            part = raw[:, b * BLOCK : (b + 1) * BLOCK]
            for h in range(3):
                head = slice(h * HEAD_SIZE, (h + 1) * HEAD_SIZE)
                qkv_ref[2 * d + b, head] = turned(part[head], cosine, sine).astype(BF16)
            qkv_ref[2 * d + b, 3 * HEAD_SIZE :] = part[3 * HEAD_SIZE :].astype(BF16)

    line.landed(0)
    line.step(1)
    g.near_half()
    out_line.landed(0)
    out_line.step(1)
    line.landed(1)
    line.step(2)
    g.near_rest()
    keep(2)
    keep(4)
    out_line.landed(1)
    out_line.step(2)
    line.landed(2)
    for d in strips:
        d.wait()
    gu_line = Line(z, depth, lambda d: gu_all.at[d], usend, urecv, gu_own)
    down_line = Line(z, depth, lambda d: down_all.at[d], dsend, drecv, down_own)
    gu_line.step(0)
    down_line.step(0)
    copies.append(pltpu.make_async_copy(gu_own, gu_all.at[z], parts.at[3]))
    copies[-1].start()
    g2 = Gather(c, own_half(grad_ref), grad_all, row_half, send2, recv2)
    g2.begin()
    project(0)
    g.far()
    project(2)
    project(4)
    for channel, k in ((0, 1), (3, 3)):
        g.paired(channel, k)
        keep(k)
        project(k)
    g2.near_half()
    g.paired(4, 5)
    keep(5)
    project(5)
    keep(6)
    project(6)
    g.paired(5, 7)
    keep(7)
    project(7)
    g2.near_rest()
    out_line.landed(2)
    gu_line.landed(0)
    down_line.landed(0)
    g2.far()
    for channel, k in ((0, 1), (3, 3), (4, 5), (5, 7)):
        g2.paired(channel, k)
    for d in copies:
        d.wait()
    for d in sent:
        d.wait_send()
    line.sent((0, 1, 2))
    out_line.sent((0, 1, 2))
    gu_line.sent((0,))
    down_line.sent((0,))
    g.sent()
    g2.sent()


def first_part(x, gains, info, base, step, weights, grad, depth, cid):
    rows, width = x.shape
    shard = gains.shape[1]
    columns = weights[4].shape[1]
    down_rows = weights[6].shape[0] // 8
    vm = pl.BlockSpec(memory_space=VMEM)
    hbm = pl.BlockSpec(memory_space=ANY)
    shape = jax.ShapeDtypeStruct
    return pl.pallas_call(
        first_kernel,
        out_shape=(
            shape((8, rows, width), BF16),
            shape((8 * rows // BLOCK, 4 * HEAD_SIZE, BLOCK), BF16),
            shape((4 * HEAD_SIZE, width), BF16),
            shape((8 * rows // BLOCK, HEAD_SIZE, BLOCK), F32),
            shape((depth,) + gains.shape, F32),
            shape((8,) + info.shape, jnp.int32),
            shape((depth, shard // 8, width), BF16),
            shape((depth, shard, 2 * columns // 8), BF16),
            shape((depth, down_rows, width), BF16),
            shape((8, rows, width), BF16),
        ),
        in_specs=[vm] * 8 + [hbm] * 5,
        out_specs=(hbm, vm, vm, vm, vm, vm, hbm, hbm, hbm, hbm),
        scratch_shapes=[
            VMEM((8, rows, width), BF16),
            VMEM((shard, 2 * columns // 8), BF16),
            VMEM((8,) + base.shape, F32),
            DMA((depth,)),
            DMA((depth,)),
            DMA((8,)),
            DMA((8,)),
            DMA((8,)),
            DMA((8,)),
            DMA((8, 2)),
            DMA((8, 2)),
        ]
        + [DMA((2, depth))] * 8
        + [DMA((8, 2)), DMA((8, 2)), DMA((8,)), DMA((4 + 2 * depth,))],
        compiler_params=params(cid),
        name="first_part",
    )(x, gains, info, base, step, *weights, grad)


CHUNK = 512


def whole_block(a):
    return pl.BlockSpec(a.shape, lambda j, *_: (0,) * len(a.shape))


def two_heads(ref, block):
    return jnp.concatenate([ref[block, :HEAD_SIZE], ref[block, HEAD_SIZE : 2 * HEAD_SIZE]], 1)


def causal(s, t, j):
    key = t * CHUNK + lax.broadcasted_iota(jnp.int32, s.shape, 0)
    query = j * BLOCK + lax.broadcasted_iota(jnp.int32, s.shape, 1) % BLOCK
    return jnp.where(key <= query, s, -jnp.inf)


def attend_kernel(
    order_ref, qkv_ref, ow_ref, gu_in, down_in, low_ref, lse_ref, ow_all, gu_all, down_all,
    keys, values, send, recv, local, usend, urecv, dsend, drecv,
):
    c = lax.axis_index("ctx")
    z = lax.axis_index("fsdp")
    depth = gu_all.shape[0]
    others = [lax.rem(z + k, depth) for k in range(1, depth)]
    greet([{"ctx": flip(c, k)} for k in (1, 2, 4)] + [{"fsdp": o} for o in others])
    few = depth // 2
    g = Gather(
        c,
        lambda h: ow_ref.at[pl.ds(h * few, few)],
        ow_all,
        lambda ref, d, h: ref.at[pl.ds(h * few, few), d],
        send,
        recv,
    )
    here = pltpu.make_async_copy(ow_ref, ow_all.at[:, c], local)
    here.start()
    g.begin()
    gu_line = Line(z, depth, lambda d: gu_all.at[d], usend, urecv)
    down_line = Line(z, depth, lambda d: down_all.at[d], dsend, drecv)
    gu_line.step(1)
    down_line.step(1)

    blocks = qkv_ref.shape[0]
    per = CHUNK // BLOCK
    factor = HEAD_SIZE ** (-0.5) * math.log2(math.e)
    for b in range(blocks):
        there = slice(b * BLOCK, (b + 1) * BLOCK)
        keys[there, :] = qkv_ref[order_ref[b], 2 * HEAD_SIZE : 3 * HEAD_SIZE].T
        values[:, there] = qkv_ref[order_ref[b], 3 * HEAD_SIZE :]

    def attend_block(j, last):
        q = two_heads(qkv_ref, order_ref[j])

        def step(t, carry, masked):
            top, denom, acc = carry
            s = jnp.dot(keys[pl.ds(t * CHUNK, CHUNK), :], q, preferred_element_type=F32)
            if masked:
                s = causal(s, t, j)
            new_top = jnp.maximum(top, jnp.max(s, 0, keepdims=True))
            p = jnp.exp2((s - new_top) * factor)
            shrink = jnp.exp2((top - new_top) * factor)
            denom = denom * shrink + jnp.sum(p, 0, keepdims=True)
            acc = acc * shrink + jnp.dot(
                values[:, pl.ds(t * CHUNK, CHUNK)], p.astype(BF16), preferred_element_type=F32
            )
            return new_top, denom, acc

        carry = (
            jnp.full((1, 2 * BLOCK), -1e30, F32),
            jnp.zeros((1, 2 * BLOCK), F32),
            jnp.zeros((HEAD_SIZE, 2 * BLOCK), F32),
        )
        for t in range(last):
            carry = step(t, carry, False)
        top, denom, acc = step(last, carry, True)
        out = acc / denom
        lse_ref[pl.ds(j, 1), :, :] = (top * factor + jnp.log2(denom)).reshape(1, 1, 2 * BLOCK)
        for h in (0, 1):
            head = slice(h * HEAD_SIZE, (h + 1) * HEAD_SIZE)
            low_ref[j, head] = out[:, h * BLOCK : (h + 1) * BLOCK].astype(BF16)

    turns = blocks // per
    for turn in range(turns):

        @pl.loop(turn * per, (turn + 1) * per)
        def _(j):
            attend_block(j, turn)

        if turn == 1:
            g.near_half()
        if turn == 2:
            g.near_rest()
    g.far()
    for channel, k in ((0, 1), (3, 3), (4, 5), (5, 7)):
        g.paired(channel, k)
    here.wait()
    gu_line.landed(1)
    down_line.landed(1)
    g.sent()
    gu_line.sent((1,))
    down_line.sent((1,))


def attend(order, qkv, out_part, gate_up, down, cid):
    blocks = qkv.shape[0]
    tokens = blocks * BLOCK
    depth, some, width = out_part.shape
    outs = (
        jax.ShapeDtypeStruct((blocks, 2 * HEAD_SIZE, BLOCK), BF16),
        jax.ShapeDtypeStruct((blocks, 1, 2 * BLOCK), F32),
        jax.ShapeDtypeStruct((depth, 8, some, width), BF16),
        jax.ShapeDtypeStruct(gate_up.shape, BF16),
        jax.ShapeDtypeStruct(down.shape, BF16),
    )
    vm = pl.BlockSpec(memory_space=VMEM)
    hbm = pl.BlockSpec(memory_space=ANY)
    return pl.pallas_call(
        attend_kernel,
        out_shape=outs,
        in_specs=[pl.BlockSpec(memory_space=pltpu.SMEM), vm, hbm, hbm, hbm],
        out_specs=(vm, vm, hbm, hbm, hbm),
        scratch_shapes=[VMEM((tokens, HEAD_SIZE), BF16), VMEM((HEAD_SIZE, tokens), BF16), DMA((8, 2)), DMA((8, 2)), DMA]
        + [DMA((2, depth))] * 4,
        input_output_aliases={3: 3, 4: 4},
        compiler_params=params(cid),
        name="attend",
    )(order, qkv, out_part, gate_up, down)


class Scatter:
    ORDER = (6, 2, 4, 0)

    def __init__(self, c, p, first, last, diagonal, s1, v1, s2, v2):
        self.c, self.p, self.first = c, p, first
        self.last, self.diagonal = last, diagonal
        self.s1, self.v1, self.s2, self.v2 = s1, v1, s2, v2
        self.half = p.shape[1] // 2
        self.pending = []
        self.settled = False

    @staticmethod
    def scratch(rows, width):
        return [
            VMEM((4, rows, width), BF16),
            VMEM((2, rows, width), BF16),
            VMEM((rows, width), BF16),
            DMA((4, 2)),
            DMA((4, 2)),
            DMA((3, 2)),
            DMA((3, 2)),
        ]

    def sl(self, q):
        return pl.ds(q * self.half, self.half)

    def go(self, d):
        d.start()
        self.pending.append(d)

    def give(self, k):
        j = self.ORDER.index(k)
        for q in (0, 1):
            source = self.p.at[flip(self.c, 1 ^ k), self.sl(q)]
            there = self.first.at[j, self.sl(q)]
            self.go(remote(source, there, self.s1.at[j, q], self.v1.at[j, q], ctx=flip(self.c, 1)))

    def paired(self, j, q):
        ref = self.first.at[j, self.sl(q)]
        remote(ref, ref, self.s1.at[j, q], self.v1.at[j, q], ctx=flip(self.c, 1)).wait_recv()

    def chip(self, j, q):
        k = self.ORDER[j]
        return self.p[flip(self.c, k), self.sl(q)].astype(F32) + self.first[j, self.sl(q)].astype(F32)

    def came(self, channel, ref, q, frm):
        remote(
            ref, ref, self.s2.at[channel, q], self.v2.at[channel, q], ctx=flip(self.c, frm)
        ).wait_recv()

    def far(self):
        for q, to in ((0, 2), (1, 4)):
            self.paired(0, q)
            self.first[0, self.sl(q)] = self.chip(0, q).astype(BF16)
            self.go(
                remote(
                    self.first.at[0, self.sl(q)],
                    self.diagonal.at[self.sl(q)],
                    self.s2.at[2, q],
                    self.v2.at[2, q],
                    ctx=flip(self.c, to),
                )
            )

    def onward(self, j, q, merged):
        v = self.chip(j, q)
        if merged:
            v = v + self.diagonal[self.sl(q)].astype(F32)
        self.first[j, self.sl(q)] = v.astype(BF16)
        self.go(
            remote(
                self.first.at[j, self.sl(q)],
                self.last.at[j - 1, self.sl(q)],
                self.s2.at[j - 1, q],
                self.v2.at[j - 1, q],
                ctx=flip(self.c, self.ORDER[j]),
            )
        )

    def direct(self):
        self.paired(1, 0)
        self.onward(1, 0, False)
        self.paired(2, 1)
        self.onward(2, 1, False)

    def merged(self):
        self.paired(2, 0)
        self.came(2, self.diagonal.at[self.sl(0)], 0, 2)
        self.onward(2, 0, True)
        self.paired(1, 1)
        self.came(2, self.diagonal.at[self.sl(1)], 1, 4)
        self.onward(1, 1, True)

    def settle(self):
        for q in (0, 1):
            self.paired(3, q)
            self.first[3, self.sl(q)] = self.chip(3, q).astype(BF16)
        self.settled = True

    def result(self, q):
        if not self.settled:
            self.paired(3, q)
        self.came(0, self.last.at[0, self.sl(q)], q, 2)
        self.came(1, self.last.at[1, self.sl(q)], q, 4)
        chip = self.first[3, self.sl(q)].astype(F32) if self.settled else self.chip(3, q)
        return chip + (
            self.last[0, self.sl(q)].astype(F32) + self.last[1, self.sl(q)].astype(F32)
        )

    def sent(self):
        for d in self.pending:
            d.wait_send()


def exchange_start(c, source, target, send, recv):
    sent = []
    for k in (6, 7, 2, 4, 3, 5, 1):
        there = target.at[pl.ds(2 * c, 2)]
        d = remote(source.at[pl.ds(2 * flip(c, k), 2)], there, send.at[k], recv.at[k], ctx=flip(c, k))
        d.start()
        sent.append(d)
    return sent


def exchange_landed(c, target, send, recv):
    for k in (6, 7, 2, 4, 3, 5, 1):
        ref = target.at[pl.ds(2 * flip(c, k), 2)]
        remote(ref, ref, send.at[k], recv.at[k], ctx=flip(c, k)).wait_recv()


def both_blocks(ref, i):
    return jnp.concatenate([ref[2 * i], ref[2 * i + 1]], 1)


def middle_kernel(
    rank_ref, low_ref, x_ref, gains_ref, g_ref, ow_ref, gu_in, down_in,
    mixed_ref, mgrad_ref, gsum_ref, do_ref, owg_ref, gug_ref, dg_ref, p1_ref, gu_all, down_all,
    out_w, wgu, wd, grads, two, p2, act, dgu, stage, give, got,
    first, last, diagonal, s1, v1, s2, v2,
    esend, erecv, fsend, frecv, send, recv, usend, urecv, dsend, drecv, load, put, wput,
):
    c = lax.axis_index("ctx")
    z = lax.axis_index("fsdp")
    depth, shard, both = gu_all.shape
    mine = both // 2
    rows, width = x_ref.shape
    rows_of_out = out_w.shape[1]
    others = [lax.rem(z + k, depth) for k in range(1, depth)]
    greet([{"ctx": flip(c, k)} for k in range(1, 8)] + [{"fsdp": o} for o in others])
    gu_line = Line(z, depth, lambda d: gu_all.at[d], usend, urecv)
    down_line = Line(z, depth, lambda d: down_all.at[d], dsend, drecv)
    gu_line.step(2)
    down_line.step(2)
    loads = [pltpu.make_async_copy(ow_ref, out_w, load.at[0]), pltpu.make_async_copy(g_ref, grads, load.at[1])]
    for d in loads:
        d.start()

    for i in range(rank_ref.shape[0]):
        give[i] = low_ref[rank_ref[i]]
    sent = exchange_start(c, give, got, esend, erecv)
    got[pl.ds(2 * c, 2)] = give[pl.ds(2 * c, 2)]
    loads[0].wait()
    exchange_landed(c, got, esend, erecv)
    x = lax.fori_loop(
        0, 8, lambda i, total: total + contract(both_blocks(got, i), out_w[i], ((0,), (0,))), x_ref[...].astype(F32)
    )
    mixed_ref[...] = x
    gain = jnp.concatenate([gains_ref[k, 4:5, :] for k in range(depth)], 1)
    factor = lax.rsqrt(jnp.mean(x * x, -1, keepdims=True) + EPS)
    two[c] = (x * factor * gain).astype(BF16)
    g = Gather(c, own_half(two.at[c]), two, row_half, send, recv)
    g.begin()
    loads[1].wait()
    gu_line.landed(2)
    weights = [pltpu.make_async_copy(gu_all, wgu, load.at[2])]
    weights[0].start()
    down_line.landed(2)
    weights.append(pltpu.make_async_copy(down_all, wd, load.at[3]))
    weights[1].start()
    for d in weights:
        d.wait()

    def block(d, slot):
        up_w = wgu[...].reshape(width, both)
        down_w = wd[...].reshape(mine, width)
        gate_up = jnp.dot(two[d], up_w, preferred_element_type=F32)
        gate, up = gate_up[:, :mine], gate_up[:, mine:]
        sigma = jax.nn.sigmoid(gate)
        silu = gate * sigma
        active = (silu * up).astype(BF16)
        act[d] = active
        active_grad = contract(grads[d], down_w, ((1,), (1,)))
        gate_grad = active_grad * up * sigma * (1.0 + gate * (1.0 - sigma))
        up_grad = active_grad * silu
        grad = jnp.concatenate([gate_grad, up_grad], 1).astype(BF16)
        dgu[d] = grad
        p2[d] = contract(grad, up_w, ((1,), (1,))).astype(BF16)
        stage[slot] = jnp.dot(active, down_w, preferred_element_type=F32).astype(BF16)
        pltpu.make_async_copy(stage.at[slot], p1_ref.at[d], put.at[slot]).start()

    def drain(slot):
        pltpu.make_async_copy(stage.at[slot], p1_ref.at[c], put.at[slot]).wait()

    def pair(k, again):
        d = flip(c, k)
        other = flip(c, 1 ^ k)

        @pl.loop(0, 2)
        def _(i):
            if again:
                drain(i)
            block(other + i * (d - other), i)

    scatter = Scatter(c, p2, first, last, diagonal, s1, v1, s2, v2)
    g.paired(0, 1)
    pair(0, False)
    scatter.give(0)
    g.near_half()
    g.near_rest()
    g.paired(3, 3)
    pair(2, True)
    scatter.give(2)
    g.far()
    g.paired(5, 7)
    pair(6, True)
    scatter.give(6)
    g.paired(4, 5)
    scatter.far()
    pair(4, True)
    scatter.give(4)
    scatter.direct()

    puts = []

    def wide(f):
        part = lambda i, total: total + contract(
            two[pl.ds(2 * i, 2), :, f * shard : (f + 1) * shard].reshape(2 * rows, shard),
            dgu[pl.ds(2 * i, 2)].reshape(2 * rows, both),
            ((0,), (0,)),
        )
        wgu[f] = lax.fori_loop(0, 4, part, jnp.zeros((shard, both), F32)).astype(BF16)
        puts.append(pltpu.make_async_copy(wgu.at[f], gug_ref.at[f], wput.at[f]))
        puts[-1].start()

    wide(0)
    scatter.merged()
    for f in range(1, depth):
        wide(f)
    strip = mine // depth
    for f in range(0, depth, 2):
        part = lambda i, total: total + contract(
            act[pl.ds(2 * i, 2), :, f * strip : (f + 2) * strip].reshape(2 * rows, 2 * strip),
            grads[pl.ds(2 * i, 2)].reshape(2 * rows, width),
            ((0,), (0,)),
        )
        part = lax.fori_loop(0, 4, part, jnp.zeros((2 * strip, width), F32))
        wd[f : f + 2] = part.astype(BF16).reshape(2, strip, width)
    puts.append(pltpu.make_async_copy(wd, dg_ref, wput.at[depth]))
    puts[-1].start()

    two_grad = jnp.concatenate([scatter.result(0), scatter.result(1)], 0)
    x = mixed_ref[...]
    factor = lax.rsqrt(jnp.mean(x * x, -1, keepdims=True) + EPS)
    scaled = two_grad * gain
    mixed_grad = (
        grads[c].astype(F32)
        + factor * scaled
        - x * (factor * factor * factor) * jnp.mean(scaled * x, -1, keepdims=True)
    )
    gsum_ref[...] = jnp.broadcast_to(jnp.sum(two_grad * x * factor, 0, keepdims=True), gsum_ref.shape)
    mgrad_ref[...] = mixed_grad
    branch = mixed_grad.astype(BF16)
    for d in sent:
        d.wait_send()
    for i in range(8):
        part = contract(out_w[i], branch, ((1,), (1,))).astype(BF16)
        give[2 * i] = part[:, :BLOCK]
        give[2 * i + 1] = part[:, BLOCK:]
    sent = exchange_start(c, give, do_ref, fsend, frecv)
    do_ref[pl.ds(2 * c, 2)] = give[pl.ds(2 * c, 2)]
    for d in puts:
        d.wait()
    for i in (0, 1):
        drain(i)
    few = rows_of_out // depth
    for i in range(8):
        part = jnp.dot(both_blocks(got, i), branch, preferred_element_type=F32).astype(BF16)
        f = i * depth // 8
        for t in range(depth):
            out_w[i * depth % 8 + t, f * few : (f + 1) * few] = part[t * few : (t + 1) * few]
    out_put = pltpu.make_async_copy(out_w, owg_ref, load.at[0])
    out_put.start()
    exchange_landed(c, do_ref, fsend, frecv)
    out_put.wait()
    for d in sent:
        d.wait_send()
    scatter.sent()
    g.sent()
    gu_line.sent((2,))
    down_line.sent((2,))


def middle(rank, low, x, gains, grad_all, out_w, gate_up, down, cid):
    rows, width = x.shape
    depth, shard, both = gate_up.shape
    shape = jax.ShapeDtypeStruct
    vm = pl.BlockSpec(memory_space=VMEM)
    hbm = pl.BlockSpec(memory_space=ANY)
    heads = (8 * rows // BLOCK, 2 * HEAD_SIZE, BLOCK)
    block = (8, rows, width)
    return pl.pallas_call(
        middle_kernel,
        out_shape=(
            shape((rows, width), F32),
            shape((rows, width), F32),
            shape((8, width), F32),
            shape(heads, BF16),
            shape(out_w.shape, BF16),
            shape(gate_up.shape, BF16),
            shape(down.shape, BF16),
            shape(block, BF16),
            shape(gate_up.shape, BF16),
            shape(down.shape, BF16),
        ),
        in_specs=[pl.BlockSpec(memory_space=pltpu.SMEM), vm, vm, vm, hbm, hbm, hbm, hbm],
        out_specs=(vm, vm, vm, vm, hbm, hbm, hbm, hbm, hbm, hbm),
        scratch_shapes=[
            VMEM(out_w.shape, BF16),
            VMEM(gate_up.shape, BF16),
            VMEM(down.shape, BF16),
            VMEM(block, BF16),
            VMEM(block, BF16),
            VMEM(block, BF16),
            VMEM((8, rows, both // 2), BF16),
            VMEM((8, rows, both), BF16),
            VMEM((2, rows, width), BF16),
            VMEM(heads, BF16),
            VMEM(heads, BF16),
        ]
        + Scatter.scratch(rows, width)
        + [DMA((8,))] * 4
        + [DMA((8, 2))] * 2
        + [DMA((2, depth))] * 4
        + [DMA((4,)), DMA((2,)), DMA((depth + 1,))],
        input_output_aliases={6: 8, 7: 9},
        compiler_params=params(cid),
        name="middle",
    )(rank, low, x, gains, grad_all, out_w, gate_up, down)


class LineScatter:
    def __init__(self, z, own, left, right, send, recv):
        self.z, self.own, self.left, self.right = z, own, left, right
        self.send, self.recv = send, recv
        self.top = own.shape[0] - 1

    @staticmethod
    def scratch(shape):
        depth = shape[0]
        hops = (depth - 1,) + tuple(shape[1:])
        return [VMEM(hops, BF16), VMEM(hops, BF16), DMA((2, depth)), DMA((2, depth))]

    def copy(self, way, s, part, to):
        there = (self.left, self.right)[way].at[s]
        return remote(self.own.at[part], there, self.send.at[way, s], self.recv.at[way, s], fsdp=to)

    def landed(self, way, s):
        ref = (self.left, self.right)[way].at[s]
        remote(ref, ref, self.send.at[way, s], self.recv.at[way, s], fsdp=self.z - 1 + 2 * way).wait_recv()

    def step(self, s):
        z, top = self.z, self.top
        for way in (0, 1):
            place = z if way == 0 else top - z
            part = top - s + z if way == 0 else s - top + z

            @pl.when((place <= s) & (place < top))
            def _():
                if s:

                    @pl.when(place > 0)
                    def _():
                        self.landed(way, s - 1)
                        came = (self.left, self.right)[way][s - 1]
                        self.own[part] = (self.own[part].astype(F32) + came.astype(F32)).astype(BF16)

                self.copy(way, s, part, z + 1 - 2 * way).start()

    def result(self):
        z, last = self.z, self.top - 1

        def close(ways):
            total = self.own[z].astype(F32)
            for way in ways:
                self.landed(way, last)
                total = total + (self.left, self.right)[way][last].astype(F32)
            self.own[z] = total.astype(BF16)

        @pl.when(z == 0)
        def _():
            close((1,))

        @pl.when((z > 0) & (z < self.top))
        def _():
            close((0, 1))

        @pl.when(z == self.top)
        def _():
            close((0,))

    def sent(self):
        z, top = self.z, self.top
        for s in range(top):
            for way in (0, 1):
                place = z if way == 0 else top - z
                part = top - s + z if way == 0 else s - top + z

                @pl.when((place <= s) & (place < top))
                def _():
                    self.copy(way, s, part, z + 1 - 2 * way).wait_send()


def back_kernel(
    order_ref, rank_ref, qkv_ref, o_ref, do_ref, lse_ref, table_ref, w_ref, gains_ref, gain_two_ref,
    mixed_ref, mgrad_ref, x_ref, all_ref, p1_ref, owg_ref, gug_ref, dg_ref,
    layer_ref, input_ref, sum_ref, gu_all, down_all, q_all, o_all,
    keys, keys_t, values, dk, dv, dqn, dqkv, acc, xs, big, owg, gug, down, heads, outs,
    gain_rows, by_z, part_sum, by_c, first, last, diagonal, first2, last2, diagonal2, *rest,
):
    scatter_sems = (rest[:4], rest[4:8], rest[8:12])
    lines = (rest[12:16], rest[16:20], rest[20:24], rest[24:28])
    send, recv, local, load, xload, zs, zr, cs, cr, free = rest[28:]
    c = lax.axis_index("ctx")
    z = lax.axis_index("fsdp")
    depth, shard = heads.shape[0], heads.shape[2]
    rows, width = xs.shape[1:]
    others = [lax.rem(z + k, depth) for k in range(1, depth)]
    greet([{"ctx": flip(c, k)} for k in range(1, 8)] + [{"fsdp": o} for o in others])
    some = acc.at[pl.ds(0, rows)]
    loads = [
        pltpu.make_async_copy(a, t, load.at[i])
        for i, (a, t) in enumerate(
            ((gug_ref, gug), (p1_ref, big), (owg_ref, owg), (dg_ref, down), (mixed_ref, some), (mgrad_ref, some), (x_ref, xs.at[0]))
        )
    ]
    for d in loads[:4]:
        d.start()
    gu_line, down_line, q_line, o_line = (
        LineScatter(z, a, *refs) for a, refs in zip((gug, down, heads, outs), lines)
    )
    layer = Scatter(c, big, first, last, diagonal, *scatter_sems[0])
    out = Scatter(c, owg, first2, last2, diagonal2, *scatter_sems[1])
    one = Scatter(c, big, first, last, diagonal, *scatter_sems[2])
    near = [flip(c, k) for k in (1, 2, 4)]

    blocks = qkv_ref.shape[0]
    per = CHUNK // BLOCK
    scale = HEAD_SIZE ** (-0.5)
    factor = scale * math.log2(math.e)
    half = HEAD_SIZE // 2
    for b in range(blocks):
        there = slice(b * BLOCK, (b + 1) * BLOCK)
        key = qkv_ref[order_ref[b], 2 * HEAD_SIZE : 3 * HEAD_SIZE]
        keys[there, :] = key.T
        keys_t[:, there] = key
        values[there, :] = qkv_ref[order_ref[b], 3 * HEAD_SIZE :].T
    dk[...] = jnp.zeros_like(dk)
    dv[...] = jnp.zeros_like(dv)
    loads[0].wait()
    gu_line.step(0)
    loads[1].wait()
    layer.give(6)
    layer.give(2)
    layer.give(4)
    loads[2].wait()
    out.give(6)
    layer.give(0)
    for k in (2, 4, 0):
        out.give(k)
    loads[3].wait()

    def attend_block(j, last):
        block = order_ref[j]
        q = two_heads(qkv_ref, block)
        do = two_heads(do_ref, block)
        delta = jnp.sum(two_heads(o_ref, j).astype(F32) * do.astype(F32), 0, keepdims=True)
        lse = lse_ref[j]

        def step(t, dq, masked):
            there = pl.ds(t * CHUNK, CHUNK)
            s = jnp.dot(keys[there, :], q, preferred_element_type=F32)
            if masked:
                s = causal(s, t, j)
            p = jnp.exp2(s * factor - lse)
            dp = jnp.dot(values[there, :], do, preferred_element_type=F32)
            ds = (p * (dp - delta)).astype(BF16)
            wide = pl.ds(t * per, per)
            dv[wide] += contract(p.astype(BF16), do, ((1,), (1,))).reshape(per, BLOCK, HEAD_SIZE)
            dk[wide] += contract(ds, q, ((1,), (1,))).reshape(per, BLOCK, HEAD_SIZE)
            return dq + jnp.dot(keys_t[:, there], ds, preferred_element_type=F32)

        dq = jnp.zeros((HEAD_SIZE, 2 * BLOCK), F32)
        for t in range(last):
            dq = step(t, dq, False)
        dq = step(last, dq, True) * scale
        cosine, sine = table_ref[block, :half], table_ref[block, half:]
        for h in (0, 1):
            part = dq[:, h * BLOCK : (h + 1) * BLOCK]
            dqn[j, h * HEAD_SIZE : (h + 1) * HEAD_SIZE] = turned(part, cosine, -sine).astype(BF16)

    for turn in range(blocks // per):

        @pl.loop(turn * per, (turn + 1) * per)
        def _(j):
            attend_block(j, turn)

        if turn == 0:
            layer.far()
            out.far()
        if turn == 1:
            layer.direct()
            out.direct()
        if turn == 2:
            layer.merged()
            gu_line.step(1)
            down_line.step(0)

    for i in range(blocks):
        to = slice(i * BLOCK, (i + 1) * BLOCK)
        natural = rank_ref[i]
        dqkv[: 2 * HEAD_SIZE, to] = dqn[natural]
        dqkv[2 * HEAD_SIZE : 3 * HEAD_SIZE, to] = turned(
            dk[natural].T * scale, table_ref[i, :half], -table_ref[i, half:]
        ).astype(BF16)
        dqkv[3 * HEAD_SIZE :, to] = dv[natural].T.astype(BF16)

    def x_load(d, slot):
        return pltpu.make_async_copy(all_ref.at[d], xs.at[slot], xload.at[slot])

    x_load(0, 0).start()
    out.merged()
    layer.settle()
    layer.sent()
    acc[...] = jnp.zeros_like(acc)
    for d in range(8):
        slot = d % 2
        if d + 1 < 8:
            x_load(d + 1, 1 - slot).start()
        part = dqkv[:, d * rows : (d + 1) * rows]
        big[d] = contract(part, w_ref[...], ((0,), (0,))).astype(BF16)
        x_load(d, slot).wait()
        acc[...] += jnp.dot(part, xs[slot], preferred_element_type=F32)
        if d == 3:
            gu_line.step(2)
    for f in range(depth):
        heads[f] = acc[:, f * shard : (f + 1) * shard].astype(BF16)
    loads[4].start()
    loads[6].start()
    down_line.step(1)
    q_line.step(0)
    loads[4].wait()
    for q in (0, 1):
        at = pl.ds(q * (rows // 2), rows // 2)
        xs[1, at] = (acc[at] + layer.result(q)).astype(BF16)
    loads[5].start()
    layer_put = pltpu.make_async_copy(xs.at[1], layer_ref, xload.at[1])
    layer_put.start()
    for d in near:
        pl.semaphore_signal(free, inc=1, device_id={"ctx": d}, device_id_type=MESH)
    pl.semaphore_wait(free, len(near))
    for k in Scatter.ORDER:
        one.give(k)
    one.far()
    outs[...] = jnp.concatenate([out.result(0), out.result(1)], 0).astype(BF16).reshape(outs.shape)
    o_line.step(0)
    one.direct()
    gu_line.result()
    here = []
    gathers = []

    def spread(i, source, everyone):
        here.append(pltpu.make_async_copy(source, everyone.at[c], local.at[i]))
        here[-1].start()
        at, own = (row_half, own_half(source)) if source.shape[0] % 32 == 0 else (column_half, own_half(source, 1))
        gathers.append(Gather(c, own, everyone, at, send.at[i], recv.at[i]))
        gathers[-1].begin()

    spread(0, gug.at[z], gu_all)
    down_line.step(2)
    q_line.step(1)
    o_line.step(1)
    one.merged()

    gain = jnp.concatenate([gains_ref[k, 0:1, :] for k in range(depth)], 1)
    one_grad = jnp.concatenate([one.result(0), one.result(1)], 0)
    gathers[0].near_half()
    loads[5].wait()
    loads[6].wait()
    layer_put.wait()
    x = xs[0].astype(F32)
    norm = lax.rsqrt(jnp.mean(x * x, -1, keepdims=True) + EPS)
    scaled = one_grad * gain
    grad = norm * scaled - x * (norm * norm * norm) * jnp.mean(scaled * x, -1, keepdims=True)
    xs[1] = (acc[:rows] + grad).astype(BF16)
    here.append(pltpu.make_async_copy(xs.at[1], input_ref, xload.at[0]))
    here[-1].start()
    gain_rows[:4] = jnp.broadcast_to(jnp.sum(one_grad * x * norm, 0, keepdims=True), (4, width))
    gain_rows[4:] = gain_two_ref[4:]
    sent = []
    for k, o in enumerate(others):
        d = remote(gain_rows.at[:, lanes(o * shard, shard)], by_z.at[z], zs.at[k], zr.at[k], fsdp=o)
        d.start()
        sent.append(d)
    gathers[0].near_rest()
    q_line.step(2)
    o_line.step(2)
    down_line.result()
    spread(1, down.at[z], down_all)
    gathers[0].far()

    total = gain_rows[:, lanes(z * shard, shard)]
    for k in range(depth - 1):
        ref = by_z.at[lax.rem(z + depth - 1 - k, depth)]
        remote(ref, ref, zs.at[k], zr.at[k], fsdp=others[k]).wait_recv()
        total = total + by_z[lax.rem(z + depth - 1 - k, depth)]
    part_sum[...] = total
    for k in range(1, 8):
        d = remote(part_sum, by_c.at[c], cs.at[k], cr.at[k], ctx=flip(c, k))
        d.start()
        sent.append(d)
    by_c[c] = total

    gathers[1].near_half()
    q_line.result()
    spread(2, heads.at[z], q_all)
    gathers[1].near_rest()
    o_line.result()
    spread(3, outs.at[z], o_all)
    gathers[1].far()
    for g in gathers[2:]:
        g.near_half()
    for g in gathers[2:]:
        g.near_rest()
    for g in gathers[2:]:
        g.far()
    for g in gathers:
        for channel, k in ((0, 1), (3, 3), (4, 5), (5, 7)):
            g.paired(channel, k)
    for k in range(1, 8):
        ref = by_c.at[flip(c, k)]
        remote(ref, ref, cs.at[k], cr.at[k], ctx=flip(c, k)).wait_recv()
    total = by_c[0]
    for k in range(1, 8):
        total = total + by_c[k]
    sum_ref[...] = total
    for d in here:
        d.wait()
    for d in sent:
        d.wait_send()
    out.sent()
    one.sent()
    for line in (gu_line, down_line, q_line, o_line):
        line.sent()
    for g in gathers:
        g.sent()


def back(order, rank, arrays, large, depth, cid):
    blocks = arrays[0].shape[0]
    tokens = blocks * BLOCK
    rows, width = large[0].shape
    out_rows = large[5].shape[1]
    gate_up, down = large[6], large[7]
    shard = gate_up.shape[1]
    shape = jax.ShapeDtypeStruct
    vm = pl.BlockSpec(memory_space=VMEM)
    hbm = pl.BlockSpec(memory_space=ANY)
    sm = pl.BlockSpec(memory_space=pltpu.SMEM)
    tall = (tokens, HEAD_SIZE)
    small = (8, shard)
    lines = (gate_up.shape, down.shape, (depth, 4 * HEAD_SIZE, shard), (depth, out_rows // depth, width))
    scatter = Scatter.scratch(rows, width)
    return pl.pallas_call(
        back_kernel,
        out_shape=[shape((rows, width), BF16), shape((rows, width), BF16), shape(small, F32)]
        + [shape((8,) + a[1:], BF16) for a in lines],
        in_specs=[sm, sm] + [vm] * len(arrays) + [hbm] * len(large),
        out_specs=[hbm, hbm, vm] + [hbm] * 4,
        scratch_shapes=[
            VMEM(tall, BF16),
            VMEM(tall[::-1], BF16),
            VMEM(tall, BF16),
            VMEM((blocks, BLOCK, HEAD_SIZE), F32),
            VMEM((blocks, BLOCK, HEAD_SIZE), F32),
            VMEM((blocks, 2 * HEAD_SIZE, BLOCK), BF16),
            VMEM((4 * HEAD_SIZE, tokens), BF16),
            VMEM((4 * HEAD_SIZE, width), F32),
            VMEM((2, rows, width), BF16),
            VMEM((8, rows, width), BF16),
            VMEM((8, out_rows, width), BF16),
        ]
        + [VMEM(a, BF16) for a in lines]
        + [VMEM((8, width), F32), VMEM((depth,) + small, F32), VMEM(small, F32), VMEM((8,) + small, F32)]
        + scatter[:3]
        + Scatter.scratch(out_rows, width)[:3]
        + scatter[3:] * 3
        + [r for a in lines for r in LineScatter.scratch(a)]
        + [DMA((4, 8, 2)), DMA((4, 8, 2)), DMA((4,)), DMA((7,)), DMA((2,))]
        + [DMA((depth,)), DMA((depth,)), DMA((8,)), DMA((8,)), pltpu.SemaphoreType.REGULAR],
        compiler_params=params(cid),
        name="back",
    )(order, rank, *arrays, *large)


def widen_mlp(gate_up, down):
    _, shard, both = gate_up.shape
    mine = both // 2
    depth = mine // LANES
    step = shard // 8

    def kernel(a_ref, d_ref, gate_ref, up_ref, down_ref):
        for i, out in enumerate((gate_ref, up_ref)):
            for c in range(8):
                for s in range(depth):
                    out[:, (s * 8 + c) * LANES : (s * 8 + c + 1) * LANES] = a_ref[
                        c, :, i * mine + s * LANES : i * mine + (s + 1) * LANES
                    ].astype(F32)
        down_ref[...] = d_ref[0].astype(F32)

    _, rows, width = down.shape
    wide = jax.ShapeDtypeStruct((shard, 8 * mine), F32)
    wide_spec = pl.BlockSpec((step, 8 * mine), lambda i: (i, 0))
    return pl.pallas_call(
        kernel,
        grid=(8,),
        out_shape=(wide, wide, jax.ShapeDtypeStruct((8 * rows, width), F32)),
        in_specs=[pl.BlockSpec((8, step, both), lambda i: (0, i, 0)), pl.BlockSpec((1, rows, width), lambda i: (i, 0, 0))],
        out_specs=(wide_spec, wide_spec, pl.BlockSpec((rows, width), lambda i: (i, 0))),
        compiler_params=pltpu.CompilerParams(vmem_limit_bytes=VMEM_BYTES),
        name="widen_mlp",
    )(gate_up, down)


def widen_attention(qkv, out):
    shard = qkv.shape[2]
    width = out.shape[2]

    def kernel(a_ref, o_ref, q_out, k_out, v_out, out_out):
        per_q = 2 * HEAD_SIZE
        for c in range(0, 8, 2):
            both = jnp.concatenate([a_ref[c + i, :per_q, :] for i in (0, 1)], 0)
            q_out[:, c * per_q : (c + 2) * per_q] = both.astype(F32).T
        for target, first in ((k_out, per_q), (v_out, per_q + HEAD_SIZE)):
            for c in range(0, 8, 4):
                four = jnp.concatenate([a_ref[c + i, first : first + HEAD_SIZE, :] for i in range(4)], 0)
                target[:, c * HEAD_SIZE : (c + 4) * HEAD_SIZE] = four.astype(F32).T
        for c in range(8):
            rows = out.shape[1]
            out_out[c * rows : (c + 1) * rows, :] = o_ref[c].astype(F32)

    vm = pl.BlockSpec(memory_space=VMEM)
    shape = lambda n: jax.ShapeDtypeStruct((shard, n), F32)
    heads = 8 * HEAD_SIZE
    return pl.pallas_call(
        kernel,
        out_shape=(shape(2 * heads), shape(heads), shape(heads), shape(width)),
        in_specs=[vm, vm],
        out_specs=(vm, vm, vm, vm),
        compiler_params=pltpu.CompilerParams(vmem_limit_bytes=VMEM_BYTES),
        name="widen_attention",
    )(qkv, out)


def in_plane(
    depth,
    hidden_in,
    positions,
    attn_gain,
    w_query,
    key_projection,
    value_projection,
    w_out,
    mlp_gain,
    w_gate,
    w_up,
    w_down,
    out_grad,
):
    plane = 8
    rows, width = hidden_in.shape[1:]
    shard = width // depth
    half = HEAD_SIZE // 2

    position = positions[0]
    lane = lax.broadcasted_iota(jnp.int32, (8, LANES), 1)
    info = jnp.where(lane < LANES // 2, position[0], position[BLOCK])
    gains = jnp.concatenate(
        [
            jnp.broadcast_to(attn_gain.astype(F32)[None], (4, shard)),
            jnp.broadcast_to(mlp_gain.astype(F32)[None], (4, shard)),
        ],
        0,
    )
    freq = THETA ** (-(jnp.arange(half, dtype=F32) * 2.0 / HEAD_SIZE))
    start = freq[:, None] * info[:1].astype(F32)
    quarter = lane[:1] // (LANES // 4)
    base = jnp.where(quarter % 2 == 0, jnp.cos(start), jnp.sin(start))
    inner = freq[:, None] * jnp.arange(BLOCK, dtype=F32)[None]
    step = jnp.concatenate([jnp.cos(inner), jnp.sin(inner)], 0)

    hidden_low = hidden_in[0]
    weights = (w_query, key_projection, value_projection, w_out, w_gate, w_up, w_down)
    grad_low = out_grad[0]
    (normed_all, qkv, qkv_w, table, gains_all, infos, out_part, gate_up_w, down_w, grad_all) = first_part(
        hidden_low, gains, info, base, step, weights, grad_low, depth, 0
    )
    starts = infos[:, 0].reshape(plane, 2, LANES // 2)[:, :, 0].reshape(2 * plane)
    rank = ((starts - jnp.min(starts)) // BLOCK).astype(jnp.int32)
    blocks = 2 * plane
    order = jnp.sum(
        jnp.where(rank[None, :] == jnp.arange(blocks)[:, None], jnp.arange(blocks)[None, :], 0), 1
    ).astype(jnp.int32)

    attended_low, lse, out_w, gate_up_w, down_w = attend(order, qkv, out_part, gate_up_w, down_w, 1)
    mixed, mixed_grad, gain_two_grad, do, out_wgrad, gate_up_wgrad, down_wgrad, down_sum, _, _ = middle(
        rank, attended_low, hidden_low, gains_all, grad_all, out_w.reshape(plane, -1, width), gate_up_w, down_w, 2
    )
    arrays = (qkv, attended_low, do, lse, table, qkv_w, gains_all, gain_two_grad)
    large = (mixed, mixed_grad, hidden_low, normed_all, down_sum, out_wgrad, gate_up_wgrad, down_wgrad)
    layer_out, input_grad, gain_sums, gate_up_all, down_all, qkv_all, out_grads = back(
        order, rank, arrays, large, depth, 3
    )
    gate_total, up_total, down_total = widen_mlp(gate_up_all, down_all)
    query_total, key_total, value_total, out_total = widen_attention(qkv_all, out_grads)
    return (
        layer_out[None],
        input_grad[None],
        gain_sums[0],
        query_total,
        key_total,
        value_total,
        out_total,
        gain_sums[4],
        gate_total,
        up_total,
        down_total,
    )


def solution(mesh):
    placed = (
        P("fsdp", "ctx", None),
        P("fsdp", "ctx"),
        P("fsdp"),
        P("fsdp", None),
        P("fsdp", None),
        P("fsdp", None),
        P("fsdp", None),
        P("fsdp"),
        P("fsdp", None),
        P("fsdp", None),
        P("fsdp", None),
        P("fsdp", "ctx", None),
    )
    body = per_device
    if mesh.shape["ctx"] == KEY_VALUE_HEADS:
        body = functools.partial(in_plane, mesh.shape["fsdp"])
    return jax.shard_map(
        body,
        mesh=mesh,
        in_specs=placed,
        out_specs=(
            P("fsdp", "ctx", None),
            P("fsdp", "ctx", None),
            P("fsdp"),
            P("fsdp", None),
            P("fsdp", None),
            P("fsdp", None),
            P("fsdp", None),
            P("fsdp"),
            P("fsdp", None),
            P("fsdp", None),
            P("fsdp", None),
        ),
        check_vma=False,
    )
```

```python
import functools
import math

import jax
import jax.numpy as jnp
import numpy as np
from jax import lax
from jax.experimental import pallas as pl
from jax.experimental.pallas import tpu as pltpu
from jax.sharding import PartitionSpec as P

QUERY_HEADS = 16
KEY_VALUE_HEADS = 8
HEAD_SIZE = 96


EPS = 1e-05
THETA = 100000.0


def tables(token_position):
    half = HEAD_SIZE // 2
    freq = THETA ** (-(jnp.arange(half, dtype=jnp.float32) * 2.0 / HEAD_SIZE))
    angle = token_position.astype(jnp.float32)[:, None] * freq[None, :]
    return (jnp.cos(angle)[:, None, :], jnp.sin(angle)[:, None, :])


def rotary_embed(value_rows, cosine_table, sine_table):
    half = value_rows.shape[-1] // 2
    first = value_rows[..., :half]
    second = value_rows[..., half:]
    return jnp.concatenate(
        [first * cosine_table - second * sine_table, second * cosine_table + first * sine_table], -1
    )


def rotary_embed_backward(grads, cosine_table, sine_table):
    half = grads.shape[-1] // 2
    first = grads[..., :half]
    second = grads[..., half:]
    return jnp.concatenate(
        [first * cosine_table + second * sine_table, second * cosine_table - first * sine_table], -1
    )


def norm_forward(hidden, gain):
    return (
        hidden
        * lax.rsqrt(jnp.mean(hidden * hidden, -1, keepdims=True) + EPS)
        * gain.astype(jnp.float32)
    )


def norm_back(hidden, gain, grad):
    factor = lax.rsqrt(jnp.mean(hidden * hidden, -1, keepdims=True) + EPS)
    scaled = grad * gain.astype(jnp.float32)
    hidden_grad = factor * scaled - hidden * factor * factor * factor * jnp.mean(
        scaled * hidden, -1, keepdims=True
    )
    gain_grad = jnp.sum(grad * hidden * factor, 0)
    return (hidden_grad, gain_grad)


def dot_first(left, right):
    return lax.dot_general(
        left, right, (((0,), (0,)), ((), ())), preferred_element_type=jnp.float32
    )


def dot_last(left, right):
    return lax.dot_general(
        left, right, (((1,), (1,)), ((), ())), preferred_element_type=jnp.float32
    )


def over_blocks(step_fn, carry, arrays):
    block_count = arrays[0].shape[0]
    size = math.gcd(block_count, 512)
    parts = block_count // size
    shaped = tuple((item.reshape((parts, size) + item.shape[1:]) for item in arrays))

    def advance(state, inputs):
        index, pieces = inputs
        return (step_fn(state, pieces, index * size), None)

    final, unused = lax.scan(advance, carry, (jnp.arange(parts, dtype=jnp.int32), shaped))
    return final


def per_device(
    hidden_in,
    positions,
    attn_gain,
    w_query,
    key_projection,
    value_projection,
    w_out,
    mlp_gain,
    w_gate,
    w_up,
    w_down,
    out_grad,
):
    hidden = hidden_in[0].astype(jnp.float32)
    local_rows = hidden.shape[0]
    query_pos = positions[0]
    query_groups = QUERY_HEADS // KEY_VALUE_HEADS
    scale = HEAD_SIZE ** (-0.5)
    cosine_table, sine_table = tables(query_pos)
    attn_set = (
        lax.all_gather(attn_gain, "fsdp", axis=0, tiled=True),
        lax.all_gather(w_query, "fsdp", axis=0, tiled=True),
        lax.all_gather(key_projection, "fsdp", axis=0, tiled=True),
        lax.all_gather(value_projection, "fsdp", axis=0, tiled=True),
        lax.all_gather(w_out, "fsdp", axis=0, tiled=True),
    )
    gain_one, query_w, key_matrix, value_matrix, out_w = attn_set
    first_normed = norm_forward(hidden, gain_one).astype(jnp.bfloat16)
    query_raw = jnp.dot(first_normed, query_w, preferred_element_type=jnp.float32)
    unrotated_key = jnp.dot(first_normed, key_matrix, preferred_element_type=jnp.float32)
    value_raw = jnp.dot(first_normed, value_matrix, preferred_element_type=jnp.float32)
    query_rows = (
        rotary_embed(
            query_raw.reshape(local_rows, QUERY_HEADS, HEAD_SIZE), cosine_table, sine_table
        )
        .astype(jnp.bfloat16)
        .reshape(local_rows, KEY_VALUE_HEADS, query_groups, HEAD_SIZE)
    )
    keys_flat = (
        rotary_embed(
            unrotated_key.reshape(local_rows, KEY_VALUE_HEADS, HEAD_SIZE), cosine_table, sine_table
        )
        .astype(jnp.bfloat16)
        .reshape(local_rows, KEY_VALUE_HEADS * HEAD_SIZE)
    )
    values_flat = value_raw.astype(jnp.bfloat16)
    key_pos_all = lax.all_gather(query_pos, "ctx", axis=0, tiled=True)
    sequence_length = key_pos_all.shape[0]

    def masked_scores(partial_keys, first):
        block_count = partial_keys.shape[0]
        key_pos = lax.dynamic_slice_in_dim(key_pos_all, first, block_count)
        scores = (
            jnp.einsum(
                "tkgd,nkd->kgtn",
                query_rows,
                partial_keys.reshape(block_count, KEY_VALUE_HEADS, HEAD_SIZE),
                preferred_element_type=jnp.float32,
            )
            * scale
        )
        visible = key_pos[None, None, None, :] <= query_pos[None, None, :, None]
        return jnp.where(visible, scores, -jnp.inf)

    def forward_part(carry, part, first):
        top, denom, accum = carry
        partial_keys, partial_values = part
        block_count = partial_keys.shape[0]
        scores = masked_scores(partial_keys, first)
        new_top = jnp.maximum(top, jnp.max(scores, -1))
        weights = jnp.exp(scores - new_top[..., None])
        factor = jnp.exp(top - new_top)
        denom = denom * factor + jnp.sum(weights, -1)
        accum = accum * factor[..., None] + jnp.einsum(
            "kgtn,nkd->kgtd",
            weights.astype(jnp.bfloat16),
            partial_values.reshape(block_count, KEY_VALUE_HEADS, HEAD_SIZE),
            preferred_element_type=jnp.float32,
        )
        return (new_top, denom, accum)

    start_state = (
        jnp.full((KEY_VALUE_HEADS, query_groups, local_rows), -1e30, jnp.float32),
        jnp.zeros((KEY_VALUE_HEADS, query_groups, local_rows), jnp.float32),
        jnp.zeros((KEY_VALUE_HEADS, query_groups, local_rows, HEAD_SIZE), jnp.float32),
    )
    top, denom, accum = over_blocks(
        forward_part,
        start_state,
        (
            lax.all_gather(keys_flat, "ctx", axis=0, tiled=True),
            lax.all_gather(values_flat, "ctx", axis=0, tiled=True),
        ),
    )
    attended_output = accum / denom[..., None]
    log_total = top + jnp.log(denom)
    attended_low = (
        attended_output.transpose(2, 0, 1, 3)
        .reshape(local_rows, QUERY_HEADS * HEAD_SIZE)
        .astype(jnp.bfloat16)
    )
    mixed = hidden + jnp.dot(attended_low, out_w, preferred_element_type=jnp.float32)
    mlp_set = (
        lax.all_gather(mlp_gain, "fsdp", axis=0, tiled=True),
        lax.all_gather(w_gate, "fsdp", axis=0, tiled=True),
        lax.all_gather(w_up, "fsdp", axis=0, tiled=True),
        lax.all_gather(w_down, "fsdp", axis=0, tiled=True),
    )
    gain_two, gate_w, up_w, down_w = mlp_set
    normed_two = norm_forward(mixed, gain_two).astype(jnp.bfloat16)
    gate = jnp.dot(normed_two, gate_w, preferred_element_type=jnp.float32)
    up = jnp.dot(normed_two, up_w, preferred_element_type=jnp.float32)
    sigma = jax.nn.sigmoid(gate)
    active = (gate * sigma * up).astype(jnp.bfloat16)
    result = mixed + jnp.dot(active, down_w, preferred_element_type=jnp.float32)
    layer_out = result.astype(jnp.bfloat16)[None]
    grad_low = out_grad[0]
    grad_out = grad_low.astype(jnp.float32)
    gain_back, gate_back, up_back, down_back = (
        lax.all_gather(mlp_gain, "fsdp", axis=0, tiled=True),
        lax.all_gather(w_gate, "fsdp", axis=0, tiled=True),
        lax.all_gather(w_up, "fsdp", axis=0, tiled=True),
        lax.all_gather(w_down, "fsdp", axis=0, tiled=True),
    )
    down_grad = dot_first(active, grad_low)
    active_grad = dot_last(grad_low, down_back)
    gate_grad = (active_grad * up * sigma * (1.0 + gate * (1.0 - sigma))).astype(jnp.bfloat16)
    up_grad = (active_grad * gate * sigma).astype(jnp.bfloat16)
    gate_wgrad = dot_first(normed_two, gate_grad)
    up_wgrad = dot_first(normed_two, up_grad)
    normed_two_grad = dot_last(gate_grad, gate_back) + dot_last(up_grad, up_back)
    mixed_part, gain_two_grad = norm_back(mixed, gain_back, normed_two_grad)
    mixed_grad = grad_out + mixed_part
    mlp_shards = (
        lax.psum_scatter(
            gain_two_grad.astype(jnp.bfloat16), "fsdp", scatter_dimension=0, tiled=True
        ).astype(jnp.float32),
        lax.psum_scatter(
            gate_wgrad.astype(jnp.bfloat16), "fsdp", scatter_dimension=0, tiled=True
        ).astype(jnp.float32),
        lax.psum_scatter(
            up_wgrad.astype(jnp.bfloat16), "fsdp", scatter_dimension=0, tiled=True
        ).astype(jnp.float32),
        lax.psum_scatter(
            down_grad.astype(jnp.bfloat16), "fsdp", scatter_dimension=0, tiled=True
        ).astype(jnp.float32),
    )
    gain_first, query_back, key_back, value_back, out_back = (
        lax.all_gather(attn_gain, "fsdp", axis=0, tiled=True),
        lax.all_gather(w_query, "fsdp", axis=0, tiled=True),
        lax.all_gather(key_projection, "fsdp", axis=0, tiled=True),
        lax.all_gather(value_projection, "fsdp", axis=0, tiled=True),
        lax.all_gather(w_out, "fsdp", axis=0, tiled=True),
    )
    branch_grad = mixed_grad.astype(jnp.bfloat16)
    out_wgrad = dot_first(attended_low, branch_grad)
    attended_grad = (
        dot_last(branch_grad, out_back)
        .astype(jnp.bfloat16)
        .reshape(local_rows, KEY_VALUE_HEADS, query_groups, HEAD_SIZE)
        .transpose(1, 2, 0, 3)
    )
    delta = jnp.sum(attended_grad.astype(jnp.float32) * attended_output, -1)

    def backward_part(carry, part, first):
        query_acc, key_value_acc = carry
        partial_keys, partial_values = part
        block_count = partial_keys.shape[0]
        probs = jnp.exp(masked_scores(partial_keys, first) - log_total[..., None])
        gradient_of_value = jnp.einsum(
            "kgtn,kgtd->nkd",
            probs.astype(jnp.bfloat16),
            attended_grad,
            preferred_element_type=jnp.float32,
        )
        prob_grad = jnp.einsum(
            "kgtd,nkd->kgtn",
            attended_grad,
            partial_values.reshape(block_count, KEY_VALUE_HEADS, HEAD_SIZE),
            preferred_element_type=jnp.float32,
        )
        score_grad = (probs * (prob_grad - delta[..., None])).astype(jnp.bfloat16)
        query_acc = (
            query_acc
            + jnp.einsum(
                "kgtn,nkd->kgtd",
                score_grad,
                partial_keys.reshape(block_count, KEY_VALUE_HEADS, HEAD_SIZE),
                preferred_element_type=jnp.float32,
            )
            * scale
        )
        gradient_of_key = (
            jnp.einsum("kgtn,tkgd->nkd", score_grad, query_rows, preferred_element_type=jnp.float32)
            * scale
        )
        joined = jnp.concatenate(
            [
                gradient_of_key.reshape(block_count, KEY_VALUE_HEADS * HEAD_SIZE),
                gradient_of_value.reshape(block_count, KEY_VALUE_HEADS * HEAD_SIZE),
            ],
            1,
        )
        key_value_acc = lax.dynamic_update_slice_in_dim(key_value_acc, joined, first, 0)
        return (query_acc, key_value_acc)

    back_state = (
        jnp.zeros((KEY_VALUE_HEADS, query_groups, local_rows, HEAD_SIZE), jnp.float32),
        jnp.zeros((sequence_length, 2 * KEY_VALUE_HEADS * HEAD_SIZE), jnp.float32),
    )
    query_acc, key_value_acc = over_blocks(
        backward_part,
        back_state,
        (
            lax.all_gather(keys_flat, "ctx", axis=0, tiled=True),
            lax.all_gather(values_flat, "ctx", axis=0, tiled=True),
        ),
    )
    local_key_value = lax.psum_scatter(
        key_value_acc.astype(jnp.bfloat16), "ctx", scatter_dimension=0, tiled=True
    ).astype(jnp.float32)
    query_raw_grad = (
        rotary_embed_backward(
            query_acc.transpose(2, 0, 1, 3).reshape(local_rows, QUERY_HEADS, HEAD_SIZE),
            cosine_table,
            sine_table,
        )
        .reshape(local_rows, QUERY_HEADS * HEAD_SIZE)
        .astype(jnp.bfloat16)
    )
    key_raw_grad = (
        rotary_embed_backward(
            local_key_value[:, : KEY_VALUE_HEADS * HEAD_SIZE].reshape(
                local_rows, KEY_VALUE_HEADS, HEAD_SIZE
            ),
            cosine_table,
            sine_table,
        )
        .reshape(local_rows, KEY_VALUE_HEADS * HEAD_SIZE)
        .astype(jnp.bfloat16)
    )
    unrotated_value_gradient = local_key_value[:, KEY_VALUE_HEADS * HEAD_SIZE :].astype(
        jnp.bfloat16
    )
    query_wgrad = dot_first(first_normed, query_raw_grad)
    key_wgrad = dot_first(first_normed, key_raw_grad)
    value_wgrad = dot_first(first_normed, unrotated_value_gradient)
    normed_one_grad = (
        dot_last(query_raw_grad, query_back)
        + dot_last(key_raw_grad, key_back)
        + dot_last(unrotated_value_gradient, value_back)
    )
    input_part, gain_one_grad = norm_back(hidden, gain_first, normed_one_grad)
    input_grad = (mixed_grad + input_part).astype(jnp.bfloat16)[None]
    attn_shards = (
        lax.psum_scatter(
            gain_one_grad.astype(jnp.bfloat16), "fsdp", scatter_dimension=0, tiled=True
        ).astype(jnp.float32),
        lax.psum_scatter(
            query_wgrad.astype(jnp.bfloat16), "fsdp", scatter_dimension=0, tiled=True
        ).astype(jnp.float32),
        lax.psum_scatter(
            key_wgrad.astype(jnp.bfloat16), "fsdp", scatter_dimension=0, tiled=True
        ).astype(jnp.float32),
        lax.psum_scatter(
            value_wgrad.astype(jnp.bfloat16), "fsdp", scatter_dimension=0, tiled=True
        ).astype(jnp.float32),
        lax.psum_scatter(
            out_wgrad.astype(jnp.bfloat16), "fsdp", scatter_dimension=0, tiled=True
        ).astype(jnp.float32),
    )
    totals = (
        lax.psum(attn_shards[0].astype(jnp.bfloat16), "ctx").astype(jnp.float32),
        lax.psum(attn_shards[1].astype(jnp.bfloat16), "ctx").astype(jnp.float32),
        lax.psum(attn_shards[2].astype(jnp.bfloat16), "ctx").astype(jnp.float32),
        lax.psum(attn_shards[3].astype(jnp.bfloat16), "ctx").astype(jnp.float32),
        lax.psum(attn_shards[4].astype(jnp.bfloat16), "ctx").astype(jnp.float32),
        lax.psum(mlp_shards[0].astype(jnp.bfloat16), "ctx").astype(jnp.float32),
        lax.psum(mlp_shards[1].astype(jnp.bfloat16), "ctx").astype(jnp.float32),
        lax.psum(mlp_shards[2].astype(jnp.bfloat16), "ctx").astype(jnp.float32),
        lax.psum(mlp_shards[3].astype(jnp.bfloat16), "ctx").astype(jnp.float32),
    )
    return (
        layer_out,
        input_grad,
        totals[0],
        totals[1],
        totals[2],
        totals[3],
        totals[4],
        totals[5],
        totals[6],
        totals[7],
        totals[8],
    )


MESH = pl.DeviceIdType.MESH
ANY = pl.ANY
VMEM = pltpu.VMEM
DMA = pltpu.SemaphoreType.DMA
LANES = 128
BLOCK = 128
F32 = jnp.float32
BF16 = jnp.bfloat16
VMEM_BYTES = 60 * 2**20


def flip(c, k):
    out = c
    for b in (1, 2, 4):
        if k & b:
            out = out + b - 2 * b * ((c // b) % 2)
    return out


def remote(src, dst, send, recv, **to):
    return pltpu.make_async_remote_copy(
        src_ref=src, dst_ref=dst, send_sem=send, recv_sem=recv, device_id=to, device_id_type=MESH
    )


def greet(peers):
    barrier = pltpu.get_barrier_semaphore()
    for peer in peers:
        pl.semaphore_signal(barrier, inc=1, device_id=peer, device_id_type=MESH)
    pl.semaphore_wait(barrier, len(peers))


class Gather:
    def __init__(self, c, own, buf, at, send, recv):
        self.c, self.own, self.buf, self.at, self.send, self.recv = c, own, buf, at, send, recv
        self.pending = []

    def start(self, channel, who, to, h, own=False):
        there = self.at(self.buf, flip(self.c, who), h)
        d = remote(
            self.own(h) if own else there,
            there,
            self.send.at[channel, h],
            self.recv.at[channel, h],
            ctx=flip(self.c, to),
        )
        d.start()
        self.pending.append(d)

    def arrived(self, channel, who, frm, h):
        ref = self.at(self.buf, flip(self.c, who), h)
        remote(
            ref, ref, self.send.at[channel, h], self.recv.at[channel, h], ctx=flip(self.c, frm)
        ).wait_recv()

    def begin(self):
        self.begin_half()
        self.begin_rest()

    def begin_half(self):
        self.start(1, 0, 2, 0, own=True)
        self.start(2, 0, 4, 1, own=True)

    def begin_rest(self):
        self.start(1, 0, 2, 1, own=True)
        self.start(2, 0, 4, 0, own=True)
        self.start(0, 0, 1, 0, own=True)
        self.start(0, 0, 1, 1, own=True)

    def near_half(self):
        self.arrived(1, 2, 2, 0)
        self.start(6, 2, 4, 0)
        self.start(3, 2, 1, 0)
        self.arrived(2, 4, 4, 1)
        self.start(7, 4, 2, 1)
        self.start(4, 4, 1, 1)

    def near_rest(self):
        self.arrived(1, 2, 2, 1)
        self.start(3, 2, 1, 1)
        self.arrived(2, 4, 4, 0)
        self.start(4, 4, 1, 0)

    def far(self):
        self.arrived(6, 6, 4, 0)
        self.start(5, 6, 1, 0)
        self.arrived(7, 6, 2, 1)
        self.start(5, 6, 1, 1)

    def paired(self, channel, who):
        for h in (0, 1):
            self.arrived(channel, who, 1, h)

    def finish(self):
        self.near_half()
        self.near_rest()
        self.far()
        for channel, who in ((0, 1), (3, 3), (4, 5), (5, 7)):
            self.paired(channel, who)

    def sent(self):
        for d in self.pending:
            d.wait_send()


def row_half(ref, d, h):
    half = ref.shape[1] // 2
    return ref.at[d, pl.ds(h * half, half)]


def column_half(ref, d, h):
    half = ref.shape[2] // 2
    return ref.at[d, :, pl.ds(h * half, half)]


def own_half(ref, axis=0):
    half = ref.shape[axis] // 2
    return lambda h: ref.at[(slice(None),) * axis + (pl.ds(h * half, half),)]


class Line:
    def __init__(self, z, depth, at, send, recv, own=None):
        self.z, self.depth, self.at, self.send, self.recv, self.own = z, depth, at, send, recv, own

    def copy(self, way, k, part, to):
        ref = self.at(part)
        source = ref if k or self.own is None else self.own
        return remote(source, ref, self.send.at[way, k], self.recv.at[way, k], fsdp=to)

    def step(self, k):
        z, top = self.z, self.depth - 1

        @pl.when((z >= k) & (z < top))
        def _():
            self.copy(0, k, z - k, z + 1).start()

        @pl.when((z + k <= top) & (z > 0))
        def _():
            self.copy(1, k, z + k, z - 1).start()

    def landed(self, k):
        z, top = self.z, self.depth - 1

        @pl.when(z >= k + 1)
        def _():
            self.copy(0, k, z - 1 - k, z - 1).wait_recv()

        @pl.when(z + 1 + k <= top)
        def _():
            self.copy(1, k, z + 1 + k, z + 1).wait_recv()

    def sent(self, steps):
        z, top = self.z, self.depth - 1
        for k in steps:

            @pl.when((z >= k) & (z < top))
            def _():
                self.copy(0, k, z - k, z + 1).wait_send()

            @pl.when((z + k <= top) & (z > 0))
            def _():
                self.copy(1, k, z + k, z - 1).wait_send()


def params(cid):
    return pltpu.CompilerParams(
        collective_id=cid, has_side_effects=True, vmem_limit_bytes=VMEM_BYTES
    )


def contract(a, b, dims):
    return lax.dot_general(a, b, ((dims[0], dims[1]), ((), ())), preferred_element_type=F32)


def lanes(start, size):
    return pl.ds(pl.multiple_of(start, LANES), size)


def turned(u, cosine, sine):
    half = HEAD_SIZE // 2
    a, b = u[:half], u[half:]
    return jnp.concatenate([a * cosine - b * sine, b * cosine + a * sine], 0)


def picked(weight, first, count):
    shape = (count, weight.shape[1])
    hit = lax.broadcasted_iota(jnp.int32, shape, 1) == first + lax.broadcasted_iota(jnp.int32, shape, 0)
    return contract(hit.astype(BF16), weight, ((1,), (1,))).astype(BF16)


CHUNK = 512


def two_heads(ref, block):
    return jnp.concatenate([ref[block, :HEAD_SIZE], ref[block, HEAD_SIZE : 2 * HEAD_SIZE]], 1)


def causal(s, t, j):
    key = t * CHUNK + lax.broadcasted_iota(jnp.int32, s.shape, 0)
    query = j * BLOCK + lax.broadcasted_iota(jnp.int32, s.shape, 1) % BLOCK
    return jnp.where(key <= query, s, -jnp.inf)


def first_kernel(
    pos_ref, x_ref, gain_one_ref, gain_two_ref, freq_ref, step_ref, wq_ref, wk_ref, wv_ref, wo_ref, wg_ref, wu_ref, wd_ref, grad_ref,
    all_ref, qkv_ref, w_ref, table_ref, gains_ref, order_ref, rank_ref, low_ref, lse_ref, ow_all, gu_all, down_all, grad_all,
    infos_ref, infos, wo_all, keys, values, xs, wz, whole, gu_own, out_mine, down_mine, grad_mine, bases, gain_ref, info_ref, base_ref, gsend, grecv, isend, irecv, bsend, brecv, send, recv, zsend, zrecv, osend, orecv,
    usend, urecv, dsend, drecv, send2, recv2, send3, recv3, local, parts,
):
    c = lax.axis_index("ctx")
    z = lax.axis_index("fsdp")
    depth = gains_ref.shape[0]
    shard, width = wq_ref.shape
    rows = x_ref.shape[0]
    strip = gu_all.shape[2] // 2 // depth
    down_rows = down_all.shape[1]
    others = [lax.rem(z + k, depth) for k in range(1, depth)]
    lane = lax.broadcasted_iota(jnp.int32, info_ref.shape, 1)
    info_ref[...] = jnp.where(lane < LANES // 2, pos_ref[0, 0], pos_ref[0, BLOCK])
    start = freq_ref[...] * info_ref[:1].astype(F32)
    base_ref[...] = jnp.where(lane[:1] // (LANES // 4) % 2 == 0, jnp.cos(start), jnp.sin(start))
    gain_ref[:4] = jnp.broadcast_to(gain_one_ref[...].astype(F32), (4, shard))
    gain_ref[4:] = jnp.broadcast_to(gain_two_ref[...].astype(F32), (4, shard))
    greet([{"ctx": flip(c, k)} for k in range(1, 8)] + [{"fsdp": o} for o in others])

    g2 = Gather(c, own_half(grad_ref), grad_all, row_half, send2, recv2)
    g2.begin_half()
    sent = []
    for k, o in enumerate(others):
        sent.append(remote(gain_ref, gains_ref.at[z], gsend.at[k], grecv.at[k], fsdp=o))
    for k in range(1, 8):
        sent.append(remote(info_ref, infos_ref.at[c], isend.at[k], irecv.at[k], ctx=flip(c, k)))
        sent.append(remote(base_ref, bases.at[c], bsend.at[k], brecv.at[k], ctx=flip(c, k)))
    for d in sent:
        d.start()
    out_rows = shard // 8
    out_own = wo_ref.at[pl.ds(c * out_rows, out_rows)]
    down_own = wd_ref.at[pl.ds(c * down_rows, down_rows)]
    strips = [
        pltpu.make_async_copy(weight, whole.at[i], parts.at[4 + i]) for i, weight in enumerate((wg_ref, wu_ref))
    ]
    for d in strips:
        d.start()
    ways = ((out_own, out_mine, ow_all.at[z, c]), (down_own, down_mine, down_all.at[z]), (grad_ref, grad_mine, grad_all.at[c]))
    incoming = [pltpu.make_async_copy(a, b, parts.at[i]) for i, (a, b, _) in enumerate(ways)]
    for d in incoming:
        d.start()
    gains_ref[z] = gain_ref[...]
    infos_ref[c] = info_ref[...]
    bases[c] = base_ref[...]

    count = 2 * HEAD_SIZE
    wz[z, :count] = picked(wq_ref[...], c * count, count)
    wz[z, count : count + HEAD_SIZE] = picked(wk_ref[...], c * HEAD_SIZE, HEAD_SIZE)
    wz[z, count + HEAD_SIZE :] = picked(wv_ref[...], c * HEAD_SIZE, HEAD_SIZE)
    line = Line(z, depth, lambda d: wz.at[d], zsend, zrecv)
    line.step(0)

    x = x_ref[...].astype(F32)
    factor = lax.rsqrt(jnp.mean(x * x, -1, keepdims=True) + EPS)
    for k in range(depth - 1):
        ref = gains_ref.at[lax.rem(z + depth - 1 - k, depth)]
        remote(ref, ref, gsend.at[k], grecv.at[k], fsdp=others[k]).wait_recv()
    gain = jnp.concatenate([gains_ref[k, 0:1, :] for k in range(depth)], 1)
    xs[c] = (x * factor * gain).astype(BF16)
    g = Gather(c, own_half(xs.at[c]), xs, row_half, send, recv)
    g.begin()
    out_line = Line(z, depth, lambda d: wo_all.at[d], osend, orecv, out_own)
    down_line = Line(z, depth, lambda d: down_all.at[d], dsend, drecv, down_own)
    out_line.step(0)
    copies = []
    for i, (_, b, there) in enumerate(ways):
        incoming[i].wait()
        copies.append(pltpu.make_async_copy(b, there, parts.at[i]))
        copies[-1].start()
    wo_all[z] = out_mine[...]

    def keep(k):
        d = pltpu.make_async_copy(xs.at[flip(c, k)], all_ref.at[flip(c, k)], local.at[k])
        d.start()
        copies.append(d)

    keep(0)

    def rotary(k):
        d = flip(c, k)
        if k:
            for ref, s, r in ((bases, bsend, brecv), (infos_ref, isend, irecv)):
                remote(ref.at[d], ref.at[d], s.at[k], r.at[k], ctx=d).wait_recv()
        half = HEAD_SIZE // 2
        step_cos, step_sin = step_ref[:half], step_ref[half:]
        for b in (0, 1):
            start = b * (LANES // 2)
            base_cos = bases[d, :, start : start + 1]
            base_sin = bases[d, :, start + LANES // 4 : start + LANES // 4 + 1]
            table_ref[2 * d + b, :half] = base_cos * step_cos - base_sin * step_sin
            table_ref[2 * d + b, half:] = base_sin * step_cos + base_cos * step_sin

    for k in range(8):
        rotary(k)

    def project(k):
        d = flip(c, k)
        half = HEAD_SIZE // 2
        raw = contract(w_ref[...], xs[d], ((1,), (1,)))
        for b in (0, 1):
            cosine, sine = table_ref[2 * d + b, :half], table_ref[2 * d + b, half:]
            part = raw[:, b * BLOCK : (b + 1) * BLOCK]
            for h in range(3):
                head = slice(h * HEAD_SIZE, (h + 1) * HEAD_SIZE)
                qkv_ref[2 * d + b, head] = turned(part[head], cosine, sine).astype(BF16)
            qkv_ref[2 * d + b, 3 * HEAD_SIZE :] = part[3 * HEAD_SIZE :].astype(BF16)

    line.landed(0)
    line.step(1)
    g.near_half()
    g2.begin_rest()
    out_line.landed(0)
    out_line.step(1)
    line.landed(1)
    line.step(2)
    g.near_rest()
    keep(2)
    keep(4)
    out_line.landed(1)
    out_line.step(2)
    for i, d in enumerate(strips):
        d.wait()
        for f in range(depth):
            gu_own[:, (i * depth + f) * strip : (i * depth + f + 1) * strip] = whole[i, :, lanes((f * 8 + c) * strip, strip)]
    gu_line = Line(z, depth, lambda d: gu_all.at[d], usend, urecv, gu_own)
    gu_line.step(0)
    copies.append(pltpu.make_async_copy(gu_own, gu_all.at[z], parts.at[3]))
    copies[-1].start()
    line.landed(2)
    for f in range(depth):
        w_ref[:, f * shard : (f + 1) * shard] = wz[f]
    g.far()
    g2.near_half()
    project(0)
    project(2)
    project(4)
    for channel, k in ((0, 1), (3, 3), (4, 5)):
        g.paired(channel, k)
        keep(k)
        project(k)
    keep(6)
    project(6)
    g.paired(5, 7)
    keep(7)
    project(7)
    out_line.landed(2)
    few = depth // 2
    g3 = Gather(
        c,
        lambda h: wo_all.at[pl.ds(h * few, few)],
        ow_all,
        lambda ref, d, h: ref.at[pl.ds(h * few, few), d],
        send3,
        recv3,
    )
    for f in range(1, depth):
        part = lax.rem(z + f, depth)
        copies.append(pltpu.make_async_copy(wo_all.at[part], ow_all.at[part, c], parts.at[4 + f]))
        copies[-1].start()

    blocks = qkv_ref.shape[0]
    per = CHUNK // BLOCK
    factor = HEAD_SIZE ** (-0.5) * math.log2(math.e)
    small = pltpu.make_async_copy(infos_ref, infos, parts.at[8])
    small.start()
    small.wait()
    starts = [infos[b // 2, 0, b % 2 * (LANES // 2)] for b in range(blocks)]
    least = functools.reduce(jnp.minimum, starts)
    ranks = [(start - least) // BLOCK for start in starts]
    for i in range(blocks):
        rank_ref[i] = ranks[i]
        order_ref[i] = functools.reduce(jnp.maximum, [jnp.where(ranks[b] == i, b, 0) for b in range(blocks)])
    for b in range(blocks):
        there = slice(b * BLOCK, (b + 1) * BLOCK)
        keys[there, :] = qkv_ref[order_ref[b], 2 * HEAD_SIZE : 3 * HEAD_SIZE].T
        values[:, there] = qkv_ref[order_ref[b], 3 * HEAD_SIZE :]

    def attend_block(j, last):
        q = two_heads(qkv_ref, order_ref[j])

        def step(t, carry, masked):
            top, denom, acc = carry
            s = jnp.dot(keys[pl.ds(t * CHUNK, CHUNK), :], q, preferred_element_type=F32)
            if masked:
                s = causal(s, t, j)
            new_top = jnp.maximum(top, jnp.max(s, 0, keepdims=True))
            p = jnp.exp2((s - new_top) * factor)
            shrink = jnp.exp2((top - new_top) * factor)
            denom = denom * shrink + jnp.sum(p, 0, keepdims=True)
            acc = acc * shrink + jnp.dot(
                values[:, pl.ds(t * CHUNK, CHUNK)], p.astype(BF16), preferred_element_type=F32
            )
            return new_top, denom, acc

        carry = (
            jnp.full((1, 2 * BLOCK), -1e30, F32),
            jnp.zeros((1, 2 * BLOCK), F32),
            jnp.zeros((HEAD_SIZE, 2 * BLOCK), F32),
        )
        for t in range(last):
            carry = step(t, carry, False)
        top, denom, acc = step(last, carry, True)
        out = acc / denom
        lse_ref[pl.ds(j, 1), :, :] = (top * factor + jnp.log2(denom)).reshape(1, 1, 2 * BLOCK)
        for h in (0, 1):
            head = slice(h * HEAD_SIZE, (h + 1) * HEAD_SIZE)
            low_ref[j, head] = out[:, h * BLOCK : (h + 1) * BLOCK].astype(BF16)

    def attend_blocks(first, count):
        @pl.loop(first, first + count)
        def _(j):
            attend_block(j, first // per)

    attend_blocks(0, per)
    g2.near_rest()
    g3.begin()
    attend_blocks(per, per)
    gu_line.landed(0)
    gu_line.step(1)
    down_line.step(0)
    attend_blocks(2 * per, per // 2)
    g2.far()
    attend_blocks(2 * per + per // 2, per // 2)
    g3.near_half()
    attend_blocks(3 * per, per // 2)
    g3.near_rest()
    attend_blocks(3 * per + per // 2, per // 2)
    g3.far()
    for gather in (g2, g3):
        for channel, k in ((0, 1), (3, 3), (4, 5), (5, 7)):
            gather.paired(channel, k)
    gu_line.landed(1)
    down_line.landed(0)
    for d in copies:
        d.wait()
    for d in sent:
        d.wait_send()
    line.sent((0, 1, 2))
    out_line.sent((0, 1, 2))
    gu_line.sent((0, 1))
    down_line.sent((0,))
    for gather in (g, g2, g3):
        gather.sent()


def first_part(positions, x, gains, freq, step, weights, grad, depth, cid):
    rows, width = x.shape
    shard = gains[0].shape[1]
    small = (8, shard)
    columns = weights[4].shape[1]
    down_rows = weights[6].shape[0] // 8
    blocks = 8 * rows // BLOCK
    sm = pl.BlockSpec(memory_space=pltpu.SMEM)
    vm = pl.BlockSpec(memory_space=VMEM)
    hbm = pl.BlockSpec(memory_space=ANY)
    shape = jax.ShapeDtypeStruct
    return pl.pallas_call(
        first_kernel,
        out_shape=(
            shape((8, rows, width), BF16),
            shape((8 * rows // BLOCK, 4 * HEAD_SIZE, BLOCK), BF16),
            shape((4 * HEAD_SIZE, width), BF16),
            shape((8 * rows // BLOCK, HEAD_SIZE, BLOCK), F32),
            shape((depth,) + small, F32),
            shape((blocks,), jnp.int32),
            shape((blocks,), jnp.int32),
            shape((blocks, 2 * HEAD_SIZE, BLOCK), BF16),
            shape((blocks, 1, 2 * BLOCK), F32),
            shape((depth, 8, shard // 8, width), BF16),
            shape((depth, shard, 2 * columns // 8), BF16),
            shape((depth, down_rows, width), BF16),
            shape((8, rows, width), BF16),
        ),
        in_specs=[pl.BlockSpec(memory_space=pltpu.SMEM)] + [vm] * 8 + [hbm] * 5,
        out_specs=(hbm, vm, vm, vm, vm, sm, sm, vm, vm, hbm, hbm, hbm, hbm),
        scratch_shapes=[
            VMEM((8, 8, LANES), jnp.int32),
            pltpu.SMEM((8, 8, LANES), jnp.int32),
            VMEM((depth, shard // 8, width), BF16),
            VMEM((8 * rows, HEAD_SIZE), BF16),
            VMEM((HEAD_SIZE, 8 * rows), BF16),
            VMEM((8, rows, width), BF16),
            VMEM((depth, 4 * HEAD_SIZE, shard), BF16),
            VMEM((2, shard, columns), BF16),
            VMEM((shard, 2 * columns // 8), BF16),
            VMEM((shard // 8, width), BF16),
            VMEM((down_rows, width), BF16),
            VMEM((rows, width), BF16),
            VMEM((8, HEAD_SIZE // 2, LANES), F32),
            VMEM(small, F32),
            VMEM((8, LANES), jnp.int32),
            VMEM((HEAD_SIZE // 2, LANES), F32),
            DMA((depth,)),
            DMA((depth,)),
            DMA((8,)),
            DMA((8,)),
            DMA((8,)),
            DMA((8,)),
            DMA((8, 2)),
            DMA((8, 2)),
        ]
        + [DMA((2, depth))] * 8
        + [DMA((8, 2))] * 4
        + [DMA((8,)), DMA((9,))],
        compiler_params=params(cid),
        name="first_part",
    )(positions, x, *gains, freq, step, *weights, grad)


class Scatter:
    ORDER = (6, 2, 4, 0)

    def __init__(self, c, p, first, last, diagonal, s1, v1, s2, v2):
        self.c, self.p, self.first = c, p, first
        self.last, self.diagonal = last, diagonal
        self.s1, self.v1, self.s2, self.v2 = s1, v1, s2, v2
        self.half = first.shape[1] // 2 if p is None else p.shape[1] // 2
        self.pending = []
        self.summed = False

    @staticmethod
    def scratch(rows, width):
        return [
            VMEM((4, rows, width), BF16),
            VMEM((2, rows, width), BF16),
            VMEM((rows, width), BF16),
            DMA((4, 2)),
            DMA((4, 2)),
            DMA((3, 2)),
            DMA((3, 2)),
        ]

    def sl(self, q):
        return pl.ds(q * self.half, self.half)

    def go(self, d):
        d.start()
        self.pending.append(d)

    def give(self, k):
        j = self.ORDER.index(k)
        for q in (0, 1):
            source = self.p.at[flip(self.c, 1 ^ k), self.sl(q)]
            there = self.first.at[j, self.sl(q)]
            self.go(remote(source, there, self.s1.at[j, q], self.v1.at[j, q], ctx=flip(self.c, 1)))

    def paired(self, j, q):
        if self.summed:
            return
        ref = self.first.at[j, self.sl(q)]
        remote(ref, ref, self.s1.at[j, q], self.v1.at[j, q], ctx=flip(self.c, 1)).wait_recv()

    def chip(self, j, q):
        if self.summed:
            return self.first[j, self.sl(q)].astype(F32)
        k = self.ORDER[j]
        return self.p[flip(self.c, k), self.sl(q)].astype(F32) + self.first[j, self.sl(q)].astype(F32)

    def came(self, channel, ref, q, frm):
        remote(
            ref, ref, self.s2.at[channel, q], self.v2.at[channel, q], ctx=flip(self.c, frm)
        ).wait_recv()

    def far(self):
        for q, to in ((0, 2), (1, 4)):
            self.paired(0, q)
            self.first[0, self.sl(q)] = self.chip(0, q).astype(BF16)
            self.go(
                remote(
                    self.first.at[0, self.sl(q)],
                    self.diagonal.at[self.sl(q)],
                    self.s2.at[2, q],
                    self.v2.at[2, q],
                    ctx=flip(self.c, to),
                )
            )

    def onward(self, j, q, merged):
        v = self.chip(j, q)
        if merged:
            v = v + self.diagonal[self.sl(q)].astype(F32)
        self.first[j, self.sl(q)] = v.astype(BF16)
        self.go(
            remote(
                self.first.at[j, self.sl(q)],
                self.last.at[j - 1, self.sl(q)],
                self.s2.at[j - 1, q],
                self.v2.at[j - 1, q],
                ctx=flip(self.c, self.ORDER[j]),
            )
        )

    def direct(self):
        self.paired(1, 0)
        self.onward(1, 0, False)
        self.paired(2, 1)
        self.onward(2, 1, False)

    def merged(self):
        self.paired(2, 0)
        self.came(2, self.diagonal.at[self.sl(0)], 0, 2)
        self.onward(2, 0, True)
        self.paired(1, 1)
        self.came(2, self.diagonal.at[self.sl(1)], 1, 4)
        self.onward(1, 1, True)

    def settle(self):
        for j in range(len(self.ORDER)):
            for q in (0, 1):
                self.paired(j, q)
                self.first[j, self.sl(q)] = self.chip(j, q).astype(BF16)
        self.summed = True

    def result(self, q):
        self.paired(3, q)
        self.came(0, self.last.at[0, self.sl(q)], q, 2)
        self.came(1, self.last.at[1, self.sl(q)], q, 4)
        return self.chip(3, q) + (
            self.last[0, self.sl(q)].astype(F32) + self.last[1, self.sl(q)].astype(F32)
        )

    def sent(self):
        for d in self.pending:
            d.wait_send()


def exchange_start(c, source, target, send, recv):
    sent = []
    for k in (6, 7, 2, 4, 3, 5, 1):
        there = target.at[pl.ds(2 * c, 2)]
        d = remote(source.at[pl.ds(2 * flip(c, k), 2)], there, send.at[k], recv.at[k], ctx=flip(c, k))
        d.start()
        sent.append(d)
    return sent


def exchange_landed(c, target, send, recv):
    for k in (6, 7, 2, 4, 3, 5, 1):
        ref = target.at[pl.ds(2 * flip(c, k), 2)]
        remote(ref, ref, send.at[k], recv.at[k], ctx=flip(c, k)).wait_recv()


def both_blocks(ref, i):
    return jnp.concatenate([ref[2 * i], ref[2 * i + 1]], 1)


def middle_kernel(
    rank_ref, low_ref, x_ref, gains_ref, g_ref, ow_ref, gu_in, down_in,
    mixed_out, sums_ref, mgrad_ref, gsum_ref, do_ref, owg_ref, gug_ref, dg_ref, left_ref, right_ref, gu_all, down_all,
    mixed_ref, p1, wgu, wd, grads, two, p2, act, dgu, give, got, *rest,
):
    scatter_refs, layer_refs = rest[:7], rest[7:10]
    esend, erecv, fsend, frecv, send, recv, usend, urecv, dsend, drecv, load, wput, hsend, hrecv = rest[10:]
    c = lax.axis_index("ctx")
    z = lax.axis_index("fsdp")
    depth, shard, both = gu_all.shape
    mine = both // 2
    rows, width = x_ref.shape
    out_rows = ow_ref.shape[1]
    out_w = p1.at[:, pl.ds(0, out_rows)]
    others = [lax.rem(z + k, depth) for k in range(1, depth)]
    greet([{"ctx": flip(c, k)} for k in range(1, 8)] + [{"fsdp": o} for o in others])
    gu_line = Line(z, depth, lambda d: gu_all.at[d], usend, urecv)
    down_line = Line(z, depth, lambda d: down_all.at[d], dsend, drecv)
    gu_line.step(2)
    down_line.step(1)
    loads = [
        pltpu.make_async_copy(ow_ref, out_w, load.at[0]),
        pltpu.make_async_copy(g_ref, grads, load.at[1]),
        pltpu.make_async_copy(x_ref, two.at[c], load.at[2]),
    ]
    for d in loads:
        d.start()

    for i in range(rank_ref.shape[0]):
        give[i] = low_ref[rank_ref[i]]
    sent = exchange_start(c, give, got, esend, erecv)
    got[pl.ds(2 * c, 2)] = give[pl.ds(2 * c, 2)]
    loads[0].wait()
    loads[2].wait()
    exchange_landed(c, got, esend, erecv)
    mixed_ref[...] = two[c].astype(F32)

    @pl.loop(0, 8)
    def _(i):
        mixed_ref[...] += contract(both_blocks(got, i), p1[i, :out_rows], ((0,), (0,)))

    gain = jnp.concatenate([gains_ref[k, 4:5, :] for k in range(depth)], 1)
    halves = [pl.ds(q * (rows // 2), rows // 2) for q in (0, 1)]
    for at in halves:
        x = mixed_ref[at]
        factor = lax.rsqrt(jnp.mean(x * x, -1, keepdims=True) + EPS)
        two[c, at] = (x * factor * gain).astype(BF16)
    g = Gather(c, own_half(two.at[c]), two, row_half, send, recv)
    g.begin()
    loads[1].wait()
    gu_line.landed(2)
    weights = [pltpu.make_async_copy(gu_all, wgu, load.at[2])]
    weights[0].start()
    down_line.landed(1)
    down_line.step(2)

    def block(d):
        up_w = wgu[...].reshape(width, both)
        down_w = wd[...].reshape(mine, width)
        gate_up = jnp.dot(two[d], up_w, preferred_element_type=F32)
        gate, up = gate_up[:, :mine], gate_up[:, mine:]
        sigma = jax.nn.sigmoid(gate)
        silu = gate * sigma
        active = (silu * up).astype(BF16)
        act[d] = active
        active_grad = contract(grads[d], down_w, ((1,), (1,)))
        gate_grad = active_grad * up * sigma * (1.0 + gate * (1.0 - sigma))
        up_grad = active_grad * silu
        grad = jnp.concatenate([gate_grad, up_grad], 1).astype(BF16)
        dgu[d] = grad
        p2[d] = contract(grad, up_w, ((1,), (1,))).astype(BF16)
        p1[d] = jnp.dot(active, down_w, preferred_element_type=F32).astype(BF16)

    def pair(k):
        d = flip(c, k)
        other = flip(c, 1 ^ k)

        @pl.loop(0, 2)
        def _(i):
            block(other + i * (d - other))

        scatter.give(k)

    scatter = Scatter(c, p2, *scatter_refs)
    layer = Scatter(c, p1, layer_refs[0], None, None, *layer_refs[1:], None, None)
    g.near_half()
    g.near_rest()
    down_line.landed(2)
    weights.append(pltpu.make_async_copy(down_all, wd, load.at[3]))
    weights[1].start()
    for d in weights:
        d.wait()
    g.paired(0, 1)
    pair(0)
    g.paired(3, 3)
    pair(2)
    g.far()
    g.paired(5, 7)
    pair(6)
    g.paired(4, 5)
    scatter.far()
    pair(4)
    scatter.direct()
    for k in Scatter.ORDER:
        layer.give(k)

    puts = []

    def wide(f):
        part = lambda i, total: total + contract(
            two[pl.ds(2 * i, 2), :, f * shard : (f + 1) * shard].reshape(2 * rows, shard),
            dgu[pl.ds(2 * i, 2)].reshape(2 * rows, both),
            ((0,), (0,)),
        )
        wgu[f] = lax.fori_loop(0, 4, part, jnp.zeros((shard, both), F32)).astype(BF16)
        puts.append(pltpu.make_async_copy(wgu.at[f], gug_ref.at[f], wput.at[f]))
        puts[-1].start()

    wide(0)
    scatter.merged()
    layer.settle()
    keeps = [
        pltpu.make_async_copy(layer.first, sums_ref, load.at[1]),
        pltpu.make_async_copy(mixed_ref, mixed_out, load.at[2]),
    ]
    for d in keeps:
        d.start()
    layer.sent()
    again = pltpu.make_async_copy(ow_ref, out_w, load.at[0])
    again.start()
    for f in range(1, depth):
        wide(f)

    hop_right = remote(wgu.at[depth - 1], left_ref, hsend.at[0], hrecv.at[0], fsdp=z + 1)
    hop_left = remote(wgu.at[0], right_ref, hsend.at[1], hrecv.at[1], fsdp=z - 1)

    @pl.when(z == 0)
    def _():
        hop_right.start()

    @pl.when(z == depth - 1)
    def _():
        hop_left.start()

    strip = mine // depth
    for f in range(0, depth, 2):
        part = lambda i, total: total + contract(
            act[pl.ds(2 * i, 2), :, f * strip : (f + 2) * strip].reshape(2 * rows, 2 * strip),
            grads[pl.ds(2 * i, 2)].reshape(2 * rows, width),
            ((0,), (0,)),
        )
        part = lax.fori_loop(0, 4, part, jnp.zeros((2 * strip, width), F32))
        wd[f : f + 2] = part.astype(BF16).reshape(2, strip, width)
    puts.append(pltpu.make_async_copy(wd, dg_ref, wput.at[depth]))
    puts[-1].start()

    g.sent()
    gain_sum = jnp.zeros((1, width), F32)
    for q, at in enumerate(halves):
        two_grad = scatter.result(q)
        x = mixed_ref[at]
        factor = lax.rsqrt(jnp.mean(x * x, -1, keepdims=True) + EPS)
        gain_sum = gain_sum + jnp.sum(two_grad * x * factor, 0, keepdims=True)
        scaled = two_grad * gain
        mixed_grad = (
            grads[c, at].astype(F32)
            + factor * scaled
            - x * (factor * factor * factor) * jnp.mean(scaled * x, -1, keepdims=True)
        )
        mgrad_ref[at] = mixed_grad
        two[0, at] = mixed_grad.astype(BF16)
    gsum_ref[...] = jnp.broadcast_to(gain_sum, gsum_ref.shape)
    for d in sent:
        d.wait_send()
    again.wait()
    for i in range(8):
        part = contract(p1[i, :out_rows], two[0], ((1,), (1,))).astype(BF16)
        give[2 * i] = part[:, :BLOCK]
        give[2 * i + 1] = part[:, BLOCK:]
    sent = exchange_start(c, give, do_ref, fsend, frecv)
    do_ref[pl.ds(2 * c, 2)] = give[pl.ds(2 * c, 2)]
    few = out_rows // depth
    for i in range(8):
        part = jnp.dot(both_blocks(got, i), two[0], preferred_element_type=F32).astype(BF16)
        f = i * depth // 8
        for t in range(depth):
            p1[i * depth % 8 + t, f * few : (f + 1) * few] = part[t * few : (t + 1) * few]
    out_put = pltpu.make_async_copy(out_w, owg_ref, load.at[0])
    out_put.start()
    exchange_landed(c, do_ref, fsend, frecv)
    scatter.sent()

    @pl.when(z == 0)
    def _():
        hop_right.wait_send()

    @pl.when(z == depth - 1)
    def _():
        hop_left.wait_send()

    @pl.when(z == 1)
    def _():
        remote(left_ref, left_ref, hsend.at[0], hrecv.at[0], fsdp=z - 1).wait_recv()

    @pl.when(z == depth - 2)
    def _():
        remote(right_ref, right_ref, hsend.at[1], hrecv.at[1], fsdp=z + 1).wait_recv()

    out_put.wait()
    for d in puts:
        d.wait()
    for d in keeps:
        d.wait()
    for d in sent:
        d.wait_send()
    gu_line.sent((2,))
    down_line.sent((1, 2))


def middle(rank, low, x, gains, grad_all, out_w, gate_up, down, cid):
    rows, width = x.shape
    depth, shard, both = gate_up.shape
    shape = jax.ShapeDtypeStruct
    vm = pl.BlockSpec(memory_space=VMEM)
    hbm = pl.BlockSpec(memory_space=ANY)
    heads = (8 * rows // BLOCK, 2 * HEAD_SIZE, BLOCK)
    block = (8, rows, width)
    return pl.pallas_call(
        middle_kernel,
        out_shape=(
            shape((rows, width), F32),
            shape((4, rows, width), BF16),
            shape((rows, width), F32),
            shape((8, width), F32),
            shape(heads, BF16),
            shape(out_w.shape, BF16),
            shape(gate_up.shape, BF16),
            shape(down.shape, BF16),
            shape((shard, both), BF16),
            shape((shard, both), BF16),
            shape(gate_up.shape, BF16),
            shape(down.shape, BF16),
        ),
        in_specs=[pl.BlockSpec(memory_space=pltpu.SMEM), vm, hbm, vm, hbm, hbm, hbm, hbm],
        out_specs=(hbm, hbm, vm, vm, vm, hbm, hbm, hbm, hbm, hbm, hbm, hbm),
        scratch_shapes=[
            VMEM((rows, width), F32),
            VMEM(block, BF16),
            VMEM(gate_up.shape, BF16),
            VMEM(down.shape, BF16),
            VMEM(block, BF16),
            VMEM(block, BF16),
            VMEM(block, BF16),
            VMEM((8, rows, both // 2), BF16),
            VMEM((8, rows, both), BF16),
            VMEM(heads, BF16),
            VMEM(heads, BF16),
        ]
        + Scatter.scratch(rows, width)
        + [VMEM((4, rows, width), BF16), DMA((4, 2)), DMA((4, 2))]
        + [DMA((8,))] * 4
        + [DMA((8, 2))] * 2
        + [DMA((2, depth))] * 4
        + [DMA((4,)), DMA((depth + 1,)), DMA((2,)), DMA((2,))],
        input_output_aliases={6: 10, 7: 11},
        compiler_params=params(cid),
        name="middle",
    )(rank, low, x, gains, grad_all, out_w, gate_up, down)


class LineScatter:
    def __init__(self, z, own, left, right, send, recv):
        self.z, self.own, self.left, self.right = z, own, left, right
        self.send, self.recv = send, recv
        self.top = own.shape[0] - 1
        self.begun = None

    @staticmethod
    def scratch(shape):
        depth = shape[0]
        hops = (depth - 1,) + tuple(shape[1:])
        return [VMEM(hops, BF16), VMEM(hops, BF16), DMA((2, depth)), DMA((2, depth))]

    def copy(self, way, s, part, to):
        there = (self.left, self.right)[way].at[s]
        return remote(self.own.at[part], there, self.send.at[way, s], self.recv.at[way, s], fsdp=to)

    def landed(self, way, s):
        if s == 0 and self.begun:
            self.begun[way].wait()
            return
        ref = (self.left, self.right)[way].at[s]
        remote(ref, ref, self.send.at[way, s], self.recv.at[way, s], fsdp=self.z - 1 + 2 * way).wait_recv()

    def step(self, s):
        z, top = self.z, self.top
        for way in (0, 1):
            place = z if way == 0 else top - z
            part = top - s + z if way == 0 else s - top + z

            @pl.when((place <= s) & (place < top))
            def _():
                if s:

                    @pl.when(place > 0)
                    def _():
                        self.landed(way, s - 1)
                        came = (self.left, self.right)[way][s - 1]
                        self.own[part] = (self.own[part].astype(F32) + came.astype(F32)).astype(BF16)

                self.copy(way, s, part, z + 1 - 2 * way).start()

    def result(self):
        z, last = self.z, self.top - 1

        def close(ways):
            total = self.own[z].astype(F32)
            for way in ways:
                self.landed(way, last)
                total = total + (self.left, self.right)[way][last].astype(F32)
            self.own[z] = total.astype(BF16)

        @pl.when(z == 0)
        def _():
            close((1,))

        @pl.when((z > 0) & (z < self.top))
        def _():
            close((0, 1))

        @pl.when(z == self.top)
        def _():
            close((0,))

    def sent(self):
        z, top = self.z, self.top
        for s in range(1 if self.begun else 0, top):
            for way in (0, 1):
                place = z if way == 0 else top - z
                part = top - s + z if way == 0 else s - top + z

                @pl.when((place <= s) & (place < top))
                def _():
                    self.copy(way, s, part, z + 1 - 2 * way).wait_send()


def back_kernel(
    order_ref, rank_ref, qkv_ref, o_ref, do_ref, lse_ref, table_ref, w_ref, gains_ref, gain_two_ref,
    mgrad_ref, x_ref, mixed_ref, sums_ref, all_ref, owg_ref, gug_ref, dg_ref, left_ref, right_ref,
    layer_ref, input_ref, sum_ref, gu_all, down_all, q_all, o_all,
    keys, keys_t, values, dk, dv, dqn, dqkv, acc, xs, big, owg, gug, down, heads, outs,
    gain_rows, by_z, part_sum, by_c, first, last, diagonal, first2, last2, diagonal2, *rest,
):
    scatter_sems = (rest[:4], rest[4:8], rest[8:12])
    lines = (rest[12:16], rest[16:20], rest[20:24], rest[24:28])
    send, recv, local, load, xload, zs, zr, cs, cr, free = rest[28:]
    c = lax.axis_index("ctx")
    z = lax.axis_index("fsdp")
    depth, shard = heads.shape[0], heads.shape[2]
    rows, width = xs.shape[1:]
    others = [lax.rem(z + k, depth) for k in range(1, depth)]
    greet([{"ctx": flip(c, k)} for k in range(1, 8)] + [{"fsdp": o} for o in others])
    some = acc.at[pl.ds(0, rows)]
    loads = [
        pltpu.make_async_copy(a, t, load.at[i])
        for i, (a, t) in enumerate(
            ((gug_ref, gug), (owg_ref, owg), (dg_ref, down), (mgrad_ref, some), (x_ref, xs.at[0]))
        )
    ]
    loads.append(pltpu.make_async_copy(sums_ref, first, load.at[7]))
    loads.append(pltpu.make_async_copy(mixed_ref, some, load.at[8]))
    for d in loads[:3] + loads[5:6]:
        d.start()
    gu_line, down_line, q_line, o_line = (
        LineScatter(z, a, *refs) for a, refs in zip((gug, down, heads, outs), lines)
    )
    gu_line.begun = (
        pltpu.make_async_copy(left_ref, gu_line.left.at[0], load.at[5]),
        pltpu.make_async_copy(right_ref, gu_line.right.at[0], load.at[6]),
    )

    @pl.when(z == 1)
    def _():
        gu_line.begun[0].start()

    @pl.when(z == depth - 2)
    def _():
        gu_line.begun[1].start()

    layer = Scatter(c, None, first, last, diagonal, *scatter_sems[2])
    layer.summed = True
    out = Scatter(c, owg, first2, last2, diagonal2, *scatter_sems[0])
    one = Scatter(c, big, first, last, diagonal, *scatter_sems[1])
    near = [flip(c, k) for k in (1, 2, 4)]

    blocks = qkv_ref.shape[0]
    per = CHUNK // BLOCK
    scale = HEAD_SIZE ** (-0.5)
    factor = scale * math.log2(math.e)
    half = HEAD_SIZE // 2
    for b in range(blocks):
        there = slice(b * BLOCK, (b + 1) * BLOCK)
        key = qkv_ref[order_ref[b], 2 * HEAD_SIZE : 3 * HEAD_SIZE]
        keys[there, :] = key.T
        keys_t[:, there] = key
        values[there, :] = qkv_ref[order_ref[b], 3 * HEAD_SIZE :].T
    dk[...] = jnp.zeros_like(dk)
    dv[...] = jnp.zeros_like(dv)
    loads[0].wait()
    gu_line.step(1)
    loads[2].wait()
    down_line.step(0)
    loads[1].wait()
    for k in Scatter.ORDER:
        out.give(k)
    loads[5].wait()
    layer.far()
    layer.direct()

    def attend_block(j, last):
        block = order_ref[j]
        q = two_heads(qkv_ref, block)
        do = two_heads(do_ref, block)
        delta = jnp.sum(two_heads(o_ref, j).astype(F32) * do.astype(F32), 0, keepdims=True)
        lse = lse_ref[j]

        def step(t, dq, masked):
            there = pl.ds(t * CHUNK, CHUNK)
            s = jnp.dot(keys[there, :], q, preferred_element_type=F32)
            if masked:
                s = causal(s, t, j)
            p = jnp.exp2(s * factor - lse)
            dp = jnp.dot(values[there, :], do, preferred_element_type=F32)
            ds = (p * (dp - delta)).astype(BF16)
            wide = pl.ds(t * per, per)
            dv[wide] += contract(p.astype(BF16), do, ((1,), (1,))).reshape(per, BLOCK, HEAD_SIZE)
            dk[wide] += contract(ds, q, ((1,), (1,))).reshape(per, BLOCK, HEAD_SIZE)
            return dq + jnp.dot(keys_t[:, there], ds, preferred_element_type=F32)

        dq = jnp.zeros((HEAD_SIZE, 2 * BLOCK), F32)
        for t in range(last):
            dq = step(t, dq, False)
        dq = step(last, dq, True) * scale
        cosine, sine = table_ref[block, :half], table_ref[block, half:]
        for h in (0, 1):
            part = dq[:, h * BLOCK : (h + 1) * BLOCK]
            dqn[j, h * HEAD_SIZE : (h + 1) * HEAD_SIZE] = turned(part, cosine, -sine).astype(BF16)

    for turn in range(blocks // per):

        @pl.loop(turn * per, (turn + 1) * per)
        def _(j):
            attend_block(j, turn)

        if turn == 0:
            out.far()
        if turn == 1:
            out.direct()
        if turn == 2:
            layer.merged()
            gu_line.step(2)
            down_line.step(1)

    for i in range(blocks):
        to = slice(i * BLOCK, (i + 1) * BLOCK)
        natural = rank_ref[i]
        dqkv[: 2 * HEAD_SIZE, to] = dqn[natural]
        dqkv[2 * HEAD_SIZE : 3 * HEAD_SIZE, to] = turned(
            dk[natural].T * scale, table_ref[i, :half], -table_ref[i, half:]
        ).astype(BF16)
        dqkv[3 * HEAD_SIZE :, to] = dv[natural].T.astype(BF16)

    def x_load(d, slot):
        return pltpu.make_async_copy(all_ref.at[d], xs.at[slot], xload.at[slot])

    out.merged()
    x_load(0, 0).start()
    acc[...] = jnp.zeros_like(acc)
    for d in range(8):
        slot = d % 2
        if d + 1 < 8:
            x_load(d + 1, 1 - slot).start()
        part = dqkv[:, d * rows : (d + 1) * rows]
        big[d] = contract(part, w_ref[...], ((0,), (0,))).astype(BF16)
        x_load(d, slot).wait()
        acc[...] += jnp.dot(part, xs[slot], preferred_element_type=F32)
    for f in range(depth):
        heads[f] = acc[:, f * shard : (f + 1) * shard].astype(BF16)
    loads[6].start()
    loads[4].start()
    q_line.step(0)
    loads[6].wait()
    for q in (0, 1):
        at = pl.ds(q * (rows // 2), rows // 2)
        xs[1, at] = (acc[at] + layer.result(q)).astype(BF16)
    loads[3].start()
    layer_put = pltpu.make_async_copy(xs.at[1], layer_ref, xload.at[1])
    layer_put.start()
    layer.sent()
    for d in near:
        pl.semaphore_signal(free, inc=1, device_id={"ctx": d}, device_id_type=MESH)
    pl.semaphore_wait(free, len(near))
    for k in Scatter.ORDER:
        one.give(k)
    outs[...] = jnp.concatenate([out.result(0), out.result(1)], 0).astype(BF16).reshape(outs.shape)
    o_line.step(0)
    one.far()
    one.direct()
    gu_line.result()
    here = []
    gathers = []

    def spread(i, source, everyone):
        here.append(pltpu.make_async_copy(source, everyone.at[c], local.at[i]))
        here[-1].start()
        at, own = (row_half, own_half(source)) if source.shape[0] % 32 == 0 else (column_half, own_half(source, 1))
        gathers.append(Gather(c, own, everyone, at, send.at[i], recv.at[i]))
        gathers[-1].begin()

    spread(0, gug.at[z], gu_all)
    down_line.step(2)
    q_line.step(1)
    o_line.step(1)
    one.merged()

    gain = jnp.concatenate([gains_ref[k, 0:1, :] for k in range(depth)], 1)
    gathers[0].near_half()
    q_line.step(2)
    o_line.step(2)
    loads[3].wait()
    loads[4].wait()
    layer_put.wait()
    gain_sum = jnp.zeros((1, width), F32)
    for q in (0, 1):
        at = pl.ds(q * (rows // 2), rows // 2)
        one_grad = one.result(q)
        x = xs[0, at].astype(F32)
        norm = lax.rsqrt(jnp.mean(x * x, -1, keepdims=True) + EPS)
        gain_sum = gain_sum + jnp.sum(one_grad * x * norm, 0, keepdims=True)
        scaled = one_grad * gain
        grad = norm * scaled - x * (norm * norm * norm) * jnp.mean(scaled * x, -1, keepdims=True)
        xs[1, at] = (acc[at] + grad).astype(BF16)
    here.append(pltpu.make_async_copy(xs.at[1], input_ref, xload.at[0]))
    here[-1].start()
    gain_rows[:4] = jnp.broadcast_to(gain_sum, (4, width))
    gain_rows[4:] = gain_two_ref[4:]
    sent = []
    for k, o in enumerate(others):
        d = remote(gain_rows.at[:, lanes(o * shard, shard)], by_z.at[z], zs.at[k], zr.at[k], fsdp=o)
        d.start()
        sent.append(d)
    gathers[0].near_rest()
    down_line.result()
    spread(1, down.at[z], down_all)
    gathers[0].far()
    q_line.result()
    spread(2, heads.at[z], q_all)
    o_line.result()
    spread(3, outs.at[z], o_all)

    total = gain_rows[:, lanes(z * shard, shard)]
    for k in range(depth - 1):
        ref = by_z.at[lax.rem(z + depth - 1 - k, depth)]
        remote(ref, ref, zs.at[k], zr.at[k], fsdp=others[k]).wait_recv()
        total = total + by_z[lax.rem(z + depth - 1 - k, depth)]
    part_sum[...] = total
    for k in range(1, 8):
        d = remote(part_sum, by_c.at[c], cs.at[k], cr.at[k], ctx=flip(c, k))
        d.start()
        sent.append(d)
    by_c[c] = total

    for g in gathers[1:]:
        g.near_half()
    for g in gathers[1:]:
        g.near_rest()
    for g in gathers[1:]:
        g.far()
    for g in gathers:
        for channel, k in ((0, 1), (3, 3), (4, 5), (5, 7)):
            g.paired(channel, k)
    for k in range(1, 8):
        ref = by_c.at[flip(c, k)]
        remote(ref, ref, cs.at[k], cr.at[k], ctx=flip(c, k)).wait_recv()
    total = by_c[0]
    for k in range(1, 8):
        total = total + by_c[k]
    sum_ref[...] = total
    for d in here:
        d.wait()
    for d in sent:
        d.wait_send()
    out.sent()
    one.sent()
    for line in (gu_line, down_line, q_line, o_line):
        line.sent()
    for g in gathers:
        g.sent()


def back(order, rank, arrays, large, depth, cid):
    blocks = arrays[0].shape[0]
    tokens = blocks * BLOCK
    rows, width = large[0].shape
    out_rows = large[5].shape[1]
    gate_up, down = large[6], large[7]
    shard = gate_up.shape[1]
    shape = jax.ShapeDtypeStruct
    vm = pl.BlockSpec(memory_space=VMEM)
    hbm = pl.BlockSpec(memory_space=ANY)
    sm = pl.BlockSpec(memory_space=pltpu.SMEM)
    tall = (tokens, HEAD_SIZE)
    small = (8, shard)
    lines = (gate_up.shape, down.shape, (depth, 4 * HEAD_SIZE, shard), (depth, out_rows // depth, width))
    scatter = Scatter.scratch(rows, width)
    return pl.pallas_call(
        back_kernel,
        out_shape=[shape((rows, width), BF16), shape((rows, width), BF16), shape(small, F32)]
        + [shape((8,) + a[1:], BF16) for a in lines],
        in_specs=[sm, sm] + [vm] * len(arrays) + [hbm] * len(large),
        out_specs=[hbm, hbm, vm] + [hbm] * 4,
        scratch_shapes=[
            VMEM(tall, BF16),
            VMEM(tall[::-1], BF16),
            VMEM(tall, BF16),
            VMEM((blocks, BLOCK, HEAD_SIZE), F32),
            VMEM((blocks, BLOCK, HEAD_SIZE), F32),
            VMEM((blocks, 2 * HEAD_SIZE, BLOCK), BF16),
            VMEM((4 * HEAD_SIZE, tokens), BF16),
            VMEM((4 * HEAD_SIZE, width), F32),
            VMEM((2, rows, width), BF16),
            VMEM((8, rows, width), BF16),
            VMEM((8, out_rows, width), BF16),
        ]
        + [VMEM(a, BF16) for a in lines]
        + [VMEM((8, width), F32), VMEM((depth,) + small, F32), VMEM(small, F32), VMEM((8,) + small, F32)]
        + scatter[:3]
        + Scatter.scratch(out_rows, width)[:3]
        + scatter[3:] * 3
        + [r for a in lines for r in LineScatter.scratch(a)]
        + [DMA((4, 8, 2)), DMA((4, 8, 2)), DMA((4,)), DMA((9,)), DMA((2,))]
        + [DMA((depth,)), DMA((depth,)), DMA((8,)), DMA((8,)), pltpu.SemaphoreType.REGULAR],
        compiler_params=params(cid),
        name="back",
    )(order, rank, *arrays, *large)


def widen(gate_up, down, out, sums):
    _, shard, both = gate_up.shape
    mine = both // 2
    strips = mine // LANES
    step = shard // 8
    _, rows, width = down.shape

    def kernel(a_ref, d_ref, o_ref, s_ref, gate_ref, up_ref, down_ref, out_ref, one_ref, two_ref):
        for i, target in enumerate((gate_ref, up_ref)):
            for c in range(8):
                for s in range(strips):
                    target[:, (s * 8 + c) * LANES : (s * 8 + c + 1) * LANES] = a_ref[
                        c, :, i * mine + s * LANES : i * mine + (s + 1) * LANES
                    ].astype(F32)
        down_ref[...] = d_ref[0].astype(F32)
        out_ref[...] = o_ref[0].astype(F32)
        one_ref[...] = s_ref[0]
        two_ref[...] = s_ref[4]

    wide = jax.ShapeDtypeStruct((shard, 8 * mine), F32)
    gain = jax.ShapeDtypeStruct((shard,), F32)
    by_rows = lambda n, columns: pl.BlockSpec((n, columns), lambda i: (i, 0))
    by_device = lambda a: pl.BlockSpec((1,) + a.shape[1:], lambda i: (i, 0, 0))
    return pl.pallas_call(
        kernel,
        grid=(8,),
        out_shape=(
            wide,
            wide,
            jax.ShapeDtypeStruct((8 * rows, width), F32),
            jax.ShapeDtypeStruct((shard, width), F32),
            gain,
            gain,
        ),
        in_specs=[
            pl.BlockSpec((8, step, both), lambda i: (0, i, 0)),
            by_device(down),
            by_device(out),
            pl.BlockSpec(sums.shape, lambda i: (0, 0)),
        ],
        out_specs=(by_rows(step, 8 * mine), by_rows(step, 8 * mine), by_rows(rows, width), by_rows(step, width))
        + (pl.BlockSpec((shard,), lambda i: (0,)),) * 2,
        compiler_params=pltpu.CompilerParams(vmem_limit_bytes=VMEM_BYTES),
        name="widen",
    )(gate_up, down, out, sums)


def widen_heads(qkv):
    shard = qkv.shape[2]
    per_q = 2 * HEAD_SIZE
    heads = 8 * HEAD_SIZE

    def kernel(a_ref, q_out, k_out, v_out):
        for c in range(0, 8, 2):
            both = jnp.concatenate([a_ref[c + i, :per_q, :] for i in (0, 1)], 0)
            q_out[:, c * per_q : (c + 2) * per_q] = both.astype(F32).T
        for target, first in ((k_out, per_q), (v_out, per_q + HEAD_SIZE)):
            for c in range(0, 8, 4):
                four = jnp.concatenate([a_ref[c + i, first : first + HEAD_SIZE, :] for i in range(4)], 0)
                target[:, c * HEAD_SIZE : (c + 4) * HEAD_SIZE] = four.astype(F32).T

    by_rows = lambda n: pl.BlockSpec((LANES, n), lambda i: (i, 0))
    shape = lambda n: jax.ShapeDtypeStruct((shard, n), F32)
    return pl.pallas_call(
        kernel,
        grid=(shard // LANES,),
        out_shape=(shape(2 * heads), shape(heads), shape(heads)),
        in_specs=[pl.BlockSpec((8, 4 * HEAD_SIZE, LANES), lambda i: (0, 0, i))],
        out_specs=(by_rows(2 * heads), by_rows(heads), by_rows(heads)),
        compiler_params=pltpu.CompilerParams(vmem_limit_bytes=VMEM_BYTES),
        name="widen_heads",
    )(qkv)


def in_plane(
    depth,
    hidden_in,
    positions,
    attn_gain,
    w_query,
    key_projection,
    value_projection,
    w_out,
    mlp_gain,
    w_gate,
    w_up,
    w_down,
    out_grad,
):
    plane = 8
    rows, width = hidden_in.shape[1:]
    shard = width // depth
    half = HEAD_SIZE // 2

    gains = (attn_gain.reshape(1, shard), mlp_gain.reshape(1, shard))
    freq = np.float32(THETA) ** (-(np.arange(half, dtype=np.float32) * np.float32(2.0) / np.float32(HEAD_SIZE)))
    inner = freq[:, None] * np.arange(BLOCK, dtype=np.float32)[None]
    step = jnp.asarray(np.concatenate([np.cos(inner), np.sin(inner)], 0).astype(np.float32))
    freq = jnp.asarray(np.broadcast_to(freq[:, None], (half, LANES)).astype(np.float32))

    hidden_low = hidden_in[0]
    weights = (w_query, key_projection, value_projection, w_out, w_gate, w_up, w_down)
    grad_low = out_grad[0]
    (normed_all, qkv, qkv_w, table, gains_all, order, rank, attended_low, lse, out_w, gate_up_w, down_w, grad_all) = first_part(
        positions, hidden_low, gains, freq, step, weights, grad_low, depth, 0
    )
    (mixed, down_sum, mixed_grad, gain_two_grad, do, out_wgrad, gate_up_wgrad, down_wgrad, left, right, _, _) = middle(
        rank, attended_low, hidden_low, gains_all, grad_all, out_w.reshape(plane, -1, width), gate_up_w, down_w, 2
    )
    arrays = (qkv, attended_low, do, lse, table, qkv_w, gains_all, gain_two_grad)
    large = (mixed_grad, hidden_low, mixed, down_sum, normed_all, out_wgrad, gate_up_wgrad, down_wgrad, left, right)
    layer_out, input_grad, gain_sums, gate_up_all, down_all, qkv_all, out_grads = back(
        order, rank, arrays, large, depth, 3
    )
    query_total, key_total, value_total = widen_heads(qkv_all)
    gate_total, up_total, down_total, out_total, gain_one, gain_two = widen(gate_up_all, down_all, out_grads, gain_sums)
    return (
        layer_out[None],
        input_grad[None],
        gain_one,
        query_total,
        key_total,
        value_total,
        out_total,
        gain_two,
        gate_total,
        up_total,
        down_total,
    )


def solution(mesh):
    placed = (
        P("fsdp", "ctx", None),
        P("fsdp", "ctx"),
        P("fsdp"),
        P("fsdp", None),
        P("fsdp", None),
        P("fsdp", None),
        P("fsdp", None),
        P("fsdp"),
        P("fsdp", None),
        P("fsdp", None),
        P("fsdp", None),
        P("fsdp", "ctx", None),
    )
    body = per_device
    if mesh.shape["ctx"] == KEY_VALUE_HEADS:
        body = functools.partial(in_plane, mesh.shape["fsdp"])
    return jax.shard_map(
        body,
        mesh=mesh,
        in_specs=placed,
        out_specs=(
            P("fsdp", "ctx", None),
            P("fsdp", "ctx", None),
            P("fsdp"),
            P("fsdp", None),
            P("fsdp", None),
            P("fsdp", None),
            P("fsdp", None),
            P("fsdp"),
            P("fsdp", None),
            P("fsdp", None),
            P("fsdp", None),
        ),
        check_vma=False,
    )
```

```python
import functools
import math

import jax
import jax.numpy as jnp
import numpy as np
from jax import lax
from jax.experimental import pallas as pl
from jax.experimental.pallas import tpu as pltpu
from jax.sharding import PartitionSpec as P

QUERY_HEADS = 16
KEY_VALUE_HEADS = 8
HEAD_SIZE = 96


EPS = 1e-05
THETA = 100000.0


def tables(token_position):
    half = HEAD_SIZE // 2
    freq = THETA ** (-(jnp.arange(half, dtype=jnp.float32) * 2.0 / HEAD_SIZE))
    angle = token_position.astype(jnp.float32)[:, None] * freq[None, :]
    return (jnp.cos(angle)[:, None, :], jnp.sin(angle)[:, None, :])


def rotary_embed(value_rows, cosine_table, sine_table):
    half = value_rows.shape[-1] // 2
    first = value_rows[..., :half]
    second = value_rows[..., half:]
    return jnp.concatenate(
        [first * cosine_table - second * sine_table, second * cosine_table + first * sine_table], -1
    )


def rotary_embed_backward(grads, cosine_table, sine_table):
    half = grads.shape[-1] // 2
    first = grads[..., :half]
    second = grads[..., half:]
    return jnp.concatenate(
        [first * cosine_table + second * sine_table, second * cosine_table - first * sine_table], -1
    )


def norm_forward(hidden, gain):
    return (
        hidden
        * lax.rsqrt(jnp.mean(hidden * hidden, -1, keepdims=True) + EPS)
        * gain.astype(jnp.float32)
    )


def norm_back(hidden, gain, grad):
    factor = lax.rsqrt(jnp.mean(hidden * hidden, -1, keepdims=True) + EPS)
    scaled = grad * gain.astype(jnp.float32)
    hidden_grad = factor * scaled - hidden * factor * factor * factor * jnp.mean(
        scaled * hidden, -1, keepdims=True
    )
    gain_grad = jnp.sum(grad * hidden * factor, 0)
    return (hidden_grad, gain_grad)


def dot_first(left, right):
    return lax.dot_general(
        left, right, (((0,), (0,)), ((), ())), preferred_element_type=jnp.float32
    )


def dot_last(left, right):
    return lax.dot_general(
        left, right, (((1,), (1,)), ((), ())), preferred_element_type=jnp.float32
    )


def over_blocks(step_fn, carry, arrays):
    block_count = arrays[0].shape[0]
    size = math.gcd(block_count, 512)
    parts = block_count // size
    shaped = tuple((item.reshape((parts, size) + item.shape[1:]) for item in arrays))

    def advance(state, inputs):
        index, pieces = inputs
        return (step_fn(state, pieces, index * size), None)

    final, unused = lax.scan(advance, carry, (jnp.arange(parts, dtype=jnp.int32), shaped))
    return final


def per_device(
    hidden_in,
    positions,
    attn_gain,
    w_query,
    key_projection,
    value_projection,
    w_out,
    mlp_gain,
    w_gate,
    w_up,
    w_down,
    out_grad,
):
    hidden = hidden_in[0].astype(jnp.float32)
    local_rows = hidden.shape[0]
    query_pos = positions[0]
    query_groups = QUERY_HEADS // KEY_VALUE_HEADS
    scale = HEAD_SIZE ** (-0.5)
    cosine_table, sine_table = tables(query_pos)
    attn_set = (
        lax.all_gather(attn_gain, "fsdp", axis=0, tiled=True),
        lax.all_gather(w_query, "fsdp", axis=0, tiled=True),
        lax.all_gather(key_projection, "fsdp", axis=0, tiled=True),
        lax.all_gather(value_projection, "fsdp", axis=0, tiled=True),
        lax.all_gather(w_out, "fsdp", axis=0, tiled=True),
    )
    gain_one, query_w, key_matrix, value_matrix, out_w = attn_set
    first_normed = norm_forward(hidden, gain_one).astype(jnp.bfloat16)
    query_raw = jnp.dot(first_normed, query_w, preferred_element_type=jnp.float32)
    unrotated_key = jnp.dot(first_normed, key_matrix, preferred_element_type=jnp.float32)
    value_raw = jnp.dot(first_normed, value_matrix, preferred_element_type=jnp.float32)
    query_rows = (
        rotary_embed(
            query_raw.reshape(local_rows, QUERY_HEADS, HEAD_SIZE), cosine_table, sine_table
        )
        .astype(jnp.bfloat16)
        .reshape(local_rows, KEY_VALUE_HEADS, query_groups, HEAD_SIZE)
    )
    keys_flat = (
        rotary_embed(
            unrotated_key.reshape(local_rows, KEY_VALUE_HEADS, HEAD_SIZE), cosine_table, sine_table
        )
        .astype(jnp.bfloat16)
        .reshape(local_rows, KEY_VALUE_HEADS * HEAD_SIZE)
    )
    values_flat = value_raw.astype(jnp.bfloat16)
    key_pos_all = lax.all_gather(query_pos, "ctx", axis=0, tiled=True)
    sequence_length = key_pos_all.shape[0]

    def masked_scores(partial_keys, first):
        block_count = partial_keys.shape[0]
        key_pos = lax.dynamic_slice_in_dim(key_pos_all, first, block_count)
        scores = (
            jnp.einsum(
                "tkgd,nkd->kgtn",
                query_rows,
                partial_keys.reshape(block_count, KEY_VALUE_HEADS, HEAD_SIZE),
                preferred_element_type=jnp.float32,
            )
            * scale
        )
        visible = key_pos[None, None, None, :] <= query_pos[None, None, :, None]
        return jnp.where(visible, scores, -jnp.inf)

    def forward_part(carry, part, first):
        top, denom, accum = carry
        partial_keys, partial_values = part
        block_count = partial_keys.shape[0]
        scores = masked_scores(partial_keys, first)
        new_top = jnp.maximum(top, jnp.max(scores, -1))
        weights = jnp.exp(scores - new_top[..., None])
        factor = jnp.exp(top - new_top)
        denom = denom * factor + jnp.sum(weights, -1)
        accum = accum * factor[..., None] + jnp.einsum(
            "kgtn,nkd->kgtd",
            weights.astype(jnp.bfloat16),
            partial_values.reshape(block_count, KEY_VALUE_HEADS, HEAD_SIZE),
            preferred_element_type=jnp.float32,
        )
        return (new_top, denom, accum)

    start_state = (
        jnp.full((KEY_VALUE_HEADS, query_groups, local_rows), -1e30, jnp.float32),
        jnp.zeros((KEY_VALUE_HEADS, query_groups, local_rows), jnp.float32),
        jnp.zeros((KEY_VALUE_HEADS, query_groups, local_rows, HEAD_SIZE), jnp.float32),
    )
    top, denom, accum = over_blocks(
        forward_part,
        start_state,
        (
            lax.all_gather(keys_flat, "ctx", axis=0, tiled=True),
            lax.all_gather(values_flat, "ctx", axis=0, tiled=True),
        ),
    )
    attended_output = accum / denom[..., None]
    log_total = top + jnp.log(denom)
    attended_low = (
        attended_output.transpose(2, 0, 1, 3)
        .reshape(local_rows, QUERY_HEADS * HEAD_SIZE)
        .astype(jnp.bfloat16)
    )
    mixed = hidden + jnp.dot(attended_low, out_w, preferred_element_type=jnp.float32)
    mlp_set = (
        lax.all_gather(mlp_gain, "fsdp", axis=0, tiled=True),
        lax.all_gather(w_gate, "fsdp", axis=0, tiled=True),
        lax.all_gather(w_up, "fsdp", axis=0, tiled=True),
        lax.all_gather(w_down, "fsdp", axis=0, tiled=True),
    )
    gain_two, gate_w, up_w, down_w = mlp_set
    normed_two = norm_forward(mixed, gain_two).astype(jnp.bfloat16)
    gate = jnp.dot(normed_two, gate_w, preferred_element_type=jnp.float32)
    up = jnp.dot(normed_two, up_w, preferred_element_type=jnp.float32)
    sigma = jax.nn.sigmoid(gate)
    active = (gate * sigma * up).astype(jnp.bfloat16)
    result = mixed + jnp.dot(active, down_w, preferred_element_type=jnp.float32)
    layer_out = result.astype(jnp.bfloat16)[None]
    grad_low = out_grad[0]
    grad_out = grad_low.astype(jnp.float32)
    gain_back, gate_back, up_back, down_back = (
        lax.all_gather(mlp_gain, "fsdp", axis=0, tiled=True),
        lax.all_gather(w_gate, "fsdp", axis=0, tiled=True),
        lax.all_gather(w_up, "fsdp", axis=0, tiled=True),
        lax.all_gather(w_down, "fsdp", axis=0, tiled=True),
    )
    down_grad = dot_first(active, grad_low)
    active_grad = dot_last(grad_low, down_back)
    gate_grad = (active_grad * up * sigma * (1.0 + gate * (1.0 - sigma))).astype(jnp.bfloat16)
    up_grad = (active_grad * gate * sigma).astype(jnp.bfloat16)
    gate_wgrad = dot_first(normed_two, gate_grad)
    up_wgrad = dot_first(normed_two, up_grad)
    normed_two_grad = dot_last(gate_grad, gate_back) + dot_last(up_grad, up_back)
    mixed_part, gain_two_grad = norm_back(mixed, gain_back, normed_two_grad)
    mixed_grad = grad_out + mixed_part
    mlp_shards = (
        lax.psum_scatter(
            gain_two_grad.astype(jnp.bfloat16), "fsdp", scatter_dimension=0, tiled=True
        ).astype(jnp.float32),
        lax.psum_scatter(
            gate_wgrad.astype(jnp.bfloat16), "fsdp", scatter_dimension=0, tiled=True
        ).astype(jnp.float32),
        lax.psum_scatter(
            up_wgrad.astype(jnp.bfloat16), "fsdp", scatter_dimension=0, tiled=True
        ).astype(jnp.float32),
        lax.psum_scatter(
            down_grad.astype(jnp.bfloat16), "fsdp", scatter_dimension=0, tiled=True
        ).astype(jnp.float32),
    )
    gain_first, query_back, key_back, value_back, out_back = (
        lax.all_gather(attn_gain, "fsdp", axis=0, tiled=True),
        lax.all_gather(w_query, "fsdp", axis=0, tiled=True),
        lax.all_gather(key_projection, "fsdp", axis=0, tiled=True),
        lax.all_gather(value_projection, "fsdp", axis=0, tiled=True),
        lax.all_gather(w_out, "fsdp", axis=0, tiled=True),
    )
    branch_grad = mixed_grad.astype(jnp.bfloat16)
    out_wgrad = dot_first(attended_low, branch_grad)
    attended_grad = (
        dot_last(branch_grad, out_back)
        .astype(jnp.bfloat16)
        .reshape(local_rows, KEY_VALUE_HEADS, query_groups, HEAD_SIZE)
        .transpose(1, 2, 0, 3)
    )
    delta = jnp.sum(attended_grad.astype(jnp.float32) * attended_output, -1)

    def backward_part(carry, part, first):
        query_acc, key_value_acc = carry
        partial_keys, partial_values = part
        block_count = partial_keys.shape[0]
        probs = jnp.exp(masked_scores(partial_keys, first) - log_total[..., None])
        gradient_of_value = jnp.einsum(
            "kgtn,kgtd->nkd",
            probs.astype(jnp.bfloat16),
            attended_grad,
            preferred_element_type=jnp.float32,
        )
        prob_grad = jnp.einsum(
            "kgtd,nkd->kgtn",
            attended_grad,
            partial_values.reshape(block_count, KEY_VALUE_HEADS, HEAD_SIZE),
            preferred_element_type=jnp.float32,
        )
        score_grad = (probs * (prob_grad - delta[..., None])).astype(jnp.bfloat16)
        query_acc = (
            query_acc
            + jnp.einsum(
                "kgtn,nkd->kgtd",
                score_grad,
                partial_keys.reshape(block_count, KEY_VALUE_HEADS, HEAD_SIZE),
                preferred_element_type=jnp.float32,
            )
            * scale
        )
        gradient_of_key = (
            jnp.einsum("kgtn,tkgd->nkd", score_grad, query_rows, preferred_element_type=jnp.float32)
            * scale
        )
        joined = jnp.concatenate(
            [
                gradient_of_key.reshape(block_count, KEY_VALUE_HEADS * HEAD_SIZE),
                gradient_of_value.reshape(block_count, KEY_VALUE_HEADS * HEAD_SIZE),
            ],
            1,
        )
        key_value_acc = lax.dynamic_update_slice_in_dim(key_value_acc, joined, first, 0)
        return (query_acc, key_value_acc)

    back_state = (
        jnp.zeros((KEY_VALUE_HEADS, query_groups, local_rows, HEAD_SIZE), jnp.float32),
        jnp.zeros((sequence_length, 2 * KEY_VALUE_HEADS * HEAD_SIZE), jnp.float32),
    )
    query_acc, key_value_acc = over_blocks(
        backward_part,
        back_state,
        (
            lax.all_gather(keys_flat, "ctx", axis=0, tiled=True),
            lax.all_gather(values_flat, "ctx", axis=0, tiled=True),
        ),
    )
    local_key_value = lax.psum_scatter(
        key_value_acc.astype(jnp.bfloat16), "ctx", scatter_dimension=0, tiled=True
    ).astype(jnp.float32)
    query_raw_grad = (
        rotary_embed_backward(
            query_acc.transpose(2, 0, 1, 3).reshape(local_rows, QUERY_HEADS, HEAD_SIZE),
            cosine_table,
            sine_table,
        )
        .reshape(local_rows, QUERY_HEADS * HEAD_SIZE)
        .astype(jnp.bfloat16)
    )
    key_raw_grad = (
        rotary_embed_backward(
            local_key_value[:, : KEY_VALUE_HEADS * HEAD_SIZE].reshape(
                local_rows, KEY_VALUE_HEADS, HEAD_SIZE
            ),
            cosine_table,
            sine_table,
        )
        .reshape(local_rows, KEY_VALUE_HEADS * HEAD_SIZE)
        .astype(jnp.bfloat16)
    )
    unrotated_value_gradient = local_key_value[:, KEY_VALUE_HEADS * HEAD_SIZE :].astype(
        jnp.bfloat16
    )
    query_wgrad = dot_first(first_normed, query_raw_grad)
    key_wgrad = dot_first(first_normed, key_raw_grad)
    value_wgrad = dot_first(first_normed, unrotated_value_gradient)
    normed_one_grad = (
        dot_last(query_raw_grad, query_back)
        + dot_last(key_raw_grad, key_back)
        + dot_last(unrotated_value_gradient, value_back)
    )
    input_part, gain_one_grad = norm_back(hidden, gain_first, normed_one_grad)
    input_grad = (mixed_grad + input_part).astype(jnp.bfloat16)[None]
    attn_shards = (
        lax.psum_scatter(
            gain_one_grad.astype(jnp.bfloat16), "fsdp", scatter_dimension=0, tiled=True
        ).astype(jnp.float32),
        lax.psum_scatter(
            query_wgrad.astype(jnp.bfloat16), "fsdp", scatter_dimension=0, tiled=True
        ).astype(jnp.float32),
        lax.psum_scatter(
            key_wgrad.astype(jnp.bfloat16), "fsdp", scatter_dimension=0, tiled=True
        ).astype(jnp.float32),
        lax.psum_scatter(
            value_wgrad.astype(jnp.bfloat16), "fsdp", scatter_dimension=0, tiled=True
        ).astype(jnp.float32),
        lax.psum_scatter(
            out_wgrad.astype(jnp.bfloat16), "fsdp", scatter_dimension=0, tiled=True
        ).astype(jnp.float32),
    )
    totals = (
        lax.psum(attn_shards[0].astype(jnp.bfloat16), "ctx").astype(jnp.float32),
        lax.psum(attn_shards[1].astype(jnp.bfloat16), "ctx").astype(jnp.float32),
        lax.psum(attn_shards[2].astype(jnp.bfloat16), "ctx").astype(jnp.float32),
        lax.psum(attn_shards[3].astype(jnp.bfloat16), "ctx").astype(jnp.float32),
        lax.psum(attn_shards[4].astype(jnp.bfloat16), "ctx").astype(jnp.float32),
        lax.psum(mlp_shards[0].astype(jnp.bfloat16), "ctx").astype(jnp.float32),
        lax.psum(mlp_shards[1].astype(jnp.bfloat16), "ctx").astype(jnp.float32),
        lax.psum(mlp_shards[2].astype(jnp.bfloat16), "ctx").astype(jnp.float32),
        lax.psum(mlp_shards[3].astype(jnp.bfloat16), "ctx").astype(jnp.float32),
    )
    return (
        layer_out,
        input_grad,
        totals[0],
        totals[1],
        totals[2],
        totals[3],
        totals[4],
        totals[5],
        totals[6],
        totals[7],
        totals[8],
    )


MESH = pl.DeviceIdType.MESH
ANY = pl.ANY
VMEM = pltpu.VMEM
DMA = pltpu.SemaphoreType.DMA
LANES = 128
BLOCK = 128
F32 = jnp.float32
BF16 = jnp.bfloat16
VMEM_BYTES = 60 * 2**20


def flip(c, k):
    out = c
    for b in (1, 2, 4):
        if k & b:
            out = out + b - 2 * b * ((c // b) % 2)
    return out


def remote(src, dst, send, recv, **to):
    return pltpu.make_async_remote_copy(
        src_ref=src, dst_ref=dst, send_sem=send, recv_sem=recv, device_id=to, device_id_type=MESH
    )


def greet(peers):
    barrier = pltpu.get_barrier_semaphore()
    for peer in peers:
        pl.semaphore_signal(barrier, inc=1, device_id=peer, device_id_type=MESH)
    pl.semaphore_wait(barrier, len(peers))


class Gather:
    def __init__(self, c, own, buf, at, send, recv):
        self.c, self.own, self.buf, self.at, self.send, self.recv = c, own, buf, at, send, recv
        self.pending = []

    def start(self, channel, who, to, h, own=False):
        there = self.at(self.buf, flip(self.c, who), h)
        d = remote(
            self.own(h) if own else there,
            there,
            self.send.at[channel, h],
            self.recv.at[channel, h],
            ctx=flip(self.c, to),
        )
        d.start()
        self.pending.append(d)

    def arrived(self, channel, who, frm, h):
        ref = self.at(self.buf, flip(self.c, who), h)
        remote(
            ref, ref, self.send.at[channel, h], self.recv.at[channel, h], ctx=flip(self.c, frm)
        ).wait_recv()

    def begin(self):
        self.begin_half()
        self.begin_rest()

    def begin_half(self):
        self.start(1, 0, 2, 0, own=True)
        self.start(2, 0, 4, 1, own=True)

    def begin_rest(self):
        self.start(1, 0, 2, 1, own=True)
        self.start(2, 0, 4, 0, own=True)
        self.start(0, 0, 1, 0, own=True)
        self.start(0, 0, 1, 1, own=True)

    def near_half(self):
        self.arrived(1, 2, 2, 0)
        self.start(6, 2, 4, 0)
        self.start(3, 2, 1, 0)
        self.arrived(2, 4, 4, 1)
        self.start(7, 4, 2, 1)
        self.start(4, 4, 1, 1)

    def near_rest(self):
        self.arrived(1, 2, 2, 1)
        self.start(3, 2, 1, 1)
        self.arrived(2, 4, 4, 0)
        self.start(4, 4, 1, 0)

    def far(self):
        self.arrived(6, 6, 4, 0)
        self.start(5, 6, 1, 0)
        self.arrived(7, 6, 2, 1)
        self.start(5, 6, 1, 1)

    def paired(self, channel, who):
        for h in (0, 1):
            self.arrived(channel, who, 1, h)

    def finish(self):
        self.near_half()
        self.near_rest()
        self.far()
        for channel, who in ((0, 1), (3, 3), (4, 5), (5, 7)):
            self.paired(channel, who)

    def sent(self):
        for d in self.pending:
            d.wait_send()


def row_half(ref, d, h):
    half = ref.shape[1] // 2
    return ref.at[d, pl.ds(h * half, half)]


def column_half(ref, d, h):
    half = ref.shape[2] // 2
    return ref.at[d, :, pl.ds(h * half, half)]


def own_half(ref, axis=0):
    half = ref.shape[axis] // 2
    return lambda h: ref.at[(slice(None),) * axis + (pl.ds(h * half, half),)]


class Line:
    def __init__(self, z, depth, at, send, recv, own=None):
        self.z, self.depth, self.at, self.send, self.recv, self.own = z, depth, at, send, recv, own

    def copy(self, way, k, part, to):
        ref = self.at(part)
        source = ref if k or self.own is None else self.own
        return remote(source, ref, self.send.at[way, k], self.recv.at[way, k], fsdp=to)

    def step(self, k):
        z, top = self.z, self.depth - 1

        @pl.when((z >= k) & (z < top))
        def _():
            self.copy(0, k, z - k, z + 1).start()

        @pl.when((z + k <= top) & (z > 0))
        def _():
            self.copy(1, k, z + k, z - 1).start()

    def landed(self, k):
        z, top = self.z, self.depth - 1

        @pl.when(z >= k + 1)
        def _():
            self.copy(0, k, z - 1 - k, z - 1).wait_recv()

        @pl.when(z + 1 + k <= top)
        def _():
            self.copy(1, k, z + 1 + k, z + 1).wait_recv()

    def sent(self, steps):
        z, top = self.z, self.depth - 1
        for k in steps:

            @pl.when((z >= k) & (z < top))
            def _():
                self.copy(0, k, z - k, z + 1).wait_send()

            @pl.when((z + k <= top) & (z > 0))
            def _():
                self.copy(1, k, z + k, z - 1).wait_send()


def params(cid):
    return pltpu.CompilerParams(
        collective_id=cid, has_side_effects=True, vmem_limit_bytes=VMEM_BYTES
    )


def contract(a, b, dims):
    return lax.dot_general(a, b, ((dims[0], dims[1]), ((), ())), preferred_element_type=F32)


def lanes(start, size):
    return pl.ds(pl.multiple_of(start, LANES), size)


def turned(u, cosine, sine):
    half = HEAD_SIZE // 2
    a, b = u[:half], u[half:]
    return jnp.concatenate([a * cosine - b * sine, b * cosine + a * sine], 0)


def picked(weight, first, count):
    shape = (count, weight.shape[1])
    hit = lax.broadcasted_iota(jnp.int32, shape, 1) == first + lax.broadcasted_iota(jnp.int32, shape, 0)
    return contract(hit.astype(BF16), weight, ((1,), (1,))).astype(BF16)


CHUNK = 512


def two_heads(ref, block):
    return jnp.concatenate([ref[block, :HEAD_SIZE], ref[block, HEAD_SIZE : 2 * HEAD_SIZE]], 1)


def causal(s, t, j):
    key = t * CHUNK + lax.broadcasted_iota(jnp.int32, s.shape, 0)
    query = j * BLOCK + lax.broadcasted_iota(jnp.int32, s.shape, 1) % BLOCK
    return jnp.where(key <= query, s, -jnp.inf)


def exchange_start(c, source, target, send, recv):
    sent = []
    for k in (6, 7, 2, 4, 3, 5, 1):
        there = target.at[pl.ds(2 * c, 2)]
        d = remote(source.at[pl.ds(2 * flip(c, k), 2)], there, send.at[k], recv.at[k], ctx=flip(c, k))
        d.start()
        sent.append(d)
    return sent


def exchange_landed(c, target, send, recv):
    for k in (6, 7, 2, 4, 3, 5, 1):
        ref = target.at[pl.ds(2 * flip(c, k), 2)]
        remote(ref, ref, send.at[k], recv.at[k], ctx=flip(c, k)).wait_recv()


def first_kernel(
    pos_ref, x_ref, gain_one_ref, gain_two_ref, freq_ref, step_ref, wq_ref, wk_ref, wv_ref, wo_ref, wg_ref, wu_ref, wd_ref, grad_ref,
    all_ref, qkv_ref, w_ref, table_ref, gains_ref, order_ref, rank_ref, low_ref, lse_ref, got_ref, ow_all, gu_all, down_all, grad_all,
    give, infos_ref, infos, wo_all, keys, values, xs, wz, whole, gu_own, out_mine, down_mine, grad_mine, bases, gain_ref, info_ref, base_ref, gsend, grecv, isend, irecv, bsend, brecv, send, recv, zsend, zrecv, osend, orecv,
    usend, urecv, dsend, drecv, send2, recv2, send3, recv3, local, esend, erecv, parts,
):
    c = lax.axis_index("ctx")
    z = lax.axis_index("fsdp")
    depth = gains_ref.shape[0]
    shard, width = wq_ref.shape
    rows = x_ref.shape[0]
    strip = gu_all.shape[2] // 2 // depth
    down_rows = down_all.shape[1]
    others = [lax.rem(z + k, depth) for k in range(1, depth)]
    lane = lax.broadcasted_iota(jnp.int32, info_ref.shape, 1)
    info_ref[...] = jnp.where(lane < LANES // 2, pos_ref[0, 0], pos_ref[0, BLOCK])
    start = freq_ref[...] * info_ref[:1].astype(F32)
    base_ref[...] = jnp.where(lane[:1] // (LANES // 4) % 2 == 0, jnp.cos(start), jnp.sin(start))
    gain_ref[:4] = jnp.broadcast_to(gain_one_ref[...].astype(F32)[None], (4, shard))
    gain_ref[4:] = jnp.broadcast_to(gain_two_ref[...].astype(F32)[None], (4, shard))
    greet([{"ctx": flip(c, k)} for k in range(1, 8)] + [{"fsdp": o} for o in others])

    g2 = Gather(c, own_half(grad_ref), grad_all, row_half, send2, recv2)
    g2.begin_half()
    sent = []
    for k, o in enumerate(others):
        sent.append(remote(gain_ref, gains_ref.at[z], gsend.at[k], grecv.at[k], fsdp=o))
    for k in range(1, 8):
        sent.append(remote(info_ref, infos_ref.at[c], isend.at[k], irecv.at[k], ctx=flip(c, k)))
        sent.append(remote(base_ref, bases.at[c], bsend.at[k], brecv.at[k], ctx=flip(c, k)))
    for d in sent:
        d.start()
    out_rows = shard // 8
    out_own = wo_ref.at[pl.ds(c * out_rows, out_rows)]
    down_own = wd_ref.at[pl.ds(c * down_rows, down_rows)]
    strips = [
        pltpu.make_async_copy(weight, whole.at[i], parts.at[4 + i]) for i, weight in enumerate((wg_ref, wu_ref))
    ]
    for d in strips:
        d.start()
    ways = ((out_own, out_mine, ow_all.at[z, c]), (down_own, down_mine, down_all.at[z]), (grad_ref, grad_mine, grad_all.at[c]))
    incoming = [pltpu.make_async_copy(a, b, parts.at[i]) for i, (a, b, _) in enumerate(ways)]
    for d in incoming:
        d.start()
    gains_ref[z] = gain_ref[...]
    infos_ref[c] = info_ref[...]
    bases[c] = base_ref[...]

    count = 2 * HEAD_SIZE
    wz[z, :count] = picked(wq_ref[...], c * count, count)
    wz[z, count : count + HEAD_SIZE] = picked(wk_ref[...], c * HEAD_SIZE, HEAD_SIZE)
    wz[z, count + HEAD_SIZE :] = picked(wv_ref[...], c * HEAD_SIZE, HEAD_SIZE)
    line = Line(z, depth, lambda d: wz.at[d], zsend, zrecv)
    line.step(0)

    x = x_ref[...].astype(F32)
    factor = lax.rsqrt(jnp.mean(x * x, -1, keepdims=True) + EPS)
    for k in range(depth - 1):
        ref = gains_ref.at[lax.rem(z + depth - 1 - k, depth)]
        remote(ref, ref, gsend.at[k], grecv.at[k], fsdp=others[k]).wait_recv()
    gain = jnp.concatenate([gains_ref[k, 0:1, :] for k in range(depth)], 1)
    xs[c] = (x * factor * gain).astype(BF16)
    g = Gather(c, own_half(xs.at[c]), xs, row_half, send, recv)
    g.begin()
    out_line = Line(z, depth, lambda d: wo_all.at[d], osend, orecv, out_own)
    down_line = Line(z, depth, lambda d: down_all.at[d], dsend, drecv, down_own)
    out_line.step(0)
    copies = []
    for i, (_, b, there) in enumerate(ways):
        incoming[i].wait()
        copies.append(pltpu.make_async_copy(b, there, parts.at[i]))
        copies[-1].start()
    wo_all[z] = out_mine[...]

    def keep(k):
        d = pltpu.make_async_copy(xs.at[flip(c, k)], all_ref.at[flip(c, k)], local.at[k])
        d.start()
        copies.append(d)

    keep(0)

    def rotary(k):
        d = flip(c, k)
        if k:
            for ref, s, r in ((bases, bsend, brecv), (infos_ref, isend, irecv)):
                remote(ref.at[d], ref.at[d], s.at[k], r.at[k], ctx=d).wait_recv()
        half = HEAD_SIZE // 2
        step_cos, step_sin = step_ref[:half], step_ref[half:]
        for b in (0, 1):
            start = b * (LANES // 2)
            base_cos = bases[d, :, start : start + 1]
            base_sin = bases[d, :, start + LANES // 4 : start + LANES // 4 + 1]
            table_ref[2 * d + b, :half] = base_cos * step_cos - base_sin * step_sin
            table_ref[2 * d + b, half:] = base_sin * step_cos + base_cos * step_sin

    for k in range(8):
        rotary(k)

    def project(k):
        d = flip(c, k)
        half = HEAD_SIZE // 2
        raw = contract(w_ref[...], xs[d], ((1,), (1,)))
        for b in (0, 1):
            cosine, sine = table_ref[2 * d + b, :half], table_ref[2 * d + b, half:]
            part = raw[:, b * BLOCK : (b + 1) * BLOCK]
            for h in range(3):
                head = slice(h * HEAD_SIZE, (h + 1) * HEAD_SIZE)
                qkv_ref[2 * d + b, head] = turned(part[head], cosine, sine).astype(BF16)
            qkv_ref[2 * d + b, 3 * HEAD_SIZE :] = part[3 * HEAD_SIZE :].astype(BF16)

    line.landed(0)
    line.step(1)
    g.near_half()
    g2.begin_rest()
    out_line.landed(0)
    out_line.step(1)
    line.landed(1)
    line.step(2)
    g.near_rest()
    keep(2)
    keep(4)
    out_line.landed(1)
    out_line.step(2)
    for i, d in enumerate(strips):
        d.wait()
        for f in range(depth):
            gu_own[:, (i * depth + f) * strip : (i * depth + f + 1) * strip] = whole[i, :, lanes((f * 8 + c) * strip, strip)]
    gu_line = Line(z, depth, lambda d: gu_all.at[d], usend, urecv, gu_own)
    gu_line.step(0)
    down_line.step(0)
    copies.append(pltpu.make_async_copy(gu_own, gu_all.at[z], parts.at[3]))
    copies[-1].start()
    line.landed(2)
    for f in range(depth):
        w_ref[:, f * shard : (f + 1) * shard] = wz[f]
    g.far()
    g2.near_half()
    project(0)
    project(2)
    project(4)
    for channel, k in ((0, 1), (3, 3), (4, 5)):
        g.paired(channel, k)
        keep(k)
        project(k)
    keep(6)
    project(6)
    g.paired(5, 7)
    keep(7)
    project(7)
    out_line.landed(2)
    few = depth // 2
    g3 = Gather(
        c,
        lambda h: wo_all.at[pl.ds(h * few, few)],
        ow_all,
        lambda ref, d, h: ref.at[pl.ds(h * few, few), d],
        send3,
        recv3,
    )
    g3.begin()
    for f in range(1, depth):
        part = lax.rem(z + f, depth)
        copies.append(pltpu.make_async_copy(wo_all.at[part], ow_all.at[part, c], parts.at[4 + f]))
        copies[-1].start()

    blocks = qkv_ref.shape[0]
    per = CHUNK // BLOCK
    factor = HEAD_SIZE ** (-0.5) * math.log2(math.e)
    small = pltpu.make_async_copy(infos_ref, infos, parts.at[8])
    small.start()
    small.wait()
    starts = [infos[b // 2, 0, b % 2 * (LANES // 2)] for b in range(blocks)]
    least = functools.reduce(jnp.minimum, starts)
    ranks = [(start - least) // BLOCK for start in starts]
    for i in range(blocks):
        rank_ref[i] = ranks[i]
        order_ref[i] = functools.reduce(jnp.maximum, [jnp.where(ranks[b] == i, b, 0) for b in range(blocks)])
    for b in range(blocks):
        there = slice(b * BLOCK, (b + 1) * BLOCK)
        keys[there, :] = qkv_ref[order_ref[b], 2 * HEAD_SIZE : 3 * HEAD_SIZE].T
        values[:, there] = qkv_ref[order_ref[b], 3 * HEAD_SIZE :]

    def attend_block(j, last):
        q = two_heads(qkv_ref, order_ref[j])

        def step(t, carry, masked):
            top, denom, acc = carry
            s = jnp.dot(keys[pl.ds(t * CHUNK, CHUNK), :], q, preferred_element_type=F32)
            if masked:
                s = causal(s, t, j)
            new_top = jnp.maximum(top, jnp.max(s, 0, keepdims=True))
            p = jnp.exp2((s - new_top) * factor)
            shrink = jnp.exp2((top - new_top) * factor)
            denom = denom * shrink + jnp.sum(p, 0, keepdims=True)
            acc = acc * shrink + jnp.dot(
                values[:, pl.ds(t * CHUNK, CHUNK)], p.astype(BF16), preferred_element_type=F32
            )
            return new_top, denom, acc

        carry = (
            jnp.full((1, 2 * BLOCK), -1e30, F32),
            jnp.zeros((1, 2 * BLOCK), F32),
            jnp.zeros((HEAD_SIZE, 2 * BLOCK), F32),
        )
        for t in range(last):
            carry = step(t, carry, False)
        top, denom, acc = step(last, carry, True)
        out = acc / denom
        lse_ref[pl.ds(j, 1), :, :] = (top * factor + jnp.log2(denom)).reshape(1, 1, 2 * BLOCK)
        for h in (0, 1):
            head = slice(h * HEAD_SIZE, (h + 1) * HEAD_SIZE)
            low_ref[j, head] = out[:, h * BLOCK : (h + 1) * BLOCK].astype(BF16)

    def attend_blocks(first, count):
        @pl.loop(first, first + count)
        def _(j):
            attend_block(j, first // per)

    attend_blocks(0, per)
    g2.near_rest()
    attend_blocks(per, per)
    gu_line.landed(0)
    gu_line.step(1)
    attend_blocks(2 * per, per // 2)
    g2.far()
    attend_blocks(2 * per + per // 2, per // 2)
    g3.near_half()
    attend_blocks(3 * per, per // 2)
    g3.near_rest()
    attend_blocks(3 * per + per // 2, per // 2)
    for i in range(blocks):
        give[i] = low_ref[rank_ref[i]]
    sent += exchange_start(c, give, got_ref, esend, erecv)
    got_ref[pl.ds(2 * c, 2)] = give[pl.ds(2 * c, 2)]
    g3.far()
    for gather in (g2, g3):
        for channel, k in ((0, 1), (3, 3), (4, 5), (5, 7)):
            gather.paired(channel, k)
    exchange_landed(c, got_ref, esend, erecv)
    gu_line.landed(1)
    down_line.landed(0)
    for d in copies:
        d.wait()
    for d in sent:
        d.wait_send()
    line.sent((0, 1, 2))
    out_line.sent((0, 1, 2))
    gu_line.sent((0, 1))
    down_line.sent((0,))
    for gather in (g, g2, g3):
        gather.sent()


def first_part(positions, x, gains, freq, step, weights, grad, depth, cid):
    rows, width = x.shape
    shard = gains[0].shape[0]
    small = (8, shard)
    columns = weights[4].shape[1]
    down_rows = weights[6].shape[0] // 8
    blocks = 8 * rows // BLOCK
    sm = pl.BlockSpec(memory_space=pltpu.SMEM)
    vm = pl.BlockSpec(memory_space=VMEM)
    hbm = pl.BlockSpec(memory_space=ANY)
    shape = jax.ShapeDtypeStruct
    return pl.pallas_call(
        first_kernel,
        out_shape=(
            shape((8, rows, width), BF16),
            shape((8 * rows // BLOCK, 4 * HEAD_SIZE, BLOCK), BF16),
            shape((4 * HEAD_SIZE, width), BF16),
            shape((8 * rows // BLOCK, HEAD_SIZE, BLOCK), F32),
            shape((depth,) + small, F32),
            shape((blocks,), jnp.int32),
            shape((blocks,), jnp.int32),
            shape((blocks, 2 * HEAD_SIZE, BLOCK), BF16),
            shape((blocks, 1, 2 * BLOCK), F32),
            shape((blocks, 2 * HEAD_SIZE, BLOCK), BF16),
            shape((depth, 8, shard // 8, width), BF16),
            shape((depth, shard, 2 * columns // 8), BF16),
            shape((depth, down_rows, width), BF16),
            shape((8, rows, width), BF16),
        ),
        in_specs=[pl.BlockSpec(memory_space=pltpu.SMEM)] + [vm] * 8 + [hbm] * 5,
        out_specs=(hbm, vm, vm, vm, vm, sm, sm, vm, vm, vm, hbm, hbm, hbm, hbm),
        scratch_shapes=[
            VMEM((blocks, 2 * HEAD_SIZE, BLOCK), BF16),
            VMEM((8, 8, LANES), jnp.int32),
            pltpu.SMEM((8, 8, LANES), jnp.int32),
            VMEM((depth, shard // 8, width), BF16),
            VMEM((8 * rows, HEAD_SIZE), BF16),
            VMEM((HEAD_SIZE, 8 * rows), BF16),
            VMEM((8, rows, width), BF16),
            VMEM((depth, 4 * HEAD_SIZE, shard), BF16),
            VMEM((2, shard, columns), BF16),
            VMEM((shard, 2 * columns // 8), BF16),
            VMEM((shard // 8, width), BF16),
            VMEM((down_rows, width), BF16),
            VMEM((rows, width), BF16),
            VMEM((8, HEAD_SIZE // 2, LANES), F32),
            VMEM(small, F32),
            VMEM((8, LANES), jnp.int32),
            VMEM((HEAD_SIZE // 2, LANES), F32),
            DMA((depth,)),
            DMA((depth,)),
            DMA((8,)),
            DMA((8,)),
            DMA((8,)),
            DMA((8,)),
            DMA((8, 2)),
            DMA((8, 2)),
        ]
        + [DMA((2, depth))] * 8
        + [DMA((8, 2))] * 4
        + [DMA((8,))] * 3
        + [DMA((9,))],
        compiler_params=params(cid),
        name="first_part",
    )(positions, x, *gains, freq, step, *weights, grad)


class Scatter:
    ORDER = (6, 2, 4, 0)

    def __init__(self, c, p, first, last, diagonal, s1, v1, s2, v2):
        self.c, self.p, self.first = c, p, first
        self.last, self.diagonal = last, diagonal
        self.s1, self.v1, self.s2, self.v2 = s1, v1, s2, v2
        self.half = first.shape[1] // 2 if p is None else p.shape[1] // 2
        self.pending = []
        self.gifts = []
        self.summed = False

    @staticmethod
    def scratch(rows, width):
        return [
            VMEM((4, rows, width), BF16),
            VMEM((2, rows, width), BF16),
            VMEM((rows, width), BF16),
            DMA((4, 2)),
            DMA((4, 2)),
            DMA((3, 2)),
            DMA((3, 2)),
        ]

    def sl(self, q):
        return pl.ds(q * self.half, self.half)

    def go(self, d):
        d.start()
        self.pending.append(d)

    def give(self, k):
        j = self.ORDER.index(k)
        for q in (0, 1):
            source = self.p.at[flip(self.c, 1 ^ k), self.sl(q)]
            there = self.first.at[j, self.sl(q)]
            d = remote(source, there, self.s1.at[j, q], self.v1.at[j, q], ctx=flip(self.c, 1))
            d.start()
            self.gifts.append(d)

    def given(self):
        for d in self.gifts:
            d.wait_send()
        self.gifts = []

    def paired(self, j, q):
        if self.summed:
            return
        ref = self.first.at[j, self.sl(q)]
        remote(ref, ref, self.s1.at[j, q], self.v1.at[j, q], ctx=flip(self.c, 1)).wait_recv()

    def chip(self, j, q):
        if self.summed:
            return self.first[j, self.sl(q)].astype(F32)
        k = self.ORDER[j]
        return self.p[flip(self.c, k), self.sl(q)].astype(F32) + self.first[j, self.sl(q)].astype(F32)

    def came(self, channel, ref, q, frm):
        remote(
            ref, ref, self.s2.at[channel, q], self.v2.at[channel, q], ctx=flip(self.c, frm)
        ).wait_recv()

    def far(self):
        for q, to in ((0, 2), (1, 4)):
            self.paired(0, q)
            self.first[0, self.sl(q)] = self.chip(0, q).astype(BF16)
            self.go(
                remote(
                    self.first.at[0, self.sl(q)],
                    self.diagonal.at[self.sl(q)],
                    self.s2.at[2, q],
                    self.v2.at[2, q],
                    ctx=flip(self.c, to),
                )
            )

    def onward(self, j, q, merged):
        v = self.chip(j, q)
        if merged:
            v = v + self.diagonal[self.sl(q)].astype(F32)
        self.first[j, self.sl(q)] = v.astype(BF16)
        self.go(
            remote(
                self.first.at[j, self.sl(q)],
                self.last.at[j - 1, self.sl(q)],
                self.s2.at[j - 1, q],
                self.v2.at[j - 1, q],
                ctx=flip(self.c, self.ORDER[j]),
            )
        )

    def direct(self):
        self.paired(1, 0)
        self.onward(1, 0, False)
        self.paired(2, 1)
        self.onward(2, 1, False)

    def merged(self):
        self.paired(2, 0)
        self.came(2, self.diagonal.at[self.sl(0)], 0, 2)
        self.onward(2, 0, True)
        self.paired(1, 1)
        self.came(2, self.diagonal.at[self.sl(1)], 1, 4)
        self.onward(1, 1, True)

    def settle(self):
        for j, q in ((2, 0), (1, 1), (3, 0), (3, 1)):
            self.paired(j, q)
            self.first[j, self.sl(q)] = self.chip(j, q).astype(BF16)
        self.summed = True

    def result(self, q):
        self.paired(3, q)
        self.came(0, self.last.at[0, self.sl(q)], q, 2)
        self.came(1, self.last.at[1, self.sl(q)], q, 4)
        return self.chip(3, q) + (
            self.last[0, self.sl(q)].astype(F32) + self.last[1, self.sl(q)].astype(F32)
        )

    def sent(self):
        self.given()
        for d in self.pending:
            d.wait_send()


def both_blocks(ref, i):
    return jnp.concatenate([ref[2 * i], ref[2 * i + 1]], 1)


def middle_kernel(
    got, x_ref, gains_ref, g_ref, ow_ref, gu_in, down_in,
    layer_ref, mgrad_ref, gsum_ref, give, owg_ref, gug_ref, dg_ref, left_ref, right_ref, gu_all, down_all,
    mixed_ref, p1, wgu, wd, grads, two, p2, act, dgu, *rest,
):
    scatter_refs, layer_refs = rest[:7], rest[7:14]
    send, recv, usend, urecv, dsend, drecv, load, wput, hsend, hrecv = rest[14:]
    c = lax.axis_index("ctx")
    z = lax.axis_index("fsdp")
    depth, shard, both = gu_all.shape
    mine = both // 2
    rows, width = x_ref.shape
    out_rows = ow_ref.shape[1]
    out_w = p1.at[:, pl.ds(0, out_rows)]
    others = [lax.rem(z + k, depth) for k in range(1, depth)]
    greet([{"ctx": flip(c, k)} for k in (1, 2, 4)] + [{"fsdp": o} for o in others])
    gu_line = Line(z, depth, lambda d: gu_all.at[d], usend, urecv)
    down_line = Line(z, depth, lambda d: down_all.at[d], dsend, drecv)
    down_line.step(1)
    gu_line.step(2)
    loads = [
        pltpu.make_async_copy(ow_ref, out_w, load.at[0]),
        pltpu.make_async_copy(g_ref, grads, load.at[1]),
        pltpu.make_async_copy(x_ref, two.at[c], load.at[2]),
    ]
    for d in loads:
        d.start()

    loads[0].wait()
    loads[2].wait()
    mixed_ref[...] = two[c].astype(F32)

    @pl.loop(0, 8)
    def _(i):
        mixed_ref[...] += contract(both_blocks(got, i), p1[i, :out_rows], ((0,), (0,)))

    gain = jnp.concatenate([gains_ref[k, 4:5, :] for k in range(depth)], 1)
    halves = [pl.ds(q * (rows // 2), rows // 2) for q in (0, 1)]
    for at in halves:
        x = mixed_ref[at]
        factor = lax.rsqrt(jnp.mean(x * x, -1, keepdims=True) + EPS)
        two[c, at] = (x * factor * gain).astype(BF16)
    g = Gather(c, own_half(two.at[c]), two, row_half, send, recv)
    g.begin()
    loads[1].wait()
    down_line.landed(1)
    down_line.step(2)

    def pair(k):
        chip = pl.ds(flip(c, k) // 2 * 2, 2)
        tall = 2 * rows
        up_w = wgu[...].reshape(width, both)
        down_w = wd[...].reshape(mine, width)
        gate_up = jnp.dot(two[chip].reshape(tall, width), up_w, preferred_element_type=F32)
        gate, up = gate_up[:, :mine], gate_up[:, mine:]
        sigma = jax.nn.sigmoid(gate)
        silu = gate * sigma
        active = (silu * up).astype(BF16)
        act[chip] = active.reshape(2, rows, mine)
        active_grad = contract(grads[chip].reshape(tall, width), down_w, ((1,), (1,)))
        gate_grad = active_grad * up * sigma * (1.0 + gate * (1.0 - sigma))
        up_grad = active_grad * silu
        grad = jnp.concatenate([gate_grad, up_grad], 1).astype(BF16)
        dgu[chip] = grad.reshape(2, rows, both)
        p2[chip] = contract(grad, up_w, ((1,), (1,))).astype(BF16).reshape(2, rows, width)
        scatter.give(k)
        p1[chip] = jnp.dot(active, down_w, preferred_element_type=F32).astype(BF16).reshape(2, rows, width)
        layer.give(k)

    scatter = Scatter(c, p2, *scatter_refs)
    layer = Scatter(c, p1, *layer_refs)
    g.near_half()
    gu_line.landed(2)
    weights = [pltpu.make_async_copy(gu_all, wgu, load.at[2]), pltpu.make_async_copy(down_all, wd, load.at[3])]
    weights[0].start()
    g.near_rest()
    down_line.landed(2)
    weights[1].start()
    g.far()
    for d in weights:
        d.wait()
    g.paired(5, 7)
    pair(6)
    g.paired(3, 3)
    scatter.far()
    pair(2)
    scatter.paired(1, 0)
    scatter.onward(1, 0, False)
    layer.far()
    g.paired(4, 5)
    pair(4)
    scatter.paired(2, 1)
    scatter.onward(2, 1, False)
    g.paired(0, 1)
    pair(0)

    puts = []

    def wide(f):
        part = lambda i, total: total + contract(
            two[pl.ds(2 * i, 2), :, f * shard : (f + 1) * shard].reshape(2 * rows, shard),
            dgu[pl.ds(2 * i, 2)].reshape(2 * rows, both),
            ((0,), (0,)),
        )
        wgu[f] = lax.fori_loop(0, 4, part, jnp.zeros((shard, both), F32)).astype(BF16)
        puts.append(pltpu.make_async_copy(wgu.at[f], gug_ref.at[f], wput.at[f]))
        puts[-1].start()

    wide(0)
    scatter.merged()
    layer.direct()
    layer.settle()
    layer.given()
    again = pltpu.make_async_copy(ow_ref, out_w, load.at[0])
    again.start()
    for f in range(1, depth):
        wide(f)

    hop_right = remote(wgu.at[depth - 1], left_ref, hsend.at[0], hrecv.at[0], fsdp=z + 1)
    hop_left = remote(wgu.at[0], right_ref, hsend.at[1], hrecv.at[1], fsdp=z - 1)

    @pl.when(z == 0)
    def _():
        hop_right.start()

    @pl.when(z == depth - 1)
    def _():
        hop_left.start()

    strip = mine // depth
    for f in range(0, depth, 2):
        part = lambda i, total: total + contract(
            act[pl.ds(2 * i, 2), :, f * strip : (f + 2) * strip].reshape(2 * rows, 2 * strip),
            grads[pl.ds(2 * i, 2)].reshape(2 * rows, width),
            ((0,), (0,)),
        )
        part = lax.fori_loop(0, 4, part, jnp.zeros((2 * strip, width), F32))
        wd[f : f + 2] = part.astype(BF16).reshape(2, strip, width)
    puts.append(pltpu.make_async_copy(wd, dg_ref, wput.at[depth]))
    puts[-1].start()

    g.sent()
    gain_sum = jnp.zeros((1, width), F32)
    for q, at in enumerate(halves):
        two_grad = scatter.result(q)
        x = mixed_ref[at]
        factor = lax.rsqrt(jnp.mean(x * x, -1, keepdims=True) + EPS)
        gain_sum = gain_sum + jnp.sum(two_grad * x * factor, 0, keepdims=True)
        scaled = two_grad * gain
        mixed_grad = (
            grads[c, at].astype(F32)
            + factor * scaled
            - x * (factor * factor * factor) * jnp.mean(scaled * x, -1, keepdims=True)
        )
        mgrad_ref[at] = mixed_grad
        two[0, at] = mixed_grad.astype(BF16)
    gsum_ref[...] = jnp.broadcast_to(gain_sum, gsum_ref.shape)
    again.wait()
    for i in range(8):
        part = contract(p1[i, :out_rows], two[0], ((1,), (1,))).astype(BF16)
        give[2 * i] = part[:, :BLOCK]
        give[2 * i + 1] = part[:, BLOCK:]
    layer.merged()
    few = out_rows // depth
    for i in range(8):
        part = jnp.dot(both_blocks(got, i), two[0], preferred_element_type=F32).astype(BF16)
        f = i * depth // 8
        for t in range(depth):
            p1[i * depth % 8 + t, f * few : (f + 1) * few] = part[t * few : (t + 1) * few]
    out_put = pltpu.make_async_copy(out_w, owg_ref, load.at[0])
    out_put.start()
    scatter.sent()
    for q, at in enumerate(halves):
        p2[0, at] = (mixed_ref[at] + layer.result(q)).astype(BF16)
    layer_put = pltpu.make_async_copy(p2.at[0], layer_ref, load.at[1])
    layer_put.start()

    @pl.when(z == 0)
    def _():
        hop_right.wait_send()

    @pl.when(z == depth - 1)
    def _():
        hop_left.wait_send()

    @pl.when(z == 1)
    def _():
        remote(left_ref, left_ref, hsend.at[0], hrecv.at[0], fsdp=z - 1).wait_recv()

    @pl.when(z == depth - 2)
    def _():
        remote(right_ref, right_ref, hsend.at[1], hrecv.at[1], fsdp=z + 1).wait_recv()

    out_put.wait()
    for d in puts:
        d.wait()
    layer_put.wait()
    layer.sent()
    gu_line.sent((2,))
    down_line.sent((1, 2))


def middle(got, x, gains, grad_all, out_w, gate_up, down, cid):
    rows, width = x.shape
    depth, shard, both = gate_up.shape
    shape = jax.ShapeDtypeStruct
    vm = pl.BlockSpec(memory_space=VMEM)
    hbm = pl.BlockSpec(memory_space=ANY)
    heads = (8 * rows // BLOCK, 2 * HEAD_SIZE, BLOCK)
    block = (8, rows, width)
    return pl.pallas_call(
        middle_kernel,
        out_shape=(
            shape((rows, width), BF16),
            shape((rows, width), F32),
            shape((8, width), F32),
            shape(heads, BF16),
            shape(out_w.shape, BF16),
            shape(gate_up.shape, BF16),
            shape(down.shape, BF16),
            shape((shard, both), BF16),
            shape((shard, both), BF16),
            shape(gate_up.shape, BF16),
            shape(down.shape, BF16),
        ),
        in_specs=[vm, hbm, vm, hbm, hbm, hbm, hbm],
        out_specs=(hbm, vm, vm, vm, hbm, hbm, hbm, hbm, hbm, hbm, hbm),
        scratch_shapes=[
            VMEM((rows, width), F32),
            VMEM(block, BF16),
            VMEM(gate_up.shape, BF16),
            VMEM(down.shape, BF16),
            VMEM(block, BF16),
            VMEM(block, BF16),
            VMEM(block, BF16),
            VMEM((8, rows, both // 2), BF16),
            VMEM((8, rows, both), BF16),
        ]
        + Scatter.scratch(rows, width)
        + Scatter.scratch(rows, width)
        + [DMA((8, 2))] * 2
        + [DMA((2, depth))] * 4
        + [DMA((4,)), DMA((depth + 1,)), DMA((2,)), DMA((2,))],
        input_output_aliases={5: 9, 6: 10},
        compiler_params=params(cid),
        name="middle",
    )(got, x, gains, grad_all, out_w, gate_up, down)


class LineScatter:
    def __init__(self, z, own, left, right, send, recv):
        self.z, self.own, self.left, self.right = z, own, left, right
        self.send, self.recv = send, recv
        self.top = own.shape[0] - 1
        self.begun = None

    @staticmethod
    def scratch(shape):
        depth = shape[0]
        hops = (depth - 1,) + tuple(shape[1:])
        return [VMEM(hops, BF16), VMEM(hops, BF16), DMA((2, depth)), DMA((2, depth))]

    def copy(self, way, s, part, to):
        there = (self.left, self.right)[way].at[s]
        return remote(self.own.at[part], there, self.send.at[way, s], self.recv.at[way, s], fsdp=to)

    def landed(self, way, s):
        if s == 0 and self.begun:
            self.begun[way].wait()
            return
        ref = (self.left, self.right)[way].at[s]
        remote(ref, ref, self.send.at[way, s], self.recv.at[way, s], fsdp=self.z - 1 + 2 * way).wait_recv()

    def step(self, s):
        z, top = self.z, self.top
        for way in (0, 1):
            place = z if way == 0 else top - z
            part = top - s + z if way == 0 else s - top + z

            @pl.when((place <= s) & (place < top))
            def _():
                if s:

                    @pl.when(place > 0)
                    def _():
                        self.landed(way, s - 1)
                        came = (self.left, self.right)[way][s - 1]
                        self.own[part] = (self.own[part].astype(F32) + came.astype(F32)).astype(BF16)

                self.copy(way, s, part, z + 1 - 2 * way).start()

    def result(self):
        z, last = self.z, self.top - 1

        def close(ways):
            total = self.own[z].astype(F32)
            for way in ways:
                self.landed(way, last)
                total = total + (self.left, self.right)[way][last].astype(F32)
            self.own[z] = total.astype(BF16)

        @pl.when(z == 0)
        def _():
            close((1,))

        @pl.when((z > 0) & (z < self.top))
        def _():
            close((0, 1))

        @pl.when(z == self.top)
        def _():
            close((0,))

    def sent(self):
        z, top = self.z, self.top
        for s in range(1 if self.begun else 0, top):
            for way in (0, 1):
                place = z if way == 0 else top - z
                part = top - s + z if way == 0 else s - top + z

                @pl.when((place <= s) & (place < top))
                def _():
                    self.copy(way, s, part, z + 1 - 2 * way).wait_send()


def back_kernel(
    order_ref, rank_ref, qkv_ref, o_ref, give, lse_ref, table_ref, w_ref, gains_ref, gain_two_ref,
    mgrad_ref, x_ref, all_ref, owg_ref, gug_ref, dg_ref, left_ref, right_ref,
    input_ref, sum_ref, gu_all, down_all, q_all, o_all,
    do_ref, keys, keys_t, values, dk, dv, dqn, dqkv, acc, xs, big, owg, gug, down, heads, outs,
    gain_rows, by_z, part_sum, by_c, first, last, diagonal, first2, last2, diagonal2, *rest,
):
    scatter_sems = (rest[:4], rest[4:8])
    lines = (rest[8:12], rest[12:16], rest[16:20], rest[20:24])
    send, recv, local, load, xload, zs, zr, cs, cr, esend, erecv = rest[24:]
    c = lax.axis_index("ctx")
    z = lax.axis_index("fsdp")
    depth, shard = heads.shape[0], heads.shape[2]
    rows, width = xs.shape[1:]
    others = [lax.rem(z + k, depth) for k in range(1, depth)]
    greet([{"ctx": flip(c, k)} for k in range(1, 8)] + [{"fsdp": o} for o in others])
    some = acc.at[pl.ds(0, rows)]
    loads = [
        pltpu.make_async_copy(a, t, load.at[i])
        for i, (a, t) in enumerate(
            ((gug_ref, gug), (owg_ref, owg), (dg_ref, down), (mgrad_ref, some), (x_ref, xs.at[0]))
        )
    ]
    for d in loads[:3]:
        d.start()
    gu_line, down_line, q_line, o_line = (
        LineScatter(z, a, *refs) for a, refs in zip((gug, down, heads, outs), lines)
    )
    gu_line.begun = (
        pltpu.make_async_copy(left_ref, gu_line.left.at[0], load.at[5]),
        pltpu.make_async_copy(right_ref, gu_line.right.at[0], load.at[6]),
    )

    @pl.when(z == 1)
    def _():
        gu_line.begun[0].start()

    @pl.when(z == depth - 2)
    def _():
        gu_line.begun[1].start()

    out = Scatter(c, owg, first2, last2, diagonal2, *scatter_sems[0])
    one = Scatter(c, big, first, last, diagonal, *scatter_sems[1])

    sent = exchange_start(c, give, do_ref, esend, erecv)
    do_ref[pl.ds(2 * c, 2)] = give[pl.ds(2 * c, 2)]
    blocks = qkv_ref.shape[0]
    per = CHUNK // BLOCK
    scale = HEAD_SIZE ** (-0.5)
    factor = scale * math.log2(math.e)
    half = HEAD_SIZE // 2
    for b in range(blocks):
        there = slice(b * BLOCK, (b + 1) * BLOCK)
        key = qkv_ref[order_ref[b], 2 * HEAD_SIZE : 3 * HEAD_SIZE]
        keys[there, :] = key.T
        keys_t[:, there] = key
        values[there, :] = qkv_ref[order_ref[b], 3 * HEAD_SIZE :].T
    dk[...] = jnp.zeros_like(dk)
    dv[...] = jnp.zeros_like(dv)
    loads[0].wait()
    gu_line.step(1)
    loads[2].wait()
    down_line.step(0)
    loads[1].wait()
    for k in Scatter.ORDER:
        out.give(k)
    exchange_landed(c, do_ref, esend, erecv)

    def attend_block(j, last):
        block = order_ref[j]
        q = two_heads(qkv_ref, block)
        do = two_heads(do_ref, block)
        delta = jnp.sum(two_heads(o_ref, j).astype(F32) * do.astype(F32), 0, keepdims=True)
        lse = lse_ref[j]

        def step(t, dq, masked):
            there = pl.ds(t * CHUNK, CHUNK)
            s = jnp.dot(keys[there, :], q, preferred_element_type=F32)
            if masked:
                s = causal(s, t, j)
            p = jnp.exp2(s * factor - lse)
            dp = jnp.dot(values[there, :], do, preferred_element_type=F32)
            ds = (p * (dp - delta)).astype(BF16)
            wide = pl.ds(t * per, per)
            dv[wide] += contract(p.astype(BF16), do, ((1,), (1,))).reshape(per, BLOCK, HEAD_SIZE)
            dk[wide] += contract(ds, q, ((1,), (1,))).reshape(per, BLOCK, HEAD_SIZE)
            return dq + jnp.dot(keys_t[:, there], ds, preferred_element_type=F32)

        dq = jnp.zeros((HEAD_SIZE, 2 * BLOCK), F32)
        for t in range(last):
            dq = step(t, dq, False)
        dq = step(last, dq, True) * scale
        cosine, sine = table_ref[block, :half], table_ref[block, half:]
        for h in (0, 1):
            part = dq[:, h * BLOCK : (h + 1) * BLOCK]
            dqn[j, h * HEAD_SIZE : (h + 1) * HEAD_SIZE] = turned(part, cosine, -sine).astype(BF16)

    for turn in range(blocks // per):

        @pl.loop(turn * per, (turn + 1) * per)
        def _(j):
            attend_block(j, turn)

        if turn == 0:
            out.far()
        if turn == 1:
            out.direct()
        if turn == 2:
            out.merged()
            gu_line.step(2)
            down_line.step(1)

    for i in range(blocks):
        to = slice(i * BLOCK, (i + 1) * BLOCK)
        natural = rank_ref[i]
        dqkv[: 2 * HEAD_SIZE, to] = dqn[natural]
        dqkv[2 * HEAD_SIZE : 3 * HEAD_SIZE, to] = turned(
            dk[natural].T * scale, table_ref[i, :half], -table_ref[i, half:]
        ).astype(BF16)
        dqkv[3 * HEAD_SIZE :, to] = dv[natural].T.astype(BF16)

    def x_load(d, slot):
        return pltpu.make_async_copy(all_ref.at[d], xs.at[slot], xload.at[slot])

    x_load(0, 0).start()
    acc[...] = jnp.zeros_like(acc)
    for d in range(8):
        slot = d % 2
        if d + 1 < 8:
            x_load(d + 1, 1 - slot).start()
        part = dqkv[:, d * rows : (d + 1) * rows]
        big[d] = contract(part, w_ref[...], ((0,), (0,))).astype(BF16)
        x_load(d, slot).wait()
        acc[...] += jnp.dot(part, xs[slot], preferred_element_type=F32)
    for f in range(depth):
        heads[f] = acc[:, f * shard : (f + 1) * shard].astype(BF16)
    loads[3].start()
    loads[4].start()
    q_line.step(0)
    gu_line.result()
    here = []
    gathers = []

    def spread(i, source, everyone):
        here.append(pltpu.make_async_copy(source, everyone.at[c], local.at[i]))
        here[-1].start()
        at, own = (row_half, own_half(source)) if source.shape[0] % 32 == 0 else (column_half, own_half(source, 1))
        gathers.append(Gather(c, own, everyone, at, send.at[i], recv.at[i]))
        gathers[-1].begin()

    spread(0, gug.at[z], gu_all)
    for k in Scatter.ORDER:
        one.give(k)
    outs[...] = jnp.concatenate([out.result(0), out.result(1)], 0).astype(BF16).reshape(outs.shape)
    o_line.step(0)
    one.far()
    one.direct()
    down_line.step(2)
    q_line.step(1)
    o_line.step(1)
    one.merged()

    gain = jnp.concatenate([gains_ref[k, 0:1, :] for k in range(depth)], 1)
    gathers[0].near_half()
    q_line.step(2)
    o_line.step(2)
    loads[3].wait()
    loads[4].wait()
    gain_sum = jnp.zeros((1, width), F32)
    for q in (0, 1):
        at = pl.ds(q * (rows // 2), rows // 2)
        one_grad = one.result(q)
        x = xs[0, at].astype(F32)
        norm = lax.rsqrt(jnp.mean(x * x, -1, keepdims=True) + EPS)
        gain_sum = gain_sum + jnp.sum(one_grad * x * norm, 0, keepdims=True)
        scaled = one_grad * gain
        grad = norm * scaled - x * (norm * norm * norm) * jnp.mean(scaled * x, -1, keepdims=True)
        xs[1, at] = (acc[at] + grad).astype(BF16)
    here.append(pltpu.make_async_copy(xs.at[1], input_ref, xload.at[0]))
    here[-1].start()
    gain_rows[:4] = jnp.broadcast_to(gain_sum, (4, width))
    gain_rows[4:] = gain_two_ref[4:]
    for k, o in enumerate(others):
        d = remote(gain_rows.at[:, lanes(o * shard, shard)], by_z.at[z], zs.at[k], zr.at[k], fsdp=o)
        d.start()
        sent.append(d)
    gathers[0].near_rest()
    down_line.result()
    spread(1, down.at[z], down_all)
    gathers[0].far()
    q_line.result()
    spread(2, heads.at[z], q_all)
    o_line.result()
    spread(3, outs.at[z], o_all)

    total = gain_rows[:, lanes(z * shard, shard)]
    for k in range(depth - 1):
        ref = by_z.at[lax.rem(z + depth - 1 - k, depth)]
        remote(ref, ref, zs.at[k], zr.at[k], fsdp=others[k]).wait_recv()
        total = total + by_z[lax.rem(z + depth - 1 - k, depth)]
    part_sum[...] = total
    for k in range(1, 8):
        d = remote(part_sum, by_c.at[c], cs.at[k], cr.at[k], ctx=flip(c, k))
        d.start()
        sent.append(d)
    by_c[c] = total

    for g in gathers[1:]:
        g.near_half()
    for g in gathers[1:]:
        g.near_rest()
    for g in gathers[1:]:
        g.far()
    for g in gathers:
        for channel, k in ((0, 1), (3, 3), (4, 5), (5, 7)):
            g.paired(channel, k)
    for k in range(1, 8):
        ref = by_c.at[flip(c, k)]
        remote(ref, ref, cs.at[k], cr.at[k], ctx=flip(c, k)).wait_recv()
    total = by_c[0]
    for k in range(1, 8):
        total = total + by_c[k]
    sum_ref[...] = total
    for d in here:
        d.wait()
    for d in sent:
        d.wait_send()
    out.sent()
    one.sent()
    for line in (gu_line, down_line, q_line, o_line):
        line.sent()
    for g in gathers:
        g.sent()


def back(order, rank, arrays, large, depth, cid):
    blocks = arrays[0].shape[0]
    tokens = blocks * BLOCK
    rows, width = large[0].shape
    out_rows = large[3].shape[1]
    gate_up, down = large[4], large[5]
    shard = gate_up.shape[1]
    shape = jax.ShapeDtypeStruct
    vm = pl.BlockSpec(memory_space=VMEM)
    hbm = pl.BlockSpec(memory_space=ANY)
    sm = pl.BlockSpec(memory_space=pltpu.SMEM)
    tall = (tokens, HEAD_SIZE)
    small = (8, shard)
    lines = (gate_up.shape, down.shape, (depth, 4 * HEAD_SIZE, shard), (depth, out_rows // depth, width))
    scatter = Scatter.scratch(rows, width)
    return pl.pallas_call(
        back_kernel,
        out_shape=[shape((rows, width), BF16), shape(small, F32)]
        + [shape((8,) + a[1:], BF16) for a in lines],
        in_specs=[sm, sm] + [vm] * len(arrays) + [hbm] * len(large),
        out_specs=[hbm, vm] + [hbm] * 4,
        scratch_shapes=[
            VMEM((blocks, 2 * HEAD_SIZE, BLOCK), BF16),
            VMEM(tall, BF16),
            VMEM(tall[::-1], BF16),
            VMEM(tall, BF16),
            VMEM((blocks, BLOCK, HEAD_SIZE), F32),
            VMEM((blocks, BLOCK, HEAD_SIZE), F32),
            VMEM((blocks, 2 * HEAD_SIZE, BLOCK), BF16),
            VMEM((4 * HEAD_SIZE, tokens), BF16),
            VMEM((4 * HEAD_SIZE, width), F32),
            VMEM((2, rows, width), BF16),
            VMEM((8, rows, width), BF16),
            VMEM((8, out_rows, width), BF16),
        ]
        + [VMEM(a, BF16) for a in lines]
        + [VMEM((8, width), F32), VMEM((depth,) + small, F32), VMEM(small, F32), VMEM((8,) + small, F32)]
        + scatter[:3]
        + Scatter.scratch(out_rows, width)[:3]
        + scatter[3:] * 2
        + [r for a in lines for r in LineScatter.scratch(a)]
        + [DMA((4, 8, 2)), DMA((4, 8, 2)), DMA((4,)), DMA((9,)), DMA((2,))]
        + [DMA((depth,)), DMA((depth,)), DMA((8,)), DMA((8,)), DMA((8,)), DMA((8,))],
        compiler_params=params(cid),
        name="back",
    )(order, rank, *arrays, *large)


def widen(gate_up, down, out, sums, layer, grad):
    _, shard, both = gate_up.shape
    mine = both // 2
    strips = mine // LANES
    step = shard // 8
    _, rows, width = down.shape

    def kernel(a_ref, d_ref, o_ref, s_ref, l_ref, g_ref, gate_ref, up_ref, down_ref, out_ref, one_ref, two_ref, layer_ref, grad_ref):
        layer_ref[0] = l_ref[...]
        grad_ref[0] = g_ref[...]
        for i, target in enumerate((gate_ref, up_ref)):
            for c in range(8):
                for s in range(strips):
                    target[:, (s * 8 + c) * LANES : (s * 8 + c + 1) * LANES] = a_ref[
                        c, :, i * mine + s * LANES : i * mine + (s + 1) * LANES
                    ].astype(F32)
        down_ref[...] = d_ref[0].astype(F32)
        out_ref[...] = o_ref[0].astype(F32)
        one_ref[...] = s_ref[0]
        two_ref[...] = s_ref[4]

    wide = jax.ShapeDtypeStruct((shard, 8 * mine), F32)
    gain = jax.ShapeDtypeStruct((shard,), F32)
    by_rows = lambda n, columns: pl.BlockSpec((n, columns), lambda i: (i, 0))
    by_device = lambda a: pl.BlockSpec((1,) + a.shape[1:], lambda i: (i, 0, 0))
    return pl.pallas_call(
        kernel,
        grid=(8,),
        out_shape=(
            wide,
            wide,
            jax.ShapeDtypeStruct((8 * rows, width), F32),
            jax.ShapeDtypeStruct((shard, width), F32),
            gain,
            gain,
        )
        + (jax.ShapeDtypeStruct((1,) + layer.shape, BF16),) * 2,
        in_specs=[
            pl.BlockSpec((8, step, both), lambda i: (0, i, 0)),
            by_device(down),
            by_device(out),
            pl.BlockSpec(sums.shape, lambda i: (0, 0)),
        ]
        + [by_rows(layer.shape[0] // 8, width)] * 2,
        out_specs=(by_rows(step, 8 * mine), by_rows(step, 8 * mine), by_rows(rows, width), by_rows(step, width))
        + (pl.BlockSpec((shard,), lambda i: (0,)),) * 2
        + (pl.BlockSpec((1, layer.shape[0] // 8, width), lambda i: (0, i, 0)),) * 2,
        compiler_params=pltpu.CompilerParams(vmem_limit_bytes=VMEM_BYTES),
        name="widen",
    )(gate_up, down, out, sums, layer, grad)


def widen_heads(qkv):
    shard = qkv.shape[2]
    per_q = 2 * HEAD_SIZE
    heads = 8 * HEAD_SIZE

    def kernel(a_ref, q_out, k_out, v_out):
        for c in range(0, 8, 2):
            both = jnp.concatenate([a_ref[c + i, :per_q, :] for i in (0, 1)], 0)
            q_out[:, c * per_q : (c + 2) * per_q] = both.T.astype(F32)
        for target, first in ((k_out, per_q), (v_out, per_q + HEAD_SIZE)):
            for c in range(0, 8, 4):
                four = jnp.concatenate([a_ref[c + i, first : first + HEAD_SIZE, :] for i in range(4)], 0)
                target[:, c * HEAD_SIZE : (c + 4) * HEAD_SIZE] = four.T.astype(F32)

    by_rows = lambda n: pl.BlockSpec((LANES, n), lambda i: (i, 0))
    shape = lambda n: jax.ShapeDtypeStruct((shard, n), F32)
    return pl.pallas_call(
        kernel,
        grid=(shard // LANES,),
        out_shape=(shape(2 * heads), shape(heads), shape(heads)),
        in_specs=[pl.BlockSpec((8, 4 * HEAD_SIZE, LANES), lambda i: (0, 0, i))],
        out_specs=(by_rows(2 * heads), by_rows(heads), by_rows(heads)),
        compiler_params=pltpu.CompilerParams(vmem_limit_bytes=VMEM_BYTES),
        name="widen_heads",
    )(qkv)


def in_plane(
    depth,
    hidden_in,
    positions,
    attn_gain,
    w_query,
    key_projection,
    value_projection,
    w_out,
    mlp_gain,
    w_gate,
    w_up,
    w_down,
    out_grad,
):
    plane = 8
    rows, width = hidden_in.shape[1:]
    shard = width // depth
    half = HEAD_SIZE // 2

    gains = (attn_gain, mlp_gain)
    freq = np.float32(THETA) ** (-(np.arange(half, dtype=np.float32) * np.float32(2.0) / np.float32(HEAD_SIZE)))
    inner = freq[:, None] * np.arange(BLOCK, dtype=np.float32)[None]
    step = jnp.asarray(np.concatenate([np.cos(inner), np.sin(inner)], 0).astype(np.float32))
    freq = jnp.asarray(np.broadcast_to(freq[:, None], (half, LANES)).astype(np.float32))

    hidden_low = hidden_in[0]
    weights = (w_query, key_projection, value_projection, w_out, w_gate, w_up, w_down)
    grad_low = out_grad[0]
    (normed_all, qkv, qkv_w, table, gains_all, order, rank, attended_low, lse, got, out_w, gate_up_w, down_w, grad_all) = first_part(
        positions, hidden_low, gains, freq, step, weights, grad_low, depth, 0
    )
    (layer_out, mixed_grad, gain_two_grad, do, out_wgrad, gate_up_wgrad, down_wgrad, left, right, _, _) = middle(
        got, hidden_low, gains_all, grad_all, out_w.reshape(plane, -1, width), gate_up_w, down_w, 2
    )
    arrays = (qkv, attended_low, do, lse, table, qkv_w, gains_all, gain_two_grad)
    large = (mixed_grad, hidden_low, normed_all, out_wgrad, gate_up_wgrad, down_wgrad, left, right)
    input_grad, gain_sums, gate_up_all, down_all, qkv_all, out_grads = back(order, rank, arrays, large, depth, 3)
    query_total, key_total, value_total = widen_heads(qkv_all)
    gate_total, up_total, down_total, out_total, gain_one, gain_two, layer_out, input_grad = widen(
        gate_up_all, down_all, out_grads, gain_sums, layer_out, input_grad
    )
    return (
        layer_out,
        input_grad,
        gain_one,
        query_total,
        key_total,
        value_total,
        out_total,
        gain_two,
        gate_total,
        up_total,
        down_total,
    )


def solution(mesh):
    placed = (
        P("fsdp", "ctx", None),
        P("fsdp", "ctx"),
        P("fsdp"),
        P("fsdp", None),
        P("fsdp", None),
        P("fsdp", None),
        P("fsdp", None),
        P("fsdp"),
        P("fsdp", None),
        P("fsdp", None),
        P("fsdp", None),
        P("fsdp", "ctx", None),
    )
    body = per_device
    if mesh.shape["ctx"] == KEY_VALUE_HEADS:
        body = functools.partial(in_plane, mesh.shape["fsdp"])
    return jax.shard_map(
        body,
        mesh=mesh,
        in_specs=placed,
        out_specs=(
            P("fsdp", "ctx", None),
            P("fsdp", "ctx", None),
            P("fsdp"),
            P("fsdp", None),
            P("fsdp", None),
            P("fsdp", None),
            P("fsdp", None),
            P("fsdp"),
            P("fsdp", None),
            P("fsdp", None),
            P("fsdp", None),
        ),
        check_vma=False,
    )
```

```python
import functools
import math

import jax
import jax.numpy as jnp
import numpy as np
from jax import lax
from jax.experimental import pallas as pl
from jax.experimental.pallas import tpu as pltpu
from jax.sharding import PartitionSpec as P

QUERY_HEADS = 16
KEY_VALUE_HEADS = 8
HEAD_SIZE = 96


EPS = 1e-05
THETA = 100000.0


def tables(token_position):
    half = HEAD_SIZE // 2
    freq = THETA ** (-(jnp.arange(half, dtype=jnp.float32) * 2.0 / HEAD_SIZE))
    angle = token_position.astype(jnp.float32)[:, None] * freq[None, :]
    return (jnp.cos(angle)[:, None, :], jnp.sin(angle)[:, None, :])


def rotary_embed(value_rows, cosine_table, sine_table):
    half = value_rows.shape[-1] // 2
    first = value_rows[..., :half]
    second = value_rows[..., half:]
    return jnp.concatenate(
        [first * cosine_table - second * sine_table, second * cosine_table + first * sine_table], -1
    )


def rotary_embed_backward(grads, cosine_table, sine_table):
    half = grads.shape[-1] // 2
    first = grads[..., :half]
    second = grads[..., half:]
    return jnp.concatenate(
        [first * cosine_table + second * sine_table, second * cosine_table - first * sine_table], -1
    )


def norm_forward(hidden, gain):
    return (
        hidden
        * lax.rsqrt(jnp.mean(hidden * hidden, -1, keepdims=True) + EPS)
        * gain.astype(jnp.float32)
    )


def norm_back(hidden, gain, grad):
    factor = lax.rsqrt(jnp.mean(hidden * hidden, -1, keepdims=True) + EPS)
    scaled = grad * gain.astype(jnp.float32)
    hidden_grad = factor * scaled - hidden * factor * factor * factor * jnp.mean(
        scaled * hidden, -1, keepdims=True
    )
    gain_grad = jnp.sum(grad * hidden * factor, 0)
    return (hidden_grad, gain_grad)


def dot_first(left, right):
    return lax.dot_general(
        left, right, (((0,), (0,)), ((), ())), preferred_element_type=jnp.float32
    )


def dot_last(left, right):
    return lax.dot_general(
        left, right, (((1,), (1,)), ((), ())), preferred_element_type=jnp.float32
    )


def over_blocks(step_fn, carry, arrays):
    block_count = arrays[0].shape[0]
    size = math.gcd(block_count, 512)
    parts = block_count // size
    shaped = tuple((item.reshape((parts, size) + item.shape[1:]) for item in arrays))

    def advance(state, inputs):
        index, pieces = inputs
        return (step_fn(state, pieces, index * size), None)

    final, unused = lax.scan(advance, carry, (jnp.arange(parts, dtype=jnp.int32), shaped))
    return final


def per_device(
    hidden_in,
    positions,
    attn_gain,
    w_query,
    key_projection,
    value_projection,
    w_out,
    mlp_gain,
    w_gate,
    w_up,
    w_down,
    out_grad,
):
    hidden = hidden_in[0].astype(jnp.float32)
    local_rows = hidden.shape[0]
    query_pos = positions[0]
    query_groups = QUERY_HEADS // KEY_VALUE_HEADS
    scale = HEAD_SIZE ** (-0.5)
    cosine_table, sine_table = tables(query_pos)
    attn_set = (
        lax.all_gather(attn_gain, "fsdp", axis=0, tiled=True),
        lax.all_gather(w_query, "fsdp", axis=0, tiled=True),
        lax.all_gather(key_projection, "fsdp", axis=0, tiled=True),
        lax.all_gather(value_projection, "fsdp", axis=0, tiled=True),
        lax.all_gather(w_out, "fsdp", axis=0, tiled=True),
    )
    gain_one, query_w, key_matrix, value_matrix, out_w = attn_set
    first_normed = norm_forward(hidden, gain_one).astype(jnp.bfloat16)
    query_raw = jnp.dot(first_normed, query_w, preferred_element_type=jnp.float32)
    unrotated_key = jnp.dot(first_normed, key_matrix, preferred_element_type=jnp.float32)
    value_raw = jnp.dot(first_normed, value_matrix, preferred_element_type=jnp.float32)
    query_rows = (
        rotary_embed(
            query_raw.reshape(local_rows, QUERY_HEADS, HEAD_SIZE), cosine_table, sine_table
        )
        .astype(jnp.bfloat16)
        .reshape(local_rows, KEY_VALUE_HEADS, query_groups, HEAD_SIZE)
    )
    keys_flat = (
        rotary_embed(
            unrotated_key.reshape(local_rows, KEY_VALUE_HEADS, HEAD_SIZE), cosine_table, sine_table
        )
        .astype(jnp.bfloat16)
        .reshape(local_rows, KEY_VALUE_HEADS * HEAD_SIZE)
    )
    values_flat = value_raw.astype(jnp.bfloat16)
    key_pos_all = lax.all_gather(query_pos, "ctx", axis=0, tiled=True)
    sequence_length = key_pos_all.shape[0]

    def masked_scores(partial_keys, first):
        block_count = partial_keys.shape[0]
        key_pos = lax.dynamic_slice_in_dim(key_pos_all, first, block_count)
        scores = (
            jnp.einsum(
                "tkgd,nkd->kgtn",
                query_rows,
                partial_keys.reshape(block_count, KEY_VALUE_HEADS, HEAD_SIZE),
                preferred_element_type=jnp.float32,
            )
            * scale
        )
        visible = key_pos[None, None, None, :] <= query_pos[None, None, :, None]
        return jnp.where(visible, scores, -jnp.inf)

    def forward_part(carry, part, first):
        top, denom, accum = carry
        partial_keys, partial_values = part
        block_count = partial_keys.shape[0]
        scores = masked_scores(partial_keys, first)
        new_top = jnp.maximum(top, jnp.max(scores, -1))
        weights = jnp.exp(scores - new_top[..., None])
        factor = jnp.exp(top - new_top)
        denom = denom * factor + jnp.sum(weights, -1)
        accum = accum * factor[..., None] + jnp.einsum(
            "kgtn,nkd->kgtd",
            weights.astype(jnp.bfloat16),
            partial_values.reshape(block_count, KEY_VALUE_HEADS, HEAD_SIZE),
            preferred_element_type=jnp.float32,
        )
        return (new_top, denom, accum)

    start_state = (
        jnp.full((KEY_VALUE_HEADS, query_groups, local_rows), -1e30, jnp.float32),
        jnp.zeros((KEY_VALUE_HEADS, query_groups, local_rows), jnp.float32),
        jnp.zeros((KEY_VALUE_HEADS, query_groups, local_rows, HEAD_SIZE), jnp.float32),
    )
    top, denom, accum = over_blocks(
        forward_part,
        start_state,
        (
            lax.all_gather(keys_flat, "ctx", axis=0, tiled=True),
            lax.all_gather(values_flat, "ctx", axis=0, tiled=True),
        ),
    )
    attended_output = accum / denom[..., None]
    log_total = top + jnp.log(denom)
    attended_low = (
        attended_output.transpose(2, 0, 1, 3)
        .reshape(local_rows, QUERY_HEADS * HEAD_SIZE)
        .astype(jnp.bfloat16)
    )
    mixed = hidden + jnp.dot(attended_low, out_w, preferred_element_type=jnp.float32)
    mlp_set = (
        lax.all_gather(mlp_gain, "fsdp", axis=0, tiled=True),
        lax.all_gather(w_gate, "fsdp", axis=0, tiled=True),
        lax.all_gather(w_up, "fsdp", axis=0, tiled=True),
        lax.all_gather(w_down, "fsdp", axis=0, tiled=True),
    )
    gain_two, gate_w, up_w, down_w = mlp_set
    normed_two = norm_forward(mixed, gain_two).astype(jnp.bfloat16)
    gate = jnp.dot(normed_two, gate_w, preferred_element_type=jnp.float32)
    up = jnp.dot(normed_two, up_w, preferred_element_type=jnp.float32)
    sigma = jax.nn.sigmoid(gate)
    active = (gate * sigma * up).astype(jnp.bfloat16)
    result = mixed + jnp.dot(active, down_w, preferred_element_type=jnp.float32)
    layer_out = result.astype(jnp.bfloat16)[None]
    grad_low = out_grad[0]
    grad_out = grad_low.astype(jnp.float32)
    gain_back, gate_back, up_back, down_back = (
        lax.all_gather(mlp_gain, "fsdp", axis=0, tiled=True),
        lax.all_gather(w_gate, "fsdp", axis=0, tiled=True),
        lax.all_gather(w_up, "fsdp", axis=0, tiled=True),
        lax.all_gather(w_down, "fsdp", axis=0, tiled=True),
    )
    down_grad = dot_first(active, grad_low)
    active_grad = dot_last(grad_low, down_back)
    gate_grad = (active_grad * up * sigma * (1.0 + gate * (1.0 - sigma))).astype(jnp.bfloat16)
    up_grad = (active_grad * gate * sigma).astype(jnp.bfloat16)
    gate_wgrad = dot_first(normed_two, gate_grad)
    up_wgrad = dot_first(normed_two, up_grad)
    normed_two_grad = dot_last(gate_grad, gate_back) + dot_last(up_grad, up_back)
    mixed_part, gain_two_grad = norm_back(mixed, gain_back, normed_two_grad)
    mixed_grad = grad_out + mixed_part
    mlp_shards = (
        lax.psum_scatter(
            gain_two_grad.astype(jnp.bfloat16), "fsdp", scatter_dimension=0, tiled=True
        ).astype(jnp.float32),
        lax.psum_scatter(
            gate_wgrad.astype(jnp.bfloat16), "fsdp", scatter_dimension=0, tiled=True
        ).astype(jnp.float32),
        lax.psum_scatter(
            up_wgrad.astype(jnp.bfloat16), "fsdp", scatter_dimension=0, tiled=True
        ).astype(jnp.float32),
        lax.psum_scatter(
            down_grad.astype(jnp.bfloat16), "fsdp", scatter_dimension=0, tiled=True
        ).astype(jnp.float32),
    )
    gain_first, query_back, key_back, value_back, out_back = (
        lax.all_gather(attn_gain, "fsdp", axis=0, tiled=True),
        lax.all_gather(w_query, "fsdp", axis=0, tiled=True),
        lax.all_gather(key_projection, "fsdp", axis=0, tiled=True),
        lax.all_gather(value_projection, "fsdp", axis=0, tiled=True),
        lax.all_gather(w_out, "fsdp", axis=0, tiled=True),
    )
    branch_grad = mixed_grad.astype(jnp.bfloat16)
    out_wgrad = dot_first(attended_low, branch_grad)
    attended_grad = (
        dot_last(branch_grad, out_back)
        .astype(jnp.bfloat16)
        .reshape(local_rows, KEY_VALUE_HEADS, query_groups, HEAD_SIZE)
        .transpose(1, 2, 0, 3)
    )
    delta = jnp.sum(attended_grad.astype(jnp.float32) * attended_output, -1)

    def backward_part(carry, part, first):
        query_acc, key_value_acc = carry
        partial_keys, partial_values = part
        block_count = partial_keys.shape[0]
        probs = jnp.exp(masked_scores(partial_keys, first) - log_total[..., None])
        gradient_of_value = jnp.einsum(
            "kgtn,kgtd->nkd",
            probs.astype(jnp.bfloat16),
            attended_grad,
            preferred_element_type=jnp.float32,
        )
        prob_grad = jnp.einsum(
            "kgtd,nkd->kgtn",
            attended_grad,
            partial_values.reshape(block_count, KEY_VALUE_HEADS, HEAD_SIZE),
            preferred_element_type=jnp.float32,
        )
        score_grad = (probs * (prob_grad - delta[..., None])).astype(jnp.bfloat16)
        query_acc = (
            query_acc
            + jnp.einsum(
                "kgtn,nkd->kgtd",
                score_grad,
                partial_keys.reshape(block_count, KEY_VALUE_HEADS, HEAD_SIZE),
                preferred_element_type=jnp.float32,
            )
            * scale
        )
        gradient_of_key = (
            jnp.einsum("kgtn,tkgd->nkd", score_grad, query_rows, preferred_element_type=jnp.float32)
            * scale
        )
        joined = jnp.concatenate(
            [
                gradient_of_key.reshape(block_count, KEY_VALUE_HEADS * HEAD_SIZE),
                gradient_of_value.reshape(block_count, KEY_VALUE_HEADS * HEAD_SIZE),
            ],
            1,
        )
        key_value_acc = lax.dynamic_update_slice_in_dim(key_value_acc, joined, first, 0)
        return (query_acc, key_value_acc)

    back_state = (
        jnp.zeros((KEY_VALUE_HEADS, query_groups, local_rows, HEAD_SIZE), jnp.float32),
        jnp.zeros((sequence_length, 2 * KEY_VALUE_HEADS * HEAD_SIZE), jnp.float32),
    )
    query_acc, key_value_acc = over_blocks(
        backward_part,
        back_state,
        (
            lax.all_gather(keys_flat, "ctx", axis=0, tiled=True),
            lax.all_gather(values_flat, "ctx", axis=0, tiled=True),
        ),
    )
    local_key_value = lax.psum_scatter(
        key_value_acc.astype(jnp.bfloat16), "ctx", scatter_dimension=0, tiled=True
    ).astype(jnp.float32)
    query_raw_grad = (
        rotary_embed_backward(
            query_acc.transpose(2, 0, 1, 3).reshape(local_rows, QUERY_HEADS, HEAD_SIZE),
            cosine_table,
            sine_table,
        )
        .reshape(local_rows, QUERY_HEADS * HEAD_SIZE)
        .astype(jnp.bfloat16)
    )
    key_raw_grad = (
        rotary_embed_backward(
            local_key_value[:, : KEY_VALUE_HEADS * HEAD_SIZE].reshape(
                local_rows, KEY_VALUE_HEADS, HEAD_SIZE
            ),
            cosine_table,
            sine_table,
        )
        .reshape(local_rows, KEY_VALUE_HEADS * HEAD_SIZE)
        .astype(jnp.bfloat16)
    )
    unrotated_value_gradient = local_key_value[:, KEY_VALUE_HEADS * HEAD_SIZE :].astype(
        jnp.bfloat16
    )
    query_wgrad = dot_first(first_normed, query_raw_grad)
    key_wgrad = dot_first(first_normed, key_raw_grad)
    value_wgrad = dot_first(first_normed, unrotated_value_gradient)
    normed_one_grad = (
        dot_last(query_raw_grad, query_back)
        + dot_last(key_raw_grad, key_back)
        + dot_last(unrotated_value_gradient, value_back)
    )
    input_part, gain_one_grad = norm_back(hidden, gain_first, normed_one_grad)
    input_grad = (mixed_grad + input_part).astype(jnp.bfloat16)[None]
    attn_shards = (
        lax.psum_scatter(
            gain_one_grad.astype(jnp.bfloat16), "fsdp", scatter_dimension=0, tiled=True
        ).astype(jnp.float32),
        lax.psum_scatter(
            query_wgrad.astype(jnp.bfloat16), "fsdp", scatter_dimension=0, tiled=True
        ).astype(jnp.float32),
        lax.psum_scatter(
            key_wgrad.astype(jnp.bfloat16), "fsdp", scatter_dimension=0, tiled=True
        ).astype(jnp.float32),
        lax.psum_scatter(
            value_wgrad.astype(jnp.bfloat16), "fsdp", scatter_dimension=0, tiled=True
        ).astype(jnp.float32),
        lax.psum_scatter(
            out_wgrad.astype(jnp.bfloat16), "fsdp", scatter_dimension=0, tiled=True
        ).astype(jnp.float32),
    )
    totals = (
        lax.psum(attn_shards[0].astype(jnp.bfloat16), "ctx").astype(jnp.float32),
        lax.psum(attn_shards[1].astype(jnp.bfloat16), "ctx").astype(jnp.float32),
        lax.psum(attn_shards[2].astype(jnp.bfloat16), "ctx").astype(jnp.float32),
        lax.psum(attn_shards[3].astype(jnp.bfloat16), "ctx").astype(jnp.float32),
        lax.psum(attn_shards[4].astype(jnp.bfloat16), "ctx").astype(jnp.float32),
        lax.psum(mlp_shards[0].astype(jnp.bfloat16), "ctx").astype(jnp.float32),
        lax.psum(mlp_shards[1].astype(jnp.bfloat16), "ctx").astype(jnp.float32),
        lax.psum(mlp_shards[2].astype(jnp.bfloat16), "ctx").astype(jnp.float32),
        lax.psum(mlp_shards[3].astype(jnp.bfloat16), "ctx").astype(jnp.float32),
    )
    return (
        layer_out,
        input_grad,
        totals[0],
        totals[1],
        totals[2],
        totals[3],
        totals[4],
        totals[5],
        totals[6],
        totals[7],
        totals[8],
    )


MESH = pl.DeviceIdType.MESH
ANY = pl.ANY
VMEM = pltpu.VMEM
DMA = pltpu.SemaphoreType.DMA
LANES = 128
BLOCK = 128
F32 = jnp.float32
BF16 = jnp.bfloat16
VMEM_BYTES = 60 * 2**20


def flip(c, k):
    out = c
    for b in (1, 2, 4):
        if k & b:
            out = out + b - 2 * b * ((c // b) % 2)
    return out


def remote(src, dst, send, recv, **to):
    return pltpu.make_async_remote_copy(
        src_ref=src, dst_ref=dst, send_sem=send, recv_sem=recv, device_id=to, device_id_type=MESH
    )


def greet(peers):
    barrier = pltpu.get_barrier_semaphore()
    for peer in peers:
        pl.semaphore_signal(barrier, inc=1, device_id=peer, device_id_type=MESH)
    pl.semaphore_wait(barrier, len(peers))


class Gather:
    def __init__(self, c, own, buf, at, send, recv):
        self.c, self.own, self.buf, self.at, self.send, self.recv = c, own, buf, at, send, recv
        self.pending = []

    def start(self, channel, who, to, h, own=False):
        there = self.at(self.buf, flip(self.c, who), h)
        d = remote(
            self.own(h) if own else there,
            there,
            self.send.at[channel, h],
            self.recv.at[channel, h],
            ctx=flip(self.c, to),
        )
        d.start()
        self.pending.append(d)

    def arrived(self, channel, who, frm, h):
        ref = self.at(self.buf, flip(self.c, who), h)
        remote(
            ref, ref, self.send.at[channel, h], self.recv.at[channel, h], ctx=flip(self.c, frm)
        ).wait_recv()

    def begin(self):
        self.begin_half()
        self.begin_rest()

    def begin_half(self):
        self.start(1, 0, 2, 0, own=True)
        self.start(2, 0, 4, 1, own=True)

    def begin_rest(self):
        self.start(1, 0, 2, 1, own=True)
        self.start(2, 0, 4, 0, own=True)
        self.start(0, 0, 1, 0, own=True)
        self.start(0, 0, 1, 1, own=True)

    def near_half(self):
        self.arrived(1, 2, 2, 0)
        self.start(6, 2, 4, 0)
        self.start(3, 2, 1, 0)
        self.arrived(2, 4, 4, 1)
        self.start(7, 4, 2, 1)
        self.start(4, 4, 1, 1)

    def near_rest(self):
        self.arrived(1, 2, 2, 1)
        self.start(3, 2, 1, 1)
        self.arrived(2, 4, 4, 0)
        self.start(4, 4, 1, 0)

    def far(self):
        self.arrived(6, 6, 4, 0)
        self.start(5, 6, 1, 0)
        self.arrived(7, 6, 2, 1)
        self.start(5, 6, 1, 1)

    def paired(self, channel, who):
        for h in (0, 1):
            self.arrived(channel, who, 1, h)

    def finish(self):
        self.near_half()
        self.near_rest()
        self.far()
        for channel, who in ((0, 1), (3, 3), (4, 5), (5, 7)):
            self.paired(channel, who)

    def sent(self):
        for d in self.pending:
            d.wait_send()


def row_half(ref, d, h):
    half = ref.shape[1] // 2
    return ref.at[d, pl.ds(h * half, half)]


def column_half(ref, d, h):
    half = ref.shape[2] // 2
    return ref.at[d, :, pl.ds(h * half, half)]


def own_half(ref, axis=0):
    half = ref.shape[axis] // 2
    return lambda h: ref.at[(slice(None),) * axis + (pl.ds(h * half, half),)]


class Line:
    def __init__(self, z, depth, at, send, recv, own=None):
        self.z, self.depth, self.at, self.send, self.recv, self.own = z, depth, at, send, recv, own

    def copy(self, way, k, part, to):
        ref = self.at(part)
        source = ref if k or self.own is None else self.own
        return remote(source, ref, self.send.at[way, k], self.recv.at[way, k], fsdp=to)

    def step(self, k):
        z, top = self.z, self.depth - 1

        @pl.when((z >= k) & (z < top))
        def _():
            self.copy(0, k, z - k, z + 1).start()

        @pl.when((z + k <= top) & (z > 0))
        def _():
            self.copy(1, k, z + k, z - 1).start()

    def landed(self, k):
        z, top = self.z, self.depth - 1

        @pl.when(z >= k + 1)
        def _():
            self.copy(0, k, z - 1 - k, z - 1).wait_recv()

        @pl.when(z + 1 + k <= top)
        def _():
            self.copy(1, k, z + 1 + k, z + 1).wait_recv()

    def sent(self, steps):
        z, top = self.z, self.depth - 1
        for k in steps:

            @pl.when((z >= k) & (z < top))
            def _():
                self.copy(0, k, z - k, z + 1).wait_send()

            @pl.when((z + k <= top) & (z > 0))
            def _():
                self.copy(1, k, z + k, z - 1).wait_send()


def params(cid):
    return pltpu.CompilerParams(
        collective_id=cid, has_side_effects=True, vmem_limit_bytes=VMEM_BYTES
    )


def contract(a, b, dims):
    return lax.dot_general(a, b, ((dims[0], dims[1]), ((), ())), preferred_element_type=F32)


def lanes(start, size):
    return pl.ds(pl.multiple_of(start, LANES), size)


def turned(u, cosine, sine):
    half = HEAD_SIZE // 2
    a, b = u[:half], u[half:]
    return jnp.concatenate([a * cosine - b * sine, b * cosine + a * sine], 0)


def picked(weight, first, count):
    shape = (count, weight.shape[1])
    hit = lax.broadcasted_iota(jnp.int32, shape, 1) == first + lax.broadcasted_iota(jnp.int32, shape, 0)
    return contract(hit.astype(BF16), weight, ((1,), (1,))).astype(BF16)


CHUNK = 512


def two_heads(ref, block):
    return jnp.concatenate([ref[block, :HEAD_SIZE], ref[block, HEAD_SIZE : 2 * HEAD_SIZE]], 1)


def causal(s, t, j):
    key = t * CHUNK + lax.broadcasted_iota(jnp.int32, s.shape, 0)
    query = j * BLOCK + lax.broadcasted_iota(jnp.int32, s.shape, 1) % BLOCK
    return jnp.where(key <= query, s, -jnp.inf)


def exchange_start(c, source, target, send, recv):
    sent = []
    for k in (6, 7, 2, 4, 3, 5, 1):
        there = target.at[pl.ds(2 * c, 2)]
        d = remote(source.at[pl.ds(2 * flip(c, k), 2)], there, send.at[k], recv.at[k], ctx=flip(c, k))
        d.start()
        sent.append(d)
    return sent


def exchange_landed(c, target, send, recv):
    for k in (6, 7, 2, 4, 3, 5, 1):
        ref = target.at[pl.ds(2 * flip(c, k), 2)]
        remote(ref, ref, send.at[k], recv.at[k], ctx=flip(c, k)).wait_recv()


def first_kernel(
    pos_ref, x_ref, gain_one_ref, gain_two_ref, freq_ref, step_ref, wq_ref, wk_ref, wv_ref, wo_ref, wg_ref, wu_ref, wd_ref, grad_ref,
    all_ref, qkv_ref, w_ref, table_ref, gains_ref, order_ref, rank_ref, low_ref, lse_ref, got_ref, ow_all, gu_all, down_all, grad_all,
    give, infos_ref, infos, wo_all, keys, values, xs, wz, whole, gu_own, out_mine, down_mine, grad_mine, bases, gain_ref, info_ref, base_ref, gsend, grecv, isend, irecv, bsend, brecv, send, recv, zsend, zrecv, osend, orecv,
    usend, urecv, dsend, drecv, send2, recv2, send3, recv3, local, esend, erecv, parts,
):
    c = lax.axis_index("ctx")
    z = lax.axis_index("fsdp")
    depth = gains_ref.shape[0]
    shard, width = wq_ref.shape
    rows = x_ref.shape[0]
    strip = gu_all.shape[2] // 2 // depth
    down_rows = down_all.shape[1]
    others = [lax.rem(z + k, depth) for k in range(1, depth)]
    lane = lax.broadcasted_iota(jnp.int32, info_ref.shape, 1)
    info_ref[...] = jnp.where(lane < LANES // 2, pos_ref[0, 0], pos_ref[0, BLOCK])
    start = freq_ref[...] * info_ref[:1].astype(F32)
    base_ref[...] = jnp.where(lane[:1] // (LANES // 4) % 2 == 0, jnp.cos(start), jnp.sin(start))
    gain_ref[:4] = jnp.broadcast_to(gain_one_ref[...].astype(F32)[None], (4, shard))
    gain_ref[4:] = jnp.broadcast_to(gain_two_ref[...].astype(F32)[None], (4, shard))
    greet([{"ctx": flip(c, k)} for k in range(1, 8)] + [{"fsdp": o} for o in others])

    g2 = Gather(c, own_half(grad_ref), grad_all, row_half, send2, recv2)
    g2.begin_half()
    sent = []
    for k, o in enumerate(others):
        sent.append(remote(gain_ref, gains_ref.at[z], gsend.at[k], grecv.at[k], fsdp=o))
    for k in range(1, 8):
        sent.append(remote(info_ref, infos_ref.at[c], isend.at[k], irecv.at[k], ctx=flip(c, k)))
        sent.append(remote(base_ref, bases.at[c], bsend.at[k], brecv.at[k], ctx=flip(c, k)))
    for d in sent:
        d.start()
    out_rows = shard // 8
    out_own = wo_ref.at[pl.ds(c * out_rows, out_rows)]
    down_own = wd_ref.at[pl.ds(c * down_rows, down_rows)]
    strips = [
        pltpu.make_async_copy(weight, whole.at[i], parts.at[4 + i]) for i, weight in enumerate((wg_ref, wu_ref))
    ]
    for d in strips:
        d.start()
    ways = ((out_own, out_mine, ow_all.at[z, c]), (down_own, down_mine, down_all.at[z]), (grad_ref, grad_mine, grad_all.at[c]))
    incoming = [pltpu.make_async_copy(a, b, parts.at[i]) for i, (a, b, _) in enumerate(ways)]
    for d in incoming:
        d.start()
    gains_ref[z] = gain_ref[...]
    infos_ref[c] = info_ref[...]
    bases[c] = base_ref[...]

    count = 2 * HEAD_SIZE
    wz[z, :count] = picked(wq_ref[...], c * count, count)
    wz[z, count : count + HEAD_SIZE] = picked(wk_ref[...], c * HEAD_SIZE, HEAD_SIZE)
    wz[z, count + HEAD_SIZE :] = picked(wv_ref[...], c * HEAD_SIZE, HEAD_SIZE)
    line = Line(z, depth, lambda d: wz.at[d], zsend, zrecv)
    line.step(0)

    x = x_ref[...].astype(F32)
    factor = lax.rsqrt(jnp.mean(x * x, -1, keepdims=True) + EPS)
    for k in range(depth - 1):
        ref = gains_ref.at[lax.rem(z + depth - 1 - k, depth)]
        remote(ref, ref, gsend.at[k], grecv.at[k], fsdp=others[k]).wait_recv()
    gain = jnp.concatenate([gains_ref[k, 0:1, :] for k in range(depth)], 1)
    xs[c] = (x * factor * gain).astype(BF16)
    g = Gather(c, own_half(xs.at[c]), xs, row_half, send, recv)
    g.begin()
    out_line = Line(z, depth, lambda d: wo_all.at[d], osend, orecv, out_own)
    down_line = Line(z, depth, lambda d: down_all.at[d], dsend, drecv, down_own)
    out_line.step(0)
    copies = []
    for i, (_, b, there) in enumerate(ways):
        incoming[i].wait()
        copies.append(pltpu.make_async_copy(b, there, parts.at[i]))
        copies[-1].start()
    wo_all[z] = out_mine[...]

    def keep(k):
        d = pltpu.make_async_copy(xs.at[flip(c, k)], all_ref.at[flip(c, k)], local.at[k])
        d.start()
        copies.append(d)

    keep(0)

    def rotary(k):
        d = flip(c, k)
        if k:
            for ref, s, r in ((bases, bsend, brecv), (infos_ref, isend, irecv)):
                remote(ref.at[d], ref.at[d], s.at[k], r.at[k], ctx=d).wait_recv()
        half = HEAD_SIZE // 2
        step_cos, step_sin = step_ref[:half], step_ref[half:]
        for b in (0, 1):
            start = b * (LANES // 2)
            base_cos = bases[d, :, start : start + 1]
            base_sin = bases[d, :, start + LANES // 4 : start + LANES // 4 + 1]
            table_ref[2 * d + b, :half] = base_cos * step_cos - base_sin * step_sin
            table_ref[2 * d + b, half:] = base_sin * step_cos + base_cos * step_sin

    for k in range(8):
        rotary(k)

    def project(k):
        d = flip(c, k)
        half = HEAD_SIZE // 2
        raw = contract(w_ref[...], xs[d], ((1,), (1,)))
        for b in (0, 1):
            cosine, sine = table_ref[2 * d + b, :half], table_ref[2 * d + b, half:]
            part = raw[:, b * BLOCK : (b + 1) * BLOCK]
            for h in range(3):
                head = slice(h * HEAD_SIZE, (h + 1) * HEAD_SIZE)
                qkv_ref[2 * d + b, head] = turned(part[head], cosine, sine).astype(BF16)
            qkv_ref[2 * d + b, 3 * HEAD_SIZE :] = part[3 * HEAD_SIZE :].astype(BF16)

    line.landed(0)
    line.step(1)
    g.near_half()
    g2.begin_rest()
    out_line.landed(0)
    out_line.step(1)
    line.landed(1)
    line.step(2)
    g.near_rest()
    keep(2)
    keep(4)
    out_line.landed(1)
    out_line.step(2)
    for i, d in enumerate(strips):
        d.wait()
        for f in range(depth):
            gu_own[:, (i * depth + f) * strip : (i * depth + f + 1) * strip] = whole[i, :, lanes((f * 8 + c) * strip, strip)]
    gu_line = Line(z, depth, lambda d: gu_all.at[d], usend, urecv, gu_own)
    gu_line.step(0)
    down_line.step(0)
    copies.append(pltpu.make_async_copy(gu_own, gu_all.at[z], parts.at[3]))
    copies[-1].start()
    line.landed(2)
    for f in range(depth):
        w_ref[:, f * shard : (f + 1) * shard] = wz[f]
    g.far()
    g2.near_half()
    project(0)
    project(2)
    project(4)
    for channel, k in ((0, 1), (3, 3), (4, 5)):
        g.paired(channel, k)
        keep(k)
        project(k)
    keep(6)
    project(6)
    g.paired(5, 7)
    keep(7)
    project(7)
    out_line.landed(2)
    few = depth // 2
    g3 = Gather(
        c,
        lambda h: wo_all.at[pl.ds(h * few, few)],
        ow_all,
        lambda ref, d, h: ref.at[pl.ds(h * few, few), d],
        send3,
        recv3,
    )
    g3.begin()
    for f in range(1, depth):
        part = lax.rem(z + f, depth)
        copies.append(pltpu.make_async_copy(wo_all.at[part], ow_all.at[part, c], parts.at[4 + f]))
        copies[-1].start()

    blocks = qkv_ref.shape[0]
    per = CHUNK // BLOCK
    factor = HEAD_SIZE ** (-0.5) * math.log2(math.e)
    small = pltpu.make_async_copy(infos_ref, infos, parts.at[8])
    small.start()
    small.wait()
    starts = [infos[b // 2, 0, b % 2 * (LANES // 2)] for b in range(blocks)]
    least = functools.reduce(jnp.minimum, starts)
    ranks = [(start - least) // BLOCK for start in starts]
    for i in range(blocks):
        rank_ref[i] = ranks[i]
        order_ref[i] = functools.reduce(jnp.maximum, [jnp.where(ranks[b] == i, b, 0) for b in range(blocks)])
    for b in range(blocks):
        there = slice(b * BLOCK, (b + 1) * BLOCK)
        keys[there, :] = qkv_ref[order_ref[b], 2 * HEAD_SIZE : 3 * HEAD_SIZE].T
        values[:, there] = qkv_ref[order_ref[b], 3 * HEAD_SIZE :]

    def attend_block(j, last):
        q = two_heads(qkv_ref, order_ref[j])

        def step(t, carry, masked):
            top, denom, acc = carry
            s = jnp.dot(keys[pl.ds(t * CHUNK, CHUNK), :], q, preferred_element_type=F32)
            if masked:
                s = causal(s, t, j)
            new_top = jnp.maximum(top, jnp.max(s, 0, keepdims=True))
            p = jnp.exp2((s - new_top) * factor)
            shrink = jnp.exp2((top - new_top) * factor)
            denom = denom * shrink + jnp.sum(p, 0, keepdims=True)
            acc = acc * shrink + jnp.dot(
                values[:, pl.ds(t * CHUNK, CHUNK)], p.astype(BF16), preferred_element_type=F32
            )
            return new_top, denom, acc

        carry = (
            jnp.full((1, 2 * BLOCK), -1e30, F32),
            jnp.zeros((1, 2 * BLOCK), F32),
            jnp.zeros((HEAD_SIZE, 2 * BLOCK), F32),
        )
        for t in range(last):
            carry = step(t, carry, False)
        top, denom, acc = step(last, carry, True)
        out = acc / denom
        lse_ref[pl.ds(j, 1), :, :] = (top * factor + jnp.log2(denom)).reshape(1, 1, 2 * BLOCK)
        for h in (0, 1):
            head = slice(h * HEAD_SIZE, (h + 1) * HEAD_SIZE)
            low_ref[j, head] = out[:, h * BLOCK : (h + 1) * BLOCK].astype(BF16)

    def attend_blocks(first, count):
        @pl.loop(first, first + count)
        def _(j):
            attend_block(j, first // per)

    attend_blocks(0, per)
    g2.near_rest()
    attend_blocks(per, per)
    gu_line.landed(0)
    gu_line.step(1)
    attend_blocks(2 * per, per // 2)
    g2.far()
    attend_blocks(2 * per + per // 2, per // 2)
    g3.near_half()
    attend_blocks(3 * per, per // 2)
    g3.near_rest()
    attend_blocks(3 * per + per // 2, per // 2)
    for i in range(blocks):
        give[i] = low_ref[rank_ref[i]]
    sent += exchange_start(c, give, got_ref, esend, erecv)
    got_ref[pl.ds(2 * c, 2)] = give[pl.ds(2 * c, 2)]
    g3.far()
    for gather in (g2, g3):
        for channel, k in ((0, 1), (3, 3), (4, 5), (5, 7)):
            gather.paired(channel, k)
    exchange_landed(c, got_ref, esend, erecv)
    gu_line.landed(1)
    down_line.landed(0)
    for d in copies:
        d.wait()
    for d in sent:
        d.wait_send()
    line.sent((0, 1, 2))
    out_line.sent((0, 1, 2))
    gu_line.sent((0, 1))
    down_line.sent((0,))
    for gather in (g, g2, g3):
        gather.sent()


def first_part(positions, x, gains, freq, step, weights, grad, depth, cid):
    rows, width = x.shape
    shard = gains[0].shape[0]
    small = (8, shard)
    columns = weights[4].shape[1]
    down_rows = weights[6].shape[0] // 8
    blocks = 8 * rows // BLOCK
    sm = pl.BlockSpec(memory_space=pltpu.SMEM)
    vm = pl.BlockSpec(memory_space=VMEM)
    hbm = pl.BlockSpec(memory_space=ANY)
    shape = jax.ShapeDtypeStruct
    return pl.pallas_call(
        first_kernel,
        out_shape=(
            shape((8, rows, width), BF16),
            shape((8 * rows // BLOCK, 4 * HEAD_SIZE, BLOCK), BF16),
            shape((4 * HEAD_SIZE, width), BF16),
            shape((8 * rows // BLOCK, HEAD_SIZE, BLOCK), F32),
            shape((depth,) + small, F32),
            shape((blocks,), jnp.int32),
            shape((blocks,), jnp.int32),
            shape((blocks, 2 * HEAD_SIZE, BLOCK), BF16),
            shape((blocks, 1, 2 * BLOCK), F32),
            shape((blocks, 2 * HEAD_SIZE, BLOCK), BF16),
            shape((depth, 8, shard // 8, width), BF16),
            shape((depth, shard, 2 * columns // 8), BF16),
            shape((depth, down_rows, width), BF16),
            shape((8, rows, width), BF16),
        ),
        in_specs=[pl.BlockSpec(memory_space=pltpu.SMEM)] + [vm] * 8 + [hbm] * 5,
        out_specs=(hbm, vm, vm, vm, vm, sm, sm, vm, vm, vm, hbm, hbm, hbm, hbm),
        scratch_shapes=[
            VMEM((blocks, 2 * HEAD_SIZE, BLOCK), BF16),
            VMEM((8, 8, LANES), jnp.int32),
            pltpu.SMEM((8, 8, LANES), jnp.int32),
            VMEM((depth, shard // 8, width), BF16),
            VMEM((8 * rows, HEAD_SIZE), BF16),
            VMEM((HEAD_SIZE, 8 * rows), BF16),
            VMEM((8, rows, width), BF16),
            VMEM((depth, 4 * HEAD_SIZE, shard), BF16),
            VMEM((2, shard, columns), BF16),
            VMEM((shard, 2 * columns // 8), BF16),
            VMEM((shard // 8, width), BF16),
            VMEM((down_rows, width), BF16),
            VMEM((rows, width), BF16),
            VMEM((8, HEAD_SIZE // 2, LANES), F32),
            VMEM(small, F32),
            VMEM((8, LANES), jnp.int32),
            VMEM((HEAD_SIZE // 2, LANES), F32),
            DMA((depth,)),
            DMA((depth,)),
            DMA((8,)),
            DMA((8,)),
            DMA((8,)),
            DMA((8,)),
            DMA((8, 2)),
            DMA((8, 2)),
        ]
        + [DMA((2, depth))] * 8
        + [DMA((8, 2))] * 4
        + [DMA((8,))] * 3
        + [DMA((9,))],
        compiler_params=params(cid),
        name="first_part",
    )(positions, x, *gains, freq, step, *weights, grad)


class Scatter:
    ORDER = (6, 2, 4, 0)

    def __init__(self, c, p, first, last, diagonal, s1, v1, s2, v2):
        self.c, self.p, self.first = c, p, first
        self.last, self.diagonal = last, diagonal
        self.s1, self.v1, self.s2, self.v2 = s1, v1, s2, v2
        self.half = first.shape[1] // 2 if p is None else p.shape[1] // 2
        self.pending = []
        self.gifts = []
        self.summed = False

    @staticmethod
    def scratch(rows, width):
        return [
            VMEM((4, rows, width), BF16),
            VMEM((2, rows, width), BF16),
            VMEM((rows, width), BF16),
            DMA((4, 2)),
            DMA((4, 2)),
            DMA((3, 2)),
            DMA((3, 2)),
        ]

    def sl(self, q):
        return pl.ds(q * self.half, self.half)

    def go(self, d):
        d.start()
        self.pending.append(d)

    def give(self, k):
        j = self.ORDER.index(k)
        for q in (0, 1):
            source = self.p.at[flip(self.c, 1 ^ k), self.sl(q)]
            there = self.first.at[j, self.sl(q)]
            d = remote(source, there, self.s1.at[j, q], self.v1.at[j, q], ctx=flip(self.c, 1))
            d.start()
            self.gifts.append(d)

    def given(self):
        for d in self.gifts:
            d.wait_send()
        self.gifts = []

    def paired(self, j, q):
        if self.summed:
            return
        ref = self.first.at[j, self.sl(q)]
        remote(ref, ref, self.s1.at[j, q], self.v1.at[j, q], ctx=flip(self.c, 1)).wait_recv()

    def chip(self, j, q):
        if self.summed:
            return self.first[j, self.sl(q)].astype(F32)
        k = self.ORDER[j]
        return self.p[flip(self.c, k), self.sl(q)].astype(F32) + self.first[j, self.sl(q)].astype(F32)

    def came(self, channel, ref, q, frm):
        remote(
            ref, ref, self.s2.at[channel, q], self.v2.at[channel, q], ctx=flip(self.c, frm)
        ).wait_recv()

    def far(self):
        for q, to in ((0, 2), (1, 4)):
            self.paired(0, q)
            self.first[0, self.sl(q)] = self.chip(0, q).astype(BF16)
            self.go(
                remote(
                    self.first.at[0, self.sl(q)],
                    self.diagonal.at[self.sl(q)],
                    self.s2.at[2, q],
                    self.v2.at[2, q],
                    ctx=flip(self.c, to),
                )
            )

    def onward(self, j, q, merged):
        v = self.chip(j, q)
        if merged:
            v = v + self.diagonal[self.sl(q)].astype(F32)
        self.first[j, self.sl(q)] = v.astype(BF16)
        self.go(
            remote(
                self.first.at[j, self.sl(q)],
                self.last.at[j - 1, self.sl(q)],
                self.s2.at[j - 1, q],
                self.v2.at[j - 1, q],
                ctx=flip(self.c, self.ORDER[j]),
            )
        )

    def direct(self):
        self.paired(1, 0)
        self.onward(1, 0, False)
        self.paired(2, 1)
        self.onward(2, 1, False)

    def merged(self):
        self.paired(2, 0)
        self.came(2, self.diagonal.at[self.sl(0)], 0, 2)
        self.onward(2, 0, True)
        self.paired(1, 1)
        self.came(2, self.diagonal.at[self.sl(1)], 1, 4)
        self.onward(1, 1, True)

    def settle(self):
        for j, q in ((2, 0), (1, 1), (3, 0), (3, 1)):
            self.paired(j, q)
            self.first[j, self.sl(q)] = self.chip(j, q).astype(BF16)
        self.summed = True

    def result(self, q):
        self.paired(3, q)
        self.came(0, self.last.at[0, self.sl(q)], q, 2)
        self.came(1, self.last.at[1, self.sl(q)], q, 4)
        return self.chip(3, q) + (
            self.last[0, self.sl(q)].astype(F32) + self.last[1, self.sl(q)].astype(F32)
        )

    def sent(self):
        self.given()
        for d in self.pending:
            d.wait_send()


def both_blocks(ref, i):
    return jnp.concatenate([ref[2 * i], ref[2 * i + 1]], 1)


def middle_kernel(
    got, x_ref, gains_ref, g_ref, ow_ref, gu_in, down_in,
    layer_ref, mgrad_ref, gsum_ref, give, owg_ref, gug_ref, dg_ref, left_ref, right_ref, gu_all, down_all,
    mixed_ref, p1, wgu, wd, grads, two, p2, act, dgu, *rest,
):
    scatter_refs, layer_refs = rest[:7], rest[7:14]
    send, recv, usend, urecv, dsend, drecv, load, wput, hsend, hrecv = rest[14:]
    c = lax.axis_index("ctx")
    z = lax.axis_index("fsdp")
    depth, shard, both = gu_all.shape
    mine = both // 2
    rows, width = x_ref.shape
    out_rows = ow_ref.shape[1]
    out_w = p1.at[:, pl.ds(0, out_rows)]
    others = [lax.rem(z + k, depth) for k in range(1, depth)]
    greet([{"ctx": flip(c, k)} for k in (1, 2, 4)] + [{"fsdp": o} for o in others])
    gu_line = Line(z, depth, lambda d: gu_all.at[d], usend, urecv)
    down_line = Line(z, depth, lambda d: down_all.at[d], dsend, drecv)
    down_line.step(1)
    gu_line.step(2)
    loads = [
        pltpu.make_async_copy(ow_ref, out_w, load.at[0]),
        pltpu.make_async_copy(g_ref, grads, load.at[1]),
        pltpu.make_async_copy(x_ref, two.at[c], load.at[2]),
    ]
    for d in loads:
        d.start()

    loads[0].wait()
    loads[2].wait()
    mixed_ref[...] = two[c].astype(F32)

    @pl.loop(0, 8)
    def _(i):
        mixed_ref[...] += contract(both_blocks(got, i), p1[i, :out_rows], ((0,), (0,)))

    gain = jnp.concatenate([gains_ref[k, 4:5, :] for k in range(depth)], 1)
    halves = [pl.ds(q * (rows // 2), rows // 2) for q in (0, 1)]
    for at in halves:
        x = mixed_ref[at]
        factor = lax.rsqrt(jnp.mean(x * x, -1, keepdims=True) + EPS)
        two[c, at] = (x * factor * gain).astype(BF16)
    g = Gather(c, own_half(two.at[c]), two, row_half, send, recv)
    g.begin()
    loads[1].wait()
    down_line.landed(1)
    down_line.step(2)

    def pair(k):
        chip = pl.ds(flip(c, k) // 2 * 2, 2)
        tall = 2 * rows
        up_w = wgu[...].reshape(width, both)
        down_w = wd[...].reshape(mine, width)
        gate_up = jnp.dot(two[chip].reshape(tall, width), up_w, preferred_element_type=F32)
        gate, up = gate_up[:, :mine], gate_up[:, mine:]
        sigma = jax.nn.sigmoid(gate)
        silu = gate * sigma
        active = (silu * up).astype(BF16)
        act[chip] = active.reshape(2, rows, mine)
        active_grad = contract(grads[chip].reshape(tall, width), down_w, ((1,), (1,)))
        gate_grad = active_grad * up * sigma * (1.0 + gate * (1.0 - sigma))
        up_grad = active_grad * silu
        grad = jnp.concatenate([gate_grad, up_grad], 1).astype(BF16)
        dgu[chip] = grad.reshape(2, rows, both)
        p2[chip] = contract(grad, up_w, ((1,), (1,))).astype(BF16).reshape(2, rows, width)
        scatter.give(k)
        p1[chip] = jnp.dot(active, down_w, preferred_element_type=F32).astype(BF16).reshape(2, rows, width)
        layer.give(k)

    scatter = Scatter(c, p2, *scatter_refs)
    layer = Scatter(c, p1, *layer_refs)
    g.near_half()
    gu_line.landed(2)
    weights = [pltpu.make_async_copy(gu_all, wgu, load.at[2]), pltpu.make_async_copy(down_all, wd, load.at[3])]
    weights[0].start()
    g.near_rest()
    down_line.landed(2)
    weights[1].start()
    g.far()
    for d in weights:
        d.wait()
    g.paired(5, 7)
    pair(6)
    g.paired(3, 3)
    scatter.far()
    pair(2)
    scatter.paired(1, 0)
    scatter.onward(1, 0, False)
    layer.far()
    g.paired(4, 5)
    pair(4)
    scatter.paired(2, 1)
    scatter.onward(2, 1, False)
    g.paired(0, 1)
    pair(0)

    puts = []

    def wide(f):
        part = lambda i, total: total + contract(
            two[pl.ds(2 * i, 2), :, f * shard : (f + 1) * shard].reshape(2 * rows, shard),
            dgu[pl.ds(2 * i, 2)].reshape(2 * rows, both),
            ((0,), (0,)),
        )
        wgu[f] = lax.fori_loop(0, 4, part, jnp.zeros((shard, both), F32)).astype(BF16)
        puts.append(pltpu.make_async_copy(wgu.at[f], gug_ref.at[f], wput.at[f]))
        puts[-1].start()

    wide(0)
    scatter.merged()
    layer.direct()
    layer.settle()
    layer.given()
    again = pltpu.make_async_copy(ow_ref, out_w, load.at[0])
    again.start()
    for f in range(1, depth):
        wide(f)

    hop_right = remote(wgu.at[depth - 1], left_ref, hsend.at[0], hrecv.at[0], fsdp=z + 1)
    hop_left = remote(wgu.at[0], right_ref, hsend.at[1], hrecv.at[1], fsdp=z - 1)

    @pl.when(z == 0)
    def _():
        hop_right.start()

    @pl.when(z == depth - 1)
    def _():
        hop_left.start()

    strip = mine // depth
    for f in range(0, depth, 2):
        part = lambda i, total: total + contract(
            act[pl.ds(2 * i, 2), :, f * strip : (f + 2) * strip].reshape(2 * rows, 2 * strip),
            grads[pl.ds(2 * i, 2)].reshape(2 * rows, width),
            ((0,), (0,)),
        )
        part = lax.fori_loop(0, 4, part, jnp.zeros((2 * strip, width), F32))
        wd[f : f + 2] = part.astype(BF16).reshape(2, strip, width)
    puts.append(pltpu.make_async_copy(wd, dg_ref, wput.at[depth]))
    puts[-1].start()

    g.sent()
    gain_sum = jnp.zeros((1, width), F32)
    for q, at in enumerate(halves):
        two_grad = scatter.result(q)
        x = mixed_ref[at]
        factor = lax.rsqrt(jnp.mean(x * x, -1, keepdims=True) + EPS)
        gain_sum = gain_sum + jnp.sum(two_grad * x * factor, 0, keepdims=True)
        scaled = two_grad * gain
        mixed_grad = (
            grads[c, at].astype(F32)
            + factor * scaled
            - x * (factor * factor * factor) * jnp.mean(scaled * x, -1, keepdims=True)
        )
        mgrad_ref[at] = mixed_grad
        two[0, at] = mixed_grad.astype(BF16)
    gsum_ref[...] = jnp.broadcast_to(gain_sum, gsum_ref.shape)
    again.wait()
    for i in range(8):
        part = contract(p1[i, :out_rows], two[0], ((1,), (1,))).astype(BF16)
        give[2 * i] = part[:, :BLOCK]
        give[2 * i + 1] = part[:, BLOCK:]
    layer.merged()
    few = out_rows // depth
    for i in range(8):
        part = jnp.dot(both_blocks(got, i), two[0], preferred_element_type=F32).astype(BF16)
        f = i * depth // 8
        for t in range(depth):
            p1[i * depth % 8 + t, f * few : (f + 1) * few] = part[t * few : (t + 1) * few]
    out_put = pltpu.make_async_copy(out_w, owg_ref, load.at[0])
    out_put.start()
    scatter.sent()
    for q, at in enumerate(halves):
        p2[0, at] = (mixed_ref[at] + layer.result(q)).astype(BF16)
    layer_put = pltpu.make_async_copy(p2.at[0], layer_ref, load.at[1])
    layer_put.start()

    @pl.when(z == 0)
    def _():
        hop_right.wait_send()

    @pl.when(z == depth - 1)
    def _():
        hop_left.wait_send()

    @pl.when(z == 1)
    def _():
        remote(left_ref, left_ref, hsend.at[0], hrecv.at[0], fsdp=z - 1).wait_recv()

    @pl.when(z == depth - 2)
    def _():
        remote(right_ref, right_ref, hsend.at[1], hrecv.at[1], fsdp=z + 1).wait_recv()

    out_put.wait()
    for d in puts:
        d.wait()
    layer_put.wait()
    layer.sent()
    gu_line.sent((2,))
    down_line.sent((1, 2))


def middle(got, x, gains, grad_all, out_w, gate_up, down, cid):
    rows, width = x.shape
    depth, shard, both = gate_up.shape
    shape = jax.ShapeDtypeStruct
    vm = pl.BlockSpec(memory_space=VMEM)
    hbm = pl.BlockSpec(memory_space=ANY)
    heads = (8 * rows // BLOCK, 2 * HEAD_SIZE, BLOCK)
    block = (8, rows, width)
    return pl.pallas_call(
        middle_kernel,
        out_shape=(
            shape((rows, width), BF16),
            shape((rows, width), F32),
            shape((8, width), F32),
            shape(heads, BF16),
            shape(out_w.shape, BF16),
            shape(gate_up.shape, BF16),
            shape(down.shape, BF16),
            shape((shard, both), BF16),
            shape((shard, both), BF16),
            shape(gate_up.shape, BF16),
            shape(down.shape, BF16),
        ),
        in_specs=[vm, hbm, vm, hbm, hbm, hbm, hbm],
        out_specs=(hbm, vm, vm, vm, hbm, hbm, hbm, hbm, hbm, hbm, hbm),
        scratch_shapes=[
            VMEM((rows, width), F32),
            VMEM(block, BF16),
            VMEM(gate_up.shape, BF16),
            VMEM(down.shape, BF16),
            VMEM(block, BF16),
            VMEM(block, BF16),
            VMEM(block, BF16),
            VMEM((8, rows, both // 2), BF16),
            VMEM((8, rows, both), BF16),
        ]
        + Scatter.scratch(rows, width)
        + Scatter.scratch(rows, width)
        + [DMA((8, 2))] * 2
        + [DMA((2, depth))] * 4
        + [DMA((4,)), DMA((depth + 1,)), DMA((2,)), DMA((2,))],
        input_output_aliases={5: 9, 6: 10},
        compiler_params=params(cid),
        name="middle",
    )(got, x, gains, grad_all, out_w, gate_up, down)


class LineScatter:
    def __init__(self, z, own, left, right, send, recv):
        self.z, self.own, self.left, self.right = z, own, left, right
        self.send, self.recv = send, recv
        self.top = own.shape[0] - 1
        self.begun = None

    @staticmethod
    def scratch(shape):
        depth = shape[0]
        hops = (depth - 1,) + tuple(shape[1:])
        return [VMEM(hops, BF16), VMEM(hops, BF16), DMA((2, depth)), DMA((2, depth))]

    def copy(self, way, s, part, to):
        there = (self.left, self.right)[way].at[s]
        return remote(self.own.at[part], there, self.send.at[way, s], self.recv.at[way, s], fsdp=to)

    def landed(self, way, s):
        if s == 0 and self.begun:
            self.begun[way].wait()
            return
        ref = (self.left, self.right)[way].at[s]
        remote(ref, ref, self.send.at[way, s], self.recv.at[way, s], fsdp=self.z - 1 + 2 * way).wait_recv()

    def step(self, s):
        z, top = self.z, self.top
        for way in (0, 1):
            place = z if way == 0 else top - z
            part = top - s + z if way == 0 else s - top + z

            @pl.when((place <= s) & (place < top))
            def _():
                if s:

                    @pl.when(place > 0)
                    def _():
                        self.landed(way, s - 1)
                        came = (self.left, self.right)[way][s - 1]
                        self.own[part] = (self.own[part].astype(F32) + came.astype(F32)).astype(BF16)

                self.copy(way, s, part, z + 1 - 2 * way).start()

    def result(self):
        z, last = self.z, self.top - 1

        def close(ways):
            total = self.own[z].astype(F32)
            for way in ways:
                self.landed(way, last)
                total = total + (self.left, self.right)[way][last].astype(F32)
            self.own[z] = total.astype(BF16)

        @pl.when(z == 0)
        def _():
            close((1,))

        @pl.when((z > 0) & (z < self.top))
        def _():
            close((0, 1))

        @pl.when(z == self.top)
        def _():
            close((0,))

    def sent(self):
        z, top = self.z, self.top
        for s in range(1 if self.begun else 0, top):
            for way in (0, 1):
                place = z if way == 0 else top - z
                part = top - s + z if way == 0 else s - top + z

                @pl.when((place <= s) & (place < top))
                def _():
                    self.copy(way, s, part, z + 1 - 2 * way).wait_send()


def back_kernel(
    order_ref, rank_ref, qkv_ref, o_ref, give, lse_ref, table_ref, w_ref, gains_ref, gain_two_ref,
    mgrad_ref, x_ref, all_ref, owg_ref, gug_ref, dg_ref, left_ref, right_ref,
    input_ref, sum_ref, gu_all, down_all, q_all, o_all,
    do_ref, keys, keys_t, values, dk, dv, dqn, dqkv, acc, xs, big, owg, gug, down, heads, outs,
    gain_rows, by_z, part_sum, by_c, first, last, diagonal, first2, last2, diagonal2, *rest,
):
    scatter_sems = (rest[:4], rest[4:8])
    lines = (rest[8:12], rest[12:16], rest[16:20], rest[20:24])
    send, recv, local, load, xload, zs, zr, cs, cr, esend, erecv = rest[24:]
    c = lax.axis_index("ctx")
    z = lax.axis_index("fsdp")
    depth, shard = heads.shape[0], heads.shape[2]
    rows, width = xs.shape[1:]
    others = [lax.rem(z + k, depth) for k in range(1, depth)]
    greet([{"ctx": flip(c, k)} for k in range(1, 8)] + [{"fsdp": o} for o in others])
    some = acc.at[pl.ds(0, rows)]
    loads = [
        pltpu.make_async_copy(a, t, load.at[i])
        for i, (a, t) in enumerate(
            ((gug_ref, gug), (owg_ref, owg), (dg_ref, down), (mgrad_ref, some), (x_ref, xs.at[0]))
        )
    ]
    for d in loads[:3]:
        d.start()
    gu_line, down_line, q_line, o_line = (
        LineScatter(z, a, *refs) for a, refs in zip((gug, down, heads, outs), lines)
    )
    gu_line.begun = (
        pltpu.make_async_copy(left_ref, gu_line.left.at[0], load.at[5]),
        pltpu.make_async_copy(right_ref, gu_line.right.at[0], load.at[6]),
    )

    @pl.when(z == 1)
    def _():
        gu_line.begun[0].start()

    @pl.when(z == depth - 2)
    def _():
        gu_line.begun[1].start()

    out = Scatter(c, owg, first2, last2, diagonal2, *scatter_sems[0])
    one = Scatter(c, big, first, last, diagonal, *scatter_sems[1])

    sent = exchange_start(c, give, do_ref, esend, erecv)
    do_ref[pl.ds(2 * c, 2)] = give[pl.ds(2 * c, 2)]
    blocks = qkv_ref.shape[0]
    per = CHUNK // BLOCK
    scale = HEAD_SIZE ** (-0.5)
    factor = scale * math.log2(math.e)
    half = HEAD_SIZE // 2
    for b in range(blocks):
        there = slice(b * BLOCK, (b + 1) * BLOCK)
        key = qkv_ref[order_ref[b], 2 * HEAD_SIZE : 3 * HEAD_SIZE]
        keys[there, :] = key.T
        keys_t[:, there] = key
        values[there, :] = qkv_ref[order_ref[b], 3 * HEAD_SIZE :].T
    dk[...] = jnp.zeros_like(dk)
    dv[...] = jnp.zeros_like(dv)
    loads[0].wait()
    gu_line.step(1)
    loads[2].wait()
    down_line.step(0)
    loads[1].wait()
    for k in Scatter.ORDER:
        out.give(k)
    exchange_landed(c, do_ref, esend, erecv)

    def attend_block(j, last):
        block = order_ref[j]
        q = two_heads(qkv_ref, block)
        do = two_heads(do_ref, block)
        delta = jnp.sum(two_heads(o_ref, j).astype(F32) * do.astype(F32), 0, keepdims=True)
        lse = lse_ref[j]

        def step(t, dq, masked):
            there = pl.ds(t * CHUNK, CHUNK)
            s = jnp.dot(keys[there, :], q, preferred_element_type=F32)
            if masked:
                s = causal(s, t, j)
            p = jnp.exp2(s * factor - lse)
            dp = jnp.dot(values[there, :], do, preferred_element_type=F32)
            ds = (p * (dp - delta)).astype(BF16)
            wide = pl.ds(t * per, per)
            dv[wide] += contract(p.astype(BF16), do, ((1,), (1,))).reshape(per, BLOCK, HEAD_SIZE)
            dk[wide] += contract(ds, q, ((1,), (1,))).reshape(per, BLOCK, HEAD_SIZE)
            return dq + jnp.dot(keys_t[:, there], ds, preferred_element_type=F32)

        dq = jnp.zeros((HEAD_SIZE, 2 * BLOCK), F32)
        for t in range(last):
            dq = step(t, dq, False)
        dq = step(last, dq, True) * scale
        cosine, sine = table_ref[block, :half], table_ref[block, half:]
        for h in (0, 1):
            part = dq[:, h * BLOCK : (h + 1) * BLOCK]
            dqn[j, h * HEAD_SIZE : (h + 1) * HEAD_SIZE] = turned(part, cosine, -sine).astype(BF16)

    for turn in range(blocks // per):

        @pl.loop(turn * per, (turn + 1) * per)
        def _(j):
            attend_block(j, turn)

        if turn == 0:
            out.far()
        if turn == 1:
            out.direct()
        if turn == 2:
            out.merged()
            gu_line.step(2)
            down_line.step(1)

    for i in range(blocks):
        to = slice(i * BLOCK, (i + 1) * BLOCK)
        natural = rank_ref[i]
        dqkv[: 2 * HEAD_SIZE, to] = dqn[natural]
        dqkv[2 * HEAD_SIZE : 3 * HEAD_SIZE, to] = turned(
            dk[natural].T * scale, table_ref[i, :half], -table_ref[i, half:]
        ).astype(BF16)
        dqkv[3 * HEAD_SIZE :, to] = dv[natural].T.astype(BF16)

    def x_load(d, slot):
        return pltpu.make_async_copy(all_ref.at[d], xs.at[slot], xload.at[slot])

    for block in Scatter.ORDER:
        for d in (flip(c, 1 ^ block), flip(c, block)):
            big[d] = contract(dqkv[:, lanes(d * rows, rows)], w_ref[...], ((0,), (0,))).astype(BF16)
        one.give(block)
    x_load(0, 0).start()
    x_load(1, 1).start()
    one.far()
    gu_line.result()
    here = []
    gathers = []

    def spread(i, source, everyone):
        here.append(pltpu.make_async_copy(source, everyone.at[c], local.at[i]))
        here[-1].start()
        at, own = (row_half, own_half(source)) if source.shape[0] % 32 == 0 else (column_half, own_half(source, 1))
        gathers.append(Gather(c, own, everyone, at, send.at[i], recv.at[i]))
        gathers[-1].begin_half()
        if i:
            gathers[-1].begin_rest()

    spread(0, gug.at[z], gu_all)
    one.direct()
    outs[...] = jnp.concatenate([out.result(0), out.result(1)], 0).astype(BF16).reshape(outs.shape)
    o_line.step(0)
    acc[...] = jnp.zeros_like(acc)
    for d in range(8):
        slot = d % 2
        x_load(d, slot).wait()
        acc[...] += jnp.dot(dqkv[:, d * rows : (d + 1) * rows], xs[slot], preferred_element_type=F32)
        if d + 2 < 8:
            x_load(d + 2, slot).start()
        if d == 3:
            one.merged()
            gathers[0].begin_rest()
    for f in range(depth):
        heads[f] = acc[:, f * shard : (f + 1) * shard].astype(BF16)
    loads[3].start()
    loads[4].start()
    q_line.step(0)
    down_line.step(2)
    q_line.step(1)
    o_line.step(1)

    gain = jnp.concatenate([gains_ref[k, 0:1, :] for k in range(depth)], 1)
    gathers[0].near_half()
    q_line.step(2)
    o_line.step(2)
    loads[3].wait()
    loads[4].wait()
    gain_sum = jnp.zeros((1, width), F32)
    for q in (0, 1):
        at = pl.ds(q * (rows // 2), rows // 2)
        one_grad = one.result(q)
        x = xs[0, at].astype(F32)
        norm = lax.rsqrt(jnp.mean(x * x, -1, keepdims=True) + EPS)
        gain_sum = gain_sum + jnp.sum(one_grad * x * norm, 0, keepdims=True)
        scaled = one_grad * gain
        grad = norm * scaled - x * (norm * norm * norm) * jnp.mean(scaled * x, -1, keepdims=True)
        xs[1, at] = (acc[at] + grad).astype(BF16)
    here.append(pltpu.make_async_copy(xs.at[1], input_ref, xload.at[0]))
    here[-1].start()
    gain_rows[:4] = jnp.broadcast_to(gain_sum, (4, width))
    gain_rows[4:] = gain_two_ref[4:]
    for k, o in enumerate(others):
        d = remote(gain_rows.at[:, lanes(o * shard, shard)], by_z.at[z], zs.at[k], zr.at[k], fsdp=o)
        d.start()
        sent.append(d)
    down_line.result()
    spread(1, down.at[z], down_all)
    gathers[0].near_rest()
    gathers[0].far()
    q_line.result()
    spread(2, heads.at[z], q_all)
    o_line.result()
    spread(3, outs.at[z], o_all)

    total = gain_rows[:, lanes(z * shard, shard)]
    for k in range(depth - 1):
        ref = by_z.at[lax.rem(z + depth - 1 - k, depth)]
        remote(ref, ref, zs.at[k], zr.at[k], fsdp=others[k]).wait_recv()
        total = total + by_z[lax.rem(z + depth - 1 - k, depth)]
    part_sum[...] = total
    for k in range(1, 8):
        d = remote(part_sum, by_c.at[c], cs.at[k], cr.at[k], ctx=flip(c, k))
        d.start()
        sent.append(d)
    by_c[c] = total

    for g in gathers[1:]:
        g.near_half()
    for g in gathers[1:]:
        g.near_rest()
    for g in gathers[1:]:
        g.far()
    for g in gathers:
        for channel, k in ((0, 1), (3, 3), (4, 5), (5, 7)):
            g.paired(channel, k)
    for k in range(1, 8):
        ref = by_c.at[flip(c, k)]
        remote(ref, ref, cs.at[k], cr.at[k], ctx=flip(c, k)).wait_recv()
    total = by_c[0]
    for k in range(1, 8):
        total = total + by_c[k]
    sum_ref[...] = total
    for d in here:
        d.wait()
    for d in sent:
        d.wait_send()
    out.sent()
    one.sent()
    for line in (gu_line, down_line, q_line, o_line):
        line.sent()
    for g in gathers:
        g.sent()


def back(order, rank, arrays, large, depth, cid):
    blocks = arrays[0].shape[0]
    tokens = blocks * BLOCK
    rows, width = large[0].shape
    out_rows = large[3].shape[1]
    gate_up, down = large[4], large[5]
    shard = gate_up.shape[1]
    shape = jax.ShapeDtypeStruct
    vm = pl.BlockSpec(memory_space=VMEM)
    hbm = pl.BlockSpec(memory_space=ANY)
    sm = pl.BlockSpec(memory_space=pltpu.SMEM)
    tall = (tokens, HEAD_SIZE)
    small = (8, shard)
    lines = (gate_up.shape, down.shape, (depth, 4 * HEAD_SIZE, shard), (depth, out_rows // depth, width))
    scatter = Scatter.scratch(rows, width)
    return pl.pallas_call(
        back_kernel,
        out_shape=[shape((rows, width), BF16), shape(small, F32)]
        + [shape((8,) + a[1:], BF16) for a in lines],
        in_specs=[sm, sm] + [vm] * len(arrays) + [hbm] * len(large),
        out_specs=[hbm, vm] + [hbm] * 4,
        scratch_shapes=[
            VMEM((blocks, 2 * HEAD_SIZE, BLOCK), BF16),
            VMEM(tall, BF16),
            VMEM(tall[::-1], BF16),
            VMEM(tall, BF16),
            VMEM((blocks, BLOCK, HEAD_SIZE), F32),
            VMEM((blocks, BLOCK, HEAD_SIZE), F32),
            VMEM((blocks, 2 * HEAD_SIZE, BLOCK), BF16),
            VMEM((4 * HEAD_SIZE, tokens), BF16),
            VMEM((4 * HEAD_SIZE, width), F32),
            VMEM((2, rows, width), BF16),
            VMEM((8, rows, width), BF16),
            VMEM((8, out_rows, width), BF16),
        ]
        + [VMEM(a, BF16) for a in lines]
        + [VMEM((8, width), F32), VMEM((depth,) + small, F32), VMEM(small, F32), VMEM((8,) + small, F32)]
        + scatter[:3]
        + Scatter.scratch(out_rows, width)[:3]
        + scatter[3:] * 2
        + [r for a in lines for r in LineScatter.scratch(a)]
        + [DMA((4, 8, 2)), DMA((4, 8, 2)), DMA((4,)), DMA((9,)), DMA((2,))]
        + [DMA((depth,)), DMA((depth,)), DMA((8,)), DMA((8,)), DMA((8,)), DMA((8,))],
        compiler_params=params(cid),
        name="back",
    )(order, rank, *arrays, *large)


def widen(gate_up, down, out, sums, layer, grad):
    _, shard, both = gate_up.shape
    mine = both // 2
    strips = mine // LANES
    step = shard // 8
    _, rows, width = down.shape

    def kernel(a_ref, d_ref, o_ref, s_ref, l_ref, g_ref, gate_ref, up_ref, down_ref, out_ref, one_ref, two_ref, layer_ref, grad_ref):
        layer_ref[0] = l_ref[...]
        grad_ref[0] = g_ref[...]
        for i, target in enumerate((gate_ref, up_ref)):
            for c in range(8):
                for s in range(strips):
                    target[:, (s * 8 + c) * LANES : (s * 8 + c + 1) * LANES] = a_ref[
                        c, :, i * mine + s * LANES : i * mine + (s + 1) * LANES
                    ].astype(F32)
        down_ref[...] = d_ref[0].astype(F32)
        out_ref[...] = o_ref[0].astype(F32)
        one_ref[...] = s_ref[0]
        two_ref[...] = s_ref[4]

    wide = jax.ShapeDtypeStruct((shard, 8 * mine), F32)
    gain = jax.ShapeDtypeStruct((shard,), F32)
    by_rows = lambda n, columns: pl.BlockSpec((n, columns), lambda i: (i, 0))
    by_device = lambda a: pl.BlockSpec((1,) + a.shape[1:], lambda i: (i, 0, 0))
    return pl.pallas_call(
        kernel,
        grid=(8,),
        out_shape=(
            wide,
            wide,
            jax.ShapeDtypeStruct((8 * rows, width), F32),
            jax.ShapeDtypeStruct((shard, width), F32),
            gain,
            gain,
        )
        + (jax.ShapeDtypeStruct((1,) + layer.shape, BF16),) * 2,
        in_specs=[
            pl.BlockSpec((8, step, both), lambda i: (0, i, 0)),
            by_device(down),
            by_device(out),
            pl.BlockSpec(sums.shape, lambda i: (0, 0)),
        ]
        + [by_rows(layer.shape[0] // 8, width)] * 2,
        out_specs=(by_rows(step, 8 * mine), by_rows(step, 8 * mine), by_rows(rows, width), by_rows(step, width))
        + (pl.BlockSpec((shard,), lambda i: (0,)),) * 2
        + (pl.BlockSpec((1, layer.shape[0] // 8, width), lambda i: (0, i, 0)),) * 2,
        compiler_params=pltpu.CompilerParams(vmem_limit_bytes=VMEM_BYTES),
        name="widen",
    )(gate_up, down, out, sums, layer, grad)


def widen_heads(qkv):
    shard = qkv.shape[2]
    per_q = 2 * HEAD_SIZE
    heads = 8 * HEAD_SIZE

    def kernel(a_ref, q_out, k_out, v_out):
        for c in range(0, 8, 2):
            both = jnp.concatenate([a_ref[c + i, :per_q, :] for i in (0, 1)], 0)
            q_out[:, c * per_q : (c + 2) * per_q] = both.T.astype(F32)
        for target, first in ((k_out, per_q), (v_out, per_q + HEAD_SIZE)):
            for c in range(0, 8, 4):
                four = jnp.concatenate([a_ref[c + i, first : first + HEAD_SIZE, :] for i in range(4)], 0)
                target[:, c * HEAD_SIZE : (c + 4) * HEAD_SIZE] = four.T.astype(F32)

    by_rows = lambda n: pl.BlockSpec((LANES, n), lambda i: (i, 0))
    shape = lambda n: jax.ShapeDtypeStruct((shard, n), F32)
    return pl.pallas_call(
        kernel,
        grid=(shard // LANES,),
        out_shape=(shape(2 * heads), shape(heads), shape(heads)),
        in_specs=[pl.BlockSpec((8, 4 * HEAD_SIZE, LANES), lambda i: (0, 0, i))],
        out_specs=(by_rows(2 * heads), by_rows(heads), by_rows(heads)),
        compiler_params=pltpu.CompilerParams(vmem_limit_bytes=VMEM_BYTES),
        name="widen_heads",
    )(qkv)


def in_plane(
    depth,
    hidden_in,
    positions,
    attn_gain,
    w_query,
    key_projection,
    value_projection,
    w_out,
    mlp_gain,
    w_gate,
    w_up,
    w_down,
    out_grad,
):
    plane = 8
    rows, width = hidden_in.shape[1:]
    shard = width // depth
    half = HEAD_SIZE // 2

    gains = (attn_gain, mlp_gain)
    freq = np.float32(THETA) ** (-(np.arange(half, dtype=np.float32) * np.float32(2.0) / np.float32(HEAD_SIZE)))
    inner = freq[:, None] * np.arange(BLOCK, dtype=np.float32)[None]
    step = jnp.asarray(np.concatenate([np.cos(inner), np.sin(inner)], 0).astype(np.float32))
    freq = jnp.asarray(np.broadcast_to(freq[:, None], (half, LANES)).astype(np.float32))

    hidden_low = hidden_in[0]
    weights = (w_query, key_projection, value_projection, w_out, w_gate, w_up, w_down)
    grad_low = out_grad[0]
    (normed_all, qkv, qkv_w, table, gains_all, order, rank, attended_low, lse, got, out_w, gate_up_w, down_w, grad_all) = first_part(
        positions, hidden_low, gains, freq, step, weights, grad_low, depth, 0
    )
    (layer_out, mixed_grad, gain_two_grad, do, out_wgrad, gate_up_wgrad, down_wgrad, left, right, _, _) = middle(
        got, hidden_low, gains_all, grad_all, out_w.reshape(plane, -1, width), gate_up_w, down_w, 2
    )
    arrays = (qkv, attended_low, do, lse, table, qkv_w, gains_all, gain_two_grad)
    large = (mixed_grad, hidden_low, normed_all, out_wgrad, gate_up_wgrad, down_wgrad, left, right)
    input_grad, gain_sums, gate_up_all, down_all, qkv_all, out_grads = back(order, rank, arrays, large, depth, 3)
    query_total, key_total, value_total = widen_heads(qkv_all)
    gate_total, up_total, down_total, out_total, gain_one, gain_two, layer_out, input_grad = widen(
        gate_up_all, down_all, out_grads, gain_sums, layer_out, input_grad
    )
    return (
        layer_out,
        input_grad,
        gain_one,
        query_total,
        key_total,
        value_total,
        out_total,
        gain_two,
        gate_total,
        up_total,
        down_total,
    )


def solution(mesh):
    placed = (
        P("fsdp", "ctx", None),
        P("fsdp", "ctx"),
        P("fsdp"),
        P("fsdp", None),
        P("fsdp", None),
        P("fsdp", None),
        P("fsdp", None),
        P("fsdp"),
        P("fsdp", None),
        P("fsdp", None),
        P("fsdp", None),
        P("fsdp", "ctx", None),
    )
    body = per_device
    if mesh.shape["ctx"] == KEY_VALUE_HEADS:
        body = functools.partial(in_plane, mesh.shape["fsdp"])
    return jax.shard_map(
        body,
        mesh=mesh,
        in_specs=placed,
        out_specs=(
            P("fsdp", "ctx", None),
            P("fsdp", "ctx", None),
            P("fsdp"),
            P("fsdp", None),
            P("fsdp", None),
            P("fsdp", None),
            P("fsdp", None),
            P("fsdp"),
            P("fsdp", None),
            P("fsdp", None),
            P("fsdp", None),
        ),
        check_vma=False,
    )
```

```python
import functools
import math

import jax
import jax.numpy as jnp
import numpy as np
from jax import lax
from jax.experimental import pallas as pl
from jax.experimental.pallas import tpu as pltpu
from jax.sharding import PartitionSpec as P

QUERY_HEADS = 16
KEY_VALUE_HEADS = 8
HEAD_SIZE = 96


EPS = 1e-05
THETA = 100000.0


def tables(token_position):
    half = HEAD_SIZE // 2
    freq = THETA ** (-(jnp.arange(half, dtype=jnp.float32) * 2.0 / HEAD_SIZE))
    angle = token_position.astype(jnp.float32)[:, None] * freq[None, :]
    return (jnp.cos(angle)[:, None, :], jnp.sin(angle)[:, None, :])


def rotary_embed(value_rows, cosine_table, sine_table):
    half = value_rows.shape[-1] // 2
    first = value_rows[..., :half]
    second = value_rows[..., half:]
    return jnp.concatenate(
        [first * cosine_table - second * sine_table, second * cosine_table + first * sine_table], -1
    )


def rotary_embed_backward(grads, cosine_table, sine_table):
    half = grads.shape[-1] // 2
    first = grads[..., :half]
    second = grads[..., half:]
    return jnp.concatenate(
        [first * cosine_table + second * sine_table, second * cosine_table - first * sine_table], -1
    )


def norm_forward(hidden, gain):
    return (
        hidden
        * lax.rsqrt(jnp.mean(hidden * hidden, -1, keepdims=True) + EPS)
        * gain.astype(jnp.float32)
    )


def norm_back(hidden, gain, grad):
    factor = lax.rsqrt(jnp.mean(hidden * hidden, -1, keepdims=True) + EPS)
    scaled = grad * gain.astype(jnp.float32)
    hidden_grad = factor * scaled - hidden * factor * factor * factor * jnp.mean(
        scaled * hidden, -1, keepdims=True
    )
    gain_grad = jnp.sum(grad * hidden * factor, 0)
    return (hidden_grad, gain_grad)


def dot_first(left, right):
    return lax.dot_general(
        left, right, (((0,), (0,)), ((), ())), preferred_element_type=jnp.float32
    )


def dot_last(left, right):
    return lax.dot_general(
        left, right, (((1,), (1,)), ((), ())), preferred_element_type=jnp.float32
    )


def over_blocks(step_fn, carry, arrays):
    block_count = arrays[0].shape[0]
    size = math.gcd(block_count, 512)
    parts = block_count // size
    shaped = tuple((item.reshape((parts, size) + item.shape[1:]) for item in arrays))

    def advance(state, inputs):
        index, pieces = inputs
        return (step_fn(state, pieces, index * size), None)

    final, unused = lax.scan(advance, carry, (jnp.arange(parts, dtype=jnp.int32), shaped))
    return final


def per_device(
    hidden_in,
    positions,
    attn_gain,
    w_query,
    key_projection,
    value_projection,
    w_out,
    mlp_gain,
    w_gate,
    w_up,
    w_down,
    out_grad,
):
    hidden = hidden_in[0].astype(jnp.float32)
    local_rows = hidden.shape[0]
    query_pos = positions[0]
    query_groups = QUERY_HEADS // KEY_VALUE_HEADS
    scale = HEAD_SIZE ** (-0.5)
    cosine_table, sine_table = tables(query_pos)
    attn_set = (
        lax.all_gather(attn_gain, "fsdp", axis=0, tiled=True),
        lax.all_gather(w_query, "fsdp", axis=0, tiled=True),
        lax.all_gather(key_projection, "fsdp", axis=0, tiled=True),
        lax.all_gather(value_projection, "fsdp", axis=0, tiled=True),
        lax.all_gather(w_out, "fsdp", axis=0, tiled=True),
    )
    gain_one, query_w, key_matrix, value_matrix, out_w = attn_set
    first_normed = norm_forward(hidden, gain_one).astype(jnp.bfloat16)
    query_raw = jnp.dot(first_normed, query_w, preferred_element_type=jnp.float32)
    unrotated_key = jnp.dot(first_normed, key_matrix, preferred_element_type=jnp.float32)
    value_raw = jnp.dot(first_normed, value_matrix, preferred_element_type=jnp.float32)
    query_rows = (
        rotary_embed(
            query_raw.reshape(local_rows, QUERY_HEADS, HEAD_SIZE), cosine_table, sine_table
        )
        .astype(jnp.bfloat16)
        .reshape(local_rows, KEY_VALUE_HEADS, query_groups, HEAD_SIZE)
    )
    keys_flat = (
        rotary_embed(
            unrotated_key.reshape(local_rows, KEY_VALUE_HEADS, HEAD_SIZE), cosine_table, sine_table
        )
        .astype(jnp.bfloat16)
        .reshape(local_rows, KEY_VALUE_HEADS * HEAD_SIZE)
    )
    values_flat = value_raw.astype(jnp.bfloat16)
    key_pos_all = lax.all_gather(query_pos, "ctx", axis=0, tiled=True)
    sequence_length = key_pos_all.shape[0]

    def masked_scores(partial_keys, first):
        block_count = partial_keys.shape[0]
        key_pos = lax.dynamic_slice_in_dim(key_pos_all, first, block_count)
        scores = (
            jnp.einsum(
                "tkgd,nkd->kgtn",
                query_rows,
                partial_keys.reshape(block_count, KEY_VALUE_HEADS, HEAD_SIZE),
                preferred_element_type=jnp.float32,
            )
            * scale
        )
        visible = key_pos[None, None, None, :] <= query_pos[None, None, :, None]
        return jnp.where(visible, scores, -jnp.inf)

    def forward_part(carry, part, first):
        top, denom, accum = carry
        partial_keys, partial_values = part
        block_count = partial_keys.shape[0]
        scores = masked_scores(partial_keys, first)
        new_top = jnp.maximum(top, jnp.max(scores, -1))
        weights = jnp.exp(scores - new_top[..., None])
        factor = jnp.exp(top - new_top)
        denom = denom * factor + jnp.sum(weights, -1)
        accum = accum * factor[..., None] + jnp.einsum(
            "kgtn,nkd->kgtd",
            weights.astype(jnp.bfloat16),
            partial_values.reshape(block_count, KEY_VALUE_HEADS, HEAD_SIZE),
            preferred_element_type=jnp.float32,
        )
        return (new_top, denom, accum)

    start_state = (
        jnp.full((KEY_VALUE_HEADS, query_groups, local_rows), -1e30, jnp.float32),
        jnp.zeros((KEY_VALUE_HEADS, query_groups, local_rows), jnp.float32),
        jnp.zeros((KEY_VALUE_HEADS, query_groups, local_rows, HEAD_SIZE), jnp.float32),
    )
    top, denom, accum = over_blocks(
        forward_part,
        start_state,
        (
            lax.all_gather(keys_flat, "ctx", axis=0, tiled=True),
            lax.all_gather(values_flat, "ctx", axis=0, tiled=True),
        ),
    )
    attended_output = accum / denom[..., None]
    log_total = top + jnp.log(denom)
    attended_low = (
        attended_output.transpose(2, 0, 1, 3)
        .reshape(local_rows, QUERY_HEADS * HEAD_SIZE)
        .astype(jnp.bfloat16)
    )
    mixed = hidden + jnp.dot(attended_low, out_w, preferred_element_type=jnp.float32)
    mlp_set = (
        lax.all_gather(mlp_gain, "fsdp", axis=0, tiled=True),
        lax.all_gather(w_gate, "fsdp", axis=0, tiled=True),
        lax.all_gather(w_up, "fsdp", axis=0, tiled=True),
        lax.all_gather(w_down, "fsdp", axis=0, tiled=True),
    )
    gain_two, gate_w, up_w, down_w = mlp_set
    normed_two = norm_forward(mixed, gain_two).astype(jnp.bfloat16)
    gate = jnp.dot(normed_two, gate_w, preferred_element_type=jnp.float32)
    up = jnp.dot(normed_two, up_w, preferred_element_type=jnp.float32)
    sigma = jax.nn.sigmoid(gate)
    active = (gate * sigma * up).astype(jnp.bfloat16)
    result = mixed + jnp.dot(active, down_w, preferred_element_type=jnp.float32)
    layer_out = result.astype(jnp.bfloat16)[None]
    grad_low = out_grad[0]
    grad_out = grad_low.astype(jnp.float32)
    gain_back, gate_back, up_back, down_back = (
        lax.all_gather(mlp_gain, "fsdp", axis=0, tiled=True),
        lax.all_gather(w_gate, "fsdp", axis=0, tiled=True),
        lax.all_gather(w_up, "fsdp", axis=0, tiled=True),
        lax.all_gather(w_down, "fsdp", axis=0, tiled=True),
    )
    down_grad = dot_first(active, grad_low)
    active_grad = dot_last(grad_low, down_back)
    gate_grad = (active_grad * up * sigma * (1.0 + gate * (1.0 - sigma))).astype(jnp.bfloat16)
    up_grad = (active_grad * gate * sigma).astype(jnp.bfloat16)
    gate_wgrad = dot_first(normed_two, gate_grad)
    up_wgrad = dot_first(normed_two, up_grad)
    normed_two_grad = dot_last(gate_grad, gate_back) + dot_last(up_grad, up_back)
    mixed_part, gain_two_grad = norm_back(mixed, gain_back, normed_two_grad)
    mixed_grad = grad_out + mixed_part
    mlp_shards = (
        lax.psum_scatter(
            gain_two_grad.astype(jnp.bfloat16), "fsdp", scatter_dimension=0, tiled=True
        ).astype(jnp.float32),
        lax.psum_scatter(
            gate_wgrad.astype(jnp.bfloat16), "fsdp", scatter_dimension=0, tiled=True
        ).astype(jnp.float32),
        lax.psum_scatter(
            up_wgrad.astype(jnp.bfloat16), "fsdp", scatter_dimension=0, tiled=True
        ).astype(jnp.float32),
        lax.psum_scatter(
            down_grad.astype(jnp.bfloat16), "fsdp", scatter_dimension=0, tiled=True
        ).astype(jnp.float32),
    )
    gain_first, query_back, key_back, value_back, out_back = (
        lax.all_gather(attn_gain, "fsdp", axis=0, tiled=True),
        lax.all_gather(w_query, "fsdp", axis=0, tiled=True),
        lax.all_gather(key_projection, "fsdp", axis=0, tiled=True),
        lax.all_gather(value_projection, "fsdp", axis=0, tiled=True),
        lax.all_gather(w_out, "fsdp", axis=0, tiled=True),
    )
    branch_grad = mixed_grad.astype(jnp.bfloat16)
    out_wgrad = dot_first(attended_low, branch_grad)
    attended_grad = (
        dot_last(branch_grad, out_back)
        .astype(jnp.bfloat16)
        .reshape(local_rows, KEY_VALUE_HEADS, query_groups, HEAD_SIZE)
        .transpose(1, 2, 0, 3)
    )
    delta = jnp.sum(attended_grad.astype(jnp.float32) * attended_output, -1)

    def backward_part(carry, part, first):
        query_acc, key_value_acc = carry
        partial_keys, partial_values = part
        block_count = partial_keys.shape[0]
        probs = jnp.exp(masked_scores(partial_keys, first) - log_total[..., None])
        gradient_of_value = jnp.einsum(
            "kgtn,kgtd->nkd",
            probs.astype(jnp.bfloat16),
            attended_grad,
            preferred_element_type=jnp.float32,
        )
        prob_grad = jnp.einsum(
            "kgtd,nkd->kgtn",
            attended_grad,
            partial_values.reshape(block_count, KEY_VALUE_HEADS, HEAD_SIZE),
            preferred_element_type=jnp.float32,
        )
        score_grad = (probs * (prob_grad - delta[..., None])).astype(jnp.bfloat16)
        query_acc = (
            query_acc
            + jnp.einsum(
                "kgtn,nkd->kgtd",
                score_grad,
                partial_keys.reshape(block_count, KEY_VALUE_HEADS, HEAD_SIZE),
                preferred_element_type=jnp.float32,
            )
            * scale
        )
        gradient_of_key = (
            jnp.einsum("kgtn,tkgd->nkd", score_grad, query_rows, preferred_element_type=jnp.float32)
            * scale
        )
        joined = jnp.concatenate(
            [
                gradient_of_key.reshape(block_count, KEY_VALUE_HEADS * HEAD_SIZE),
                gradient_of_value.reshape(block_count, KEY_VALUE_HEADS * HEAD_SIZE),
            ],
            1,
        )
        key_value_acc = lax.dynamic_update_slice_in_dim(key_value_acc, joined, first, 0)
        return (query_acc, key_value_acc)

    back_state = (
        jnp.zeros((KEY_VALUE_HEADS, query_groups, local_rows, HEAD_SIZE), jnp.float32),
        jnp.zeros((sequence_length, 2 * KEY_VALUE_HEADS * HEAD_SIZE), jnp.float32),
    )
    query_acc, key_value_acc = over_blocks(
        backward_part,
        back_state,
        (
            lax.all_gather(keys_flat, "ctx", axis=0, tiled=True),
            lax.all_gather(values_flat, "ctx", axis=0, tiled=True),
        ),
    )
    local_key_value = lax.psum_scatter(
        key_value_acc.astype(jnp.bfloat16), "ctx", scatter_dimension=0, tiled=True
    ).astype(jnp.float32)
    query_raw_grad = (
        rotary_embed_backward(
            query_acc.transpose(2, 0, 1, 3).reshape(local_rows, QUERY_HEADS, HEAD_SIZE),
            cosine_table,
            sine_table,
        )
        .reshape(local_rows, QUERY_HEADS * HEAD_SIZE)
        .astype(jnp.bfloat16)
    )
    key_raw_grad = (
        rotary_embed_backward(
            local_key_value[:, : KEY_VALUE_HEADS * HEAD_SIZE].reshape(
                local_rows, KEY_VALUE_HEADS, HEAD_SIZE
            ),
            cosine_table,
            sine_table,
        )
        .reshape(local_rows, KEY_VALUE_HEADS * HEAD_SIZE)
        .astype(jnp.bfloat16)
    )
    unrotated_value_gradient = local_key_value[:, KEY_VALUE_HEADS * HEAD_SIZE :].astype(
        jnp.bfloat16
    )
    query_wgrad = dot_first(first_normed, query_raw_grad)
    key_wgrad = dot_first(first_normed, key_raw_grad)
    value_wgrad = dot_first(first_normed, unrotated_value_gradient)
    normed_one_grad = (
        dot_last(query_raw_grad, query_back)
        + dot_last(key_raw_grad, key_back)
        + dot_last(unrotated_value_gradient, value_back)
    )
    input_part, gain_one_grad = norm_back(hidden, gain_first, normed_one_grad)
    input_grad = (mixed_grad + input_part).astype(jnp.bfloat16)[None]
    attn_shards = (
        lax.psum_scatter(
            gain_one_grad.astype(jnp.bfloat16), "fsdp", scatter_dimension=0, tiled=True
        ).astype(jnp.float32),
        lax.psum_scatter(
            query_wgrad.astype(jnp.bfloat16), "fsdp", scatter_dimension=0, tiled=True
        ).astype(jnp.float32),
        lax.psum_scatter(
            key_wgrad.astype(jnp.bfloat16), "fsdp", scatter_dimension=0, tiled=True
        ).astype(jnp.float32),
        lax.psum_scatter(
            value_wgrad.astype(jnp.bfloat16), "fsdp", scatter_dimension=0, tiled=True
        ).astype(jnp.float32),
        lax.psum_scatter(
            out_wgrad.astype(jnp.bfloat16), "fsdp", scatter_dimension=0, tiled=True
        ).astype(jnp.float32),
    )
    totals = (
        lax.psum(attn_shards[0].astype(jnp.bfloat16), "ctx").astype(jnp.float32),
        lax.psum(attn_shards[1].astype(jnp.bfloat16), "ctx").astype(jnp.float32),
        lax.psum(attn_shards[2].astype(jnp.bfloat16), "ctx").astype(jnp.float32),
        lax.psum(attn_shards[3].astype(jnp.bfloat16), "ctx").astype(jnp.float32),
        lax.psum(attn_shards[4].astype(jnp.bfloat16), "ctx").astype(jnp.float32),
        lax.psum(mlp_shards[0].astype(jnp.bfloat16), "ctx").astype(jnp.float32),
        lax.psum(mlp_shards[1].astype(jnp.bfloat16), "ctx").astype(jnp.float32),
        lax.psum(mlp_shards[2].astype(jnp.bfloat16), "ctx").astype(jnp.float32),
        lax.psum(mlp_shards[3].astype(jnp.bfloat16), "ctx").astype(jnp.float32),
    )
    return (
        layer_out,
        input_grad,
        totals[0],
        totals[1],
        totals[2],
        totals[3],
        totals[4],
        totals[5],
        totals[6],
        totals[7],
        totals[8],
    )


MESH = pl.DeviceIdType.MESH
ANY = pl.ANY
VMEM = pltpu.VMEM
DMA = pltpu.SemaphoreType.DMA
LANES = 128
BLOCK = 128
F32 = jnp.float32
BF16 = jnp.bfloat16
VMEM_BYTES = 60 * 2**20


def flip(c, k):
    out = c
    for b in (1, 2, 4):
        if k & b:
            out = out + b - 2 * b * ((c // b) % 2)
    return out


def remote(src, dst, send, recv, **to):
    return pltpu.make_async_remote_copy(
        src_ref=src, dst_ref=dst, send_sem=send, recv_sem=recv, device_id=to, device_id_type=MESH
    )


def greet(peers):
    barrier = pltpu.get_barrier_semaphore()
    for peer in peers:
        pl.semaphore_signal(barrier, inc=1, device_id=peer, device_id_type=MESH)
    pl.semaphore_wait(barrier, len(peers))


class Gather:
    def __init__(self, c, own, buf, at, send, recv):
        self.c, self.own, self.buf, self.at, self.send, self.recv = c, own, buf, at, send, recv
        self.pending = []

    def start(self, channel, who, to, h, own=False):
        there = self.at(self.buf, flip(self.c, who), h)
        d = remote(
            self.own(h) if own else there,
            there,
            self.send.at[channel, h],
            self.recv.at[channel, h],
            ctx=flip(self.c, to),
        )
        d.start()
        self.pending.append(d)

    def arrived(self, channel, who, frm, h):
        ref = self.at(self.buf, flip(self.c, who), h)
        remote(
            ref, ref, self.send.at[channel, h], self.recv.at[channel, h], ctx=flip(self.c, frm)
        ).wait_recv()

    def begin(self):
        self.begin_half()
        self.begin_rest()

    def begin_half(self):
        self.start(1, 0, 2, 0, own=True)
        self.start(2, 0, 4, 1, own=True)

    def begin_rest(self):
        self.start(1, 0, 2, 1, own=True)
        self.start(2, 0, 4, 0, own=True)
        self.start(0, 0, 1, 0, own=True)
        self.start(0, 0, 1, 1, own=True)

    def near_half(self):
        self.arrived(1, 2, 2, 0)
        self.start(6, 2, 4, 0)
        self.start(3, 2, 1, 0)
        self.arrived(2, 4, 4, 1)
        self.start(7, 4, 2, 1)
        self.start(4, 4, 1, 1)

    def near_rest(self):
        self.arrived(1, 2, 2, 1)
        self.start(3, 2, 1, 1)
        self.arrived(2, 4, 4, 0)
        self.start(4, 4, 1, 0)

    def far(self):
        self.arrived(6, 6, 4, 0)
        self.start(5, 6, 1, 0)
        self.arrived(7, 6, 2, 1)
        self.start(5, 6, 1, 1)

    def paired(self, channel, who):
        for h in (0, 1):
            self.arrived(channel, who, 1, h)

    def finish(self):
        self.near_half()
        self.near_rest()
        self.far()
        for channel, who in ((0, 1), (3, 3), (4, 5), (5, 7)):
            self.paired(channel, who)

    def sent(self):
        for d in self.pending:
            d.wait_send()


def row_half(ref, d, h):
    half = ref.shape[1] // 2
    return ref.at[d, pl.ds(h * half, half)]


def column_half(ref, d, h):
    half = ref.shape[2] // 2
    return ref.at[d, :, pl.ds(h * half, half)]


def own_half(ref, axis=0):
    half = ref.shape[axis] // 2
    return lambda h: ref.at[(slice(None),) * axis + (pl.ds(h * half, half),)]


class Line:
    def __init__(self, z, depth, at, send, recv, own=None):
        self.z, self.depth, self.at, self.send, self.recv, self.own = z, depth, at, send, recv, own

    def copy(self, way, k, part, to):
        ref = self.at(part)
        source = ref if k or self.own is None else self.own
        return remote(source, ref, self.send.at[way, k], self.recv.at[way, k], fsdp=to)

    def step(self, k):
        z, top = self.z, self.depth - 1

        @pl.when((z >= k) & (z < top))
        def _():
            self.copy(0, k, z - k, z + 1).start()

        @pl.when((z + k <= top) & (z > 0))
        def _():
            self.copy(1, k, z + k, z - 1).start()

    def landed(self, k):
        z, top = self.z, self.depth - 1

        @pl.when(z >= k + 1)
        def _():
            self.copy(0, k, z - 1 - k, z - 1).wait_recv()

        @pl.when(z + 1 + k <= top)
        def _():
            self.copy(1, k, z + 1 + k, z + 1).wait_recv()

    def sent(self, steps):
        z, top = self.z, self.depth - 1
        for k in steps:

            @pl.when((z >= k) & (z < top))
            def _():
                self.copy(0, k, z - k, z + 1).wait_send()

            @pl.when((z + k <= top) & (z > 0))
            def _():
                self.copy(1, k, z + k, z - 1).wait_send()


def params(cid):
    return pltpu.CompilerParams(
        collective_id=cid, has_side_effects=True, vmem_limit_bytes=VMEM_BYTES
    )


def contract(a, b, dims):
    return lax.dot_general(a, b, ((dims[0], dims[1]), ((), ())), preferred_element_type=F32)


def lanes(start, size):
    return pl.ds(pl.multiple_of(start, LANES), size)


def turned(u, cosine, sine):
    half = HEAD_SIZE // 2
    a, b = u[:half], u[half:]
    return jnp.concatenate([a * cosine - b * sine, b * cosine + a * sine], 0)


def picked(weight, first, count):
    shape = (count, weight.shape[1])
    hit = lax.broadcasted_iota(jnp.int32, shape, 1) == first + lax.broadcasted_iota(jnp.int32, shape, 0)
    return contract(hit.astype(BF16), weight, ((1,), (1,))).astype(BF16)


CHUNK = 512


def two_heads(ref, block):
    return jnp.concatenate([ref[block, :HEAD_SIZE], ref[block, HEAD_SIZE : 2 * HEAD_SIZE]], 1)


def causal(s, t, j):
    key = t * CHUNK + lax.broadcasted_iota(jnp.int32, s.shape, 0)
    query = j * BLOCK + lax.broadcasted_iota(jnp.int32, s.shape, 1) % BLOCK
    return jnp.where(key <= query, s, -jnp.inf)


def exchange_start(c, source, target, send, recv):
    sent = []
    for k in (6, 7, 2, 4, 3, 5, 1):
        there = target.at[pl.ds(2 * c, 2)]
        d = remote(source.at[pl.ds(2 * flip(c, k), 2)], there, send.at[k], recv.at[k], ctx=flip(c, k))
        d.start()
        sent.append(d)
    return sent


def exchange_landed(c, target, send, recv):
    for k in (6, 7, 2, 4, 3, 5, 1):
        ref = target.at[pl.ds(2 * flip(c, k), 2)]
        remote(ref, ref, send.at[k], recv.at[k], ctx=flip(c, k)).wait_recv()


def first_kernel(
    pos_ref, x_ref, gain_one_ref, gain_two_ref, freq_ref, step_ref, wq_ref, wk_ref, wv_ref, wo_ref, wg_ref, wu_ref, wd_ref, grad_ref,
    all_ref, qkv_ref, w_ref, table_ref, gains_ref, order_ref, rank_ref, low_ref, lse_ref, got_ref, ow_all, gu_all, down_all, grad_all,
    give, infos_ref, infos, wo_all, keys, values, xs, wz, whole, gu_own, out_mine, down_mine, grad_mine, bases, gain_ref, info_ref, base_ref, gsend, grecv, isend, irecv, bsend, brecv, send, recv, zsend, zrecv, osend, orecv,
    usend, urecv, dsend, drecv, send2, recv2, send3, recv3, local, esend, erecv, parts,
):
    c = lax.axis_index("ctx")
    z = lax.axis_index("fsdp")
    depth = gains_ref.shape[0]
    shard, width = wq_ref.shape
    rows = x_ref.shape[0]
    strip = gu_all.shape[2] // 2 // depth
    down_rows = down_all.shape[1]
    others = [lax.rem(z + k, depth) for k in range(1, depth)]
    lane = lax.broadcasted_iota(jnp.int32, info_ref.shape, 1)
    info_ref[...] = jnp.where(lane < LANES // 2, pos_ref[0, 0], pos_ref[0, BLOCK])
    start = freq_ref[...] * info_ref[:1].astype(F32)
    base_ref[...] = jnp.where(lane[:1] // (LANES // 4) % 2 == 0, jnp.cos(start), jnp.sin(start))
    gain_ref[:4] = jnp.broadcast_to(gain_one_ref[...].astype(F32)[None], (4, shard))
    gain_ref[4:] = jnp.broadcast_to(gain_two_ref[...].astype(F32)[None], (4, shard))
    greet([{"ctx": flip(c, k)} for k in range(1, 8)] + [{"fsdp": o} for o in others])

    g2 = Gather(c, own_half(grad_ref), grad_all, row_half, send2, recv2)
    g2.begin_half()
    sent = []
    for k, o in enumerate(others):
        sent.append(remote(gain_ref, gains_ref.at[z], gsend.at[k], grecv.at[k], fsdp=o))
    for k in range(1, 8):
        sent.append(remote(info_ref, infos_ref.at[c], isend.at[k], irecv.at[k], ctx=flip(c, k)))
        sent.append(remote(base_ref, bases.at[c], bsend.at[k], brecv.at[k], ctx=flip(c, k)))
    for d in sent:
        d.start()
    out_rows = shard // 8
    out_own = wo_ref.at[pl.ds(c * out_rows, out_rows)]
    down_own = wd_ref.at[pl.ds(c * down_rows, down_rows)]
    strips = [
        pltpu.make_async_copy(weight, whole.at[i], parts.at[4 + i]) for i, weight in enumerate((wg_ref, wu_ref))
    ]
    for d in strips:
        d.start()
    ways = ((out_own, out_mine, ow_all.at[z, c]), (down_own, down_mine, down_all.at[z]), (grad_ref, grad_mine, grad_all.at[c]))
    incoming = [pltpu.make_async_copy(a, b, parts.at[i]) for i, (a, b, _) in enumerate(ways)]
    for d in incoming:
        d.start()
    gains_ref[z] = gain_ref[...]
    infos_ref[c] = info_ref[...]
    bases[c] = base_ref[...]

    count = 2 * HEAD_SIZE
    wz[z, :count] = picked(wq_ref[...], c * count, count)
    wz[z, count : count + HEAD_SIZE] = picked(wk_ref[...], c * HEAD_SIZE, HEAD_SIZE)
    wz[z, count + HEAD_SIZE :] = picked(wv_ref[...], c * HEAD_SIZE, HEAD_SIZE)
    line = Line(z, depth, lambda d: wz.at[d], zsend, zrecv)
    line.step(0)

    x = x_ref[...].astype(F32)
    factor = lax.rsqrt(jnp.mean(x * x, -1, keepdims=True) + EPS)
    for k in range(depth - 1):
        ref = gains_ref.at[lax.rem(z + depth - 1 - k, depth)]
        remote(ref, ref, gsend.at[k], grecv.at[k], fsdp=others[k]).wait_recv()
    gain = jnp.concatenate([gains_ref[k, 0:1, :] for k in range(depth)], 1)
    xs[c] = (x * factor * gain).astype(BF16)
    g = Gather(c, own_half(xs.at[c]), xs, row_half, send, recv)
    g.begin()
    out_line = Line(z, depth, lambda d: wo_all.at[d], osend, orecv, out_own)
    down_line = Line(z, depth, lambda d: down_all.at[d], dsend, drecv, down_own)
    out_line.step(0)
    copies = []
    for i, (_, b, there) in enumerate(ways):
        incoming[i].wait()
        copies.append(pltpu.make_async_copy(b, there, parts.at[i]))
        copies[-1].start()
    wo_all[z] = out_mine[...]

    def keep(k):
        d = pltpu.make_async_copy(xs.at[flip(c, k)], all_ref.at[flip(c, k)], local.at[k])
        d.start()
        copies.append(d)

    keep(0)

    def rotary(k):
        d = flip(c, k)
        if k:
            for ref, s, r in ((bases, bsend, brecv), (infos_ref, isend, irecv)):
                remote(ref.at[d], ref.at[d], s.at[k], r.at[k], ctx=d).wait_recv()
        half = HEAD_SIZE // 2
        step_cos, step_sin = step_ref[:half], step_ref[half:]
        for b in (0, 1):
            start = b * (LANES // 2)
            base_cos = bases[d, :, start : start + 1]
            base_sin = bases[d, :, start + LANES // 4 : start + LANES // 4 + 1]
            table_ref[2 * d + b, :half] = base_cos * step_cos - base_sin * step_sin
            table_ref[2 * d + b, half:] = base_sin * step_cos + base_cos * step_sin

    for k in range(8):
        rotary(k)

    def project(k):
        d = flip(c, k)
        half = HEAD_SIZE // 2
        raw = contract(w_ref[...], xs[d], ((1,), (1,)))
        for b in (0, 1):
            cosine, sine = table_ref[2 * d + b, :half], table_ref[2 * d + b, half:]
            part = raw[:, b * BLOCK : (b + 1) * BLOCK]
            for h in range(3):
                head = slice(h * HEAD_SIZE, (h + 1) * HEAD_SIZE)
                qkv_ref[2 * d + b, head] = turned(part[head], cosine, sine).astype(BF16)
            qkv_ref[2 * d + b, 3 * HEAD_SIZE :] = part[3 * HEAD_SIZE :].astype(BF16)

    line.landed(0)
    line.step(1)
    g.near_half()
    g2.begin_rest()
    out_line.landed(0)
    out_line.step(1)
    line.landed(1)
    line.step(2)
    g.near_rest()
    keep(2)
    keep(4)
    out_line.landed(1)
    out_line.step(2)
    for i, d in enumerate(strips):
        d.wait()
        for f in range(depth):
            gu_own[:, (i * depth + f) * strip : (i * depth + f + 1) * strip] = whole[i, :, lanes((f * 8 + c) * strip, strip)]
    gu_line = Line(z, depth, lambda d: gu_all.at[d], usend, urecv, gu_own)
    gu_line.step(0)
    down_line.step(0)
    copies.append(pltpu.make_async_copy(gu_own, gu_all.at[z], parts.at[3]))
    copies[-1].start()
    line.landed(2)
    for f in range(depth):
        w_ref[:, f * shard : (f + 1) * shard] = wz[f]
    g.far()
    g2.near_half()
    project(0)
    project(2)
    project(4)
    for channel, k in ((0, 1), (3, 3), (4, 5)):
        g.paired(channel, k)
        keep(k)
        project(k)
    keep(6)
    project(6)
    g.paired(5, 7)
    keep(7)
    project(7)
    out_line.landed(2)
    few = depth // 2
    g3 = Gather(
        c,
        lambda h: wo_all.at[pl.ds(h * few, few)],
        ow_all,
        lambda ref, d, h: ref.at[pl.ds(h * few, few), d],
        send3,
        recv3,
    )
    g3.begin()
    for f in range(1, depth):
        part = lax.rem(z + f, depth)
        copies.append(pltpu.make_async_copy(wo_all.at[part], ow_all.at[part, c], parts.at[4 + f]))
        copies[-1].start()

    blocks = qkv_ref.shape[0]
    per = CHUNK // BLOCK
    factor = HEAD_SIZE ** (-0.5) * math.log2(math.e)
    small = pltpu.make_async_copy(infos_ref, infos, parts.at[8])
    small.start()
    small.wait()
    starts = [infos[b // 2, 0, b % 2 * (LANES // 2)] for b in range(blocks)]
    least = functools.reduce(jnp.minimum, starts)
    ranks = [(start - least) // BLOCK for start in starts]
    for i in range(blocks):
        rank_ref[i] = ranks[i]
        order_ref[i] = functools.reduce(jnp.maximum, [jnp.where(ranks[b] == i, b, 0) for b in range(blocks)])
    for b in range(blocks):
        there = slice(b * BLOCK, (b + 1) * BLOCK)
        keys[there, :] = qkv_ref[order_ref[b], 2 * HEAD_SIZE : 3 * HEAD_SIZE].T
        values[:, there] = qkv_ref[order_ref[b], 3 * HEAD_SIZE :]

    def attend_block(j, last):
        q = two_heads(qkv_ref, order_ref[j])

        def step(t, carry, masked):
            top, denom, acc = carry
            s = jnp.dot(keys[pl.ds(t * CHUNK, CHUNK), :], q, preferred_element_type=F32)
            if masked:
                s = causal(s, t, j)
            new_top = jnp.maximum(top, jnp.max(s, 0, keepdims=True))
            p = jnp.exp2((s - new_top) * factor)
            shrink = jnp.exp2((top - new_top) * factor)
            denom = denom * shrink + jnp.sum(p, 0, keepdims=True)
            acc = acc * shrink + jnp.dot(
                values[:, pl.ds(t * CHUNK, CHUNK)], p.astype(BF16), preferred_element_type=F32
            )
            return new_top, denom, acc

        carry = (
            jnp.full((1, 2 * BLOCK), -1e30, F32),
            jnp.zeros((1, 2 * BLOCK), F32),
            jnp.zeros((HEAD_SIZE, 2 * BLOCK), F32),
        )
        for t in range(last):
            carry = step(t, carry, False)
        top, denom, acc = step(last, carry, True)
        out = acc / denom
        lse_ref[pl.ds(j, 1), :, :] = (top * factor + jnp.log2(denom)).reshape(1, 1, 2 * BLOCK)
        for h in (0, 1):
            head = slice(h * HEAD_SIZE, (h + 1) * HEAD_SIZE)
            low_ref[j, head] = out[:, h * BLOCK : (h + 1) * BLOCK].astype(BF16)

    def attend_blocks(first, count):
        @pl.loop(first, first + count)
        def _(j):
            attend_block(j, first // per)

    attend_blocks(0, per)
    g2.near_rest()
    attend_blocks(per, per)
    gu_line.landed(0)
    gu_line.step(1)
    attend_blocks(2 * per, per // 2)
    g2.far()
    attend_blocks(2 * per + per // 2, per // 2)
    g3.near_half()
    attend_blocks(3 * per, per // 2)
    g3.near_rest()
    attend_blocks(3 * per + per // 2, per // 2)
    for i in range(blocks):
        give[i] = low_ref[rank_ref[i]]
    sent += exchange_start(c, give, got_ref, esend, erecv)
    got_ref[pl.ds(2 * c, 2)] = give[pl.ds(2 * c, 2)]
    g3.far()
    for gather in (g2, g3):
        for channel, k in ((0, 1), (3, 3), (4, 5), (5, 7)):
            gather.paired(channel, k)
    exchange_landed(c, got_ref, esend, erecv)
    gu_line.landed(1)
    down_line.landed(0)
    for d in copies:
        d.wait()
    for d in sent:
        d.wait_send()
    line.sent((0, 1, 2))
    out_line.sent((0, 1, 2))
    gu_line.sent((0, 1))
    down_line.sent((0,))
    for gather in (g, g2, g3):
        gather.sent()


def first_part(positions, x, gains, freq, step, weights, grad, depth, cid):
    rows, width = x.shape
    shard = gains[0].shape[0]
    small = (8, shard)
    columns = weights[4].shape[1]
    down_rows = weights[6].shape[0] // 8
    blocks = 8 * rows // BLOCK
    sm = pl.BlockSpec(memory_space=pltpu.SMEM)
    vm = pl.BlockSpec(memory_space=VMEM)
    hbm = pl.BlockSpec(memory_space=ANY)
    shape = jax.ShapeDtypeStruct
    return pl.pallas_call(
        first_kernel,
        out_shape=(
            shape((8, rows, width), BF16),
            shape((8 * rows // BLOCK, 4 * HEAD_SIZE, BLOCK), BF16),
            shape((4 * HEAD_SIZE, width), BF16),
            shape((8 * rows // BLOCK, HEAD_SIZE, BLOCK), F32),
            shape((depth,) + small, F32),
            shape((blocks,), jnp.int32),
            shape((blocks,), jnp.int32),
            shape((blocks, 2 * HEAD_SIZE, BLOCK), BF16),
            shape((blocks, 1, 2 * BLOCK), F32),
            shape((blocks, 2 * HEAD_SIZE, BLOCK), BF16),
            shape((depth, 8, shard // 8, width), BF16),
            shape((depth, shard, 2 * columns // 8), BF16),
            shape((depth, down_rows, width), BF16),
            shape((8, rows, width), BF16),
        ),
        in_specs=[pl.BlockSpec(memory_space=pltpu.SMEM)] + [vm] * 8 + [hbm] * 5,
        out_specs=(hbm, vm, vm, vm, vm, sm, sm, vm, vm, vm, hbm, hbm, hbm, hbm),
        scratch_shapes=[
            VMEM((blocks, 2 * HEAD_SIZE, BLOCK), BF16),
            VMEM((8, 8, LANES), jnp.int32),
            pltpu.SMEM((8, 8, LANES), jnp.int32),
            VMEM((depth, shard // 8, width), BF16),
            VMEM((8 * rows, HEAD_SIZE), BF16),
            VMEM((HEAD_SIZE, 8 * rows), BF16),
            VMEM((8, rows, width), BF16),
            VMEM((depth, 4 * HEAD_SIZE, shard), BF16),
            VMEM((2, shard, columns), BF16),
            VMEM((shard, 2 * columns // 8), BF16),
            VMEM((shard // 8, width), BF16),
            VMEM((down_rows, width), BF16),
            VMEM((rows, width), BF16),
            VMEM((8, HEAD_SIZE // 2, LANES), F32),
            VMEM(small, F32),
            VMEM((8, LANES), jnp.int32),
            VMEM((HEAD_SIZE // 2, LANES), F32),
            DMA((depth,)),
            DMA((depth,)),
            DMA((8,)),
            DMA((8,)),
            DMA((8,)),
            DMA((8,)),
            DMA((8, 2)),
            DMA((8, 2)),
        ]
        + [DMA((2, depth))] * 8
        + [DMA((8, 2))] * 4
        + [DMA((8,))] * 3
        + [DMA((9,))],
        compiler_params=params(cid),
        name="first_part",
    )(positions, x, *gains, freq, step, *weights, grad)


class Scatter:
    ORDER = (6, 2, 4, 0)

    def __init__(self, c, p, first, last, diagonal, s1, v1, s2, v2):
        self.c, self.p, self.first = c, p, first
        self.last, self.diagonal = last, diagonal
        self.s1, self.v1, self.s2, self.v2 = s1, v1, s2, v2
        self.half = first.shape[1] // 2 if p is None else p.shape[1] // 2
        self.pending = []
        self.gifts = []
        self.summed = False

    @staticmethod
    def scratch(rows, width):
        return [
            VMEM((4, rows, width), BF16),
            VMEM((2, rows, width), BF16),
            VMEM((rows, width), BF16),
            DMA((4, 2)),
            DMA((4, 2)),
            DMA((3, 2)),
            DMA((3, 2)),
        ]

    def sl(self, q):
        return pl.ds(q * self.half, self.half)

    def go(self, d):
        d.start()
        self.pending.append(d)

    def give(self, k):
        j = self.ORDER.index(k)
        for q in (0, 1):
            source = self.p.at[flip(self.c, 1 ^ k), self.sl(q)]
            there = self.first.at[j, self.sl(q)]
            d = remote(source, there, self.s1.at[j, q], self.v1.at[j, q], ctx=flip(self.c, 1))
            d.start()
            self.gifts.append(d)

    def given(self):
        for d in self.gifts:
            d.wait_send()
        self.gifts = []

    def paired(self, j, q):
        if self.summed:
            return
        ref = self.first.at[j, self.sl(q)]
        remote(ref, ref, self.s1.at[j, q], self.v1.at[j, q], ctx=flip(self.c, 1)).wait_recv()

    def chip(self, j, q):
        if self.summed:
            return self.first[j, self.sl(q)].astype(F32)
        k = self.ORDER[j]
        return self.p[flip(self.c, k), self.sl(q)].astype(F32) + self.first[j, self.sl(q)].astype(F32)

    def came(self, channel, ref, q, frm):
        remote(
            ref, ref, self.s2.at[channel, q], self.v2.at[channel, q], ctx=flip(self.c, frm)
        ).wait_recv()

    def far(self):
        for q, to in ((0, 2), (1, 4)):
            self.paired(0, q)
            self.first[0, self.sl(q)] = self.chip(0, q).astype(BF16)
            self.go(
                remote(
                    self.first.at[0, self.sl(q)],
                    self.diagonal.at[self.sl(q)],
                    self.s2.at[2, q],
                    self.v2.at[2, q],
                    ctx=flip(self.c, to),
                )
            )

    def onward(self, j, q, merged):
        v = self.chip(j, q)
        if merged:
            v = v + self.diagonal[self.sl(q)].astype(F32)
        self.first[j, self.sl(q)] = v.astype(BF16)
        self.go(
            remote(
                self.first.at[j, self.sl(q)],
                self.last.at[j - 1, self.sl(q)],
                self.s2.at[j - 1, q],
                self.v2.at[j - 1, q],
                ctx=flip(self.c, self.ORDER[j]),
            )
        )

    def direct(self):
        self.paired(1, 0)
        self.onward(1, 0, False)
        self.paired(2, 1)
        self.onward(2, 1, False)

    def merged(self):
        self.paired(2, 0)
        self.came(2, self.diagonal.at[self.sl(0)], 0, 2)
        self.onward(2, 0, True)
        self.paired(1, 1)
        self.came(2, self.diagonal.at[self.sl(1)], 1, 4)
        self.onward(1, 1, True)

    def settle(self):
        for j, q in ((2, 0), (1, 1), (3, 0), (3, 1)):
            self.paired(j, q)
            self.first[j, self.sl(q)] = self.chip(j, q).astype(BF16)
        self.summed = True

    def result(self, q):
        self.paired(3, q)
        self.came(0, self.last.at[0, self.sl(q)], q, 2)
        self.came(1, self.last.at[1, self.sl(q)], q, 4)
        return self.chip(3, q) + (
            self.last[0, self.sl(q)].astype(F32) + self.last[1, self.sl(q)].astype(F32)
        )

    def sent(self):
        self.given()
        for d in self.pending:
            d.wait_send()


def both_blocks(ref, i):
    return jnp.concatenate([ref[2 * i], ref[2 * i + 1]], 1)


def middle_kernel(
    got, x_ref, gains_ref, g_ref, ow_ref, gu_in, down_in,
    layer_ref, mgrad_ref, gsum_ref, give, owg_ref, gug_ref, dg_ref, left_ref, right_ref, gu_all, down_all,
    mixed_ref, p1, wgu, wd, grads, two, p2, act, dgu, *rest,
):
    scatter_refs, layer_refs = rest[:7], rest[7:14]
    send, recv, usend, urecv, dsend, drecv, load, wput, hsend, hrecv = rest[14:]
    c = lax.axis_index("ctx")
    z = lax.axis_index("fsdp")
    depth, shard, both = gu_all.shape
    mine = both // 2
    rows, width = x_ref.shape
    out_rows = ow_ref.shape[1]
    out_w = p1.at[:, pl.ds(0, out_rows)]
    others = [lax.rem(z + k, depth) for k in range(1, depth)]
    greet([{"ctx": flip(c, k)} for k in (1, 2, 4)] + [{"fsdp": o} for o in others])
    gu_line = Line(z, depth, lambda d: gu_all.at[d], usend, urecv)
    down_line = Line(z, depth, lambda d: down_all.at[d], dsend, drecv)
    down_line.step(1)
    gu_line.step(2)
    loads = [
        pltpu.make_async_copy(ow_ref, out_w, load.at[0]),
        pltpu.make_async_copy(g_ref, grads, load.at[1]),
        pltpu.make_async_copy(x_ref, two.at[c], load.at[2]),
    ]
    for d in loads:
        d.start()

    loads[0].wait()
    loads[2].wait()
    mixed_ref[...] = two[c].astype(F32)

    @pl.loop(0, 8)
    def _(i):
        mixed_ref[...] += contract(both_blocks(got, i), p1[i, :out_rows], ((0,), (0,)))

    gain = jnp.concatenate([gains_ref[k, 4:5, :] for k in range(depth)], 1)
    halves = [pl.ds(q * (rows // 2), rows // 2) for q in (0, 1)]
    for at in halves:
        x = mixed_ref[at]
        factor = lax.rsqrt(jnp.mean(x * x, -1, keepdims=True) + EPS)
        two[c, at] = (x * factor * gain).astype(BF16)
    g = Gather(c, own_half(two.at[c]), two, row_half, send, recv)
    g.begin()
    loads[1].wait()
    down_line.landed(1)
    down_line.step(2)

    def pair(k):
        chip = pl.ds(flip(c, k) // 2 * 2, 2)
        tall = 2 * rows
        up_w = wgu[...].reshape(width, both)
        down_w = wd[...].reshape(mine, width)
        gate_up = jnp.dot(two[chip].reshape(tall, width), up_w, preferred_element_type=F32)
        gate, up = gate_up[:, :mine], gate_up[:, mine:]
        sigma = jax.nn.sigmoid(gate)
        silu = gate * sigma
        active = (silu * up).astype(BF16)
        act[chip] = active.reshape(2, rows, mine)
        active_grad = contract(grads[chip].reshape(tall, width), down_w, ((1,), (1,)))
        gate_grad = active_grad * up * sigma * (1.0 + gate * (1.0 - sigma))
        up_grad = active_grad * silu
        grad = jnp.concatenate([gate_grad, up_grad], 1).astype(BF16)
        dgu[chip] = grad.reshape(2, rows, both)
        p2[chip] = contract(grad, up_w, ((1,), (1,))).astype(BF16).reshape(2, rows, width)
        scatter.give(k)
        p1[chip] = jnp.dot(active, down_w, preferred_element_type=F32).astype(BF16).reshape(2, rows, width)
        layer.give(k)

    scatter = Scatter(c, p2, *scatter_refs)
    layer = Scatter(c, p1, *layer_refs)
    g.near_half()
    gu_line.landed(2)
    weights = [pltpu.make_async_copy(gu_all, wgu, load.at[2]), pltpu.make_async_copy(down_all, wd, load.at[3])]
    weights[0].start()
    g.near_rest()
    down_line.landed(2)
    weights[1].start()
    g.far()
    for d in weights:
        d.wait()
    g.paired(5, 7)
    pair(6)
    g.paired(3, 3)
    scatter.far()
    pair(2)
    scatter.paired(1, 0)
    scatter.onward(1, 0, False)
    layer.far()
    g.paired(4, 5)
    pair(4)
    scatter.paired(2, 1)
    scatter.onward(2, 1, False)
    g.paired(0, 1)
    pair(0)

    puts = []

    def wide(f):
        part = lambda i, total: total + contract(
            two[pl.ds(2 * i, 2), :, f * shard : (f + 1) * shard].reshape(2 * rows, shard),
            dgu[pl.ds(2 * i, 2)].reshape(2 * rows, both),
            ((0,), (0,)),
        )
        wgu[f] = lax.fori_loop(0, 4, part, jnp.zeros((shard, both), F32)).astype(BF16)
        puts.append(pltpu.make_async_copy(wgu.at[f], gug_ref.at[f], wput.at[f]))
        puts[-1].start()

    wide(0)
    scatter.merged()
    layer.direct()
    layer.settle()
    layer.given()
    again = pltpu.make_async_copy(ow_ref, out_w, load.at[0])
    again.start()
    for f in range(1, depth):
        wide(f)

    hop_right = remote(wgu.at[depth - 1], left_ref, hsend.at[0], hrecv.at[0], fsdp=z + 1)
    hop_left = remote(wgu.at[0], right_ref, hsend.at[1], hrecv.at[1], fsdp=z - 1)

    @pl.when(z == 0)
    def _():
        hop_right.start()

    @pl.when(z == depth - 1)
    def _():
        hop_left.start()

    strip = mine // depth
    for f in range(0, depth, 2):
        part = lambda i, total: total + contract(
            act[pl.ds(2 * i, 2), :, f * strip : (f + 2) * strip].reshape(2 * rows, 2 * strip),
            grads[pl.ds(2 * i, 2)].reshape(2 * rows, width),
            ((0,), (0,)),
        )
        part = lax.fori_loop(0, 4, part, jnp.zeros((2 * strip, width), F32))
        wd[f : f + 2] = part.astype(BF16).reshape(2, strip, width)
    puts.append(pltpu.make_async_copy(wd, dg_ref, wput.at[depth]))
    puts[-1].start()

    g.sent()
    gain_sum = jnp.zeros((1, width), F32)
    for q, at in enumerate(halves):
        two_grad = scatter.result(q)
        x = mixed_ref[at]
        factor = lax.rsqrt(jnp.mean(x * x, -1, keepdims=True) + EPS)
        gain_sum = gain_sum + jnp.sum(two_grad * x * factor, 0, keepdims=True)
        scaled = two_grad * gain
        mixed_grad = (
            grads[c, at].astype(F32)
            + factor * scaled
            - x * (factor * factor * factor) * jnp.mean(scaled * x, -1, keepdims=True)
        )
        mgrad_ref[at] = mixed_grad
        two[0, at] = mixed_grad.astype(BF16)
    gsum_ref[...] = jnp.broadcast_to(gain_sum, gsum_ref.shape)
    again.wait()
    for i in range(8):
        part = contract(p1[i, :out_rows], two[0], ((1,), (1,))).astype(BF16)
        give[2 * i] = part[:, :BLOCK]
        give[2 * i + 1] = part[:, BLOCK:]
    layer.merged()
    few = out_rows // depth
    for i in range(8):
        part = jnp.dot(both_blocks(got, i), two[0], preferred_element_type=F32).astype(BF16)
        f = i * depth // 8
        for t in range(depth):
            p1[i * depth % 8 + t, f * few : (f + 1) * few] = part[t * few : (t + 1) * few]
    out_put = pltpu.make_async_copy(out_w, owg_ref, load.at[0])
    out_put.start()
    scatter.sent()
    for q, at in enumerate(halves):
        p2[0, at] = (mixed_ref[at] + layer.result(q)).astype(BF16)
    layer_put = pltpu.make_async_copy(p2.at[0], layer_ref, load.at[1])
    layer_put.start()

    @pl.when(z == 0)
    def _():
        hop_right.wait_send()

    @pl.when(z == depth - 1)
    def _():
        hop_left.wait_send()

    @pl.when(z == 1)
    def _():
        remote(left_ref, left_ref, hsend.at[0], hrecv.at[0], fsdp=z - 1).wait_recv()

    @pl.when(z == depth - 2)
    def _():
        remote(right_ref, right_ref, hsend.at[1], hrecv.at[1], fsdp=z + 1).wait_recv()

    out_put.wait()
    for d in puts:
        d.wait()
    layer_put.wait()
    layer.sent()
    gu_line.sent((2,))
    down_line.sent((1, 2))


def middle(got, x, gains, grad_all, out_w, gate_up, down, cid):
    rows, width = x.shape
    depth, shard, both = gate_up.shape
    shape = jax.ShapeDtypeStruct
    vm = pl.BlockSpec(memory_space=VMEM)
    hbm = pl.BlockSpec(memory_space=ANY)
    heads = (8 * rows // BLOCK, 2 * HEAD_SIZE, BLOCK)
    block = (8, rows, width)
    return pl.pallas_call(
        middle_kernel,
        out_shape=(
            shape((rows, width), BF16),
            shape((rows, width), F32),
            shape((8, width), F32),
            shape(heads, BF16),
            shape(out_w.shape, BF16),
            shape(gate_up.shape, BF16),
            shape(down.shape, BF16),
            shape((shard, both), BF16),
            shape((shard, both), BF16),
            shape(gate_up.shape, BF16),
            shape(down.shape, BF16),
        ),
        in_specs=[vm, hbm, vm, hbm, hbm, hbm, hbm],
        out_specs=(hbm, vm, vm, vm, hbm, hbm, hbm, hbm, hbm, hbm, hbm),
        scratch_shapes=[
            VMEM((rows, width), F32),
            VMEM(block, BF16),
            VMEM(gate_up.shape, BF16),
            VMEM(down.shape, BF16),
            VMEM(block, BF16),
            VMEM(block, BF16),
            VMEM(block, BF16),
            VMEM((8, rows, both // 2), BF16),
            VMEM((8, rows, both), BF16),
        ]
        + Scatter.scratch(rows, width)
        + Scatter.scratch(rows, width)
        + [DMA((8, 2))] * 2
        + [DMA((2, depth))] * 4
        + [DMA((4,)), DMA((depth + 1,)), DMA((2,)), DMA((2,))],
        input_output_aliases={5: 9, 6: 10},
        compiler_params=params(cid),
        name="middle",
    )(got, x, gains, grad_all, out_w, gate_up, down)


class LineScatter:
    def __init__(self, z, own, left, right, send, recv):
        self.z, self.own, self.left, self.right = z, own, left, right
        self.send, self.recv = send, recv
        self.top = own.shape[0] - 1
        self.begun = None

    @staticmethod
    def scratch(shape):
        depth = shape[0]
        hops = (depth - 1,) + tuple(shape[1:])
        return [VMEM(hops, BF16), VMEM(hops, BF16), DMA((2, depth)), DMA((2, depth))]

    def copy(self, way, s, part, to):
        there = (self.left, self.right)[way].at[s]
        return remote(self.own.at[part], there, self.send.at[way, s], self.recv.at[way, s], fsdp=to)

    def landed(self, way, s):
        if s == 0 and self.begun:
            self.begun[way].wait()
            return
        ref = (self.left, self.right)[way].at[s]
        remote(ref, ref, self.send.at[way, s], self.recv.at[way, s], fsdp=self.z - 1 + 2 * way).wait_recv()

    def step(self, s):
        z, top = self.z, self.top
        for way in (0, 1):
            place = z if way == 0 else top - z
            part = top - s + z if way == 0 else s - top + z

            @pl.when((place <= s) & (place < top))
            def _():
                if s:

                    @pl.when(place > 0)
                    def _():
                        self.landed(way, s - 1)
                        came = (self.left, self.right)[way][s - 1]
                        self.own[part] = (self.own[part].astype(F32) + came.astype(F32)).astype(BF16)

                self.copy(way, s, part, z + 1 - 2 * way).start()

    def result(self):
        z, last = self.z, self.top - 1

        def close(ways):
            total = self.own[z].astype(F32)
            for way in ways:
                self.landed(way, last)
                total = total + (self.left, self.right)[way][last].astype(F32)
            self.own[z] = total.astype(BF16)

        @pl.when(z == 0)
        def _():
            close((1,))

        @pl.when((z > 0) & (z < self.top))
        def _():
            close((0, 1))

        @pl.when(z == self.top)
        def _():
            close((0,))

    def sent(self):
        z, top = self.z, self.top
        for s in range(1 if self.begun else 0, top):
            for way in (0, 1):
                place = z if way == 0 else top - z
                part = top - s + z if way == 0 else s - top + z

                @pl.when((place <= s) & (place < top))
                def _():
                    self.copy(way, s, part, z + 1 - 2 * way).wait_send()


def back_kernel(
    order_ref, rank_ref, qkv_ref, o_ref, give, lse_ref, table_ref, w_ref, gains_ref, gain_two_ref,
    mgrad_ref, x_ref, all_ref, owg_ref, gug_ref, dg_ref, left_ref, right_ref,
    input_ref, sum_ref, gu_all, down_all, q_all, o_all,
    do_ref, keys, keys_t, values, dk, dv, dqn, dqkv, acc, xs, big, owg, gug, down, heads, outs,
    gain_rows, by_z, part_sum, by_c, first, last, diagonal, first2, last2, diagonal2, *rest,
):
    scatter_sems = (rest[:4], rest[4:8])
    lines = (rest[8:12], rest[12:16], rest[16:20], rest[20:24])
    send, recv, local, load, xload, zs, zr, cs, cr, esend, erecv = rest[24:]
    c = lax.axis_index("ctx")
    z = lax.axis_index("fsdp")
    depth, shard = heads.shape[0], heads.shape[2]
    rows, width = xs.shape[1:]
    others = [lax.rem(z + k, depth) for k in range(1, depth)]
    greet([{"ctx": flip(c, k)} for k in range(1, 8)] + [{"fsdp": o} for o in others])
    some = acc.at[pl.ds(0, rows)]
    loads = [
        pltpu.make_async_copy(a, t, load.at[i])
        for i, (a, t) in enumerate(
            ((gug_ref, gug), (owg_ref, owg), (dg_ref, down), (mgrad_ref, some), (x_ref, xs.at[0]))
        )
    ]
    for d in loads[:3]:
        d.start()
    gu_line, down_line, q_line, o_line = (
        LineScatter(z, a, *refs) for a, refs in zip((gug, down, heads, outs), lines)
    )
    gu_line.begun = (
        pltpu.make_async_copy(left_ref, gu_line.left.at[0], load.at[5]),
        pltpu.make_async_copy(right_ref, gu_line.right.at[0], load.at[6]),
    )

    @pl.when(z == 1)
    def _():
        gu_line.begun[0].start()

    @pl.when(z == depth - 2)
    def _():
        gu_line.begun[1].start()

    out = Scatter(c, owg, first2, last2, diagonal2, *scatter_sems[0])
    one = Scatter(c, big, first, last, diagonal, *scatter_sems[1])

    sent = exchange_start(c, give, do_ref, esend, erecv)
    do_ref[pl.ds(2 * c, 2)] = give[pl.ds(2 * c, 2)]
    blocks = qkv_ref.shape[0]
    per = CHUNK // BLOCK
    scale = HEAD_SIZE ** (-0.5)
    factor = scale * math.log2(math.e)
    half = HEAD_SIZE // 2
    for b in range(blocks):
        there = slice(b * BLOCK, (b + 1) * BLOCK)
        key = qkv_ref[order_ref[b], 2 * HEAD_SIZE : 3 * HEAD_SIZE]
        keys[there, :] = key.T
        keys_t[:, there] = key
        values[there, :] = qkv_ref[order_ref[b], 3 * HEAD_SIZE :].T
    dk[...] = jnp.zeros_like(dk)
    dv[...] = jnp.zeros_like(dv)
    loads[0].wait()
    gu_line.step(1)
    loads[2].wait()
    down_line.step(0)
    loads[1].wait()
    for k in Scatter.ORDER:
        out.give(k)
    exchange_landed(c, do_ref, esend, erecv)

    def attend_block(j, last):
        block = order_ref[j]
        q = two_heads(qkv_ref, block)
        do = two_heads(do_ref, block)
        delta = jnp.sum(two_heads(o_ref, j).astype(F32) * do.astype(F32), 0, keepdims=True)
        lse = lse_ref[j]

        def step(t, dq, masked):
            there = pl.ds(t * CHUNK, CHUNK)
            s = jnp.dot(keys[there, :], q, preferred_element_type=F32)
            if masked:
                s = causal(s, t, j)
            p = jnp.exp2(s * factor - lse)
            dp = jnp.dot(values[there, :], do, preferred_element_type=F32)
            ds = (p * (dp - delta)).astype(BF16)
            wide = pl.ds(t * per, per)
            dv[wide] += contract(p.astype(BF16), do, ((1,), (1,))).reshape(per, BLOCK, HEAD_SIZE)
            dk[wide] += contract(ds, q, ((1,), (1,))).reshape(per, BLOCK, HEAD_SIZE)
            return dq + jnp.dot(keys_t[:, there], ds, preferred_element_type=F32)

        dq = jnp.zeros((HEAD_SIZE, 2 * BLOCK), F32)
        for t in range(last):
            dq = step(t, dq, False)
        dq = step(last, dq, True) * scale
        cosine, sine = table_ref[block, :half], table_ref[block, half:]
        for h in (0, 1):
            part = dq[:, h * BLOCK : (h + 1) * BLOCK]
            dqn[j, h * HEAD_SIZE : (h + 1) * HEAD_SIZE] = turned(part, cosine, -sine).astype(BF16)

    for turn in range(blocks // per):

        @pl.loop(turn * per, (turn + 1) * per)
        def _(j):
            attend_block(j, turn)

        if turn == 0:
            out.far()
        if turn == 1:
            out.direct()
        if turn == 2:
            out.merged()
            gu_line.step(2)

    for i in range(blocks):
        to = slice(i * BLOCK, (i + 1) * BLOCK)
        natural = rank_ref[i]
        dqkv[: 2 * HEAD_SIZE, to] = dqn[natural]
        dqkv[2 * HEAD_SIZE : 3 * HEAD_SIZE, to] = turned(
            dk[natural].T * scale, table_ref[i, :half], -table_ref[i, half:]
        ).astype(BF16)
        dqkv[3 * HEAD_SIZE :, to] = dv[natural].T.astype(BF16)

    def x_load(d, slot):
        return pltpu.make_async_copy(all_ref.at[d], xs.at[slot], xload.at[slot])

    down_line.step(1)
    for block in Scatter.ORDER:
        for d in (flip(c, 1 ^ block), flip(c, block)):
            big[d] = contract(dqkv[:, lanes(d * rows, rows)], w_ref[...], ((0,), (0,))).astype(BF16)
        one.give(block)
    x_load(0, 0).start()
    x_load(1, 1).start()
    one.far()
    gu_line.result()
    here = []
    gathers = []

    def spread(i, source, everyone):
        here.append(pltpu.make_async_copy(source, everyone.at[c], local.at[i]))
        here[-1].start()
        at, own = (row_half, own_half(source)) if source.shape[0] % 32 == 0 else (column_half, own_half(source, 1))
        gathers.append(Gather(c, own, everyone, at, send.at[i], recv.at[i]))
        gathers[-1].begin_half()
        if i:
            gathers[-1].begin_rest()

    spread(0, gug.at[z], gu_all)
    one.direct()
    outs[...] = jnp.concatenate([out.result(0), out.result(1)], 0).astype(BF16).reshape(outs.shape)
    o_line.step(0)
    acc[...] = jnp.zeros_like(acc)
    for d in range(8):
        slot = d % 2
        x_load(d, slot).wait()
        acc[...] += jnp.dot(dqkv[:, d * rows : (d + 1) * rows], xs[slot], preferred_element_type=F32)
        if d + 2 < 8:
            x_load(d + 2, slot).start()
        if d == 3:
            one.merged()
            gathers[0].begin_rest()
    for f in range(depth):
        heads[f] = acc[:, f * shard : (f + 1) * shard].astype(BF16)
    loads[3].start()
    loads[4].start()
    q_line.step(0)
    down_line.step(2)
    q_line.step(1)
    o_line.step(1)

    gain = jnp.concatenate([gains_ref[k, 0:1, :] for k in range(depth)], 1)
    gathers[0].near_half()
    loads[3].wait()
    loads[4].wait()
    gain_sum = jnp.zeros((1, width), F32)
    for q in (0, 1):
        at = pl.ds(q * (rows // 2), rows // 2)
        one_grad = one.result(q)
        x = xs[0, at].astype(F32)
        norm = lax.rsqrt(jnp.mean(x * x, -1, keepdims=True) + EPS)
        gain_sum = gain_sum + jnp.sum(one_grad * x * norm, 0, keepdims=True)
        scaled = one_grad * gain
        grad = norm * scaled - x * (norm * norm * norm) * jnp.mean(scaled * x, -1, keepdims=True)
        xs[1, at] = (acc[at] + grad).astype(BF16)
    here.append(pltpu.make_async_copy(xs.at[1], input_ref, xload.at[0]))
    here[-1].start()
    gain_rows[:4] = jnp.broadcast_to(gain_sum, (4, width))
    gain_rows[4:] = gain_two_ref[4:]
    for k, o in enumerate(others):
        d = remote(gain_rows.at[:, lanes(o * shard, shard)], by_z.at[z], zs.at[k], zr.at[k], fsdp=o)
        d.start()
        sent.append(d)
    q_line.step(2)
    o_line.step(2)
    down_line.result()
    spread(1, down.at[z], down_all)
    gathers[0].near_rest()
    gathers[0].far()
    q_line.result()
    spread(2, heads.at[z], q_all)
    o_line.result()
    spread(3, outs.at[z], o_all)

    total = gain_rows[:, lanes(z * shard, shard)]
    for k in range(depth - 1):
        ref = by_z.at[lax.rem(z + depth - 1 - k, depth)]
        remote(ref, ref, zs.at[k], zr.at[k], fsdp=others[k]).wait_recv()
        total = total + by_z[lax.rem(z + depth - 1 - k, depth)]
    part_sum[...] = total
    for k in range(1, 8):
        d = remote(part_sum, by_c.at[c], cs.at[k], cr.at[k], ctx=flip(c, k))
        d.start()
        sent.append(d)
    by_c[c] = total

    for g in gathers[1:]:
        g.near_half()
    for g in gathers[1:]:
        g.near_rest()
    for g in gathers[1:]:
        g.far()
    for g in gathers:
        for channel, k in ((0, 1), (3, 3), (4, 5), (5, 7)):
            g.paired(channel, k)
    for k in range(1, 8):
        ref = by_c.at[flip(c, k)]
        remote(ref, ref, cs.at[k], cr.at[k], ctx=flip(c, k)).wait_recv()
    total = by_c[0]
    for k in range(1, 8):
        total = total + by_c[k]
    sum_ref[...] = total
    for d in here:
        d.wait()
    for d in sent:
        d.wait_send()
    out.sent()
    one.sent()
    for line in (gu_line, down_line, q_line, o_line):
        line.sent()
    for g in gathers:
        g.sent()


def back(order, rank, arrays, large, depth, cid):
    blocks = arrays[0].shape[0]
    tokens = blocks * BLOCK
    rows, width = large[0].shape
    out_rows = large[3].shape[1]
    gate_up, down = large[4], large[5]
    shard = gate_up.shape[1]
    shape = jax.ShapeDtypeStruct
    vm = pl.BlockSpec(memory_space=VMEM)
    hbm = pl.BlockSpec(memory_space=ANY)
    sm = pl.BlockSpec(memory_space=pltpu.SMEM)
    tall = (tokens, HEAD_SIZE)
    small = (8, shard)
    lines = (gate_up.shape, down.shape, (depth, 4 * HEAD_SIZE, shard), (depth, out_rows // depth, width))
    scatter = Scatter.scratch(rows, width)
    return pl.pallas_call(
        back_kernel,
        out_shape=[shape((rows, width), BF16), shape(small, F32)]
        + [shape((8,) + a[1:], BF16) for a in lines],
        in_specs=[sm, sm] + [vm] * len(arrays) + [hbm] * len(large),
        out_specs=[hbm, vm] + [hbm] * 4,
        scratch_shapes=[
            VMEM((blocks, 2 * HEAD_SIZE, BLOCK), BF16),
            VMEM(tall, BF16),
            VMEM(tall[::-1], BF16),
            VMEM(tall, BF16),
            VMEM((blocks, BLOCK, HEAD_SIZE), F32),
            VMEM((blocks, BLOCK, HEAD_SIZE), F32),
            VMEM((blocks, 2 * HEAD_SIZE, BLOCK), BF16),
            VMEM((4 * HEAD_SIZE, tokens), BF16),
            VMEM((4 * HEAD_SIZE, width), F32),
            VMEM((2, rows, width), BF16),
            VMEM((8, rows, width), BF16),
            VMEM((8, out_rows, width), BF16),
        ]
        + [VMEM(a, BF16) for a in lines]
        + [VMEM((8, width), F32), VMEM((depth,) + small, F32), VMEM(small, F32), VMEM((8,) + small, F32)]
        + scatter[:3]
        + Scatter.scratch(out_rows, width)[:3]
        + scatter[3:] * 2
        + [r for a in lines for r in LineScatter.scratch(a)]
        + [DMA((4, 8, 2)), DMA((4, 8, 2)), DMA((4,)), DMA((9,)), DMA((2,))]
        + [DMA((depth,)), DMA((depth,)), DMA((8,)), DMA((8,)), DMA((8,)), DMA((8,))],
        compiler_params=params(cid),
        name="back",
    )(order, rank, *arrays, *large)


def widen(gate_up, down, out, sums, layer, grad):
    _, shard, both = gate_up.shape
    mine = both // 2
    strips = mine // LANES
    step = shard // 8
    _, rows, width = down.shape

    def kernel(a_ref, d_ref, o_ref, s_ref, l_ref, g_ref, gate_ref, up_ref, down_ref, out_ref, one_ref, two_ref, layer_ref, grad_ref):
        layer_ref[0] = l_ref[...]
        grad_ref[0] = g_ref[...]
        for i, target in enumerate((gate_ref, up_ref)):
            for c in range(8):
                for s in range(strips):
                    target[:, (s * 8 + c) * LANES : (s * 8 + c + 1) * LANES] = a_ref[
                        c, :, i * mine + s * LANES : i * mine + (s + 1) * LANES
                    ].astype(F32)
        down_ref[...] = d_ref[0].astype(F32)
        out_ref[...] = o_ref[0].astype(F32)
        one_ref[...] = s_ref[0]
        two_ref[...] = s_ref[4]

    wide = jax.ShapeDtypeStruct((shard, 8 * mine), F32)
    gain = jax.ShapeDtypeStruct((shard,), F32)
    by_rows = lambda n, columns: pl.BlockSpec((n, columns), lambda i: (i, 0))
    by_device = lambda a: pl.BlockSpec((1,) + a.shape[1:], lambda i: (i, 0, 0))
    return pl.pallas_call(
        kernel,
        grid=(8,),
        out_shape=(
            wide,
            wide,
            jax.ShapeDtypeStruct((8 * rows, width), F32),
            jax.ShapeDtypeStruct((shard, width), F32),
            gain,
            gain,
        )
        + (jax.ShapeDtypeStruct((1,) + layer.shape, BF16),) * 2,
        in_specs=[
            pl.BlockSpec((8, step, both), lambda i: (0, i, 0)),
            by_device(down),
            by_device(out),
            pl.BlockSpec(sums.shape, lambda i: (0, 0)),
        ]
        + [by_rows(layer.shape[0] // 8, width)] * 2,
        out_specs=(by_rows(step, 8 * mine), by_rows(step, 8 * mine), by_rows(rows, width), by_rows(step, width))
        + (pl.BlockSpec((shard,), lambda i: (0,)),) * 2
        + (pl.BlockSpec((1, layer.shape[0] // 8, width), lambda i: (0, i, 0)),) * 2,
        compiler_params=pltpu.CompilerParams(vmem_limit_bytes=VMEM_BYTES),
        name="widen",
    )(gate_up, down, out, sums, layer, grad)


def widen_heads(qkv):
    shard = qkv.shape[2]
    per_q = 2 * HEAD_SIZE
    heads = 8 * HEAD_SIZE

    def kernel(a_ref, q_out, k_out, v_out):
        for c in range(0, 8, 2):
            both = jnp.concatenate([a_ref[c + i, :per_q, :] for i in (0, 1)], 0)
            q_out[:, c * per_q : (c + 2) * per_q] = both.T.astype(F32)
        for target, first in ((k_out, per_q), (v_out, per_q + HEAD_SIZE)):
            for c in range(0, 8, 4):
                four = jnp.concatenate([a_ref[c + i, first : first + HEAD_SIZE, :] for i in range(4)], 0)
                target[:, c * HEAD_SIZE : (c + 4) * HEAD_SIZE] = four.T.astype(F32)

    by_rows = lambda n: pl.BlockSpec((LANES, n), lambda i: (i, 0))
    shape = lambda n: jax.ShapeDtypeStruct((shard, n), F32)
    return pl.pallas_call(
        kernel,
        grid=(shard // LANES,),
        out_shape=(shape(2 * heads), shape(heads), shape(heads)),
        in_specs=[pl.BlockSpec((8, 4 * HEAD_SIZE, LANES), lambda i: (0, 0, i))],
        out_specs=(by_rows(2 * heads), by_rows(heads), by_rows(heads)),
        compiler_params=pltpu.CompilerParams(vmem_limit_bytes=VMEM_BYTES),
        name="widen_heads",
    )(qkv)


def in_plane(
    depth,
    hidden_in,
    positions,
    attn_gain,
    w_query,
    key_projection,
    value_projection,
    w_out,
    mlp_gain,
    w_gate,
    w_up,
    w_down,
    out_grad,
):
    plane = 8
    rows, width = hidden_in.shape[1:]
    shard = width // depth
    half = HEAD_SIZE // 2

    gains = (attn_gain, mlp_gain)
    freq = np.float32(THETA) ** (-(np.arange(half, dtype=np.float32) * np.float32(2.0) / np.float32(HEAD_SIZE)))
    inner = freq[:, None] * np.arange(BLOCK, dtype=np.float32)[None]
    step = jnp.asarray(np.concatenate([np.cos(inner), np.sin(inner)], 0).astype(np.float32))
    freq = jnp.asarray(np.broadcast_to(freq[:, None], (half, LANES)).astype(np.float32))

    hidden_low = hidden_in[0]
    weights = (w_query, key_projection, value_projection, w_out, w_gate, w_up, w_down)
    grad_low = out_grad[0]
    (normed_all, qkv, qkv_w, table, gains_all, order, rank, attended_low, lse, got, out_w, gate_up_w, down_w, grad_all) = first_part(
        positions, hidden_low, gains, freq, step, weights, grad_low, depth, 0
    )
    (layer_out, mixed_grad, gain_two_grad, do, out_wgrad, gate_up_wgrad, down_wgrad, left, right, _, _) = middle(
        got, hidden_low, gains_all, grad_all, out_w.reshape(plane, -1, width), gate_up_w, down_w, 2
    )
    arrays = (qkv, attended_low, do, lse, table, qkv_w, gains_all, gain_two_grad)
    large = (mixed_grad, hidden_low, normed_all, out_wgrad, gate_up_wgrad, down_wgrad, left, right)
    input_grad, gain_sums, gate_up_all, down_all, qkv_all, out_grads = back(order, rank, arrays, large, depth, 3)
    query_total, key_total, value_total = widen_heads(qkv_all)
    gate_total, up_total, down_total, out_total, gain_one, gain_two, layer_out, input_grad = widen(
        gate_up_all, down_all, out_grads, gain_sums, layer_out, input_grad
    )
    return (
        layer_out,
        input_grad,
        gain_one,
        query_total,
        key_total,
        value_total,
        out_total,
        gain_two,
        gate_total,
        up_total,
        down_total,
    )


def solution(mesh):
    placed = (
        P("fsdp", "ctx", None),
        P("fsdp", "ctx"),
        P("fsdp"),
        P("fsdp", None),
        P("fsdp", None),
        P("fsdp", None),
        P("fsdp", None),
        P("fsdp"),
        P("fsdp", None),
        P("fsdp", None),
        P("fsdp", None),
        P("fsdp", "ctx", None),
    )
    body = per_device
    if mesh.shape["ctx"] == KEY_VALUE_HEADS:
        body = functools.partial(in_plane, mesh.shape["fsdp"])
    return jax.shard_map(
        body,
        mesh=mesh,
        in_specs=placed,
        out_specs=(
            P("fsdp", "ctx", None),
            P("fsdp", "ctx", None),
            P("fsdp"),
            P("fsdp", None),
            P("fsdp", None),
            P("fsdp", None),
            P("fsdp", None),
            P("fsdp"),
            P("fsdp", None),
            P("fsdp", None),
            P("fsdp", None),
        ),
        check_vma=False,
    )
```
